32 devices in a mesh: batch: 8 (over z, core), seq: 4 (over y, x).
Axes of the slice: x: 2, y: 2, z: 4, core: 2. Of those that a mesh axis runs over, the one named last changes fastest.
Arguments:
- hidden_in: bfloat16 [16, 1024, 768], P('batch', 'seq'), may hold values from -7 to 7
- seg_bounds: int32 [16, 65], P('batch'), may hold values from 0 to 1024, as said below
- qkv_weight: bfloat16 [768, 2304], replicated, may hold values from -0.3125 to 0.3125
- query_bias: float32 [768], replicated, may hold values from -3 to 3
- value_bias: float32 [768], replicated, may hold values from -3 to 3
- conv_taps: float32 [12, 33], replicated, may hold values from -3 to 3
- out_weight: bfloat16 [768, 768], replicated, may hold values from -0.21875 to 0.21875
- out_bias: float32 [768], replicated, may hold values from -3 to 3
- first_gain: float32 [768], replicated, may hold values from 0.5 to 1.5
- first_shift: float32 [768], replicated, may hold values from -3 to 3
- up_weight: bfloat16 [768, 3072], replicated, may hold values from -0.21875 to 0.21875
- up_bias: float32 [3072], replicated, may hold values from -3 to 3
- down_weight: bfloat16 [3072, 768], replicated, may hold values from -0.109375 to 0.109375
- down_bias: float32 [768], replicated, may hold values from -3 to 3
- second_gain: float32 [768], replicated, may hold values from 0.5 to 1.5
- second_shift: float32 [768], replicated, may hold values from -3 to 3
- grad_out: bfloat16 [16, 1024, 768], P('batch', 'seq'), may hold values from -6 to 6
Outputs:
- layer_out: bfloat16 [16, 1024, 768], P('batch', 'seq')
- input_grad: bfloat16 [16, 1024, 768], P('batch', 'seq')
- qkv_grad: float32 [768, 2304], replicated
- query_bias_grad: float32 [768], replicated
- value_bias_grad: float32 [768], replicated
- conv_grad: float32 [12, 33], replicated
- out_weight_grad: float32 [768, 768], replicated
- out_bias_grad: float32 [768], replicated
- first_gain_grad: float32 [768], replicated
- first_shift_grad: float32 [768], replicated
- up_weight_grad: float32 [768, 3072], replicated
- up_bias_grad: float32 [3072], replicated
- down_weight_grad: float32 [3072, 768], replicated
- down_bias_grad: float32 [768], replicated
- second_gain_grad: float32 [768], replicated
- second_shift_grad: float32 [768], replicated
- condition: float32 [12], replicated
The draws below stay inside these ranges and needn't reach their ends.
Inputs may be any that keep to these rules, and one draw needn't show every extreme that they name: `seg_bounds`: each row rises strictly from 0 and ends at the sequence's true length, at least 512; among the 2 sequences of each index of batch one has the length 1024.
All inputs are finite; a program needn't handle non-finite values.
Results may differ from the reference program's by a relative error of at most 0.03.
Values may be sent and summed in bfloat16 or wider, within the bound.
A program may use at most 192 MiB of HBM per device.

```python
import math
import jax
import jax.numpy as jnp
from jax import lax

D = 768
HEADS = 12
FF = 3072
SEGS = 64
CONV = 33
NEWTON = 6
SEQS = 2
LEN = 1024
NSEQ = 16


def draw_hidden_in(key, part):
    key = jax.random.fold_in(key, 11)
    base_key, noise_key = jax.random.split(key)
    base = jnp.clip(jax.random.normal(base_key, (NSEQ, LEN // 16, D), jnp.float32), -4.0, 4.0)
    noise = 0.7 * jnp.clip(jax.random.normal(noise_key, (NSEQ, LEN, D), jnp.float32), -4.0, 4.0)
    return (jnp.repeat(base, 16, axis=1) + noise).astype(jnp.bfloat16)


def draw_seg_bounds(key, part):
    key = jax.random.fold_in(key, 7)
    length_key, chosen_key, weight_key = jax.random.split(key, 3)
    lengths = jax.random.randint(length_key, (NSEQ,), LEN // 2, LEN + 1)
    full_index = jax.random.randint(chosen_key, (NSEQ // SEQS,), 0, SEQS)
    chosen = jnp.arange(NSEQ, dtype=jnp.int32) % SEQS == jnp.repeat(full_index, SEQS)
    lengths = jnp.where(chosen, LEN, lengths).astype(jnp.int32)
    seg_weights = jax.random.randint(weight_key, (NSEQ, SEGS), 1, 4)
    cumulative = jnp.cumsum(seg_weights, axis=1)
    edges = cumulative * lengths[:, None] // cumulative[:, SEGS - 1:SEGS]
    return jnp.concatenate([jnp.zeros((NSEQ, 1), jnp.int32), edges.astype(jnp.int32)], axis=1)


def block_scale(own_key, extent, cuts, smallest, largest):
    factor_of, own = 1.0, jax.random.fold_in(own_key, 6)
    for dim, blocks in cuts:
        heights = jnp.exp(jax.random.uniform(jax.random.fold_in(own, dim), (blocks,), jnp.float32, smallest / len(cuts), largest / len(cuts)))
        factor_of = factor_of * jnp.repeat(heights, extent[dim] // blocks).reshape([-1 if axis == dim else 1 for axis in range(len(extent))])
    return factor_of


def bell_draw(own_key, shape, scale, most, pieces=(), held_as=jnp.bfloat16):
    values = jax.random.normal(own_key, shape, jnp.float32) * scale
    if len(pieces) > 0:
        values = block_scale(own_key, shape, pieces, -0.22, 0.18) * values
    return jnp.clip(values, min=-most, max=most).astype(held_as)


def setup_inputs(seed: int = 0) -> dict:
    key_of = jax.random.split(jax.random.key(seed), 18)
    hidden_in = draw_hidden_in(jax.random.fold_in(key_of[17], 71), 0)
    seg_bounds = draw_seg_bounds(jax.random.fold_in(key_of[17], 71), 0)
    qkv_weight = bell_draw(key_of[2], (D, 3 * D), (D // 2) ** -0.5, 0.3125)
    query_bias = bell_draw(key_of[3], (D,), 0.5, 3.0, (), jnp.float32)
    value_bias = bell_draw(key_of[4], (D,), 0.5, 3.0, (), jnp.float32)
    conv_taps = bell_draw(key_of[5], (HEADS, CONV), (max(1, CONV // 8)) ** -0.5, 3.0, (), jnp.float32)
    out_weight = bell_draw(key_of[6], (D, D), D ** -0.5, 0.21875)
    out_bias = bell_draw(key_of[7], (D,), 0.5, 3.0, (), jnp.float32)
    first_gain = jnp.clip(1.0 + 0.1 * jax.random.normal(key_of[8], (D,), jnp.float32), 0.5, 1.5)
    first_shift = bell_draw(key_of[9], (D,), 0.5, 3.0, (), jnp.float32)
    up_weight = bell_draw(key_of[10], (D, FF), D ** -0.5, 0.21875)
    up_bias = bell_draw(key_of[11], (FF,), 0.5, 3.0, (), jnp.float32)
    down_weight = bell_draw(key_of[12], (FF, D), FF ** -0.5, 0.109375)
    down_bias = bell_draw(key_of[13], (D,), 0.5, 3.0, (), jnp.float32)
    second_gain = jnp.clip(1.0 + 0.1 * jax.random.normal(key_of[14], (D,), jnp.float32), 0.5, 1.5)
    second_shift = bell_draw(key_of[15], (D,), 0.5, 3.0, (), jnp.float32)
    grad_out = bell_draw(key_of[16], (NSEQ, LEN, D), 1.0, 6.0, ((0, 8), (1, 4)))
    return dict(hidden_in=hidden_in, seg_bounds=seg_bounds, qkv_weight=qkv_weight, query_bias=query_bias, value_bias=value_bias, conv_taps=conv_taps, out_weight=out_weight, out_bias=out_bias, first_gain=first_gain, first_shift=first_shift, up_weight=up_weight, up_bias=up_bias, down_weight=down_weight, down_bias=down_bias, second_gain=second_gain, second_shift=second_shift, grad_out=grad_out)


precise = lax.Precision.HIGHEST
epsilon = 1e-05

@jax.custom_vjp
def low(v):
    return lax.optimization_barrier(v.astype(jnp.bfloat16)).astype(jnp.float32)

@jax.custom_vjp
def low_back(v):
    return v

def low_keep(v):
    return (low(v), None)

def low_pass(kept, grad):
    return (grad,)

def back_keep(v):
    return (v, None)

def back_low(kept, grad):
    return (low(grad),)
low.defvjp(low_keep, low_pass)
low_back.defvjp(back_keep, back_low)

def layer_norm(hidden):
    row_mean = lax.optimization_barrier(jnp.mean(hidden, axis=-1, keepdims=True))
    centered = hidden - row_mean
    return centered * lax.rsqrt(lax.optimization_barrier(jnp.mean(centered * centered, axis=-1, keepdims=True)) + epsilon)

def pseudo_inverse(kernel):
    identity = jnp.eye(kernel.shape[-1], dtype=kernel.dtype)
    fro_square = lax.optimization_barrier(jnp.sum(kernel * kernel, axis=(-2, -1), keepdims=True))
    approx = jnp.swapaxes(kernel, -1, -2) / fro_square
    for newton_step in range(NEWTON):
        product = jnp.matmul(kernel, approx, precision=precise)
        inner_term = 7.0 * identity - product
        inner_term = 15.0 * identity - jnp.matmul(product, inner_term, precision=precise)
        inner_term = 13.0 * identity - jnp.matmul(product, inner_term, precision=precise)
        approx = 0.25 * jnp.matmul(approx, inner_term, precision=precise)
    return approx

def layer_forward(hidden, params, bounds):
    qkv_weight, query_bias, value_bias, conv_taps, out_weight, out_bias, first_gain, first_shift, up_weight, up_bias, down_weight, down_bias, second_gain, second_shift = params
    group_size, seq_length, model_width = hidden.shape
    head_count, tap_count = conv_taps.shape
    head_width = model_width // head_count
    seg_count = bounds.shape[1] - 1
    halo_width = (tap_count - 1) // 2
    quarter = float(head_width) ** (-0.25)
    position = jnp.arange(seq_length, dtype=jnp.int32)
    valid_mask = (position[None, :] < bounds[:, seg_count:]).astype(jnp.float32)
    member = ((position[None, None, :] >= bounds[:, :seg_count, None]) & (position[None, None, :] < bounds[:, 1:, None])).astype(jnp.float32)
    counts = (bounds[:, 1:] - bounds[:, :seg_count]).astype(jnp.float32)
    bias_qkv = jnp.concatenate([query_bias, jnp.zeros_like(query_bias), value_bias])
    qkv_rows = low_back(jnp.einsum('gtd,de->gte', hidden, qkv_weight, precision=precise) + bias_qkv)
    queries = low(qkv_rows[..., :model_width] * quarter)
    key_rows = low(qkv_rows[..., model_width:2 * model_width] * quarter)
    values = low(qkv_rows[..., 2 * model_width:] * valid_mask[..., None])
    land_query = low(low_back(jnp.einsum('gmt,gtd->gmd', member, queries, precision=precise)) / counts[..., None])
    land_key = low(low_back(jnp.einsum('gmt,gtd->gmd', member, key_rows, precision=precise)) / counts[..., None])
    split_q = queries.reshape(group_size, seq_length, head_count, head_width)
    split_k = key_rows.reshape(group_size, seq_length, head_count, head_width)
    split_v = values.reshape(group_size, seq_length, head_count, head_width)
    split_lq = land_query.reshape(group_size, seg_count, head_count, head_width)
    split_lk = land_key.reshape(group_size, seg_count, head_count, head_width)
    first_score = low_back(jnp.einsum('gthe,gmhe->ghmt', split_q, split_lk, precision=precise))
    kernel_one = low(jax.nn.softmax(first_score, axis=2))
    second_score = jnp.einsum('gmhe,gnhe->ghmn', split_lq, split_lk, precision=precise)
    kernel_two = jax.nn.softmax(second_score, axis=-1)
    approx = pseudo_inverse(kernel_two)
    third_score = low_back(jnp.einsum('gmhe,gthe->ghmt', split_lq, split_k, precision=precise))
    third_score = jnp.where(valid_mask[:, None, None, :] > 0.5, third_score, -1e+30)
    score_top = lax.optimization_barrier(jnp.max(third_score, axis=-1, keepdims=True))
    expo_val = jnp.exp(third_score - score_top)
    exp_total = lax.optimization_barrier(jnp.sum(expo_val, axis=-1, keepdims=True))
    acc_sum = low_back(jnp.einsum('ghmt,gthe->ghme', low(expo_val), split_v, precision=precise))
    kv_mean = acc_sum / exp_total
    mixed_low = low(jnp.einsum('ghmn,ghne->ghme', approx, kv_mean, precision=precise))
    attn_out = jnp.einsum('ghmt,ghme->gthe', kernel_one, mixed_low, precision=precise)
    padded = jnp.pad(split_v, ((0, 0), (halo_width, halo_width), (0, 0), (0, 0)))
    conv_out = jnp.zeros_like(attn_out)
    for tap_index in range(tap_count):
        conv_out = conv_out + conv_taps[None, None, :, tap_index, None] * padded[:, tap_index:tap_index + seq_length]
    branch = low(low_back((attn_out + conv_out).reshape(group_size, seq_length, model_width)))
    projected = low_back(jnp.einsum('gtd,de->gte', branch, out_weight, precision=precise) + out_bias)
    mid_rows = layer_norm(hidden + projected) * first_gain + first_shift
    up_pre = low_back(jnp.einsum('gtd,df->gtf', low(mid_rows), up_weight, precision=precise) + up_bias)
    act_low = low(jax.nn.gelu(up_pre, approximate=False))
    down_out = low_back(jnp.einsum('gtf,fd->gtd', act_low, down_weight, precision=precise) + down_bias)
    result = layer_norm(mid_rows + down_out) * second_gain + second_shift
    proxy_vals = jnp.sqrt(lax.optimization_barrier(jnp.sum(kernel_two * kernel_two, axis=(-2, -1)))) * jnp.sqrt(lax.optimization_barrier(jnp.sum(approx * approx, axis=(-2, -1))))
    return (result, proxy_vals)

def reference(hidden_in, seg_bounds, qkv_weight, query_bias, value_bias, conv_taps, out_weight, out_bias, first_gain, first_shift, up_weight, up_bias, down_weight, down_bias, second_gain, second_shift, grad_out):
    params = tuple((weight.astype(jnp.float32) for weight in (qkv_weight, query_bias, value_bias, conv_taps, out_weight, out_bias, first_gain, first_shift, up_weight, up_bias, down_weight, down_bias, second_gain, second_shift)))
    seq_total, seq_length, model_width = hidden_in.shape
    group_size = math.gcd(seq_total, max(1, 4096 // seq_length))
    block_count = seq_total // group_size
    x_blocks = hidden_in.astype(jnp.float32).reshape(block_count, group_size, seq_length, model_width)
    bound_blocks = seg_bounds.reshape(block_count, group_size, seg_bounds.shape[1])
    grad_blocks = grad_out.astype(jnp.float32).reshape(block_count, group_size, seq_length, model_width)

    def block_step(carried, block_item):
        hidden, bounds, cotangent = block_item

        def forward(hidden_val, param_val):
            return layer_forward(hidden_val, param_val, bounds)
        result, pull_back, proxy_vals = jax.vjp(forward, hidden, params, has_aux=True)
        grad_hidden, grad_params = pull_back(cotangent)
        summed = tuple((earlier + update for earlier, update in zip(carried[0], grad_params)))
        return ((summed, carried[1] + lax.optimization_barrier(jnp.sum(proxy_vals, axis=0))), (result.astype(jnp.bfloat16), grad_hidden.astype(jnp.bfloat16)))
    start_state = (tuple((jnp.zeros_like(weight) for weight in params)), jnp.zeros((conv_taps.shape[0],), jnp.float32))
    (grads, proxy_sum), (outputs, grad_rows) = lax.scan(block_step, start_state, (x_blocks, bound_blocks, grad_blocks))
    layer_out = outputs.reshape(hidden_in.shape)
    input_grad = grad_rows.reshape(hidden_in.shape)
    condition = proxy_sum / seq_total
    return (layer_out, input_grad, grads[0], grads[1], grads[2], grads[3], grads[4], grads[5], grads[6], grads[7], grads[8], grads[9], grads[10], grads[11], grads[12], grads[13], condition)
```

```python
import math
from functools import partial

import jax
import jax.numpy as jnp
from jax import lax
from jax.experimental import pallas as pl
from jax.experimental.pallas import tpu as pltpu
from jax.sharding import PartitionSpec as P

NEWTON = 6

MESH_IDS = pl.DeviceIdType.MESH
HALF = 384
LANES = 128


def plane_sides(count):
    wide = max(d for d in range(1, math.isqrt(count) + 1) if count % d == 0)
    return wide, count // wide


class Place:
    def __init__(self, batch_size, seq_size):
        x_size, y_size = plane_sides(seq_size)
        self.sizes = {"core": 2, "x": x_size, "y": y_size, "z": batch_size // 2}
        batch = lax.axis_index("batch")
        seq = lax.axis_index("seq")
        self.at = {
            "core": lax.rem(batch, 2),
            "z": lax.div(batch, 2),
            "x": lax.rem(seq, x_size),
            "y": lax.div(seq, x_size),
        }
        self.seq_size = seq_size
        self.seq = seq
        self.batch = batch

    def peer_index(self, axis, step):
        size = self.sizes[axis]
        return lax.rem(self.at[axis] + step, size)

    def device(self, **moved):
        spot = {**self.at, **moved}
        return (spot["z"] * 2 + spot["core"], spot["y"] * self.sizes["x"] + spot["x"])

    def peers(self, axes):
        for axis in axes:
            for step in range(1, self.sizes[axis]):
                yield self.device(**{axis: self.peer_index(axis, step)})

    def seq_peer(self, step):
        return (self.batch, lax.rem(self.seq + step, self.seq_size))


def greet(devices):
    barrier = pltpu.get_barrier_semaphore()
    devices = list(devices)
    for device in devices:
        pl.semaphore_signal(barrier, inc=1, device_id=device, device_id_type=MESH_IDS)
    return lambda: pl.semaphore_wait(barrier, len(devices))


def tile_rows(rows):
    return max(t for t in (96, 64, 48, 32, 16) if rows % t == 0)


def add_rows(out_ref, in_ref, at, parts, rows):
    tile = tile_rows(rows)

    def step(index, carry):
        start = pl.multiple_of(at + index * tile, 16)
        total = in_ref[pl.ds(start, tile), :].astype(jnp.float32)
        for ref, first in parts:
            total = total + ref[pl.ds(pl.multiple_of(first + index * tile, 16), tile), :].astype(
                jnp.float32
            )
        out_ref[pl.ds(start, tile), :] = total.astype(out_ref.dtype)
        return carry

    lax.fori_loop(0, rows // tile, step, 0)


class Reduce:
    ORDERS = (("x", "y", "z"), ("y", "x", "z"))

    def __init__(self, place, stage, whole, recv, send_sem, recv_sem, free_sem, rows):
        self.place, self.stage, self.whole, self.recv = place, stage, whole, recv
        self.send_sem, self.recv_sem, self.rows = send_sem, recv_sem, rows
        self.free_sem = free_sem
        self.sem = 0
        self.mine = stage.at[place.at["core"]]
        self.levels = []
        for half, order in enumerate(self.ORDERS):
            base, size, slot, levels = half * (rows // 2), rows // 2, 0, []
            for axis in order:
                count = place.sizes[axis]
                chunk = size // count
                levels.append((axis, count, base, chunk, slot))
                slot += (count - 1) * chunk
                base = base + place.at[axis] * chunk
                size = chunk
            self.levels.append(levels)

    @staticmethod
    def slots(sizes, rows):
        need = []
        for order in Reduce.ORDERS:
            size, slot = rows // 2, 0
            for axis in order:
                size //= sizes[axis]
                slot += (sizes[axis] - 1) * size
            need.append(slot)
        return max(need)

    @staticmethod
    def copies(sizes):
        return 2 * (1 + 2 * sum(sizes[a] - 1 for a in ("x", "y", "z")))

    def copy(self, src, dst, device):
        index = self.sem
        self.sem += 1
        return pltpu.make_async_remote_copy(
            src_ref=src,
            dst_ref=dst,
            send_sem=self.send_sem.at[index],
            recv_sem=self.recv_sem.at[index],
            device_id=device,
            device_id_type=MESH_IDS,
        )

    @staticmethod
    def rows_of(ref, start, rows):
        return ref.at[pl.ds(pl.multiple_of(start, 16), rows)]

    def scatter(self, half, level):
        axis, count, base, chunk, slot = self.levels[half][level]
        copies = []
        for step in range(1, count):
            peer = self.place.peer_index(axis, step)
            copies.append(
                self.copy(
                    self.rows_of(self.mine, base + peer * chunk, chunk),
                    self.recv.at[half, pl.ds(slot + (step - 1) * chunk, chunk)],
                    self.place.device(**{axis: peer}),
                )
            )
        return copies

    def add_level(self, half, level):
        axis, count, base, chunk, slot = self.levels[half][level]
        add_rows(
            self.whole if level == 2 else self.mine,
            self.mine,
            base + self.place.at[axis] * chunk,
            [(self.recv.at[half], slot + k * chunk) for k in range(count - 1)],
            chunk,
        )

    def run(self):
        place, rows = self.place, self.rows
        core = place.at["core"]
        out = self.copy(
            self.stage.at[1 - core], self.whole, place.device(core=1 - core)
        )
        out.start()
        yield
        out.wait()
        pl.semaphore_signal(
            self.free_sem, inc=1, device_id=place.device(core=1 - core), device_id_type=MESH_IDS
        )
        pending = []
        for half in range(2):
            add_rows(
                self.mine,
                self.mine,
                half * (rows // 2),
                [(self.whole, half * (rows // 2))],
                rows // 2,
            )
            copies = self.scatter(half, 0)
            for copy in copies:
                copy.start()
            pending.append(copies)
        for level in range(3):
            yield
            later = []
            for half in range(2):
                for copy in pending[half]:
                    copy.wait()
                self.add_level(half, level)
                copies = self.scatter(half, level + 1) if level < 2 else self.spread(half, 2)
                for copy in copies:
                    copy.start()
                later.append(copies)
            pending = later
        for level in (2, 1, 0):
            yield
            later = []
            for half in range(2):
                for copy in pending[half]:
                    copy.wait()
                if level:
                    copies = self.spread(half, level - 1)
                    for copy in copies:
                        copy.start()
                    later.append(copies)
            pending = later
        pl.semaphore_wait(self.free_sem, 1)
        out = self.copy(self.whole, self.stage.at[core], place.device(core=1 - core))
        out.start()
        yield
        out.wait()

    def spread(self, half, level):
        axis, count, base, chunk, slot = self.levels[half][level]
        here = self.rows_of(self.whole, base + self.place.at[axis] * chunk, chunk)
        return [
            self.copy(here, here, self.place.device(**{axis: self.place.peer_index(axis, step)}))
            for step in range(1, count)
        ]


def vec_reduce(place, acc, slots, send_sem, recv_sem):
    sem = 0
    level = 0
    for axis in ("core", "x", "y", "z"):
        count = place.sizes[axis]
        copies = []
        here = place.at[axis]
        for step in range(1, count):
            copies.append(
                pltpu.make_async_remote_copy(
                    src_ref=acc,
                    dst_ref=slots.at[level + here],
                    send_sem=send_sem.at[sem],
                    recv_sem=recv_sem.at[sem],
                    device_id=place.device(**{axis: place.peer_index(axis, step)}),
                    device_id_type=MESH_IDS,
                )
            )
            sem += 1
        for copy in copies:
            copy.start()
        slots[level + here] = acc[...]
        yield
        for copy in copies:
            copy.wait()
        total = slots[level]
        for index in range(1, count):
            total = total + slots[level + index]
        acc[...] = total
        level += count


def interleave(generators, offsets):
    live = [(g, o) for g, o in zip(generators, offsets)]
    step = 0
    while live:
        keep = []
        for generator, offset in live:
            if step < offset:
                keep.append((generator, offset))
                continue
            try:
                next(generator)
                keep.append((generator, offset))
            except StopIteration:
                pass
        live = keep
        step += 1


def grad_kernel(batch_size, seq_size, plan, rows, *refs):
    arrays = refs[:4]
    (
        vec_in, out_ref, vec_out, stage, whole, recv, slots, copy_sem, send_sem, recv_sem,
        free_sem, vsend, vrecv, out_sem,
    ) = refs[4:]
    place = Place(batch_size, seq_size)
    wait_greet = greet(place.peers(("core", "x", "y", "z")))
    fills = []
    for piece, blocks in enumerate(plan):
        fill = []
        for spot, (array, row, col) in enumerate(blocks):
            for core in range(2):
                fill.append(
                    pltpu.make_async_copy(
                        arrays[array].at[pl.ds(row, 768), pl.ds(col + core * HALF, HALF)],
                        stage.at[piece, core, pl.ds(spot * 768, 768)],
                        copy_sem.at[piece, spot * 2 + core],
                    )
                )
        for copy in fill:
            copy.start()
        fills.append(fill)
    vec_out[...] = vec_in[...]
    wait_greet()

    def piece_run(piece):
        for copy in fills[piece]:
            copy.wait()
        yield from Reduce(
            place, stage.at[piece], whole.at[piece], recv.at[piece],
            send_sem.at[piece], recv_sem.at[piece], free_sem.at[piece], rows,
        ).run()
        core = place.at["core"]
        outs = [
            pltpu.make_async_copy(
                whole.at[piece], out_ref.at[piece, core], out_sem.at[piece, 0]
            ),
            pltpu.make_async_copy(
                stage.at[piece, 1 - core], out_ref.at[piece, 1 - core], out_sem.at[piece, 1]
            ),
        ]
        for out in outs:
            out.start()
        yield
        for out in outs:
            out.wait()

    runs = [piece_run(p) for p in range(len(plan))]
    runs.append(vec_reduce(place, vec_out, slots, vsend, vrecv))
    interleave(runs, list(range(len(plan))) + [0])


BLOCKS = (
    (0, 0, 0), (0, 768, 0), (0, 1536, 0), (0, 2304, 0),
    (1, 0, 0), (1, 0, 768), (1, 0, 1536), (1, 0, 2304),
    (2, 0, 0), (3, 0, 0), (3, 0, 768), (3, 0, 1536),
)


def piece_plan(sizes):
    unit = 32 * sizes["x"] * sizes["y"] * sizes["z"]
    many = 2 if 1536 % unit == 0 else 4
    return many, -(-many * 768 // unit) * unit


def grad_reduce(down, up, out, qkv, vec, batch_size, seq_size):
    x_size, y_size = plane_sides(seq_size)
    sizes = {"core": 2, "x": x_size, "y": y_size, "z": batch_size // 2}
    many, rows = piece_plan(sizes)
    plan = [BLOCKS[i : i + many] for i in range(0, len(BLOCKS), many)]
    pieces = len(plan)
    copies = Reduce.copies(sizes)
    vec_steps = sum(sizes[a] - 1 for a in sizes)
    vec_slots = sum(sizes.values())
    any_spec = pl.BlockSpec(memory_space=pl.ANY)
    vmem = pl.BlockSpec(memory_space=pltpu.VMEM)
    gathered, vec = pl.pallas_call(
        partial(grad_kernel, batch_size, seq_size, plan, rows),
        out_shape=(
            jax.ShapeDtypeStruct((pieces, 2, rows, HALF), jnp.bfloat16),
            jax.ShapeDtypeStruct(vec.shape, jnp.float32),
        ),
        in_specs=[any_spec] * 4 + [vmem],
        out_specs=(any_spec, vmem),
        scratch_shapes=[
            pltpu.VMEM((pieces, 2, rows, HALF), jnp.bfloat16),
            pltpu.VMEM((pieces, rows, HALF), jnp.bfloat16),
            pltpu.VMEM((pieces, 2, Reduce.slots(sizes, rows), HALF), jnp.bfloat16),
            pltpu.VMEM((vec_slots, *vec.shape), jnp.float32),
            pltpu.SemaphoreType.DMA((pieces, 2 * many)),
            pltpu.SemaphoreType.DMA((pieces, copies)),
            pltpu.SemaphoreType.DMA((pieces, copies)),
            pltpu.SemaphoreType.REGULAR((pieces,)),
            pltpu.SemaphoreType.DMA((vec_steps,)),
            pltpu.SemaphoreType.DMA((vec_steps,)),
            pltpu.SemaphoreType.DMA((pieces, 2)),
        ],
        compiler_params=pltpu.CompilerParams(
            collective_id=0, has_side_effects=True, vmem_limit_bytes=58 * 2**20
        ),
        name="grad_reduce",
    )(down, up, out, qkv, vec)
    return many, gathered, vec


def widen_kernel(in_ref, out_ref):
    out_ref[...] = in_ref[0, 0].astype(jnp.float32)


def widen(gathered, many, first, shape):
    down_way = shape[0] > shape[1]
    count = shape[0] // 768 * (shape[1] // 768)
    return pl.pallas_call(
        widen_kernel,
        out_shape=jax.ShapeDtypeStruct(shape, jnp.float32),
        grid=(count, 2),
        in_specs=[
            pl.BlockSpec(
                (1, 1, 768, HALF), lambda b, c: (lax.div(first + b, many), c, lax.rem(first + b, many), 0)
            )
        ],
        out_specs=pl.BlockSpec(
            (768, HALF), (lambda b, c: (b, c)) if down_way else (lambda b, c: (0, b * 2 + c))
        ),
        name="widen",
    )(gathered)


precise = lax.Precision.HIGHEST
epsilon = 1e-05


def with_halo(cells, sides, width):
    for axis, dim in sides:
        count = lax.axis_size(axis)
        ends = count - 1
        head = lax.slice_in_dim(cells, 0, width, axis=dim)
        tail = lax.slice_in_dim(cells, cells.shape[dim] - width, cells.shape[dim], axis=dim)
        cells = jnp.concatenate(
            [
                lax.ppermute(tail, axis, [(i, (i + 1) % count) for i in range(ends)]),
                cells,
                lax.ppermute(head, axis, [((i + 1) % count, i) for i in range(ends)]),
            ],
            axis=dim,
        )
    return cells


def layer_norm(hidden):
    row_mean = jnp.mean(hidden, axis=-1, keepdims=True)
    centered = hidden - row_mean
    inv_std = lax.rsqrt(jnp.mean(centered * centered, axis=-1, keepdims=True) + epsilon)
    return (centered * inv_std, inv_std)


def norm_back(grad_normed, normed, inv_std):
    return inv_std * (
        grad_normed
        - jnp.mean(grad_normed, axis=-1, keepdims=True)
        - normed * jnp.mean(grad_normed * normed, axis=-1, keepdims=True)
    )


def pseudo_inverse(kernel):
    identity = jnp.eye(kernel.shape[-1], dtype=kernel.dtype)
    fro_square = jnp.sum(kernel * kernel, axis=(-2, -1), keepdims=True)
    approx = jnp.swapaxes(kernel, -1, -2) / fro_square
    for newton_step in range(NEWTON):
        product = jnp.matmul(kernel, approx, precision=precise)
        inner_term = 7.0 * identity - product
        inner_term = 15.0 * identity - jnp.matmul(product, inner_term, precision=precise)
        inner_term = 13.0 * identity - jnp.matmul(product, inner_term, precision=precise)
        approx = 0.25 * jnp.matmul(approx, inner_term, precision=precise)
    return approx


def solve_mix(land_query, land_key, kv_mean):
    second_score = jnp.einsum("smhe,snhe->shmn", land_query, land_key, precision=precise)
    kernel_two = jax.nn.softmax(second_score, axis=-1)
    approx = pseudo_inverse(kernel_two)
    mixed_val = jnp.einsum("shmn,shne->shme", approx, kv_mean, precision=precise)
    proxy_vals = jnp.sqrt(jnp.sum(kernel_two * kernel_two, axis=(-2, -1))) * jnp.sqrt(
        jnp.sum(approx * approx, axis=(-2, -1))
    )
    return (mixed_val, proxy_vals)


def heads_split(array, head_count):
    return array.reshape(array.shape[0], array.shape[1], head_count, array.shape[2] // head_count)


def landmark_total(partial_sum, extra_term, counts):
    whole_sum = lax.psum(partial_sum, "seq")
    landmarks = ((whole_sum + extra_term) / counts[:, None, :, None]).astype(jnp.bfloat16)
    return landmarks


def conv_apply(padded, tap_weights, row_count):
    conv_sum = jnp.zeros((padded.shape[0], row_count, padded.shape[2]), jnp.float32)
    for tap_index in range(tap_weights.shape[1]):
        conv_sum = (
            conv_sum + tap_weights[:, tap_index] * padded[:, tap_index : tap_index + row_count]
        )
    return conv_sum


def pack_vectors(vectors):
    flat_vec = jnp.concatenate(vectors)
    return jnp.pad(flat_vec, (0, -flat_vec.shape[0] % 1024)).reshape(-1, 128)


def unpack_vectors(flat_vec, piece_sizes):
    pieces = []
    offset = 0
    for length_val in piece_sizes:
        pieces.append(flat_vec[offset : offset + length_val])
        offset = offset + length_val
    return pieces


def body(
    hidden_in,
    seg_bounds,
    qkv_weight,
    query_bias,
    value_bias,
    conv_taps,
    out_weight,
    out_bias,
    first_gain,
    first_shift,
    up_weight,
    up_bias,
    down_weight,
    down_bias,
    second_gain,
    second_shift,
    grad_out,
):
    seq_count, tok_count, model_width = hidden_in.shape
    head_count, tap_count = conv_taps.shape
    head_width = model_width // head_count
    ff_width = up_weight.shape[1]
    seg_count = seg_bounds.shape[1] - 1
    halo_width = (tap_count - 1) // 2
    quarter = float(head_width) ** (-0.25)
    row_total = seq_count * tok_count
    batch_size, seq_size = lax.axis_size("batch"), lax.axis_size("seq")
    device_total = batch_size * seq_size
    position = lax.axis_index("seq") * tok_count + jnp.arange(tok_count, dtype=jnp.int32)
    valid_mask = (position[None, :] < seg_bounds[:, seg_count:]).astype(jnp.float32)
    member = (
        (position[None, None, :] >= seg_bounds[:, :seg_count, None])
        & (position[None, None, :] < seg_bounds[:, 1:, None])
    ).astype(jnp.bfloat16)
    counts = (seg_bounds[:, 1:] - seg_bounds[:, :seg_count]).astype(jnp.float32)
    input_rows = hidden_in.reshape(row_total, model_width)
    bias_qkv = jnp.concatenate([query_bias, jnp.zeros_like(query_bias), value_bias])
    qkv_rows = (
        jnp.dot(input_rows, qkv_weight, preferred_element_type=jnp.float32) + bias_qkv
    ).reshape(seq_count, tok_count, 3 * model_width)
    queries = (qkv_rows[..., :model_width] * quarter).astype(jnp.bfloat16)
    key_rows = (qkv_rows[..., model_width : 2 * model_width] * quarter).astype(jnp.bfloat16)
    values = (qkv_rows[..., 2 * model_width :] * valid_mask[..., None]).astype(jnp.bfloat16)
    query_sums = jnp.einsum("smt,std->smd", member, queries, preferred_element_type=jnp.float32)
    key_sums = jnp.einsum("smt,std->smd", member, key_rows, preferred_element_type=jnp.float32)
    land_sums = jnp.stack([query_sums, key_sums], axis=1)
    landmarks = landmark_total(land_sums, jnp.zeros_like(land_sums), counts)
    land_query = landmarks[:, 0].reshape(seq_count, seg_count, head_count, head_width)
    land_key = landmarks[:, 1].reshape(seq_count, seg_count, head_count, head_width)
    split_q = heads_split(queries, head_count)
    split_k = heads_split(key_rows, head_count)
    split_v = heads_split(values, head_count)
    first_score = jnp.einsum(
        "sthe,smhe->shmt", split_q, land_key, preferred_element_type=jnp.float32
    )
    kernel_one = jax.nn.softmax(first_score, axis=2)
    kernel_low = kernel_one.astype(jnp.bfloat16)
    third_score = jnp.einsum(
        "smhe,sthe->shmt", land_query, split_k, preferred_element_type=jnp.float32
    )
    third_score = jnp.where(valid_mask[:, None, None, :] > 0.5, third_score, -1e30)
    score_top = lax.pmax(jnp.max(third_score, axis=-1), "seq")
    expo_val = jnp.exp(third_score - score_top[..., None])
    expo_low = expo_val.astype(jnp.bfloat16)
    acc_part = jnp.einsum("shmt,sthe->shme", expo_low, split_v, preferred_element_type=jnp.float32)
    acc_sum, exp_total = lax.psum((acc_part, jnp.sum(expo_val, axis=-1)), "seq")
    kv_mean = acc_sum / exp_total[..., None]
    mixed_val, mix_back, proxy_vals = jax.vjp(
        solve_mix,
        land_query.astype(jnp.float32),
        land_key.astype(jnp.float32),
        kv_mean,
        has_aux=True,
    )
    mixed_low = mixed_val.astype(jnp.bfloat16)
    attn_out = jnp.einsum(
        "shmt,shme->sthe", kernel_low, mixed_low, preferred_element_type=jnp.float32
    ).reshape(seq_count, tok_count, model_width)
    tap_weights = jnp.repeat(conv_taps, head_width, axis=0)
    padded_values = with_halo(values, (("seq", 1),), halo_width)
    branch = (
        (attn_out + conv_apply(padded_values, tap_weights, tok_count))
        .astype(jnp.bfloat16)
        .reshape(row_total, model_width)
    )
    first_sum = (
        input_rows.astype(jnp.float32)
        + jnp.dot(branch, out_weight, preferred_element_type=jnp.float32)
        + out_bias
    )
    normed_one, inv_one = layer_norm(first_sum)
    mid_rows = normed_one * first_gain + first_shift
    mid_low = mid_rows.astype(jnp.bfloat16)
    up_pre = jnp.dot(mid_low, up_weight, preferred_element_type=jnp.float32) + up_bias
    act_val, gelu_back = jax.vjp(partial(jax.nn.gelu, approximate=False), up_pre)
    act_low = act_val.astype(jnp.bfloat16)
    second_sum = (
        mid_rows + jnp.dot(act_low, down_weight, preferred_element_type=jnp.float32) + down_bias
    )
    normed_two, inv_two = layer_norm(second_sum)
    layer_out = (
        (normed_two * second_gain + second_shift)
        .astype(jnp.bfloat16)
        .reshape(seq_count, tok_count, model_width)
    )
    grad_rows = grad_out.reshape(row_total, model_width).astype(jnp.float32)
    second_gain_grad = jnp.sum(grad_rows * normed_two, axis=0)
    second_shift_grad = jnp.sum(grad_rows, axis=0)
    grad_second = norm_back(grad_rows * second_gain, normed_two, inv_two)
    grad_down = grad_second.astype(jnp.bfloat16)
    down_weight_grad = jnp.einsum(
        "nf,nd->fd", act_low, grad_down, preferred_element_type=jnp.float32
    )
    down_bias_grad = jnp.sum(grad_down.astype(jnp.float32), axis=0)
    (grad_up_val,) = gelu_back(
        jnp.einsum("nd,fd->nf", grad_down, down_weight, preferred_element_type=jnp.float32)
    )
    grad_up = grad_up_val.astype(jnp.bfloat16)
    up_weight_grad = jnp.einsum("nd,nf->df", mid_low, grad_up, preferred_element_type=jnp.float32)
    up_bias_grad = jnp.sum(grad_up.astype(jnp.float32), axis=0)
    grad_mid = grad_second + jnp.einsum(
        "nf,df->nd", grad_up, up_weight, preferred_element_type=jnp.float32
    )
    first_gain_grad = jnp.sum(grad_mid * normed_one, axis=0)
    first_shift_grad = jnp.sum(grad_mid, axis=0)
    grad_first = norm_back(grad_mid * first_gain, normed_one, inv_one)
    grad_proj = grad_first.astype(jnp.bfloat16)
    out_weight_grad = jnp.einsum("nd,ne->de", branch, grad_proj, preferred_element_type=jnp.float32)
    out_bias_grad = jnp.sum(grad_proj.astype(jnp.float32), axis=0)
    grad_branch = (
        jnp.einsum("ne,de->nd", grad_proj, out_weight, preferred_element_type=jnp.float32)
        .astype(jnp.bfloat16)
        .reshape(seq_count, tok_count, model_width)
    )
    grad_heads = heads_split(grad_branch, head_count)
    grad_kernel = jnp.einsum(
        "sthe,shme->shmt", grad_heads, mixed_low, preferred_element_type=jnp.float32
    )
    grad_first_score = (
        kernel_one * (grad_kernel - jnp.sum(kernel_one * grad_kernel, axis=2, keepdims=True))
    ).astype(jnp.bfloat16)
    grad_mix_part = jnp.einsum(
        "shmt,sthe->shme", kernel_low, grad_heads, preferred_element_type=jnp.float32
    )
    grad_mixed = lax.psum(grad_mix_part, "seq")
    grad_lq_two, grad_lk_two, grad_kv = mix_back(grad_mixed)
    grad_query_one = jnp.einsum(
        "shmt,smhe->sthe", grad_first_score, land_key, preferred_element_type=jnp.float32
    )
    grad_lk_one = jnp.einsum(
        "shmt,sthe->smhe", grad_first_score, split_q, preferred_element_type=jnp.float32
    )
    grad_acc = (grad_kv / exp_total[..., None]).astype(jnp.bfloat16)
    grad_total = -jnp.sum(grad_kv * kv_mean, axis=-1) / exp_total
    grad_expo = (
        jnp.einsum("shme,sthe->shmt", grad_acc, split_v, preferred_element_type=jnp.float32)
        + grad_total[..., None]
    )
    grad_third = (expo_val * grad_expo).astype(jnp.bfloat16)
    grad_value_att = jnp.einsum(
        "shmt,shme->sthe", expo_low, grad_acc, preferred_element_type=jnp.float32
    )
    grad_key_three = jnp.einsum(
        "shmt,smhe->sthe", grad_third, land_query, preferred_element_type=jnp.float32
    )
    grad_lq_three = jnp.einsum(
        "shmt,sthe->smhe", grad_third, split_k, preferred_element_type=jnp.float32
    )
    grad_parts = jnp.stack(
        [
            grad_lq_three.reshape(seq_count, seg_count, model_width),
            grad_lk_one.reshape(seq_count, seg_count, model_width),
        ],
        axis=1,
    )
    grad_extra = jnp.stack(
        [
            grad_lq_two.reshape(seq_count, seg_count, model_width),
            grad_lk_two.reshape(seq_count, seg_count, model_width),
        ],
        axis=1,
    )
    grad_land = landmark_total(grad_parts, grad_extra, counts)
    padded_grad = with_halo(grad_branch, (("seq", 1),), halo_width)
    grad_values = grad_value_att.reshape(seq_count, tok_count, model_width) + conv_apply(
        padded_grad, tap_weights[:, ::-1], tok_count
    )
    grad_branch_wide = grad_branch.astype(jnp.float32)
    tap_grads = jnp.stack(
        [
            jnp.sum(
                grad_branch_wide * padded_values[:, tap_index : tap_index + tok_count], axis=(0, 1)
            )
            for tap_index in range(tap_count)
        ]
    )
    conv_grad = jnp.transpose(
        jnp.sum(tap_grads.reshape(tap_count, head_count, head_width), axis=-1)
    )
    grad_queries = (
        jnp.einsum("smt,smd->std", member, grad_land[:, 0], preferred_element_type=jnp.float32)
        + grad_query_one.reshape(seq_count, tok_count, model_width)
    ) * quarter
    grad_keys = (
        jnp.einsum("smt,smd->std", member, grad_land[:, 1], preferred_element_type=jnp.float32)
        + grad_key_three.reshape(seq_count, tok_count, model_width)
    ) * quarter
    grad_qkv = (
        jnp.concatenate([grad_queries, grad_keys, grad_values * valid_mask[..., None]], axis=-1)
        .astype(jnp.bfloat16)
        .reshape(row_total, 3 * model_width)
    )
    qkv_grad = jnp.einsum("nd,ne->de", input_rows, grad_qkv, preferred_element_type=jnp.float32)
    bias_cols = jnp.sum(grad_qkv.astype(jnp.float32), axis=0)
    query_bias_grad = bias_cols[:model_width]
    value_bias_grad = bias_cols[2 * model_width :]
    input_grad = (
        (
            grad_first
            + jnp.einsum("ne,de->nd", grad_qkv, qkv_weight, preferred_element_type=jnp.float32)
        )
        .astype(jnp.bfloat16)
        .reshape(seq_count, tok_count, model_width)
    )
    proxy_local = jnp.sum(proxy_vals, axis=0)
    vector = pack_vectors(
        [
            up_bias_grad,
            down_bias_grad,
            second_gain_grad,
            second_shift_grad,
            query_bias_grad,
            value_bias_grad,
            conv_grad.reshape(-1),
            out_bias_grad,
            first_gain_grad,
            first_shift_grad,
            proxy_local,
        ]
    )
    many, gathered, vector = grad_reduce(
        down_weight_grad.astype(jnp.bfloat16),
        up_weight_grad.astype(jnp.bfloat16),
        out_weight_grad.astype(jnp.bfloat16),
        qkv_grad.astype(jnp.bfloat16),
        vector,
        batch_size,
        seq_size,
    )
    small = unpack_vectors(
        vector.reshape(-1),
        [
            ff_width,
            model_width,
            model_width,
            model_width,
            model_width,
            model_width,
            head_count * tap_count,
            model_width,
            model_width,
            model_width,
            head_count,
        ],
    )
    return (
        layer_out,
        input_grad,
        widen(gathered, many, 9, qkv_grad.shape),
        small[4],
        small[5],
        small[6].reshape(head_count, tap_count),
        widen(gathered, many, 8, out_weight_grad.shape),
        small[7],
        small[8],
        small[9],
        widen(gathered, many, 4, up_weight_grad.shape),
        small[0],
        widen(gathered, many, 0, down_weight_grad.shape),
        small[1],
        small[2],
        small[3],
        small[10] / (device_total * seq_count),
    )


def solution(mesh):
    placed = (
        P("batch", "seq", None),
        P("batch", None),
        P(),
        P(),
        P(),
        P(),
        P(),
        P(),
        P(),
        P(),
        P(),
        P(),
        P(),
        P(),
        P(),
        P(),
        P("batch", "seq", None),
    )
    return jax.shard_map(
        body,
        mesh=mesh,
        in_specs=placed,
        out_specs=(
            P("batch", "seq", None),
            P("batch", "seq", None),
            P(),
            P(),
            P(),
            P(),
            P(),
            P(),
            P(),
            P(),
            P(),
            P(),
            P(),
            P(),
            P(),
            P(),
            P(),
        ),
        check_vma=False,
    )
```

```python
import math
from functools import partial

import jax
import jax.numpy as jnp
from jax import lax
from jax.experimental import pallas as pl
from jax.experimental.pallas import tpu as pltpu
from jax.sharding import PartitionSpec as P

MESH_IDS = pl.DeviceIdType.MESH
HALF = 384
LANES = 128


def plane_sides(count):
    wide = max(d for d in range(1, math.isqrt(count) + 1) if count % d == 0)
    return wide, count // wide


class Place:
    def __init__(self, batch_size, seq_size):
        x_size, y_size = plane_sides(seq_size)
        self.sizes = {"core": 2, "x": x_size, "y": y_size, "z": batch_size // 2}
        batch = lax.axis_index("batch")
        seq = lax.axis_index("seq")
        self.at = {
            "core": lax.rem(batch, 2),
            "z": lax.div(batch, 2),
            "x": lax.rem(seq, x_size),
            "y": lax.div(seq, x_size),
        }
        self.seq_size = seq_size
        self.seq = seq
        self.batch = batch

    def peer_index(self, axis, step):
        size = self.sizes[axis]
        return lax.rem(self.at[axis] + step, size)

    def device(self, **moved):
        spot = {**self.at, **moved}
        return (spot["z"] * 2 + spot["core"], spot["y"] * self.sizes["x"] + spot["x"])

    def peers(self, axes):
        for axis in axes:
            for step in range(1, self.sizes[axis]):
                yield self.device(**{axis: self.peer_index(axis, step)})

    def seq_peer(self, step):
        return (self.batch, lax.rem(self.seq + step, self.seq_size))


def greet(devices):
    barrier = pltpu.get_barrier_semaphore()
    devices = list(devices)
    for device in devices:
        pl.semaphore_signal(barrier, inc=1, device_id=device, device_id_type=MESH_IDS)
    return lambda: pl.semaphore_wait(barrier, len(devices))


def tile_rows(rows):
    return max(t for t in (96, 64, 48, 32, 16) if rows % t == 0)


def add_rows(out_ref, in_ref, at, parts, rows):
    tile = tile_rows(rows)

    def step(index, carry):
        start = pl.multiple_of(at + index * tile, 16)
        total = in_ref[pl.ds(start, tile), :].astype(jnp.float32)
        for ref, first in parts:
            total = total + ref[pl.ds(pl.multiple_of(first + index * tile, 16), tile), :].astype(
                jnp.float32
            )
        out_ref[pl.ds(start, tile), :] = total.astype(out_ref.dtype)
        return carry

    lax.fori_loop(0, rows // tile, step, 0)


class Reduce:
    ORDERS = (("x", "y", "z"), ("y", "x", "z"))

    def __init__(self, place, stage, whole, recv, send_sem, recv_sem, free_sem, rows):
        self.place, self.stage, self.whole, self.recv = place, stage, whole, recv
        self.send_sem, self.recv_sem, self.rows = send_sem, recv_sem, rows
        self.free_sem = free_sem
        self.sem = 0
        self.mine = stage.at[place.at["core"]]
        self.levels = []
        for half, order in enumerate(self.ORDERS):
            base, size, slot, levels = half * (rows // 2), rows // 2, 0, []
            for axis in order:
                count = place.sizes[axis]
                chunk = size // count
                levels.append((axis, count, base, chunk, slot))
                slot += (count - 1) * chunk
                base = base + place.at[axis] * chunk
                size = chunk
            self.levels.append(levels)

    @staticmethod
    def slots(sizes, rows):
        need = []
        for order in Reduce.ORDERS:
            size, slot = rows // 2, 0
            for axis in order:
                size //= sizes[axis]
                slot += (sizes[axis] - 1) * size
            need.append(slot)
        return max(need)

    @staticmethod
    def copies(sizes):
        return 2 * (1 + 2 * sum(sizes[a] - 1 for a in ("x", "y", "z")))

    def copy(self, src, dst, device):
        index = self.sem
        self.sem += 1
        return pltpu.make_async_remote_copy(
            src_ref=src,
            dst_ref=dst,
            send_sem=self.send_sem.at[index],
            recv_sem=self.recv_sem.at[index],
            device_id=device,
            device_id_type=MESH_IDS,
        )

    @staticmethod
    def rows_of(ref, start, rows):
        return ref.at[pl.ds(pl.multiple_of(start, 16), rows)]

    def scatter(self, half, level):
        axis, count, base, chunk, slot = self.levels[half][level]
        copies = []
        for step in range(1, count):
            peer = self.place.peer_index(axis, step)
            copies.append(
                self.copy(
                    self.rows_of(self.mine, base + peer * chunk, chunk),
                    self.recv.at[half, pl.ds(slot + (step - 1) * chunk, chunk)],
                    self.place.device(**{axis: peer}),
                )
            )
        return copies

    def add_level(self, half, level):
        axis, count, base, chunk, slot = self.levels[half][level]
        add_rows(
            self.whole if level == 2 else self.mine,
            self.mine,
            base + self.place.at[axis] * chunk,
            [(self.recv.at[half], slot + k * chunk) for k in range(count - 1)],
            chunk,
        )

    def run(self):
        place, rows = self.place, self.rows
        core = place.at["core"]
        out = self.copy(
            self.stage.at[1 - core], self.whole, place.device(core=1 - core)
        )
        out.start()
        yield
        out.wait()
        pl.semaphore_signal(
            self.free_sem, inc=1, device_id=place.device(core=1 - core), device_id_type=MESH_IDS
        )
        pending = []
        for half in range(2):
            add_rows(
                self.mine,
                self.mine,
                half * (rows // 2),
                [(self.whole, half * (rows // 2))],
                rows // 2,
            )
            copies = self.scatter(half, 0)
            for copy in copies:
                copy.start()
            pending.append(copies)
        for level in range(3):
            yield
            later = []
            for half in range(2):
                for copy in pending[half]:
                    copy.wait()
                self.add_level(half, level)
                copies = self.scatter(half, level + 1) if level < 2 else self.spread(half, 2)
                for copy in copies:
                    copy.start()
                later.append(copies)
            pending = later
        for level in (2, 1, 0):
            yield
            later = []
            for half in range(2):
                for copy in pending[half]:
                    copy.wait()
                if level:
                    copies = self.spread(half, level - 1)
                    for copy in copies:
                        copy.start()
                    later.append(copies)
            pending = later
        pl.semaphore_wait(self.free_sem, 1)
        out = self.copy(self.whole, self.stage.at[core], place.device(core=1 - core))
        out.start()
        yield
        out.wait()

    def spread(self, half, level):
        axis, count, base, chunk, slot = self.levels[half][level]
        here = self.rows_of(self.whole, base + self.place.at[axis] * chunk, chunk)
        return [
            self.copy(here, here, self.place.device(**{axis: self.place.peer_index(axis, step)}))
            for step in range(1, count)
        ]


def vec_reduce(place, acc, slots, send_sem, recv_sem):
    sem = 0
    level = 0
    for axis in ("core", "x", "y", "z"):
        count = place.sizes[axis]
        copies = []
        here = place.at[axis]
        for step in range(1, count):
            copies.append(
                pltpu.make_async_remote_copy(
                    src_ref=acc,
                    dst_ref=slots.at[level + here],
                    send_sem=send_sem.at[sem],
                    recv_sem=recv_sem.at[sem],
                    device_id=place.device(**{axis: place.peer_index(axis, step)}),
                    device_id_type=MESH_IDS,
                )
            )
            sem += 1
        for copy in copies:
            copy.start()
        slots[level + here] = acc[...]
        yield
        for copy in copies:
            copy.wait()
        total = slots[level]
        for index in range(1, count):
            total = total + slots[level + index]
        acc[...] = total
        level += count


def piece_plan(sizes):
    unit = 32 * sizes["x"] * sizes["y"] * sizes["z"]
    many = 2 if 1536 % unit == 0 else 4
    return many, -(-many * 768 // unit) * unit


SEG = 64
PAIR = 128
HALO = 16
BLOCK = 128
FAR = -1e30
NT = ((1,), (1,))
TN = ((0,), (0,))
NN = ((1,), (0,))


def mm(left, right, dims=NN):
    return lax.dot_general(left, right, (dims, ((), ())), preferred_element_type=jnp.float32)


def split(array):
    high = array.astype(jnp.bfloat16)
    return high, (array - high.astype(jnp.float32)).astype(jnp.bfloat16)


def mm3(left, right, dims=NN):
    left_high, left_low = left
    right_high, right_low = right
    (left_dim,), (right_dim,) = dims
    return mm(
        jnp.concatenate([left_high, left_high, left_low], axis=left_dim),
        jnp.concatenate([right_high, right_low, right_high], axis=right_dim),
        dims,
    )


def eye_mask(size):
    rows = lax.broadcasted_iota(jnp.int32, (size, size), 0)
    return rows == lax.broadcasted_iota(jnp.int32, (size, size), 1)


def column(row):
    return jnp.sum(jnp.where(eye_mask(row.shape[1]), row, 0.0), axis=1, keepdims=True)


def row_of(col):
    return jnp.sum(jnp.where(eye_mask(col.shape[0]), col, 0.0), axis=0, keepdims=True)


def first_head(shape):
    return lax.broadcasted_iota(jnp.int32, shape, len(shape) - 1) < SEG


def spread_heads(pair):
    first = first_head(pair.shape)
    zero = jnp.zeros_like(pair)
    return jnp.concatenate([jnp.where(first, pair, zero), jnp.where(first, zero, pair)], axis=0)


def join_heads(blocks):
    shape = (SEG, PAIR)
    return jnp.where(
        first_head(shape),
        jnp.broadcast_to(blocks[:SEG], shape),
        jnp.broadcast_to(blocks[SEG:], shape),
    )


def heads_sum(col):
    first = jnp.sum(col[:SEG], axis=0, keepdims=True)
    second = jnp.sum(col[SEG:], axis=0, keepdims=True)
    return jnp.concatenate(
        [jnp.broadcast_to(first, (SEG, 1)), jnp.broadcast_to(second, (SEG, 1))], axis=0
    )


def shared_out(place, source, target, many, send_sem, recv_sem):
    copies = []
    for step in range(1, place.seq_size):
        device = place.seq_peer(step)
        copies.append(
            pltpu.make_async_remote_copy(
                src_ref=source.at[pl.ds(device[1] * many, many)],
                dst_ref=target.at[step - 1],
                send_sem=send_sem.at[step - 1],
                recv_sem=recv_sem.at[step - 1],
                device_id=device,
                device_id_type=MESH_IDS,
            )
        )
    return copies


def passed_on(place, array, many, send_sem, recv_sem):
    copies = []
    here = array.at[pl.ds(place.seq * many, many)]
    for step in range(1, place.seq_size):
        copies.append(
            pltpu.make_async_remote_copy(
                src_ref=here,
                dst_ref=here,
                send_sem=send_sem.at[step - 1],
                recv_sem=recv_sem.at[step - 1],
                device_id=place.seq_peer(step),
                device_id_type=MESH_IDS,
            )
        )
    return copies


def halo_copies(place, padded, tokens, send_sem, recv_sem):
    copies = []
    for index, (step, first, there) in enumerate(
        ((1, tokens, 0), (place.seq_size - 1, HALO, tokens + HALO))
    ):
        copies.append(
            pltpu.make_async_remote_copy(
                src_ref=padded.at[:, pl.ds(first, HALO)],
                dst_ref=padded.at[:, pl.ds(there, HALO)],
                send_sem=send_sem.at[index],
                recv_sem=recv_sem.at[index],
                device_id=place.seq_peer(step),
                device_id_type=MESH_IDS,
            )
        )
    return copies


def trim_halo(place, padded, tokens):
    zero = jnp.zeros((padded.shape[0], HALO, padded.shape[2]), padded.dtype)
    low, high = pl.ds(0, HALO), pl.ds(tokens + HALO, HALO)
    padded[:, low] = jnp.where(place.seq > 0, padded[:, low], zero)
    padded[:, high] = jnp.where(place.seq < place.seq_size - 1, padded[:, high], zero)


def zero_past(padded, tokens):
    past = tokens + 2 * HALO
    rest = padded.shape[1] - past
    padded[:, pl.ds(past, rest)] = jnp.zeros(
        (padded.shape[0], rest, padded.shape[2]), padded.dtype
    )


def band(taps):
    wide = jnp.broadcast_to(taps, (BLOCK, 2 * BLOCK))
    return pltpu.roll(wide, 0, 1, stride=1, stride_axis=0).astype(jnp.bfloat16)


def conv_rows(padded, taps, out, tokens):
    seqs, _, width = padded.shape

    def step(pair, carry):
        lanes = pl.ds(pl.multiple_of(pair * PAIR, PAIR), PAIR)
        first = band(taps[pl.ds(2 * pair, 1), :])
        second = band(taps[pl.ds(2 * pair + 1, 1), :])
        for seq in range(seqs):
            for block in range(tokens // BLOCK):
                window = padded[seq, pl.ds(block * BLOCK, 2 * BLOCK), lanes]
                both = jnp.where(
                    first_head((BLOCK, PAIR)), mm(first, window), mm(second, window)
                )
                out[pl.ds(seq * tokens + block * BLOCK, BLOCK), lanes] = both
        return carry

    lax.fori_loop(0, width // PAIR, step, 0)


def segment_edges(bounds, seq):
    low = column(bounds[pl.ds(seq, 1), pl.ds(0, SEG)].astype(jnp.float32))
    high = column(bounds[pl.ds(seq, 1), pl.ds(1, SEG)].astype(jnp.float32))
    return low, high


def positions(place, tokens, axis):
    shape = (tokens, 1) if axis == 0 else (1, tokens)
    return (place.seq * tokens + lax.broadcasted_iota(jnp.int32, shape, axis)).astype(jnp.float32)


def member_of(place, bounds, seq, tokens):
    low, high = segment_edges(bounds, seq)
    where = positions(place, tokens, 1)
    return jnp.where((where >= low) & (where < high), 1.0, 0.0).astype(jnp.bfloat16)


def length_of(bounds, seq):
    return bounds[pl.ds(seq, 1), pl.ds(SEG, 1)].astype(jnp.float32)


def newton_forward(kernels, keep):
    eye = jnp.where(eye_mask(PAIR), 1.0, 0.0)
    approx = []
    for kernel in kernels:
        fro = heads_sum(jnp.sum(kernel * kernel, axis=1, keepdims=True))
        approx.append(kernel.T / fro)
    halves = [split(kernel) for kernel in kernels]
    units = range(len(kernels))
    for step in range(6):
        wide = [split(a) for a in approx]
        product = [mm3(halves[u], wide[u]) for u in units]
        lefts = [split(p) for p in product]
        inner = [15.0 * eye - mm3(lefts[u], split(7.0 * eye - product[u])) for u in units]
        outer = [13.0 * eye - mm3(lefts[u], split(inner[u])) for u in units]
        for u in units:
            for slot, value in enumerate((approx[u], product[u], inner[u], outer[u])):
                keep[u, step, slot] = value
        approx = [0.25 * mm3(wide[u], split(outer[u])) for u in units]
    return approx


def attend_kernel(
    batch_size, seq_size, seqs, tokens, many,
    x, bounds, weight, bias, taps,
    queries, keys, values, kernel_one, expo, land, mixed, branch, kernel_two, approx_out, keep,
    kv_own, shares, proxies,
    land_send, land_recv, kv_send, kv_recv, conv,
    land_sem, land_back_sem, kv_sem, mixed_sem, halo_sem,
):
    place = Place(batch_size, seq_size)
    width = x.shape[1]
    pairs = width // PAIR
    units = seqs * pairs
    wait_greet = greet(place.seq_peer(step) for step in range(1, seq_size))
    quarter = float(SEG) ** -0.25

    def project(out_ref, third):
        def step(tile, carry):
            lanes = pl.ds(pl.multiple_of(third * width + tile * 256, 256), 256)
            here = pl.ds(pl.multiple_of(tile * 256, 256), 256)
            rows = mm(x[...], weight[:, lanes]) + bias[:, lanes]
            if third < 2:
                out_ref[:, here] = (rows * quarter).astype(jnp.bfloat16)
            else:
                for seq in range(seqs):
                    valid = positions(place, tokens, 0) < length_of(bounds, seq)
                    out_ref[seq, pl.ds(HALO, tokens), here] = jnp.where(
                        valid, rows[seq * tokens : (seq + 1) * tokens], 0.0
                    ).astype(jnp.bfloat16)
            return carry

        lax.fori_loop(0, width // 256, step, 0)

    project(queries, 0)
    project(keys, 1)
    for seq in range(seqs):
        member = member_of(place, bounds, seq, tokens)
        for slot, rows in enumerate((queries, keys)):
            sums = mm(member, rows[pl.ds(seq * tokens, tokens), :])
            for pair in range(pairs):
                land_send[seq * pairs + pair, slot] = sums[:, pair * PAIR : (pair + 1) * PAIR]
    for unit in range(units, seq_size * many):
        land_send[unit] = jnp.ones_like(land_send[unit])
        kv_send[unit] = jnp.ones_like(kv_send[unit])
    wait_greet()
    land_out = shared_out(place, land_send, land_recv, many, *land_sem)
    for copy in land_out:
        copy.start()
    project(values, 2)
    halo = halo_copies(place, values, tokens, *halo_sem)
    for copy in halo:
        copy.start()
    zero_past(values, tokens)
    for copy in land_out:
        copy.wait()
    first_unit = place.seq * many
    for own in range(many):
        unit = first_unit + own
        total = land_send[unit]
        for step in range(seq_size - 1):
            total = total + land_recv[step, own]
        low, high = segment_edges(bounds, jnp.minimum(lax.div(unit, pairs), seqs - 1))
        land[unit] = (total / (high - low)).astype(jnp.bfloat16)
    land_back = passed_on(place, land, many, *land_back_sem)
    for copy in land_back:
        copy.start()
    for copy in halo:
        copy.wait()
    trim_halo(place, values, tokens)
    conv_rows(values, taps, conv, tokens)
    for copy in land_back:
        copy.wait()

    def spots(unit):
        seq, pair = lax.div(unit, pairs), lax.rem(unit, pairs)
        rows = pl.ds(pl.multiple_of(seq * tokens, tokens), tokens)
        lanes = pl.ds(pl.multiple_of(pair * PAIR, PAIR), PAIR)
        return seq, rows, lanes

    def third_scores(unit, carry):
        seq, rows, lanes = spots(unit)
        score = mm(spread_heads(land[unit, 0]), keys[rows, lanes], NT)
        valid = positions(place, tokens, 1) < length_of(bounds, seq)
        score = jnp.where(valid, score, FAR)
        top = jnp.max(score, axis=1, keepdims=True)
        weights = jnp.exp(score - top)
        expo[unit] = weights
        total = jnp.sum(weights, axis=1, keepdims=True)
        part = mm(weights.astype(jnp.bfloat16), values[seq, pl.ds(HALO, tokens), lanes])
        kv_send[unit, pl.ds(0, SEG)] = join_heads(part)
        kv_send[unit, pl.ds(SEG, 8)] = jnp.concatenate(
            [row_of(top), row_of(total), jnp.zeros((6, PAIR), jnp.float32)], axis=0
        )
        return carry

    lax.fori_loop(0, units, third_scores, 0, unroll=2)
    kv_out = shared_out(place, kv_send, kv_recv, many, *kv_sem)
    for copy in kv_out:
        copy.start()

    kernels = []
    same = (
        lax.broadcasted_iota(jnp.int32, (PAIR, PAIR), 0) < SEG
    ) == first_head((PAIR, PAIR))
    for own in range(many):
        both = land[first_unit + own]
        score = jnp.where(same, mm(spread_heads(both[0]), spread_heads(both[1]), NT), FAR)
        weights = jnp.exp(score - jnp.max(score, axis=1, keepdims=True))
        kernels.append(weights / jnp.sum(weights, axis=1, keepdims=True))
        kernel_two[own] = kernels[own]
    approx = newton_forward(kernels, keep)
    for own in range(many):
        approx_out[own] = approx[own]
        proxy = jnp.sqrt(
            heads_sum(jnp.sum(kernels[own] * kernels[own], axis=1, keepdims=True))
        ) * jnp.sqrt(heads_sum(jnp.sum(approx[own] * approx[own], axis=1, keepdims=True)))
        proxies[own] = jnp.broadcast_to(row_of(proxy), (8, PAIR))

    def first_scores(unit, carry):
        seq, rows, lanes = spots(unit)
        score = mm(spread_heads(land[unit, 1]), queries[rows, lanes], NT)
        score = score.reshape(2, SEG, tokens)
        weights = jnp.exp(score - jnp.max(score, axis=1, keepdims=True))
        weights = weights / jnp.sum(weights, axis=1, keepdims=True)
        kernel_one[unit] = weights.reshape(2 * SEG, tokens)
        return carry

    lax.fori_loop(0, units, first_scores, 0, unroll=2)
    for copy in kv_out:
        copy.wait()
    for own in range(many):
        parts = [kv_send[first_unit + own]] + [kv_recv[step, own] for step in range(seq_size - 1)]
        top = parts[0][SEG : SEG + 1]
        for part in parts[1:]:
            top = jnp.maximum(top, part[SEG : SEG + 1])
        scales = [jnp.exp(part[SEG : SEG + 1] - top) for part in parts]
        total = scales[0] * parts[0][SEG + 1 : SEG + 2]
        for scale, part in zip(scales[1:], parts[1:]):
            total = total + scale * part[SEG + 1 : SEG + 2]
        kv_mean = jnp.zeros((SEG, PAIR), jnp.float32)
        for slot, (scale, part) in enumerate(zip(scales, parts)):
            share = scale / total
            shares[own, slot] = jnp.broadcast_to(share, (8, PAIR))
            kv_mean = kv_mean + join_heads(column(share)) * part[:SEG]
        kv_own[own] = kv_mean
        mixed[first_unit + own] = join_heads(
            mm3(split(approx[own]), split(spread_heads(kv_mean)))
        ).astype(jnp.bfloat16)
    mixed_out = passed_on(place, mixed, many, *mixed_sem)
    for copy in mixed_out:
        copy.start()
    for copy in mixed_out:
        copy.wait()

    def combine(unit, carry):
        seq, rows, lanes = spots(unit)
        attended = mm(
            kernel_one[unit].astype(jnp.bfloat16), spread_heads(mixed[unit]), TN
        )
        branch[rows, lanes] = (attended + conv[rows, lanes]).astype(jnp.bfloat16)
        return carry

    lax.fori_loop(0, units, combine, 0, unroll=2)


def attend(x, bounds, weight, bias, taps, batch_size, seq_size, seqs):
    rows, width = x.shape
    tokens = rows // seqs
    units = seqs * (width // PAIR)
    many = -(-units // seq_size)
    slots = seq_size * many
    f32, bf16 = jnp.float32, jnp.bfloat16
    vmem = pl.BlockSpec(memory_space=pltpu.VMEM)
    sems = pltpu.SemaphoreType.DMA
    shapes = (
        ((rows, width), bf16),
        ((rows, width), bf16),
        ((seqs, tokens + BLOCK, width), bf16),
        ((units, 2 * SEG, tokens), f32),
        ((units, 2 * SEG, tokens), f32),
        ((slots, 2, SEG, PAIR), bf16),
        ((slots, SEG, PAIR), bf16),
        ((rows, width), bf16),
        ((many, PAIR, PAIR), f32),
        ((many, PAIR, PAIR), f32),
        ((many, 6, 4, PAIR, PAIR), f32),
        ((many, SEG, PAIR), f32),
        ((many, seq_size, 8, PAIR), f32),
        ((many, 8, PAIR), f32),
    )
    return pl.pallas_call(
        partial(attend_kernel, batch_size, seq_size, seqs, tokens, many),
        out_shape=tuple(jax.ShapeDtypeStruct(*shape) for shape in shapes),
        in_specs=[vmem] * 5,
        out_specs=tuple([vmem] * len(shapes)),
        scratch_shapes=[
            pltpu.VMEM((slots, 2, SEG, PAIR), f32),
            pltpu.VMEM((seq_size - 1, many, 2, SEG, PAIR), f32),
            pltpu.VMEM((slots, SEG + 8, PAIR), f32),
            pltpu.VMEM((seq_size - 1, many, SEG + 8, PAIR), f32),
            pltpu.VMEM((rows, width), f32),
            (sems((seq_size - 1,)),) * 2,
            (sems((seq_size - 1,)),) * 2,
            (sems((seq_size - 1,)),) * 2,
            (sems((seq_size - 1,)),) * 2,
            (sems((2,)),) * 2,
        ],
        compiler_params=pltpu.CompilerParams(
            collective_id=1, has_side_effects=True, vmem_limit_bytes=58 * 2**20
        ),
        name="attend",
    )(x, bounds, weight, bias, taps)


class Ticker:
    def __init__(self):
        self.live = []

    def add(self, generator):
        self.live.append(generator)

    def tick(self):
        keep = []
        for generator in self.live:
            try:
                next(generator)
                keep.append(generator)
            except StopIteration:
                pass
        self.live = keep

    def drain(self):
        while self.live:
            self.tick()


def newton_backward(kernels, approx_grads, keep, tick):
    units = range(len(kernels))
    eye = jnp.where(eye_mask(PAIR), 1.0, 0.0)
    kernel_halves = [split(kernel) for kernel in kernels]
    grads = [jnp.zeros((PAIR, PAIR), jnp.float32) for _ in units]
    after = approx_grads
    for step in reversed(range(6)):
        approx = [split(keep[u, step, 0]) for u in units]
        product = [keep[u, step, 1] for u in units]
        halves = [split(p) for p in product]
        first = [split(7.0 * eye - p) for p in product]
        second = [split(keep[u, step, 2]) for u in units]
        third = [split(keep[u, step, 3]) for u in units]
        wide = [split(0.25 * a) for a in after]
        third_grad = [split(mm3(wide[u], approx[u])) for u in units]
        second_grad = [split(-mm3(third_grad[u], halves[u])) for u in units]
        first_grad = [-mm3(second_grad[u], halves[u]) for u in units]
        product_grad = [
            split(
                -mm3(second[u], third_grad[u]) - mm3(first[u], second_grad[u]) - first_grad[u]
            )
            for u in units
        ]
        grads = [grads[u] + mm3(approx[u], product_grad[u]) for u in units]
        after = [
            mm3(third[u], wide[u]) + mm3(product_grad[u], kernel_halves[u]) for u in units
        ]
        tick()
    out = []
    for u in units:
        kernel = kernels[u]
        fro = heads_sum(jnp.sum(kernel * kernel, axis=1, keepdims=True))
        fro_grad = heads_sum(jnp.sum(after[u] * kernel, axis=1, keepdims=True)) / (fro * fro)
        out.append(grads[u].T + after[u] / fro - 2.0 * kernel * fro_grad)
    return out


def tap_grads(padded_grad, padded, vec, first_row, tokens):
    seqs, _, width = padded.shape
    rows = lax.broadcasted_iota(jnp.int32, (BLOCK, BLOCK), 0)
    cols = lax.broadcasted_iota(jnp.int32, (BLOCK, BLOCK), 1)
    turn = jnp.where(rows + cols == BLOCK - 1, 1.0, 0.0).astype(jnp.bfloat16)

    def step(pair, carry):
        lanes = pl.ds(pl.multiple_of(pair * PAIR, PAIR), PAIR)
        total = [jnp.zeros((BLOCK, 2 * BLOCK), jnp.float32) for _ in range(2)]
        for seq in range(seqs):
            for block in range(tokens // BLOCK):
                window = padded[seq, pl.ds(block * BLOCK, 2 * BLOCK), lanes]
                grad = padded_grad[seq, pl.ds(HALO + block * BLOCK, BLOCK), lanes]
                grad = mm(turn, grad).astype(jnp.bfloat16)
                first = first_head(grad.shape)
                zero = jnp.zeros_like(grad)
                total[0] = total[0] + mm(jnp.where(first, grad, zero), window, NT)
                total[1] = total[1] + mm(jnp.where(first, zero, grad), window, NT)
        for head in range(2):
            turned = pltpu.roll(total[head], 0, 1, stride=1, stride_axis=0)
            sums = jnp.sum(turned, axis=0, keepdims=True)
            sums = pltpu.roll(sums, BLOCK + 1, 1)
            vec[pl.ds(first_row + 2 * pair + head, 1), :] = sums[:, :PAIR]
        return carry

    lax.fori_loop(0, width // PAIR, step, 0)


def back_kernel(
    batch_size, seq_size, seqs, tokens, many, plan, rows,
    grad_branch, x, bounds, weight, taps, queries, keys, values, kernel_one, expo, land, mixed,
    kernel_two, approx, keep, kv_own, shares, proxies, grad_first, vec_in, down_grad, up_grad,
    out_grad,
    input_grad, gathered, vec,
    stage, whole, recv, slots, padded, rest, grad_qkv, turned, acc_send,
    acc_all, land_send, land_recv, land_all, rows_of_weight,
    fill_sem, send_sem, recv_sem, free_sem, vec_sem, out_sem, load_sem, weight_sem, halo_sem, mixed_sem,
    acc_sem, land_sem, land_back_sem,
):
    place = Place(batch_size, seq_size)
    width = x.shape[1]
    pairs = width // PAIR
    units = seqs * pairs
    own_slots = seq_size * many
    quarter = float(SEG) ** -0.25
    core = place.at["core"]
    peers = [place.seq_peer(step) for step in range(1, seq_size)]
    wait_greet = greet(peers + list(place.peers(("core", "z"))))

    loads = [
        pltpu.make_async_copy(
            grad_branch.at[pl.ds(seq * tokens, tokens)],
            padded.at[seq, pl.ds(HALO, tokens)],
            load_sem.at[1 + seq],
        )
        for seq in range(seqs)
    ]
    for copy in loads:
        copy.start()

    arrays = (down_grad, up_grad, out_grad)
    fills = []
    for piece, blocks in enumerate(plan):
        fill = []
        for spot, (array, row, col) in enumerate(blocks):
            for half in range(2):
                if array < 3:
                    fill.append(
                        pltpu.make_async_copy(
                            arrays[array].at[pl.ds(row, 768), pl.ds(col + half * HALF, HALF)],
                            stage.at[piece, half, pl.ds(spot * 768, 768)],
                            fill_sem.at[piece, spot * 2 + half],
                        )
                    )
        for copy in fill:
            copy.start()
        fills.append(fill)

    def piece_run(piece):
        for copy in fills[piece]:
            copy.wait()
        yield from Reduce(
            place, stage.at[piece], whole.at[piece], recv.at[piece],
            send_sem.at[piece], recv_sem.at[piece], free_sem.at[piece], rows,
        ).run()
        outs = [
            pltpu.make_async_copy(
                whole.at[piece], gathered.at[piece, core], out_sem.at[piece, 0]
            ),
            pltpu.make_async_copy(
                stage.at[piece, 1 - core], gathered.at[piece, 1 - core], out_sem.at[piece, 1]
            ),
        ]
        for out in outs:
            out.start()
        yield
        for out in outs:
            out.wait()

    ready = [p for p, blocks in enumerate(plan) if all(b[0] < 3 for b in blocks)]
    ticker = Ticker()

    def tick():
        if ready:
            ticker.add(piece_run(ready.pop(0)))
        ticker.tick()

    zero_past(padded, tokens)
    for copy in loads:
        copy.wait()

    def spots(unit):
        seq, pair = lax.div(unit, pairs), lax.rem(unit, pairs)
        span = pl.ds(pl.multiple_of(seq * tokens, tokens), tokens)
        lanes = pl.ds(pl.multiple_of(pair * PAIR, PAIR), PAIR)
        return seq, span, lanes

    def mixed_parts(unit, carry):
        seq, span, lanes = spots(unit)
        grad = padded[seq, pl.ds(HALO, tokens), lanes]
        land_send[unit, 0] = join_heads(mm(kernel_one[unit].astype(jnp.bfloat16), grad))
        return carry

    lax.fori_loop(0, units, mixed_parts, 0, unroll=2)
    for unit in range(units, own_slots):
        land_send[unit] = jnp.ones_like(land_send[unit])
    wait_greet()
    mixed_out = shared_out(
        place, land_send.at[:, 0], land_recv.at[:, :, 0], many, *mixed_sem
    )
    for copy in mixed_out:
        copy.start()
    halo = halo_copies(place, padded, tokens, *halo_sem)
    for copy in halo:
        copy.start()
    tick()

    def first_grads(unit, carry):
        seq, span, lanes = spots(unit)
        weights = kernel_one[unit]
        grad = mm(spread_heads(mixed[unit]), padded[seq, pl.ds(HALO, tokens), lanes], NT)
        both = (weights * grad).reshape(2, SEG, tokens)
        both = jnp.broadcast_to(jnp.sum(both, axis=1, keepdims=True), both.shape)
        score_grad = (weights * (grad - both.reshape(2 * SEG, tokens))).astype(jnp.bfloat16)
        land_send[unit, 1] = join_heads(mm(score_grad, queries[span, lanes]))
        rest[0, span, lanes] = mm(score_grad, spread_heads(land[unit, 1]), TN)
        return carry

    lax.fori_loop(0, units, first_grads, 0, unroll=2)
    tick()
    for copy in mixed_out:
        copy.wait()
    first_unit = place.seq * many
    kernels, approx_grads = [], []
    for own in range(many):
        total = land_send[first_unit + own, 0]
        for step in range(seq_size - 1):
            total = total + land_recv[step, own, 0]
        total = split(spread_heads(total))
        kv_mean = kv_own[own]
        kv_grad = join_heads(mm3(split(approx[own]), total, TN))
        approx_grads.append(mm3(split(spread_heads(kv_mean)), total, NT))
        kernels.append(kernel_two[own])
        dots = kv_grad * kv_mean
        first = first_head(dots.shape)
        dots = jnp.concatenate(
            [
                jnp.sum(jnp.where(first, dots, 0.0), axis=1, keepdims=True),
                jnp.sum(jnp.where(first, 0.0, dots), axis=1, keepdims=True),
            ],
            axis=0,
        )
        dots = row_of(dots)
        for slot in range(seq_size):
            share = shares[own, slot, pl.ds(0, 1), :]
            scaled = (kv_grad * join_heads(column(share))).astype(jnp.bfloat16)
            high, low = split(-dots * share)
            tail = jnp.concatenate(
                [high, low, jnp.zeros((14, PAIR), jnp.bfloat16)], axis=0
            )
            acc_send[slot, own] = jnp.concatenate([scaled, tail], axis=0)
    acc_out = []
    for step in range(1, seq_size):
        acc_out.append(
            pltpu.make_async_remote_copy(
                src_ref=acc_send.at[seq_size - step],
                dst_ref=acc_all.at[pl.ds(first_unit, many)],
                send_sem=acc_sem[0].at[step - 1],
                recv_sem=acc_sem[1].at[step - 1],
                device_id=place.seq_peer(step),
                device_id_type=MESH_IDS,
            )
        )
    for copy in acc_out:
        copy.start()
    for own in range(many):
        acc_all[first_unit + own] = acc_send[0, own]
    tick()
    for copy in halo:
        copy.wait()
    trim_halo(place, padded, tokens)
    conv_rows(padded, taps, rest.at[2], tokens)
    tick()
    for copy in acc_out:
        copy.wait()

    def third_grads(unit, carry):
        seq, span, lanes = spots(unit)
        packed = acc_all[unit]
        acc = spread_heads(packed[:SEG])
        tail = packed[SEG:].astype(jnp.float32)
        part = mm(acc, values[seq, pl.ds(HALO, tokens), lanes], NT)
        weights = expo[unit]
        score_grad = (weights * (part + column(tail[0:1] + tail[1:2]))).astype(jnp.bfloat16)
        land_send[unit, 0] = join_heads(mm(score_grad, keys[span, lanes]))
        rest[1, span, lanes] = mm(score_grad, spread_heads(land[unit, 0]), TN)
        value_grad = mm(weights.astype(jnp.bfloat16), acc, TN) + rest[2, span, lanes]
        valid = positions(place, tokens, 0) < length_of(bounds, seq)
        grad_qkv[2, span, lanes] = jnp.where(valid, value_grad, 0.0).astype(jnp.bfloat16)
        return carry

    lax.fori_loop(0, units, third_grads, 0, unroll=2)
    land_out = shared_out(place, land_send, land_recv, many, *land_sem)
    for copy in land_out:
        copy.start()
    tick()
    vec[...] = vec_in[...]
    tap_grads(padded, values, vec, 72, tokens)
    tick()
    kernel_grads = newton_backward(kernels, approx_grads, keep, tick)
    extra = []
    for own in range(many):
        kernel, grad = kernels[own], kernel_grads[own]
        score_grad = split(
            kernel * (grad - jnp.sum(kernel * grad, axis=1, keepdims=True))
        )
        both = land[first_unit + own]
        left, right = spread_heads(both[0]), spread_heads(both[1])
        extra.append(
            (
                join_heads(mm(score_grad[0], right) + mm(score_grad[1], right)),
                join_heads(mm(score_grad[0], left, TN) + mm(score_grad[1], left, TN)),
            )
        )
    for copy in land_out:
        copy.wait()
    for own in range(many):
        unit = first_unit + own
        low, high = segment_edges(bounds, jnp.minimum(lax.div(unit, pairs), seqs - 1))
        for slot in range(2):
            total = land_send[unit, slot] + extra[own][slot]
            for step in range(seq_size - 1):
                total = total + land_recv[step, own, slot]
            land_all[unit, slot] = (total / (high - low)).astype(jnp.bfloat16)
        here = unit < units
        row = pl.ds(84 + lax.rem(unit, pairs), 1)
        vec[row, :] = vec[row, :] + jnp.where(here, proxies[own, pl.ds(0, 1), :], 0.0)
    land_back = passed_on(place, land_all, many, *land_back_sem)
    for copy in land_back:
        copy.start()
    turned[...] = x[...].T

    homes = {
        block[2] // width: (piece, spot)
        for piece, blocks in enumerate(plan)
        for spot, block in enumerate(blocks)
        if block[0] == 3
    }

    def weight_grad(third):
        piece, spot = homes[third]

        def step(tile, carry):
            half, part = lax.div(tile, 3), lax.rem(tile, 3)
            lanes = pl.ds(pl.multiple_of(tile * PAIR, PAIR), PAIR)
            here = pl.ds(pl.multiple_of(part * PAIR, PAIR), PAIR)
            grad = mm(turned[...], grad_qkv[third, :, lanes])
            stage[piece, half, pl.ds(spot * 768, 768), here] = grad.astype(jnp.bfloat16)
            return carry

        lax.fori_loop(0, width // PAIR, step, 0)

    def bias_grad(third, first_row):
        for pair in range(pairs):
            cols = grad_qkv[third, :, pl.ds(pair * PAIR, PAIR)].astype(jnp.float32)
            vec[pl.ds(first_row + pair, 1), :] = jnp.sum(cols, axis=0, keepdims=True)

    weight_grad(2)
    bias_grad(2, 66)
    early = [
        p for p, blocks in enumerate(plan)
        if any(b[0] == 3 for b in blocks) and all(b[0] < 3 or b[2] == 2 * width for b in blocks)
    ]
    ready.extend(early)
    tick()
    for copy in land_back:
        copy.wait()
    for seq in range(seqs):
        member = member_of(place, bounds, seq, tokens)
        span = pl.ds(seq * tokens, tokens)
        for pair in range(pairs):
            lanes = pl.ds(pair * PAIR, PAIR)
            both = land_all[seq * pairs + pair]
            for slot in range(2):
                grad = (mm(member, both[slot], TN) + rest[slot, span, lanes]) * quarter
                grad_qkv[slot, span, lanes] = grad.astype(jnp.bfloat16)
    weight_grad(0)
    weight_grad(1)
    ready.extend(
        p for p, blocks in enumerate(plan)
        if any(b[0] == 3 for b in blocks) and p not in early
    )
    bias_grad(0, 60)
    ticker.add(vec_reduce(place, vec, slots, *vec_sem))
    tick()
    load = pltpu.make_async_copy(grad_first, rest.at[0], load_sem.at[0])
    load.start()

    def weight_load(tile):
        return pltpu.make_async_copy(
            weight.at[pl.ds(tile * PAIR, PAIR)], rows_of_weight.at[tile % 2], weight_sem.at[tile % 2]
        )

    weight_load(0).start()
    load.wait()
    for tile in range(pairs):
        if tile + 1 < pairs:
            weight_load(tile + 1).start()
        weight_load(tile).wait()
        lanes = pl.ds(tile * PAIR, PAIR)
        total = rest[0, :, lanes]
        for third in range(3):
            total = total + mm(
                grad_qkv[third], rows_of_weight[tile % 2, :, pl.ds(third * width, width)], NT
            )
        input_grad[:, lanes] = total.astype(jnp.bfloat16)
    while ready:
        tick()
    ticker.drain()


BLOCKS = (
    (0, 0, 0), (0, 768, 0), (0, 1536, 0), (0, 2304, 0),
    (1, 0, 0), (1, 0, 768), (1, 0, 1536), (1, 0, 2304),
    (2, 0, 0), (3, 0, 1536), (3, 0, 0), (3, 0, 768),
)


def attend_back(
    saved, grad_branch, x, bounds, weight, taps, grad_first, vec, down, up, out,
    batch_size, seq_size, seqs,
):
    (
        queries, keys, values, kernel_one, expo, land, mixed, _, kernel_two, approx, keep,
        kv_own, shares, proxies,
    ) = saved
    rows, width = x.shape
    tokens = rows // seqs
    pairs = width // PAIR
    own = -(-seqs * pairs // seq_size)
    owned = seq_size * own
    x_size, y_size = plane_sides(seq_size)
    sizes = {"core": 2, "x": x_size, "y": y_size, "z": batch_size // 2}
    many, piece = piece_plan(sizes)
    plan = [BLOCKS[i : i + many] for i in range(0, len(BLOCKS), many)]
    pieces = len(plan)
    copies = Reduce.copies(sizes)
    vec_steps = sum(sizes[a] - 1 for a in sizes)
    f32, bf16 = jnp.float32, jnp.bfloat16
    vmem = pl.BlockSpec(memory_space=pltpu.VMEM)
    anywhere = pl.BlockSpec(memory_space=pl.ANY)
    sems = pltpu.SemaphoreType.DMA
    pair_sems = (sems((seq_size - 1,)),) * 2
    input_grad, gathered, vec = pl.pallas_call(
        partial(back_kernel, batch_size, seq_size, seqs, tokens, own, plan, piece),
        out_shape=(
            jax.ShapeDtypeStruct((rows, width), bf16),
            jax.ShapeDtypeStruct((pieces, 2, piece, HALF), bf16),
            jax.ShapeDtypeStruct(vec.shape, f32),
        ),
        in_specs=[anywhere] + [vmem] * 2 + [anywhere] + [vmem] * 14 + [anywhere, vmem] + [anywhere] * 3,
        out_specs=(vmem, anywhere, vmem),
        scratch_shapes=[
            pltpu.VMEM((pieces, 2, piece, HALF), bf16),
            pltpu.VMEM((pieces, piece, HALF), bf16),
            pltpu.VMEM((pieces, 2, Reduce.slots(sizes, piece), HALF), bf16),
            pltpu.VMEM((sum(sizes.values()), *vec.shape), f32),
            pltpu.VMEM(values.shape, bf16),
            pltpu.VMEM((3, rows, width), f32),
            pltpu.VMEM((3, rows, width), bf16),
            pltpu.VMEM((width, rows), bf16),
            pltpu.VMEM((seq_size, own, SEG + 16, PAIR), bf16),
            pltpu.VMEM((owned, SEG + 16, PAIR), bf16),
            pltpu.VMEM((owned, 2, SEG, PAIR), f32),
            pltpu.VMEM((seq_size - 1, own, 2, SEG, PAIR), f32),
            pltpu.VMEM((owned, 2, SEG, PAIR), bf16),
            pltpu.VMEM((2, PAIR, 3 * width), bf16),
            sems((pieces, 2 * many)),
            sems((pieces, copies)),
            sems((pieces, copies)),
            pltpu.SemaphoreType.REGULAR((pieces,)),
            (sems((vec_steps,)),) * 2,
            sems((pieces, 2)),
            sems((1 + seqs,)),
            sems((2,)),
            (sems((2,)),) * 2,
            pair_sems,
            pair_sems,
            pair_sems,
            pair_sems,
        ],
        compiler_params=pltpu.CompilerParams(
            collective_id=0, has_side_effects=True, vmem_limit_bytes=62 * 2**20
        ),
        name="attend_back",
    )(
        grad_branch, x, bounds, weight, taps, queries, keys, values, kernel_one, expo, land,
        mixed, kernel_two, approx, keep, kv_own, shares, proxies, grad_first, vec, down, up, out,
    )
    return many, input_grad, gathered, vec


def widen_kernel(in_ref, out_ref):
    out_ref[...] = in_ref[0, 0].astype(jnp.float32)


def widen(gathered, many, first, shape, shift=0):
    down_way = shape[0] > shape[1]
    count = shape[0] // 768 * (shape[1] // 768)

    def source(block, core):
        number = first + lax.rem(block + shift, count)
        return (lax.div(number, many), core, lax.rem(number, many), 0)

    return pl.pallas_call(
        widen_kernel,
        out_shape=jax.ShapeDtypeStruct(shape, jnp.float32),
        grid=(count, 2),
        in_specs=[pl.BlockSpec((1, 1, 768, HALF), source)],
        out_specs=pl.BlockSpec(
            (768, HALF), (lambda b, c: (b, c)) if down_way else (lambda b, c: (0, b * 2 + c))
        ),
        name="widen",
    )(gathered)


epsilon = 1e-05


def layer_norm(hidden):
    row_mean = jnp.mean(hidden, axis=-1, keepdims=True)
    centered = hidden - row_mean
    inv_std = lax.rsqrt(jnp.mean(centered * centered, axis=-1, keepdims=True) + epsilon)
    return (centered * inv_std, inv_std)


def norm_back(grad_normed, normed, inv_std):
    return inv_std * (
        grad_normed
        - jnp.mean(grad_normed, axis=-1, keepdims=True)
        - normed * jnp.mean(grad_normed * normed, axis=-1, keepdims=True)
    )


def body(
    hidden_in,
    seg_bounds,
    qkv_weight,
    query_bias,
    value_bias,
    conv_taps,
    out_weight,
    out_bias,
    first_gain,
    first_shift,
    up_weight,
    up_bias,
    down_weight,
    down_bias,
    second_gain,
    second_shift,
    grad_out,
):
    seq_count, tok_count, model_width = hidden_in.shape
    head_count, tap_count = conv_taps.shape
    ff_width = up_weight.shape[1]
    row_total = seq_count * tok_count
    batch_size, seq_size = lax.axis_size("batch"), lax.axis_size("seq")
    input_rows = hidden_in.reshape(row_total, model_width)
    bias_qkv = jnp.concatenate([query_bias, jnp.zeros_like(query_bias), value_bias])[None]
    tap_rows = jnp.pad(conv_taps, ((0, 0), (0, 2 * BLOCK - tap_count)))
    tap_turned = jnp.pad(conv_taps[:, ::-1], ((0, 0), (0, 2 * BLOCK - tap_count)))
    saved = attend(
        input_rows, seg_bounds, qkv_weight, bias_qkv, tap_rows, batch_size, seq_size, seq_count
    )
    branch = saved[7]
    first_sum = (
        input_rows.astype(jnp.float32)
        + jnp.dot(branch, out_weight, preferred_element_type=jnp.float32)
        + out_bias
    )
    normed_one, inv_one = layer_norm(first_sum)
    mid_rows = normed_one * first_gain + first_shift
    mid_low = mid_rows.astype(jnp.bfloat16)
    up_pre = jnp.dot(mid_low, up_weight, preferred_element_type=jnp.float32) + up_bias
    act_val, gelu_back = jax.vjp(partial(jax.nn.gelu, approximate=False), up_pre)
    act_low = act_val.astype(jnp.bfloat16)
    second_sum = (
        mid_rows + jnp.dot(act_low, down_weight, preferred_element_type=jnp.float32) + down_bias
    )
    normed_two, inv_two = layer_norm(second_sum)
    layer_out = (
        (normed_two * second_gain + second_shift)
        .astype(jnp.bfloat16)
        .reshape(seq_count, tok_count, model_width)
    )
    grad_rows = grad_out.reshape(row_total, model_width).astype(jnp.float32)
    second_gain_grad = jnp.sum(grad_rows * normed_two, axis=0)
    second_shift_grad = jnp.sum(grad_rows, axis=0)
    grad_second = norm_back(grad_rows * second_gain, normed_two, inv_two)
    grad_down = grad_second.astype(jnp.bfloat16)
    down_weight_grad = jnp.einsum(
        "nf,nd->fd", act_low, grad_down, preferred_element_type=jnp.float32
    )
    down_bias_grad = jnp.sum(grad_down.astype(jnp.float32), axis=0)
    (grad_up_val,) = gelu_back(
        jnp.einsum("nd,fd->nf", grad_down, down_weight, preferred_element_type=jnp.float32)
    )
    grad_up = grad_up_val.astype(jnp.bfloat16)
    up_weight_grad = jnp.einsum("nd,nf->df", mid_low, grad_up, preferred_element_type=jnp.float32)
    up_bias_grad = jnp.sum(grad_up.astype(jnp.float32), axis=0)
    grad_mid = grad_second + jnp.einsum(
        "nf,df->nd", grad_up, up_weight, preferred_element_type=jnp.float32
    )
    first_gain_grad = jnp.sum(grad_mid * normed_one, axis=0)
    first_shift_grad = jnp.sum(grad_mid, axis=0)
    grad_first = norm_back(grad_mid * first_gain, normed_one, inv_one)
    grad_proj = grad_first.astype(jnp.bfloat16)
    out_weight_grad = jnp.einsum("nd,ne->de", branch, grad_proj, preferred_element_type=jnp.float32)
    out_bias_grad = jnp.sum(grad_proj.astype(jnp.float32), axis=0)
    grad_branch = (
        jnp.einsum("ne,de->nd", grad_proj, out_weight, preferred_element_type=jnp.float32)
        .astype(jnp.bfloat16)
        .reshape(seq_count, tok_count, model_width)
    )
    vec = jnp.concatenate(
        [
            up_bias_grad,
            down_bias_grad,
            second_gain_grad,
            second_shift_grad,
            out_bias_grad,
            first_gain_grad,
            first_shift_grad,
        ]
    ).reshape(-1, PAIR)
    vec = jnp.pad(vec, ((0, 96 - vec.shape[0]), (0, 0)))
    many, input_grad, gathered, vec = attend_back(
        saved,
        grad_branch.reshape(row_total, model_width),
        input_rows,
        seg_bounds,
        qkv_weight,
        tap_turned,
        grad_first,
        vec,
        down_weight_grad.astype(jnp.bfloat16),
        up_weight_grad.astype(jnp.bfloat16),
        out_weight_grad.astype(jnp.bfloat16),
        batch_size,
        seq_size,
        seq_count,
    )

    def small(first, length):
        return vec[first : first + length // PAIR].reshape(length)

    condition = vec[84:90, ::SEG].reshape(head_count)
    return (
        layer_out,
        input_grad.reshape(hidden_in.shape),
        widen(gathered, many, 9, qkv_weight.shape, 1),
        small(60, model_width),
        small(66, model_width),
        vec[72:84, :tap_count],
        widen(gathered, many, 8, out_weight.shape),
        small(42, model_width),
        small(48, model_width),
        small(54, model_width),
        widen(gathered, many, 4, up_weight.shape),
        small(0, ff_width),
        widen(gathered, many, 0, down_weight.shape),
        small(24, model_width),
        small(30, model_width),
        small(36, model_width),
        condition / (batch_size * seq_count),
    )


def solution(mesh):
    placed = (
        P("batch", "seq", None),
        P("batch", None),
        P(),
        P(),
        P(),
        P(),
        P(),
        P(),
        P(),
        P(),
        P(),
        P(),
        P(),
        P(),
        P(),
        P(),
        P("batch", "seq", None),
    )
    return jax.shard_map(
        body,
        mesh=mesh,
        in_specs=placed,
        out_specs=(
            P("batch", "seq", None),
            P("batch", "seq", None),
            P(),
            P(),
            P(),
            P(),
            P(),
            P(),
            P(),
            P(),
            P(),
            P(),
            P(),
            P(),
            P(),
            P(),
            P(),
        ),
        check_vma=False,
    )
```

```python
import math
from functools import partial

import jax
import jax.numpy as jnp
from jax import lax
from jax.experimental import pallas as pl
from jax.experimental.pallas import tpu as pltpu
from jax.sharding import PartitionSpec as P

epsilon = 1e-05
MESH_IDS = pl.DeviceIdType.MESH
HALF = 384
LANES = 128


def plane_sides(count):
    wide = max(d for d in range(1, math.isqrt(count) + 1) if count % d == 0)
    return wide, count // wide


def axis_sizes(batch_size, seq_size):
    x_size, y_size = plane_sides(seq_size)
    z_size = batch_size // 2
    z_low = 2 if z_size % 2 == 0 else 1
    return {
        "core": 2, "x": x_size, "y": y_size, "z": z_size, "z0": z_low, "z1": z_size // z_low,
    }


class Place:
    def __init__(self, batch_size, seq_size):
        x_size, y_size = plane_sides(seq_size)
        self.sizes = axis_sizes(batch_size, seq_size)
        batch = lax.axis_index("batch")
        seq = lax.axis_index("seq")
        z_low = self.sizes["z0"]
        self.at = {
            "core": lax.rem(batch, 2),
            "z": lax.div(batch, 2),
            "z0": lax.rem(lax.div(batch, 2), z_low),
            "z1": lax.div(batch, 2 * z_low),
            "x": lax.rem(seq, x_size),
            "y": lax.div(seq, x_size),
        }
        self.seq_size = seq_size
        self.seq = seq
        self.batch = batch

    def peer_index(self, axis, step):
        size = self.sizes[axis]
        return lax.rem(self.at[axis] + step, size)

    def device(self, **moved):
        spot = {**self.at, **moved}
        if "z0" in moved or "z1" in moved:
            spot["z"] = spot["z1"] * self.sizes["z0"] + spot["z0"]
        return (spot["z"] * 2 + spot["core"], spot["y"] * self.sizes["x"] + spot["x"])

    def peers(self, axes):
        for axis in axes:
            for step in range(1, self.sizes[axis]):
                yield self.device(**{axis: self.peer_index(axis, step)})

    def seq_peer(self, step):
        return (self.batch, lax.rem(self.seq + step, self.seq_size))


def greet(devices):
    barrier = pltpu.get_barrier_semaphore()
    devices = list(devices)
    for device in devices:
        pl.semaphore_signal(barrier, inc=1, device_id=device, device_id_type=MESH_IDS)
    return lambda: pl.semaphore_wait(barrier, len(devices))


def tile_rows(rows):
    return max(t for t in (96, 64, 48, 32, 16) if rows % t == 0)


def add_rows(out_ref, in_ref, at, parts, rows):
    tile = tile_rows(rows)

    def step(index, carry):
        start = pl.multiple_of(at + index * tile, 16)
        total = in_ref[pl.ds(start, tile), :].astype(jnp.float32)
        for ref, first in parts:
            total = total + ref[pl.ds(pl.multiple_of(first + index * tile, 16), tile), :].astype(
                jnp.float32
            )
        out_ref[pl.ds(start, tile), :] = total.astype(out_ref.dtype)
        return carry

    lax.fori_loop(0, rows // tile, step, 0)


class Reduce:
    def __init__(
        self, number, place, orders, stage, whole, recv, send_sem, recv_sem, free_sem, rows
    ):
        self.number, self.make_place, self.orders = number, place, orders
        self.stage, self.whole, self.recv = stage, whole, recv
        self.send_sem, self.recv_sem, self.free_sem = send_sem, recv_sem, free_sem
        self.part = rows // len(orders)

    @staticmethod
    def slots(sizes, orders, rows):
        need = []
        for order in orders:
            size, slot = rows // len(orders), 0
            for axis in order:
                size //= sizes[axis]
                slot += (sizes[axis] - 1) * size
            need.append(slot)
        return max(need)

    @staticmethod
    def copies(sizes, orders):
        return 2 + 2 * sum(sizes[axis] - 1 for order in orders for axis in order)

    def level_of(self, place, half, level):
        base, size, slot = half * self.part, self.part, 0
        order = self.orders[half]
        sem = 2 + 2 * half * sum(place.sizes[axis] - 1 for axis in order)
        for axis in order[:level]:
            count = place.sizes[axis]
            size //= count
            slot += (count - 1) * size
            sem += 2 * (count - 1)
            base = base + place.at[axis] * size
        count = place.sizes[order[level]]
        return order[level], count, base, size // count, slot, sem

    def copy(self, index, src, dst, device):
        return pltpu.make_async_remote_copy(
            src_ref=src,
            dst_ref=dst,
            send_sem=self.send_sem.at[self.number, index],
            recv_sem=self.recv_sem.at[self.number, index],
            device_id=device,
            device_id_type=MESH_IDS,
        )

    @staticmethod
    def rows_of(ref, start, rows):
        return ref.at[pl.ds(pl.multiple_of(start, 16), rows)]

    def scatter(self, half, level):
        place = self.make_place()
        axis, count, base, chunk, slot, sem = self.level_of(place, half, level)
        mine = self.stage.at[place.at["core"]]
        copies = []
        for step in range(1, count):
            peer = place.peer_index(axis, step)
            copies.append(
                self.copy(
                    sem + step - 1,
                    self.rows_of(mine, base + peer * chunk, chunk),
                    self.recv.at[half, pl.ds(slot + (step - 1) * chunk, chunk)],
                    place.device(**{axis: peer}),
                )
            )
        return copies

    def spread(self, half, level):
        place = self.make_place()
        axis, count, base, chunk, slot, sem = self.level_of(place, half, level)
        here = self.rows_of(self.whole, base + place.at[axis] * chunk, chunk)
        return [
            self.copy(
                sem + count - 1 + step - 1,
                here,
                here,
                place.device(**{axis: place.peer_index(axis, step)}),
            )
            for step in range(1, count)
        ]

    def add_level(self, half, level):
        place = self.make_place()
        axis, count, base, chunk, slot, _ = self.level_of(place, half, level)
        mine = self.stage.at[place.at["core"]]
        add_rows(
            self.whole if level == len(self.orders[half]) - 1 else mine,
            mine,
            base + place.at[axis] * chunk,
            [(self.recv.at[half], slot + k * chunk) for k in range(count - 1)],
            chunk,
        )

    def core_out(self):
        place = self.make_place()
        core = place.at["core"]
        return self.copy(0, self.stage.at[1 - core], self.whole, place.device(core=1 - core))

    def core_back(self):
        place = self.make_place()
        core = place.at["core"]
        return self.copy(1, self.whole, self.stage.at[core], place.device(core=1 - core))

    def run(self):
        halves = range(len(self.orders))
        self.core_out().start()
        yield
        self.core_out().wait()
        place = self.make_place()
        other = place.device(core=1 - place.at["core"])
        pl.semaphore_signal(
            self.free_sem.at[self.number], inc=1, device_id=other, device_id_type=MESH_IDS
        )
        mine = self.stage.at[place.at["core"]]
        for half in halves:
            start = half * self.part
            add_rows(mine, mine, start, [(self.whole, start)], self.part)
            for copy in self.scatter(half, 0):
                copy.start()
        last = len(self.orders[0]) - 1
        for level in range(last + 1):
            yield
            for half in halves:
                for copy in self.scatter(half, level):
                    copy.wait()
                self.add_level(half, level)
                later = self.scatter if level < last else self.spread
                for copy in later(half, min(level + 1, last)):
                    copy.start()
        for level in reversed(range(last + 1)):
            yield
            for half in halves:
                for copy in self.spread(half, level):
                    copy.wait()
                for copy in self.spread(half, level - 1) if level else ():
                    copy.start()
        pl.semaphore_wait(self.free_sem.at[self.number], 1)
        self.core_back().start()
        yield
        self.core_back().wait()


def vec_reduce(place, acc, slots, send_sem, recv_sem):
    sem = 0
    level = 0
    for axis in ("core", "x", "y", "z"):
        count = place.sizes[axis]
        copies = []
        here = place.at[axis]
        for step in range(1, count):
            copies.append(
                pltpu.make_async_remote_copy(
                    src_ref=acc,
                    dst_ref=slots.at[level + here],
                    send_sem=send_sem.at[sem],
                    recv_sem=recv_sem.at[sem],
                    device_id=place.device(**{axis: place.peer_index(axis, step)}),
                    device_id_type=MESH_IDS,
                )
            )
            sem += 1
        for copy in copies:
            copy.start()
        slots[level + here] = acc[...]
        yield
        for copy in copies:
            copy.wait()
        total = slots[level]
        for index in range(1, count):
            total = total + slots[level + index]
        acc[...] = total
        level += count


SEG = 64
PAIR = 128
HALO = 16
BLOCK = 128
FAR = -1e30
NT = ((1,), (1,))
TN = ((0,), (0,))
NN = ((1,), (0,))


def mm(left, right, dims=NN):
    return lax.dot_general(left, right, (dims, ((), ())), preferred_element_type=jnp.float32)


def split(array):
    high = array.astype(jnp.bfloat16)
    return high, (array - high.astype(jnp.float32)).astype(jnp.bfloat16)


def thirds(array):
    high = array.astype(jnp.bfloat16)
    middle = (array - high.astype(jnp.float32)).astype(jnp.bfloat16)
    rest = array - high.astype(jnp.float32) - middle.astype(jnp.float32)
    return high, middle, rest.astype(jnp.bfloat16)


def mm3(left, right, dims=NN):
    left_high, left_low = left
    right_high, right_low = right
    (left_dim,), (right_dim,) = dims
    return mm(
        jnp.concatenate([left_high, left_high, left_low], axis=left_dim),
        jnp.concatenate([right_high, right_low, right_high], axis=right_dim),
        dims,
    )


def eye_mask(size):
    rows = lax.broadcasted_iota(jnp.int32, (size, size), 0)
    return rows == lax.broadcasted_iota(jnp.int32, (size, size), 1)


def column(row):
    return jnp.sum(jnp.where(eye_mask(row.shape[1]), row, 0.0), axis=1, keepdims=True)


def row_of(col):
    return jnp.sum(jnp.where(eye_mask(col.shape[0]), col, 0.0), axis=0, keepdims=True)


def first_head(shape):
    return lax.broadcasted_iota(jnp.int32, shape, len(shape) - 1) < SEG


def spread_heads(pair):
    first = first_head(pair.shape)
    zero = jnp.zeros_like(pair)
    return jnp.concatenate([jnp.where(first, pair, zero), jnp.where(first, zero, pair)], axis=0)


def join_heads(blocks):
    shape = (SEG, PAIR)
    return jnp.where(
        first_head(shape),
        jnp.broadcast_to(blocks[:SEG], shape),
        jnp.broadcast_to(blocks[SEG:], shape),
    )


def heads_sum(col):
    first = jnp.sum(col[:SEG], axis=0, keepdims=True)
    second = jnp.sum(col[SEG:], axis=0, keepdims=True)
    return jnp.concatenate(
        [jnp.broadcast_to(first, (SEG, 1)), jnp.broadcast_to(second, (SEG, 1))], axis=0
    )


def shared_out(place, source, target, many, send_sem, recv_sem):
    copies = []
    for step in range(1, place.seq_size):
        device = place.seq_peer(step)
        copies.append(
            pltpu.make_async_remote_copy(
                src_ref=source.at[pl.ds(device[1] * many, many)],
                dst_ref=target.at[step - 1],
                send_sem=send_sem.at[step - 1],
                recv_sem=recv_sem.at[step - 1],
                device_id=device,
                device_id_type=MESH_IDS,
            )
        )
    return copies


def passed_on(place, array, many, send_sem, recv_sem):
    copies = []
    here = array.at[pl.ds(place.seq * many, many)]
    for step in range(1, place.seq_size):
        copies.append(
            pltpu.make_async_remote_copy(
                src_ref=here,
                dst_ref=here,
                send_sem=send_sem.at[step - 1],
                recv_sem=recv_sem.at[step - 1],
                device_id=place.seq_peer(step),
                device_id_type=MESH_IDS,
            )
        )
    return copies


def halo_copies(place, padded, tokens, send_sem, recv_sem):
    copies = []
    for index, (step, first, there) in enumerate(
        ((1, tokens, 0), (place.seq_size - 1, HALO, tokens + HALO))
    ):
        copies.append(
            pltpu.make_async_remote_copy(
                src_ref=padded.at[:, pl.ds(first, HALO)],
                dst_ref=padded.at[:, pl.ds(there, HALO)],
                send_sem=send_sem.at[index],
                recv_sem=recv_sem.at[index],
                device_id=place.seq_peer(step),
                device_id_type=MESH_IDS,
            )
        )
    return copies


def trim_halo(place, padded, tokens):
    zero = jnp.zeros((padded.shape[0], HALO, padded.shape[2]), padded.dtype)
    low, high = pl.ds(0, HALO), pl.ds(tokens + HALO, HALO)
    padded[:, low] = jnp.where(place.seq > 0, padded[:, low], zero)
    padded[:, high] = jnp.where(place.seq < place.seq_size - 1, padded[:, high], zero)


def zero_past(padded, tokens):
    past = tokens + 2 * HALO
    rest = padded.shape[1] - past
    padded[:, pl.ds(past, rest)] = jnp.zeros(
        (padded.shape[0], rest, padded.shape[2]), padded.dtype
    )


def band(taps):
    wide = jnp.broadcast_to(taps, (BLOCK, 2 * BLOCK))
    return pltpu.roll(wide, 0, 1, stride=1, stride_axis=0).astype(jnp.bfloat16)


def tap_lanes(taps):
    heads, count = taps.shape
    wide = jnp.concatenate(
        [taps[...], jnp.zeros((heads, 2 * BLOCK - count), jnp.float32)], axis=1
    )
    return jnp.concatenate([wide, jnp.zeros((16 - heads, 2 * BLOCK), jnp.float32)], axis=0)


def turned_taps(taps):
    shape = (2 * BLOCK, 2 * BLOCK)
    ends = lax.broadcasted_iota(jnp.int32, shape, 0) + lax.broadcasted_iota(jnp.int32, shape, 1)
    turn = jnp.where(ends == taps.shape[1] - 1, 1.0, 0.0).astype(jnp.bfloat16)
    return mm(tap_lanes(taps).astype(jnp.bfloat16), turn)


def conv_rows(padded, taps, out, tokens, span=None):
    seqs, _, width = padded.shape

    def step(pair, carry):
        lanes = pl.ds(pl.multiple_of(pair * PAIR, PAIR), PAIR)
        first = band(taps[pl.ds(2 * pair, 1), :])
        second = band(taps[pl.ds(2 * pair + 1, 1), :])
        for seq in range(seqs):
            for block in range(tokens // BLOCK):
                window = padded[seq, pl.ds(block * BLOCK, 2 * BLOCK), lanes]
                both = jnp.where(
                    first_head((BLOCK, PAIR)), mm(first, window), mm(second, window)
                )
                out[pl.ds(seq * tokens + block * BLOCK, BLOCK), lanes] = both
        return carry

    lax.fori_loop(*(span or (0, width // PAIR)), step, 0)


def segment_edges(bounds, seq):
    low = column(bounds[pl.ds(seq, 1), pl.ds(0, SEG)].astype(jnp.float32))
    high = column(bounds[pl.ds(seq, 1), pl.ds(1, SEG)].astype(jnp.float32))
    return low, high


def positions(place, tokens, axis):
    shape = (tokens, 1) if axis == 0 else (1, tokens)
    return (place.seq * tokens + lax.broadcasted_iota(jnp.int32, shape, axis)).astype(jnp.float32)


def member_of(place, bounds, seq, tokens):
    low, high = segment_edges(bounds, seq)
    where = positions(place, tokens, 1)
    return jnp.where((where >= low) & (where < high), 1.0, 0.0).astype(jnp.bfloat16)


def length_of(bounds, seq):
    return bounds[pl.ds(seq, 1), pl.ds(SEG, 1)].astype(jnp.float32)


def newton_forward(kernels, keep):
    eye = jnp.where(eye_mask(PAIR), 1.0, 0.0)
    approx = []
    for kernel in kernels:
        fro = heads_sum(jnp.sum(kernel * kernel, axis=1, keepdims=True))
        approx.append(kernel.T / fro)
    halves = [split(kernel) for kernel in kernels]
    units = range(len(kernels))
    for step in range(6):
        wide = [split(a) for a in approx]
        product = [mm3(halves[u], wide[u]) for u in units]
        lefts = [split(p) for p in product]
        inner = [15.0 * eye - mm3(lefts[u], split(7.0 * eye - product[u])) for u in units]
        outer = [13.0 * eye - mm3(lefts[u], split(inner[u])) for u in units]
        for u in units:
            for slot, value in enumerate((approx[u], product[u], inner[u], outer[u])):
                keep[u, step, slot] = value
        approx = [0.25 * mm3(wide[u], split(outer[u])) for u in units]
    return approx


def attend_kernel(
    batch_size, seq_size, seqs, tokens, many,
    x, bounds, weight, query_bias, value_bias, taps,
    queries, keys, values, kernel_one, expo, land, mixed, branch, kernel_two, approx_out, keep,
    kv_own, shares, proxies,
    land_send, land_recv, kv_send, kv_recv, conv, tap_rows, biases,
    land_sem, land_back_sem, kv_sem, mixed_sem, halo_sem,
):
    place = Place(batch_size, seq_size)
    width = x.shape[1]
    pairs = width // PAIR
    units = seqs * pairs
    wait_greet = greet(place.seq_peer(step) for step in range(1, seq_size))
    quarter = float(SEG) ** -0.25

    tap_rows[...] = tap_lanes(taps)
    biases[...] = jnp.zeros_like(biases)
    biases[pl.ds(0, 1), :] = query_bias[...].reshape(1, width)
    biases[pl.ds(2, 1), :] = value_bias[...].reshape(1, width)

    def project(out_ref, third):
        def step(tile, carry):
            lanes = pl.ds(pl.multiple_of(third * width + tile * 256, 256), 256)
            here = pl.ds(pl.multiple_of(tile * 256, 256), 256)
            rows = mm(x[...], weight[:, lanes]) + biases[pl.ds(third, 1), here]
            if third < 2:
                out_ref[:, here] = (rows * quarter).astype(jnp.bfloat16)
            else:
                for seq in range(seqs):
                    valid = positions(place, tokens, 0) < length_of(bounds, seq)
                    out_ref[seq, pl.ds(HALO, tokens), here] = jnp.where(
                        valid, rows[seq * tokens : (seq + 1) * tokens], 0.0
                    ).astype(jnp.bfloat16)
            return carry

        lax.fori_loop(0, width // 256, step, 0)

    project(queries, 0)
    project(keys, 1)
    for seq in range(seqs):
        member = member_of(place, bounds, seq, tokens)
        for slot, rows in enumerate((queries, keys)):
            sums = mm(member, rows[pl.ds(seq * tokens, tokens), :])
            for pair in range(pairs):
                land_send[seq * pairs + pair, slot] = sums[:, pair * PAIR : (pair + 1) * PAIR]
    for unit in range(units, seq_size * many):
        land_send[unit] = jnp.ones_like(land_send[unit])
        kv_send[unit] = jnp.ones_like(kv_send[unit])
    wait_greet()
    land_out = shared_out(place, land_send, land_recv, many, *land_sem)
    for copy in land_out:
        copy.start()
    project(values, 2)
    halo = halo_copies(place, values, tokens, *halo_sem)
    for copy in halo:
        copy.start()
    zero_past(values, tokens)
    for copy in land_out:
        copy.wait()
    first_unit = place.seq * many
    for own in range(many):
        unit = first_unit + own
        total = land_send[unit]
        for step in range(seq_size - 1):
            total = total + land_recv[step, own]
        low, high = segment_edges(bounds, jnp.minimum(lax.div(unit, pairs), seqs - 1))
        land[unit] = (total / (high - low)).astype(jnp.bfloat16)
    land_back = passed_on(place, land, many, *land_back_sem)
    for copy in land_back:
        copy.start()
    for copy in halo:
        copy.wait()
    trim_halo(place, values, tokens)
    conv_rows(values, tap_rows, conv, tokens)
    for copy in land_back:
        copy.wait()

    def spots(unit):
        seq, pair = lax.div(unit, pairs), lax.rem(unit, pairs)
        rows = pl.ds(pl.multiple_of(seq * tokens, tokens), tokens)
        lanes = pl.ds(pl.multiple_of(pair * PAIR, PAIR), PAIR)
        return seq, rows, lanes

    def third_scores(unit, carry):
        seq, rows, lanes = spots(unit)
        score = mm(spread_heads(land[unit, 0]), keys[rows, lanes], NT)
        valid = positions(place, tokens, 1) < length_of(bounds, seq)
        score = jnp.where(valid, score, FAR)
        top = jnp.max(score, axis=1, keepdims=True)
        weights = jnp.exp(score - top)
        expo[unit] = weights
        total = jnp.sum(weights, axis=1, keepdims=True)
        part = mm(weights.astype(jnp.bfloat16), values[seq, pl.ds(HALO, tokens), lanes])
        kv_send[unit, pl.ds(0, SEG)] = join_heads(part).astype(jnp.bfloat16)
        kv_send[unit, pl.ds(SEG, 16)] = jnp.concatenate(
            [*thirds(row_of(top)), *thirds(row_of(total)), jnp.zeros((10, PAIR), jnp.bfloat16)],
            axis=0,
        )
        return carry

    lax.fori_loop(0, units, third_scores, 0, unroll=2)
    kv_out = shared_out(place, kv_send, kv_recv, many, *kv_sem)
    for copy in kv_out:
        copy.start()

    kernels = []
    same = (
        lax.broadcasted_iota(jnp.int32, (PAIR, PAIR), 0) < SEG
    ) == first_head((PAIR, PAIR))
    for own in range(many):
        both = land[first_unit + own]
        score = jnp.where(same, mm(spread_heads(both[0]), spread_heads(both[1]), NT), FAR)
        weights = jnp.exp(score - jnp.max(score, axis=1, keepdims=True))
        kernels.append(weights / jnp.sum(weights, axis=1, keepdims=True))
        kernel_two[own] = kernels[own]
    approx = newton_forward(kernels, keep)
    for own in range(many):
        approx_out[own] = approx[own]
        proxy = jnp.sqrt(
            heads_sum(jnp.sum(kernels[own] * kernels[own], axis=1, keepdims=True))
        ) * jnp.sqrt(heads_sum(jnp.sum(approx[own] * approx[own], axis=1, keepdims=True)))
        proxies[own] = jnp.broadcast_to(row_of(proxy), (8, PAIR))

    def first_scores(unit, carry):
        seq, rows, lanes = spots(unit)
        score = mm(spread_heads(land[unit, 1]), queries[rows, lanes], NT)
        score = score.reshape(2, SEG, tokens)
        weights = jnp.exp(score - jnp.max(score, axis=1, keepdims=True))
        weights = weights / jnp.sum(weights, axis=1, keepdims=True)
        kernel_one[unit] = weights.reshape(2 * SEG, tokens)
        return carry

    lax.fori_loop(0, units, first_scores, 0, unroll=2)
    for copy in kv_out:
        copy.wait()
    for own in range(many):
        parts, tops, totals = [], [], []
        for packed in [kv_send[first_unit + own]] + [
            kv_recv[step, own] for step in range(seq_size - 1)
        ]:
            packed = packed.astype(jnp.float32)
            tail = packed[SEG:]
            parts.append(packed[:SEG])
            tops.append(tail[0:1] + tail[1:2] + tail[2:3])
            totals.append(tail[3:4] + tail[4:5] + tail[5:6])
        top = tops[0]
        for other in tops[1:]:
            top = jnp.maximum(top, other)
        scales = [jnp.exp(other - top) for other in tops]
        total = sum(scale * part for scale, part in zip(scales, totals))
        kv_mean = jnp.zeros((SEG, PAIR), jnp.float32)
        for slot, (scale, part) in enumerate(zip(scales, parts)):
            share = scale / total
            shares[own, slot] = jnp.broadcast_to(share, (8, PAIR))
            kv_mean = kv_mean + join_heads(column(share)) * part
        kv_own[own] = kv_mean
        mixed[first_unit + own] = join_heads(
            mm3(split(approx[own]), split(spread_heads(kv_mean)))
        ).astype(jnp.bfloat16)
    mixed_out = passed_on(place, mixed, many, *mixed_sem)
    for copy in mixed_out:
        copy.start()
    for copy in mixed_out:
        copy.wait()

    def combine(unit, carry):
        seq, rows, lanes = spots(unit)
        attended = mm(
            kernel_one[unit].astype(jnp.bfloat16), spread_heads(mixed[unit]), TN
        )
        branch[rows, lanes] = (attended + conv[rows, lanes]).astype(jnp.bfloat16)
        return carry

    lax.fori_loop(0, units, combine, 0, unroll=2)


def attend(
    x, bounds, weight, query_bias, value_bias, taps, batch_size, seq_size, seqs
):
    rows, width = x.shape
    tokens = rows // seqs
    units = seqs * (width // PAIR)
    many = -(-units // seq_size)
    slots = seq_size * many
    f32, bf16 = jnp.float32, jnp.bfloat16
    vmem = pl.BlockSpec(memory_space=pltpu.VMEM)
    sems = pltpu.SemaphoreType.DMA
    shapes = (
        ((rows, width), bf16),
        ((rows, width), bf16),
        ((seqs, tokens + BLOCK, width), bf16),
        ((units, 2 * SEG, tokens), f32),
        ((units, 2 * SEG, tokens), f32),
        ((slots, 2, SEG, PAIR), bf16),
        ((slots, SEG, PAIR), bf16),
        ((rows, width), bf16),
        ((many, PAIR, PAIR), f32),
        ((many, PAIR, PAIR), f32),
        ((many, 6, 4, PAIR, PAIR), f32),
        ((many, SEG, PAIR), f32),
        ((many, seq_size, 8, PAIR), f32),
        ((many, 8, PAIR), f32),
    )
    return pl.pallas_call(
        partial(attend_kernel, batch_size, seq_size, seqs, tokens, many),
        out_shape=tuple(jax.ShapeDtypeStruct(*shape) for shape in shapes),
        in_specs=[vmem] * 6,
        out_specs=tuple([vmem] * len(shapes)),
        scratch_shapes=[
            pltpu.VMEM((slots, 2, SEG, PAIR), f32),
            pltpu.VMEM((seq_size - 1, many, 2, SEG, PAIR), f32),
            pltpu.VMEM((slots, SEG + 16, PAIR), bf16),
            pltpu.VMEM((seq_size - 1, many, SEG + 16, PAIR), bf16),
            pltpu.VMEM((rows, width), f32),
            pltpu.VMEM((16, 2 * BLOCK), f32),
            pltpu.VMEM((8, width), f32),
            (sems((seq_size - 1,)),) * 2,
            (sems((seq_size - 1,)),) * 2,
            (sems((seq_size - 1,)),) * 2,
            (sems((seq_size - 1,)),) * 2,
            (sems((2,)),) * 2,
        ],
        compiler_params=pltpu.CompilerParams(
            collective_id=1, has_side_effects=True, vmem_limit_bytes=58 * 2**20
        ),
        name="attend",
    )(x, bounds, weight, query_bias, value_bias, taps)


def newton_backward(kernels, approx_grads, keep, tick):
    units = range(len(kernels))
    eye = jnp.where(eye_mask(PAIR), 1.0, 0.0)
    kernel_halves = [split(kernel) for kernel in kernels]
    grads = [jnp.zeros((PAIR, PAIR), jnp.float32) for _ in units]
    after = approx_grads
    for step in reversed(range(6)):
        approx = [split(keep[u, step, 0]) for u in units]
        product = [keep[u, step, 1] for u in units]
        halves = [split(p) for p in product]
        first = [split(7.0 * eye - p) for p in product]
        second = [split(keep[u, step, 2]) for u in units]
        third = [split(keep[u, step, 3]) for u in units]
        wide = [split(0.25 * a) for a in after]
        third_grad = [split(mm3(wide[u], approx[u])) for u in units]
        second_grad = [split(-mm3(third_grad[u], halves[u])) for u in units]
        first_grad = [-mm3(second_grad[u], halves[u]) for u in units]
        product_grad = [
            split(
                -mm3(second[u], third_grad[u]) - mm3(first[u], second_grad[u]) - first_grad[u]
            )
            for u in units
        ]
        grads = [grads[u] + mm3(approx[u], product_grad[u]) for u in units]
        after = [
            mm3(third[u], wide[u]) + mm3(product_grad[u], kernel_halves[u]) for u in units
        ]
        tick(f"newton{step}")
    out = []
    for u in units:
        kernel = kernels[u]
        fro = heads_sum(jnp.sum(kernel * kernel, axis=1, keepdims=True))
        fro_grad = heads_sum(jnp.sum(after[u] * kernel, axis=1, keepdims=True)) / (fro * fro)
        out.append(grads[u].T + after[u] / fro - 2.0 * kernel * fro_grad)
    return out


def tap_grads(padded_grad, padded, vec, first_row, tokens, span):
    seqs, _, width = padded.shape
    rows = lax.broadcasted_iota(jnp.int32, (BLOCK, BLOCK), 0)
    cols = lax.broadcasted_iota(jnp.int32, (BLOCK, BLOCK), 1)
    turn = jnp.where(rows + cols == BLOCK - 1, 1.0, 0.0).astype(jnp.bfloat16)

    def step(pair, carry):
        lanes = pl.ds(pl.multiple_of(pair * PAIR, PAIR), PAIR)
        total = [jnp.zeros((BLOCK, 2 * BLOCK), jnp.float32) for _ in range(2)]
        for seq in range(seqs):
            for block in range(tokens // BLOCK):
                window = padded[seq, pl.ds(block * BLOCK, 2 * BLOCK), lanes]
                grad = padded_grad[seq, pl.ds(HALO + block * BLOCK, BLOCK), lanes]
                grad = mm(turn, grad).astype(jnp.bfloat16)
                first = first_head(grad.shape)
                zero = jnp.zeros_like(grad)
                total[0] = total[0] + mm(jnp.where(first, grad, zero), window, NT)
                total[1] = total[1] + mm(jnp.where(first, zero, grad), window, NT)
        for head in range(2):
            turned = pltpu.roll(total[head], 0, 1, stride=1, stride_axis=0)
            sums = jnp.sum(turned, axis=0, keepdims=True)
            sums = pltpu.roll(sums, BLOCK + 1, 1)
            vec[pl.ds(first_row + 2 * pair + head, 1), :] = sums[:, :PAIR]
        return carry

    lax.fori_loop(*span, step, 0)


class Ticker:
    def __init__(self, points):
        self.live = {}
        self.points = points

    def add(self, number, generator):
        next(generator)
        self.live[number] = generator

    def step(self, number):
        try:
            next(self.live[number])
        except StopIteration:
            del self.live[number]

    def tick(self, point):
        for number in self.points.get(point, ()):
            if number in self.live:
                self.step(number)

    def drain(self, order=()):
        for number in order:
            if number in self.live:
                self.step(number)
        while self.live:
            for number in list(self.live):
                self.step(number)


POINTS = {
    "back1": (0,),
    "back2": (1,),
    "mid0": (2, 3, 0, 1),
    "wait_mixed": (0, 1),
    "conv0": (2, 3),
    "third2": (0,),
    "value": (1,),
    "taps0": (2, 3),
    "taps2": (4,),
    "wait_back": (4, 0),
    "grads": (1, 4, 0, 3, 2),
    "input5": (1,),
}
LAST = (5, 0, 4, 0, 3, "vec", 2, 0, 1, 5, 1, "vec", 4, 1, 3, 2, 5, "vec", 4, 5, 3, 2, 4, "vec", 5, 3, 2, 4, 5, 3, 2, 4, 5, 5, 5)


class Sums:
    def __init__(self, ref):
        self.ref = ref

    def clear(self):
        self.ref[...] = jnp.zeros_like(self.ref)

    def add(self, row, array):
        here = pl.ds(row, 1)
        self.ref[here, :] = self.ref[here, :] + jnp.sum(array, axis=0, keepdims=True)


def normalize(hidden):
    centered = hidden - jnp.mean(hidden, axis=1, keepdims=True)
    inverse = lax.rsqrt(jnp.mean(centered * centered, axis=1, keepdims=True) + epsilon)
    return centered * inverse, inverse


def normalize_back(grad, normed, inverse):
    return inverse * (
        grad
        - jnp.mean(grad, axis=1, keepdims=True)
        - normed * jnp.mean(grad * normed, axis=1, keepdims=True)
    )


def row_vector(ref):
    return ref[...].reshape(1, ref.shape[0])


def back_kernel(
    batch_size, seq_size, seqs, tokens, many, plan,
    x_in, grad_out, branch_in, out_weight, up_weight, down_weight, qkv_weight,
    queries_in, keys_in, values_in, kernel_one_in, expo_in, keep_in,
    bounds, taps, land, mixed, kernel_two, approx, kv_own, shares, proxies,
    out_bias, first_gain, first_shift, up_bias, down_bias, second_gain, second_shift,
    layer_out, input_grad, gathered, vec,
    stage, whole, recv, slots, padded, grad_first, tap_rows, sums, up_sums, acc_send, acc_all,
    land_send, land_recv, land_all,
    load_sem, weight_sem, send_sem, recv_sem, free_sem, vec_sem, out_sem, halo_sem, mixed_sem,
    acc_sem, land_sem, land_back_sem,
):
    place = Place(batch_size, seq_size)
    rows, width = x_in.shape
    ff_blocks = down_weight.shape[0] // width
    pairs = width // PAIR
    units = seqs * pairs
    quarter = float(SEG) ** -0.25
    wait_greet = greet(
        [place.seq_peer(step) for step in range(1, seq_size)] + list(place.peers(("core", "z")))
    )
    ticker = Ticker(POINTS)
    tick = ticker.tick
    bf16 = jnp.bfloat16

    def piece_run(number):
        piece = plan[number]
        here = pl.ds(piece.start, piece.rows)
        yield from Reduce(
            number, lambda: Place(batch_size, seq_size), piece.orders, stage.at[:, here],
            whole.at[here], recv.at[:, piece.slots], send_sem, recv_sem, free_sem, piece.rows,
        ).run()

        def outs():
            core = Place(batch_size, seq_size).at["core"]
            return (
                pltpu.make_async_copy(
                    whole.at[here], gathered.at[core, here], out_sem.at[number, 0]
                ),
                pltpu.make_async_copy(
                    stage.at[1 - core, here], gathered.at[1 - core, here], out_sem.at[number, 1]
                ),
            )

        for out in outs():
            out.start()
        yield
        for out in outs():
            out.wait()

    done = set()

    def staged(*blocks):
        done.update(blocks)
        for number, piece in enumerate(plan):
            if done.issuperset(piece.blocks) and not set(blocks).isdisjoint(piece.blocks):
                ticker.add(number, piece_run(number))

    def store_block(block, first, grad):
        at = pl.ds(pl.multiple_of(block * width + first, 16), grad.shape[0])
        grad = grad.astype(bf16)
        stage[0, at, :] = grad[:, :HALF]
        stage[1, at, :] = grad[:, HALF:]

    def loop(count, step):
        def run(index, carry):
            step(index)
            return carry

        lax.fori_loop(0, count, run, 0)

    def feed_forward(
        x, branch, grads, mid_low, turned, low, normed_one, grad_second, inverse_one, out_w, ff_w,
        act, slope, up_bias_row,
    ):
        def load(index, source, target):
            return pltpu.make_async_copy(source, target, load_sem.at[index])

        first = [load(0, out_weight, out_w), load(1, branch_in, branch), load(2, x_in, x)]
        for copy in first:
            copy.start()
        grads_load = load(3, grad_out, grads)

        def up_load(block):
            return pltpu.make_async_copy(
                up_weight.at[:, pl.ds(block * width, width)], ff_w.at[block], weight_sem.at[block]
            )

        def down_load(block):
            return pltpu.make_async_copy(
                down_weight.at[pl.ds(block * width, width)], ff_w.at[block], weight_sem.at[block]
            )

        for block in range(ff_blocks):
            up_load(block).start()
        grads_load.start()
        total = Sums(sums)
        total.clear()
        up_bias_row[...] = row_vector(up_bias)
        for copy in first:
            copy.wait()
        tile = 128

        def project(index):
            here = pl.ds(pl.multiple_of(index * tile, tile), tile)
            hidden = x[here, :].astype(jnp.float32) + mm(branch[here, :], out_w[...])
            normed, inverse = normalize(hidden + row_vector(out_bias))
            normed_one[here, :] = normed
            inverse_one[here, :] = jnp.broadcast_to(inverse, (tile, PAIR))
            mid = normed * row_vector(first_gain) + row_vector(first_shift)
            mid_low[here, :] = mid.astype(bf16)

        loop(rows // tile, project)
        for block in range(ff_blocks):
            up_load(block).wait()

            def up(index, block=block):
                here = pl.ds(pl.multiple_of(lax.rem(index, rows // 256) * 256, 256), 256)
                part = pl.multiple_of(lax.div(index, rows // 256) * 256, 256)
                lanes = pl.ds(block * width + part, 256)
                pre = mm(mid_low[here, :], ff_w[block, :, pl.ds(part, 256)])
                pre = pre + up_bias_row[:, lanes]
                half = 0.5 * (1.0 + lax.erf(pre * (0.5**0.5)))
                act[here, lanes] = (pre * half).astype(bf16)
                bell = jnp.exp(-0.5 * pre * pre) * (2.0 * math.pi) ** -0.5
                slope[here, lanes] = (half + pre * bell).astype(bf16)

            loop(rows // 256 * (width // 256), up)
            down_load(block).start()
        turned[...] = mid_low[...].T
        for block in range(ff_blocks):
            down_load(block).wait()
        grads_load.wait()

        def down(index):
            here = pl.ds(pl.multiple_of(index * tile, tile), tile)
            mid = normed_one[here, :] * row_vector(first_gain) + row_vector(first_shift)
            hidden = mid + row_vector(down_bias)
            for block in range(ff_blocks):
                hidden = hidden + mm(act[here, pl.ds(block * width, width)], ff_w[block])
            normed, inverse = normalize(hidden)
            grad = grads[here, :].astype(jnp.float32)
            total.add(1, grad * normed)
            total.add(2, grad)
            grads[here, :] = (
                normed * row_vector(second_gain) + row_vector(second_shift)
            ).astype(bf16)
            grad = normalize_back(grad * row_vector(second_gain), normed, inverse)
            grad_second[here, :] = grad
            grad = grad.astype(bf16)
            low[here, :] = grad
            total.add(0, grad.astype(jnp.float32))

        loop(rows // tile, down)
        out_copy = load(4, grads, layer_out)
        out_copy.start()
        for block in range(ff_blocks):

            def down_grad(index, block=block):
                at = pl.multiple_of(index * 256, 256)
                grad = mm(act[:, pl.ds(block * width + at, 256)], low[...], TN)
                store_block(block, at, grad)

            loop(width // 256, down_grad)
            if block == 0:
                wait_greet()
            staged(block)
            tick(f"down{block}")
        for block in range(ff_blocks):

            def up_back(index, block=block):
                at = pl.multiple_of(index * 256, 256)
                lanes = pl.ds(block * width + at, 256)
                grad = mm(low[...], ff_w[block, pl.ds(at, 256), :], NT)
                grad = (grad * slope[:, lanes].astype(jnp.float32)).astype(bf16)
                slope[:, lanes] = grad
                up_sums[:, lanes] = jnp.sum(grad.astype(jnp.float32), axis=0, keepdims=True)

            loop(width // 256, up_back)
            up_load(block).start()
            tick(f"back{block}")
        for block in range(ff_blocks):

            def up_grad(index, block=block):
                at = pl.multiple_of(index * 256, 256)
                grad = mm(turned[pl.ds(at, 256), :], slope[:, pl.ds(block * width, width)])
                store_block(ff_blocks + block, at, grad)

            loop(width // 256, up_grad)
            staged(ff_blocks + block)
            tick(f"up{block}")
        for block in range(ff_blocks):
            up_load(block).wait()

        def mid_back(index):
            here = pl.ds(pl.multiple_of(index * tile, tile), tile)
            grad = grad_second[here, :]
            for block in range(ff_blocks):
                grad = grad + mm(slope[here, pl.ds(block * width, width)], ff_w[block], NT)
            normed = normed_one[here, :]
            total.add(4, grad * normed)
            total.add(5, grad)
            grad = normalize_back(
                grad * row_vector(first_gain), normed, inverse_one[here, pl.ds(0, 1)]
            )
            grad_first[here, :] = grad
            grad = grad.astype(bf16)
            low[here, :] = grad
            total.add(3, grad.astype(jnp.float32))

        for part in range(2):
            loop(rows // tile // 2, lambda index, part=part: mid_back(index + part * (rows // tile // 2)))
            tick(f"mid{part}")
        for seq in range(seqs):
            padded[seq, pl.ds(HALO, tokens)] = mm(
                low[pl.ds(seq * tokens, tokens), :], out_w[...], NT
            ).astype(bf16)

        def out_grad(index):
            at = pl.multiple_of(index * 256, 256)
            store_block(2 * ff_blocks, at, mm(branch[:, pl.ds(at, 256)], low[...], TN))

        loop(width // 256, out_grad)
        staged(2 * ff_blocks)
        tick("out")
        vec[...] = jnp.zeros_like(vec)
        for part in range(ff_blocks * pairs):
            vec[pl.ds(part, 1), :] = up_sums[:, pl.ds(part * PAIR, PAIR)]
        for row in range(6):
            for part in range(pairs):
                vec[pl.ds((ff_blocks + row) * pairs + part, 1), :] = sums[
                    pl.ds(row, 1), pl.ds(part * PAIR, PAIR)
                ]
        out_copy.wait()

    narrow = pltpu.VMEM((rows, width), bf16)
    wide = pltpu.VMEM((rows, width), jnp.float32)
    hidden = pltpu.VMEM((rows, ff_blocks * width), bf16)
    pl.run_scoped(
        feed_forward,
        narrow, narrow, narrow, narrow,
        pltpu.VMEM((width, rows), bf16),
        narrow, wide, wide,
        pltpu.VMEM((rows, PAIR), jnp.float32),
        pltpu.VMEM((width, width), bf16),
        pltpu.VMEM((ff_blocks, width, width), bf16),
        hidden, hidden,
        pltpu.VMEM((1, ff_blocks * width), jnp.float32),
    )
    first_row = (ff_blocks + 6) * pairs
    tap_row = first_row + 2 * pairs
    proxy_row = tap_row + 2 * pairs

    def attention(
        x, queries, keys, values, kernel_one, expo, keep, rest, grad_qkv, turned, rows_of_weight
    ):
        place = Place(batch_size, seq_size)
        loads = {}
        for index, (name, source, target) in enumerate(
            (
                ("kernel_one", kernel_one_in, kernel_one),
                ("queries", queries_in, queries),
                ("values", values_in, values),
                ("expo", expo_in, expo),
                ("keys", keys_in, keys),
                ("keep", keep_in, keep),
                ("x", x_in, x),
            )
        ):
            loads[name] = pltpu.make_async_copy(source, target, load_sem.at[index])
            loads[name].start()
        zero_past(padded, tokens)
        halo = halo_copies(place, padded, tokens, *halo_sem)
        for copy in halo:
            copy.start()

        def spots(unit):
            seq, pair = lax.div(unit, pairs), lax.rem(unit, pairs)
            span = pl.ds(pl.multiple_of(seq * tokens, tokens), tokens)
            lanes = pl.ds(pl.multiple_of(pair * PAIR, PAIR), PAIR)
            return seq, span, lanes

        def paced(step, name, chunks=1):
            size = -(-units // chunks)
            for chunk, first in enumerate(range(0, units, size)):
                lax.fori_loop(first, min(first + size, units), step, 0, unroll=2)
                tick(f"{name}{chunk}")

        def mixed_parts(unit, carry):
            seq, span, lanes = spots(unit)
            grad = padded[seq, pl.ds(HALO, tokens), lanes]
            land_send[unit, 0] = join_heads(mm(kernel_one[unit].astype(bf16), grad)).astype(bf16)
            return carry

        loads["kernel_one"].wait()
        lax.fori_loop(0, units, mixed_parts, 0, unroll=2)
        for unit in range(units, seq_size * many):
            land_send[unit] = jnp.ones_like(land_send[unit])
        mixed_out = shared_out(
            place, land_send.at[:, 0], land_recv.at[:, :, 0], many, *mixed_sem
        )
        for copy in mixed_out:
            copy.start()
        tick("start")

        def first_grads(unit, carry):
            seq, span, lanes = spots(unit)
            weights = kernel_one[unit]
            grad = mm(spread_heads(mixed[unit]), padded[seq, pl.ds(HALO, tokens), lanes], NT)
            both = (weights * grad).reshape(2, SEG, tokens)
            both = jnp.broadcast_to(jnp.sum(both, axis=1, keepdims=True), both.shape)
            score_grad = (weights * (grad - both.reshape(2 * SEG, tokens))).astype(bf16)
            land_send[unit, 1] = join_heads(mm(score_grad, queries[span, lanes])).astype(bf16)
            rest[0, span, lanes] = mm(score_grad, spread_heads(land[unit, 1]), TN)
            return carry

        loads["queries"].wait()
        paced(first_grads, "first", 3)
        tick("wait_mixed")
        for copy in mixed_out:
            copy.wait()
        first_unit = place.seq * many
        kernels, approx_grads = [], []
        for own in range(many):
            total = land_send[first_unit + own, 0].astype(jnp.float32)
            for step in range(seq_size - 1):
                total = total + land_recv[step, own, 0].astype(jnp.float32)
            total = split(spread_heads(total))
            kv_mean = kv_own[own]
            kv_grad = join_heads(mm3(split(approx[own]), total, TN))
            approx_grads.append(mm3(split(spread_heads(kv_mean)), total, NT))
            kernels.append(kernel_two[own])
            dots = kv_grad * kv_mean
            first = first_head(dots.shape)
            dots = jnp.concatenate(
                [
                    jnp.sum(jnp.where(first, dots, 0.0), axis=1, keepdims=True),
                    jnp.sum(jnp.where(first, 0.0, dots), axis=1, keepdims=True),
                ],
                axis=0,
            )
            dots = row_of(dots)
            for slot in range(seq_size):
                share = shares[own, slot, pl.ds(0, 1), :]
                scaled = (kv_grad * join_heads(column(share))).astype(bf16)
                high, low = split(-dots * share)
                tail = jnp.concatenate([high, low, jnp.zeros((14, PAIR), bf16)], axis=0)
                acc_send[slot, own] = jnp.concatenate([scaled, tail], axis=0)
        acc_out = []
        for step in range(1, seq_size):
            acc_out.append(
                pltpu.make_async_remote_copy(
                    src_ref=acc_send.at[seq_size - step],
                    dst_ref=acc_all.at[pl.ds(first_unit, many)],
                    send_sem=acc_sem[0].at[step - 1],
                    recv_sem=acc_sem[1].at[step - 1],
                    device_id=place.seq_peer(step),
                    device_id_type=MESH_IDS,
                )
            )
        for copy in acc_out:
            copy.start()
        for own in range(many):
            acc_all[first_unit + own] = acc_send[0, own]
        tick("acc")
        for copy in halo:
            copy.wait()
        trim_halo(place, padded, tokens)
        tap_rows[...] = turned_taps(taps)
        for part in range(2):
            span = (part * pairs // 2, (part + 1) * pairs // 2)
            conv_rows(padded, tap_rows, rest.at[2], tokens, span)
            tick(f"conv{part}")
        loads["values"].wait()
        loads["expo"].wait()
        loads["keys"].wait()
        tick("wait_acc")
        for copy in acc_out:
            copy.wait()

        def third_grads(unit, carry):
            seq, span, lanes = spots(unit)
            packed = acc_all[unit]
            acc = spread_heads(packed[:SEG])
            tail = packed[SEG:].astype(jnp.float32)
            part = mm(acc, values[seq, pl.ds(HALO, tokens), lanes], NT)
            weights = expo[unit]
            score_grad = (weights * (part + column(tail[0:1] + tail[1:2]))).astype(bf16)
            land_send[unit, 0] = join_heads(mm(score_grad, keys[span, lanes])).astype(bf16)
            rest[1, span, lanes] = mm(score_grad, spread_heads(land[unit, 0]), TN)
            value_grad = mm(weights.astype(bf16), acc, TN) + rest[2, span, lanes]
            valid = positions(place, tokens, 0) < length_of(bounds, seq)
            grad_qkv[2, span, lanes] = jnp.where(valid, value_grad, 0.0).astype(bf16)
            return carry

        paced(third_grads, "third", 3)
        land_out = shared_out(place, land_send, land_recv, many, *land_sem)
        for copy in land_out:
            copy.start()
        loads["x"].wait()
        turned[...] = x[...].T

        def weight_grad(third, block):
            def step(index):
                at = pl.multiple_of(index * 256, 256)
                store_block(block, at, mm(turned[pl.ds(at, 256), :], grad_qkv[third]))

            loop(width // 256, step)

        def bias_grad(third, row):
            for pair in range(pairs):
                cols = grad_qkv[third, :, pl.ds(pair * PAIR, PAIR)].astype(jnp.float32)
                vec[pl.ds(row + pair, 1), :] = jnp.sum(cols, axis=0, keepdims=True)

        weight_grad(2, 2 * ff_blocks + 1)
        staged(2 * ff_blocks + 1)
        tick("value")
        bias_grad(2, first_row + pairs)
        for part in range(3):
            span = (part * pairs // 3, (part + 1) * pairs // 3)
            tap_grads(padded, values, vec, tap_row, tokens, span)
            tick(f"taps{part}")
        loads["keep"].wait()
        kernel_grads = newton_backward(kernels, approx_grads, keep, tick)
        extra = []
        for own in range(many):
            kernel, grad = kernels[own], kernel_grads[own]
            score_grad = split(
                kernel * (grad - jnp.sum(kernel * grad, axis=1, keepdims=True))
            )
            both = land[first_unit + own]
            left, right = spread_heads(both[0]), spread_heads(both[1])
            extra.append(
                (
                    join_heads(mm(score_grad[0], right) + mm(score_grad[1], right)),
                    join_heads(mm(score_grad[0], left, TN) + mm(score_grad[1], left, TN)),
                )
            )
        tick("wait_land")
        for copy in land_out:
            copy.wait()
        for own in range(many):
            unit = first_unit + own
            low, high = segment_edges(bounds, jnp.minimum(lax.div(unit, pairs), seqs - 1))
            for slot in range(2):
                total = land_send[unit, slot].astype(jnp.float32) + extra[own][slot]
                for step in range(seq_size - 1):
                    total = total + land_recv[step, own, slot].astype(jnp.float32)
                land_all[unit, slot] = (total / (high - low)).astype(bf16)
            row = pl.ds(proxy_row + lax.rem(unit, pairs), 1)
            vec[row, :] = vec[row, :] + jnp.where(
                unit < units, proxies[own, pl.ds(0, 1), :], 0.0
            )
        land_back = passed_on(place, land_all, many, *land_back_sem)
        for copy in land_back:
            copy.start()
        tick("land")
        tick("wait_back")
        for copy in land_back:
            copy.wait()
        for seq in range(seqs):
            member = member_of(place, bounds, seq, tokens)
            span = pl.ds(seq * tokens, tokens)
            for pair in range(pairs):
                lanes = pl.ds(pair * PAIR, PAIR)
                both = land_all[seq * pairs + pair]
                for slot in range(2):
                    grad = (mm(member, both[slot], TN) + rest[slot, span, lanes]) * quarter
                    grad_qkv[slot, span, lanes] = grad.astype(bf16)
        tick("grads")
        weight_grad(0, 2 * ff_blocks + 2)
        weight_grad(1, 2 * ff_blocks + 3)
        staged(2 * ff_blocks + 2, 2 * ff_blocks + 3)
        bias_grad(0, first_row)
        ticker.add("vec", vec_reduce(place, vec, slots, *vec_sem))
        tick("last")

        def weight_load(tile):
            return pltpu.make_async_copy(
                qkv_weight.at[pl.ds(tile * PAIR, PAIR)],
                rows_of_weight.at[tile % 2],
                weight_sem.at[tile % 2],
            )

        weight_load(0).start()
        for tile in range(pairs):
            if tile + 1 < pairs:
                weight_load(tile + 1).start()
            weight_load(tile).wait()
            lanes = pl.ds(tile * PAIR, PAIR)
            total = grad_first[:, lanes]
            for third in range(3):
                total = total + mm(
                    grad_qkv[third], rows_of_weight[tile % 2, :, pl.ds(third * width, width)], NT
                )
            x[:, lanes] = total.astype(bf16)
            tick(f"input{tile}")
        out_copy = pltpu.make_async_copy(x, input_grad, load_sem.at[0])
        out_copy.start()
        ticker.drain(LAST)
        out_copy.wait()

    pl.run_scoped(
        attention,
        narrow, narrow, narrow,
        pltpu.VMEM(values_in.shape, bf16),
        pltpu.VMEM(kernel_one_in.shape, jnp.float32),
        pltpu.VMEM(expo_in.shape, jnp.float32),
        pltpu.VMEM(keep_in.shape, jnp.float32),
        pltpu.VMEM((2 + 1, rows, width), jnp.float32),
        pltpu.VMEM((3, rows, width), bf16),
        pltpu.VMEM((width, rows), bf16),
        pltpu.VMEM((2, PAIR, 3 * width), bf16),
    )


Z_FIRST = ()


class Piece:
    def __init__(self, blocks, start, rows, orders, slots):
        self.blocks, self.start, self.rows, self.orders, self.slots = (
            blocks, start, rows, orders, slots,
        )


def make_plan(sizes, block_count, width):
    split_rows = 16 * sizes["x"] * sizes["y"] * sizes["z"]
    orders = (("x", "y", "z"), ("y", "x", "z"))
    z_first = (("z0", "z1", "x", "y"), ("z0", "z1", "y", "x"))
    if 2 * width % (2 * split_rows) == 0:
        counts = [2] * (block_count // 2)
    else:
        orders = orders[:1]
        z_first = z_first[:1]
        counts = [8, block_count - 8] if 8 * width % split_rows == 0 else [block_count]
    plan, block, slot = [], 0, 0
    for count in counts:
        rows = -(-count * width // (len(orders) * split_rows)) * len(orders) * split_rows
        own = z_first if len(plan) in Z_FIRST else orders
        need = Reduce.slots(sizes, own, rows)
        plan.append(
            Piece(list(range(block, block + count)), block * width, rows, own, pl.ds(slot, need))
        )
        block += count
        slot += need
    return plan, slot


def layer_back(
    x, grad_out, branch, out_weight, up_weight, down_weight, qkv_weight, saved, bounds, taps,
    vectors, batch_size, seq_size, seqs,
):
    (
        queries, keys, values, kernel_one, expo, land, mixed, _, kernel_two, approx, keep,
        kv_own, shares, proxies,
    ) = saved
    rows, width = x.shape
    tokens = rows // seqs
    pairs = width // PAIR
    own = -(-seqs * pairs // seq_size)
    owned = seq_size * own
    sizes = axis_sizes(batch_size, seq_size)
    ff_blocks = down_weight.shape[0] // width
    plan, slot_rows = make_plan(sizes, 2 * ff_blocks + 4, width)
    pieces, stage_rows = len(plan), plan[-1].start + plan[-1].rows
    parts = len(plan[0].orders)
    copies = max(Reduce.copies(sizes, piece.orders) for piece in plan)
    vec_axes = ("core", "x", "y", "z")
    vec_steps = sum(sizes[axis] - 1 for axis in vec_axes)
    vec_shape = (-(-((ff_blocks + 11) * pairs) // 8) * 8, PAIR)
    f32, bf16 = jnp.float32, jnp.bfloat16
    vmem = pl.BlockSpec(memory_space=pltpu.VMEM)
    anywhere = pl.BlockSpec(memory_space=pl.ANY)
    sems = pltpu.SemaphoreType.DMA
    pair_sems = (sems((seq_size - 1,)),) * 2
    return pl.pallas_call(
        partial(back_kernel, batch_size, seq_size, seqs, tokens, own, plan),
        out_shape=(
            jax.ShapeDtypeStruct((rows, width), bf16),
            jax.ShapeDtypeStruct((rows, width), bf16),
            jax.ShapeDtypeStruct((2, stage_rows, HALF), bf16),
            jax.ShapeDtypeStruct(vec_shape, f32),
        ),
        in_specs=[anywhere] * 13 + [vmem] * (9 + len(vectors)),
        out_specs=(anywhere, anywhere, anywhere, vmem),
        scratch_shapes=[
            pltpu.VMEM((2, stage_rows, HALF), bf16),
            pltpu.VMEM((stage_rows, HALF), bf16),
            pltpu.VMEM((parts, slot_rows, HALF), bf16),
            pltpu.VMEM((sum(sizes[axis] for axis in vec_axes), *vec_shape), f32),
            pltpu.VMEM(values.shape, bf16),
            pltpu.VMEM((rows, width), f32),
            pltpu.VMEM((16, 2 * BLOCK), f32),
            pltpu.VMEM((8, width), f32),
            pltpu.VMEM((1, ff_blocks * width), f32),
            pltpu.VMEM((seq_size, own, SEG + 16, PAIR), bf16),
            pltpu.VMEM((owned, SEG + 16, PAIR), bf16),
            pltpu.VMEM((owned, 2, SEG, PAIR), bf16),
            pltpu.VMEM((seq_size - 1, own, 2, SEG, PAIR), bf16),
            pltpu.VMEM((owned, 2, SEG, PAIR), bf16),
            sems((7,)),
            sems((ff_blocks,)),
            sems((pieces, copies)),
            sems((pieces, copies)),
            pltpu.SemaphoreType.REGULAR((pieces,)),
            (sems((vec_steps,)),) * 2,
            sems((pieces, 2)),
            (sems((2,)),) * 2,
            pair_sems,
            pair_sems,
            pair_sems,
            pair_sems,
        ],
        compiler_params=pltpu.CompilerParams(
            collective_id=0, has_side_effects=True, vmem_limit_bytes=63 * 2**20
        ),
        name="layer_back",
    )(
        x, grad_out, branch, out_weight, up_weight, down_weight, qkv_weight,
        queries, keys, values, kernel_one, expo, keep,
        bounds, taps, land, mixed, kernel_two, approx, kv_own, shares, proxies, *vectors,
    )


def widen_kernel(in_ref, out_ref):
    out_ref[...] = in_ref[0].astype(jnp.float32)


def widen(gathered, first, shape, shift=0):
    down_way = shape[0] > shape[1]
    count = shape[0] // 768 * (shape[1] // 768)
    return pl.pallas_call(
        widen_kernel,
        out_shape=jax.ShapeDtypeStruct(shape, jnp.float32),
        grid=(count, 2),
        in_specs=[
            pl.BlockSpec((1, 768, HALF), lambda b, c: (c, first + lax.rem(b + shift, count), 0))
        ],
        out_specs=pl.BlockSpec(
            (768, HALF), (lambda b, c: (b, c)) if down_way else (lambda b, c: (0, b * 2 + c))
        ),
        name="widen",
    )(gathered)


def body(
    hidden_in,
    seg_bounds,
    qkv_weight,
    query_bias,
    value_bias,
    conv_taps,
    out_weight,
    out_bias,
    first_gain,
    first_shift,
    up_weight,
    up_bias,
    down_weight,
    down_bias,
    second_gain,
    second_shift,
    grad_out,
):
    seq_count, tok_count, model_width = hidden_in.shape
    head_count, tap_count = conv_taps.shape
    ff_width = up_weight.shape[1]
    row_total = seq_count * tok_count
    batch_size, seq_size = lax.axis_size("batch"), lax.axis_size("seq")
    input_rows = hidden_in.reshape(row_total, model_width)
    saved = attend(
        input_rows, seg_bounds, qkv_weight, query_bias, value_bias, conv_taps,
        batch_size, seq_size, seq_count,
    )
    layer_out, input_grad, gathered, vec = layer_back(
        input_rows,
        grad_out.reshape(row_total, model_width),
        saved[7],
        out_weight,
        up_weight,
        down_weight,
        qkv_weight,
        saved,
        seg_bounds,
        conv_taps,
        (out_bias, first_gain, first_shift, up_bias, down_bias, second_gain, second_shift),
        batch_size,
        seq_size,
        seq_count,
    )

    def small(first, length):
        return vec[first : first + length // PAIR].reshape(length)

    ff_rows, row_count = ff_width // PAIR, model_width // PAIR
    ff_blocks = ff_width // model_width
    names = (
        "down_bias", "second_gain", "second_shift", "out_bias", "first_gain", "first_shift",
        "query_bias", "value_bias",
    )
    grads = {
        name: small(ff_rows + index * row_count, model_width) for index, name in enumerate(names)
    }
    tap_row = ff_rows + len(names) * row_count
    condition = vec[tap_row + head_count : tap_row + head_count + row_count, ::SEG]
    return (
        layer_out.reshape(hidden_in.shape),
        input_grad.reshape(hidden_in.shape),
        widen(gathered, 2 * ff_blocks + 1, qkv_weight.shape, 1),
        grads["query_bias"],
        grads["value_bias"],
        vec[tap_row : tap_row + head_count, :tap_count],
        widen(gathered, 2 * ff_blocks, out_weight.shape),
        grads["out_bias"],
        grads["first_gain"],
        grads["first_shift"],
        widen(gathered, ff_blocks, up_weight.shape),
        small(0, ff_width),
        widen(gathered, 0, down_weight.shape),
        grads["down_bias"],
        grads["second_gain"],
        grads["second_shift"],
        condition.reshape(head_count) / (batch_size * seq_count),
    )


def solution(mesh):
    placed = (
        P("batch", "seq", None),
        P("batch", None),
        P(),
        P(),
        P(),
        P(),
        P(),
        P(),
        P(),
        P(),
        P(),
        P(),
        P(),
        P(),
        P(),
        P(),
        P("batch", "seq", None),
    )
    return jax.shard_map(
        body,
        mesh=mesh,
        in_specs=placed,
        out_specs=(
            P("batch", "seq", None),
            P("batch", "seq", None),
            P(),
            P(),
            P(),
            P(),
            P(),
            P(),
            P(),
            P(),
            P(),
            P(),
            P(),
            P(),
            P(),
            P(),
            P(),
        ),
        check_vma=False,
    )
```

```python
import math
from functools import partial

import jax
import jax.numpy as jnp
from jax import lax
from jax.experimental import pallas as pl
from jax.experimental.pallas import tpu as pltpu
from jax.sharding import PartitionSpec as P

epsilon = 1e-05
MESH_IDS = pl.DeviceIdType.MESH
HALF = 384
LANES = 128


def plane_sides(count):
    wide = max(d for d in range(1, math.isqrt(count) + 1) if count % d == 0)
    return wide, count // wide


def axis_sizes(batch_size, seq_size):
    x_size, y_size = plane_sides(seq_size)
    z_size = batch_size // 2
    z_low = 2 if z_size % 2 == 0 else 1
    return {
        "core": 2, "x": x_size, "y": y_size, "z": z_size, "z0": z_low, "z1": z_size // z_low,
    }


class Place:
    def __init__(self, batch_size, seq_size):
        x_size, y_size = plane_sides(seq_size)
        self.sizes = axis_sizes(batch_size, seq_size)
        batch = lax.axis_index("batch")
        seq = lax.axis_index("seq")
        z_low = self.sizes["z0"]
        self.at = {
            "core": lax.rem(batch, 2),
            "z": lax.div(batch, 2),
            "z0": lax.rem(lax.div(batch, 2), z_low),
            "z1": lax.div(batch, 2 * z_low),
            "x": lax.rem(seq, x_size),
            "y": lax.div(seq, x_size),
        }
        self.seq_size = seq_size
        self.seq = seq
        self.batch = batch

    def peer_index(self, axis, step):
        size = self.sizes[axis]
        return lax.rem(self.at[axis] + step, size)

    def device(self, **moved):
        spot = {**self.at, **moved}
        if "z0" in moved or "z1" in moved:
            spot["z"] = spot["z1"] * self.sizes["z0"] + spot["z0"]
        return (spot["z"] * 2 + spot["core"], spot["y"] * self.sizes["x"] + spot["x"])

    def peers(self, axes):
        for axis in axes:
            for step in range(1, self.sizes[axis]):
                yield self.device(**{axis: self.peer_index(axis, step)})

    def seq_peer(self, step):
        return (self.batch, lax.rem(self.seq + step, self.seq_size))


def greet(devices):
    barrier = pltpu.get_barrier_semaphore()
    devices = list(devices)
    for device in devices:
        pl.semaphore_signal(barrier, inc=1, device_id=device, device_id_type=MESH_IDS)
    return lambda: pl.semaphore_wait(barrier, len(devices))


def tile_rows(rows):
    return max(t for t in (96, 64, 48, 32, 16) if rows % t == 0)


def add_rows(out_ref, in_ref, at, parts, rows):
    tile = tile_rows(rows)

    def step(index, carry):
        start = pl.multiple_of(at + index * tile, 16)
        total = in_ref[pl.ds(start, tile), :].astype(jnp.float32)
        for ref, first in parts:
            total = total + ref[pl.ds(pl.multiple_of(first + index * tile, 16), tile), :].astype(
                jnp.float32
            )
        out_ref[pl.ds(start, tile), :] = total.astype(out_ref.dtype)
        return carry

    lax.fori_loop(0, rows // tile, step, 0)


class Reduce:
    def __init__(
        self, number, place, orders, stage, whole, recv, send_sem, recv_sem, free_sem, rows
    ):
        self.number, self.make_place, self.orders = number, place, orders
        self.stage, self.whole, self.recv = stage, whole, recv
        self.send_sem, self.recv_sem, self.free_sem = send_sem, recv_sem, free_sem
        self.part = rows // len(orders)

    @staticmethod
    def slots(sizes, orders, rows):
        need = []
        for order in orders:
            size, slot = rows // len(orders), 0
            for axis in order:
                size //= sizes[axis]
                slot += (sizes[axis] - 1) * size
            need.append(slot)
        return max(need)

    @staticmethod
    def copies(sizes, orders):
        return 2 + 2 * sum(sizes[axis] - 1 for order in orders for axis in order)

    def level_of(self, place, half, level):
        base, size, slot = half * self.part, self.part, 0
        order = self.orders[half]
        sem = 2 + 2 * half * sum(place.sizes[axis] - 1 for axis in order)
        for axis in order[:level]:
            count = place.sizes[axis]
            size //= count
            slot += (count - 1) * size
            sem += 2 * (count - 1)
            base = base + place.at[axis] * size
        count = place.sizes[order[level]]
        return order[level], count, base, size // count, slot, sem

    def copy(self, index, src, dst, device):
        return pltpu.make_async_remote_copy(
            src_ref=src,
            dst_ref=dst,
            send_sem=self.send_sem.at[self.number, index],
            recv_sem=self.recv_sem.at[self.number, index],
            device_id=device,
            device_id_type=MESH_IDS,
        )

    @staticmethod
    def rows_of(ref, start, rows):
        return ref.at[pl.ds(pl.multiple_of(start, 16), rows)]

    def scatter(self, half, level):
        place = self.make_place()
        axis, count, base, chunk, slot, sem = self.level_of(place, half, level)
        mine = self.stage.at[place.at["core"]]
        copies = []
        for step in range(1, count):
            peer = place.peer_index(axis, step)
            copies.append(
                self.copy(
                    sem + step - 1,
                    self.rows_of(mine, base + peer * chunk, chunk),
                    self.recv.at[half, pl.ds(slot + (step - 1) * chunk, chunk)],
                    place.device(**{axis: peer}),
                )
            )
        return copies

    def spread(self, half, level):
        place = self.make_place()
        axis, count, base, chunk, slot, sem = self.level_of(place, half, level)
        here = self.rows_of(self.whole, base + place.at[axis] * chunk, chunk)
        return [
            self.copy(
                sem + count - 1 + step - 1,
                here,
                here,
                place.device(**{axis: place.peer_index(axis, step)}),
            )
            for step in range(1, count)
        ]

    def add_level(self, half, level):
        place = self.make_place()
        axis, count, base, chunk, slot, _ = self.level_of(place, half, level)
        mine = self.stage.at[place.at["core"]]
        add_rows(
            self.whole if level == len(self.orders[half]) - 1 else mine,
            mine,
            base + place.at[axis] * chunk,
            [(self.recv.at[half], slot + k * chunk) for k in range(count - 1)],
            chunk,
        )

    def core_out(self):
        place = self.make_place()
        core = place.at["core"]
        return self.copy(0, self.stage.at[1 - core], self.whole, place.device(core=1 - core))

    def core_back(self):
        place = self.make_place()
        core = place.at["core"]
        return self.copy(1, self.whole, self.stage.at[core], place.device(core=1 - core))

    def run(self):
        halves = range(len(self.orders))
        self.core_out().start()
        yield
        self.core_out().wait()
        place = self.make_place()
        other = place.device(core=1 - place.at["core"])
        pl.semaphore_signal(
            self.free_sem.at[self.number], inc=1, device_id=other, device_id_type=MESH_IDS
        )
        mine = self.stage.at[place.at["core"]]
        for half in halves:
            start = half * self.part
            add_rows(mine, mine, start, [(self.whole, start)], self.part)
            for copy in self.scatter(half, 0):
                copy.start()
        last = len(self.orders[0]) - 1
        for level in range(last + 1):
            yield
            for half in halves:
                for copy in self.scatter(half, level):
                    copy.wait()
                self.add_level(half, level)
                later = self.scatter if level < last else self.spread
                for copy in later(half, min(level + 1, last)):
                    copy.start()
        for level in reversed(range(last + 1)):
            yield
            for half in halves:
                for copy in self.spread(half, level):
                    copy.wait()
                for copy in self.spread(half, level - 1) if level else ():
                    copy.start()
        pl.semaphore_wait(self.free_sem.at[self.number], 1)
        self.core_back().start()
        yield
        self.core_back().wait()


def vec_reduce(place, acc, slots, send_sem, recv_sem):
    sem = 0
    level = 0
    for axis in ("core", "x", "y", "z"):
        count = place.sizes[axis]
        copies = []
        here = place.at[axis]
        for step in range(1, count):
            copies.append(
                pltpu.make_async_remote_copy(
                    src_ref=acc,
                    dst_ref=slots.at[level + here],
                    send_sem=send_sem.at[sem],
                    recv_sem=recv_sem.at[sem],
                    device_id=place.device(**{axis: place.peer_index(axis, step)}),
                    device_id_type=MESH_IDS,
                )
            )
            sem += 1
        for copy in copies:
            copy.start()
        slots[level + here] = acc[...]
        yield
        for copy in copies:
            copy.wait()
        total = slots[level]
        for index in range(1, count):
            total = total + slots[level + index]
        acc[...] = total
        level += count


SEG = 64
PAIR = 128
HALO = 16
BLOCK = 128
FAR = -1e30
NT = ((1,), (1,))
TN = ((0,), (0,))
NN = ((1,), (0,))


def mm(left, right, dims=NN):
    return lax.dot_general(left, right, (dims, ((), ())), preferred_element_type=jnp.float32)


def split(array):
    high = array.astype(jnp.bfloat16)
    return high, (array - high.astype(jnp.float32)).astype(jnp.bfloat16)


def thirds(array):
    high = array.astype(jnp.bfloat16)
    middle = (array - high.astype(jnp.float32)).astype(jnp.bfloat16)
    rest = array - high.astype(jnp.float32) - middle.astype(jnp.float32)
    return high, middle, rest.astype(jnp.bfloat16)


def mm3(left, right, dims=NN):
    left_high, left_low = left
    right_high, right_low = right
    (left_dim,), (right_dim,) = dims
    return mm(
        jnp.concatenate([left_high, left_high, left_low], axis=left_dim),
        jnp.concatenate([right_high, right_low, right_high], axis=right_dim),
        dims,
    )


def eye_mask(size):
    rows = lax.broadcasted_iota(jnp.int32, (size, size), 0)
    return rows == lax.broadcasted_iota(jnp.int32, (size, size), 1)


def column(row):
    return jnp.sum(jnp.where(eye_mask(row.shape[1]), row, 0.0), axis=1, keepdims=True)


def row_of(col):
    return jnp.sum(jnp.where(eye_mask(col.shape[0]), col, 0.0), axis=0, keepdims=True)


def first_head(shape):
    return lax.broadcasted_iota(jnp.int32, shape, len(shape) - 1) < SEG


def spread_heads(pair):
    first = first_head(pair.shape)
    zero = jnp.zeros_like(pair)
    return jnp.concatenate([jnp.where(first, pair, zero), jnp.where(first, zero, pair)], axis=0)


def join_heads(blocks):
    shape = (SEG, PAIR)
    return jnp.where(
        first_head(shape),
        jnp.broadcast_to(blocks[:SEG], shape),
        jnp.broadcast_to(blocks[SEG:], shape),
    )


def heads_sum(col):
    first = jnp.sum(col[:SEG], axis=0, keepdims=True)
    second = jnp.sum(col[SEG:], axis=0, keepdims=True)
    return jnp.concatenate(
        [jnp.broadcast_to(first, (SEG, 1)), jnp.broadcast_to(second, (SEG, 1))], axis=0
    )


def shared_out(place, source, target, many, send_sem, recv_sem):
    copies = []
    for step in range(1, place.seq_size):
        device = place.seq_peer(step)
        copies.append(
            pltpu.make_async_remote_copy(
                src_ref=source.at[pl.ds(device[1] * many, many)],
                dst_ref=target.at[step - 1],
                send_sem=send_sem.at[step - 1],
                recv_sem=recv_sem.at[step - 1],
                device_id=device,
                device_id_type=MESH_IDS,
            )
        )
    return copies


def passed_on(place, array, many, send_sem, recv_sem):
    copies = []
    here = array.at[pl.ds(place.seq * many, many)]
    for step in range(1, place.seq_size):
        copies.append(
            pltpu.make_async_remote_copy(
                src_ref=here,
                dst_ref=here,
                send_sem=send_sem.at[step - 1],
                recv_sem=recv_sem.at[step - 1],
                device_id=place.seq_peer(step),
                device_id_type=MESH_IDS,
            )
        )
    return copies


def halo_copies(place, padded, tokens, send_sem, recv_sem):
    copies = []
    for index, (step, first, there) in enumerate(
        ((1, tokens, 0), (place.seq_size - 1, HALO, tokens + HALO))
    ):
        copies.append(
            pltpu.make_async_remote_copy(
                src_ref=padded.at[:, pl.ds(first, HALO)],
                dst_ref=padded.at[:, pl.ds(there, HALO)],
                send_sem=send_sem.at[index],
                recv_sem=recv_sem.at[index],
                device_id=place.seq_peer(step),
                device_id_type=MESH_IDS,
            )
        )
    return copies


def trim_halo(place, padded, tokens):
    zero = jnp.zeros((padded.shape[0], HALO, padded.shape[2]), padded.dtype)
    low, high = pl.ds(0, HALO), pl.ds(tokens + HALO, HALO)
    padded[:, low] = jnp.where(place.seq > 0, padded[:, low], zero)
    padded[:, high] = jnp.where(place.seq < place.seq_size - 1, padded[:, high], zero)


def zero_past(padded, tokens):
    past = tokens + 2 * HALO
    rest = padded.shape[1] - past
    padded[:, pl.ds(past, rest)] = jnp.zeros(
        (padded.shape[0], rest, padded.shape[2]), padded.dtype
    )


def band(taps):
    wide = jnp.broadcast_to(taps, (BLOCK, 2 * BLOCK))
    return pltpu.roll(wide, 0, 1, stride=1, stride_axis=0).astype(jnp.bfloat16)


def tap_lanes(taps):
    heads, count = taps.shape
    wide = jnp.concatenate(
        [taps[...], jnp.zeros((heads, 2 * BLOCK - count), jnp.float32)], axis=1
    )
    return jnp.concatenate([wide, jnp.zeros((16 - heads, 2 * BLOCK), jnp.float32)], axis=0)


def turned_taps(taps):
    shape = (2 * BLOCK, 2 * BLOCK)
    ends = lax.broadcasted_iota(jnp.int32, shape, 0) + lax.broadcasted_iota(jnp.int32, shape, 1)
    turn = jnp.where(ends == taps.shape[1] - 1, 1.0, 0.0).astype(jnp.bfloat16)
    return mm(tap_lanes(taps).astype(jnp.bfloat16), turn)


def conv_rows(padded, taps, out, tokens, span=None):
    seqs, _, width = padded.shape

    def step(pair, carry):
        lanes = pl.ds(pl.multiple_of(pair * PAIR, PAIR), PAIR)
        first = band(taps[pl.ds(2 * pair, 1), :])
        second = band(taps[pl.ds(2 * pair + 1, 1), :])
        for seq in range(seqs):
            for block in range(tokens // BLOCK):
                window = padded[seq, pl.ds(block * BLOCK, 2 * BLOCK), lanes]
                both = jnp.where(
                    first_head((BLOCK, PAIR)), mm(first, window), mm(second, window)
                )
                out[pl.ds(seq * tokens + block * BLOCK, BLOCK), lanes] = both
        return carry

    lax.fori_loop(*(span or (0, width // PAIR)), step, 0)


def segment_edges(bounds, seq):
    low = column(bounds[pl.ds(seq, 1), pl.ds(0, SEG)].astype(jnp.float32))
    high = column(bounds[pl.ds(seq, 1), pl.ds(1, SEG)].astype(jnp.float32))
    return low, high


def positions(place, tokens, axis):
    shape = (tokens, 1) if axis == 0 else (1, tokens)
    return (place.seq * tokens + lax.broadcasted_iota(jnp.int32, shape, axis)).astype(jnp.float32)


def member_of(place, bounds, seq, tokens):
    low, high = segment_edges(bounds, seq)
    where = positions(place, tokens, 1)
    return jnp.where((where >= low) & (where < high), 1.0, 0.0).astype(jnp.bfloat16)


def length_of(bounds, seq):
    return bounds[pl.ds(seq, 1), pl.ds(SEG, 1)].astype(jnp.float32)


def newton_forward(kernels, keep):
    eye = jnp.where(eye_mask(PAIR), 1.0, 0.0)
    approx = []
    for kernel in kernels:
        fro = heads_sum(jnp.sum(kernel * kernel, axis=1, keepdims=True))
        approx.append(kernel.T / fro)
    halves = [split(kernel) for kernel in kernels]
    units = range(len(kernels))
    for step in range(6):
        wide = [split(a) for a in approx]
        product = [mm3(halves[u], wide[u]) for u in units]
        lefts = [split(p) for p in product]
        inner = [15.0 * eye - mm3(lefts[u], split(7.0 * eye - product[u])) for u in units]
        outer = [13.0 * eye - mm3(lefts[u], split(inner[u])) for u in units]
        for u in units:
            for slot, value in enumerate((approx[u], product[u], inner[u], outer[u])):
                keep[u, step, slot] = value
        approx = [0.25 * mm3(wide[u], split(outer[u])) for u in units]
    return approx


def attend_kernel(
    batch_size, seq_size, seqs, tokens, many,
    x_in, weight_in, bounds, query_bias, value_bias, taps, *refs
):
    outs, refs = refs[:14], refs[14:]
    saved, refs = refs[:14], refs[14:]
    (
        queries, keys, values, kernel_one, expo, land, mixed, branch, kernel_two, approx_out,
        keep, kv_own, shares, proxies,
    ) = saved
    (
        x, weight, load_sem, save_sem, land_send, land_recv, kv_send, kv_recv, conv, tap_rows, biases,
        land_sem, land_back_sem, kv_sem, mixed_sem, halo_sem,
    ) = refs
    place = Place(batch_size, seq_size)
    width = x.shape[1]
    loads = [pltpu.make_async_copy(x_in, x, load_sem.at[3])]
    for third in range(3):
        lanes = pl.ds(third * width, width)
        loads.append(
            pltpu.make_async_copy(
                weight_in.at[:, lanes], weight.at[:, lanes], load_sem.at[third]
            )
        )
    for copy in loads:
        copy.start()
    saves = []

    def save(*names):
        for ref in names:
            index = [ref is other for other in saved].index(True)
            copy = pltpu.make_async_copy(ref, outs[index], save_sem.at[index])
            copy.start()
            saves.append(copy)

    pairs = width // PAIR
    units = seqs * pairs
    wait_greet = greet(place.seq_peer(step) for step in range(1, seq_size))
    quarter = float(SEG) ** -0.25

    tap_rows[...] = tap_lanes(taps)
    biases[...] = jnp.zeros_like(biases)
    biases[pl.ds(0, 1), :] = query_bias[...].reshape(1, width)
    biases[pl.ds(2, 1), :] = value_bias[...].reshape(1, width)

    def project(out_ref, third):
        def step(tile, carry):
            lanes = pl.ds(pl.multiple_of(third * width + tile * 256, 256), 256)
            here = pl.ds(pl.multiple_of(tile * 256, 256), 256)
            rows = mm(x[...], weight[:, lanes]) + biases[pl.ds(third, 1), here]
            if third < 2:
                out_ref[:, here] = (rows * quarter).astype(jnp.bfloat16)
            else:
                for seq in range(seqs):
                    valid = positions(place, tokens, 0) < length_of(bounds, seq)
                    out_ref[seq, pl.ds(HALO, tokens), here] = jnp.where(
                        valid, rows[seq * tokens : (seq + 1) * tokens], 0.0
                    ).astype(jnp.bfloat16)
            return carry

        loads[1 + third].wait()
        lax.fori_loop(0, width // 256, step, 0)

    loads[0].wait()
    project(queries, 0)
    project(keys, 1)
    save(queries, keys)
    for seq in range(seqs):
        member = member_of(place, bounds, seq, tokens)
        for slot, rows in enumerate((queries, keys)):
            sums = mm(member, rows[pl.ds(seq * tokens, tokens), :])
            for pair in range(pairs):
                land_send[seq * pairs + pair, slot] = sums[:, pair * PAIR : (pair + 1) * PAIR]
    for unit in range(units, seq_size * many):
        land_send[unit] = jnp.ones_like(land_send[unit])
        kv_send[unit] = jnp.ones_like(kv_send[unit])
    wait_greet()
    land_out = shared_out(place, land_send, land_recv, many, *land_sem)
    for copy in land_out:
        copy.start()
    project(values, 2)
    halo = halo_copies(place, values, tokens, *halo_sem)
    for copy in halo:
        copy.start()
    zero_past(values, tokens)
    for copy in land_out:
        copy.wait()
    first_unit = place.seq * many
    for own in range(many):
        unit = first_unit + own
        total = land_send[unit]
        for step in range(seq_size - 1):
            total = total + land_recv[step, own]
        low, high = segment_edges(bounds, jnp.minimum(lax.div(unit, pairs), seqs - 1))
        land[unit] = (total / (high - low)).astype(jnp.bfloat16)
    land_back = passed_on(place, land, many, *land_back_sem)
    for copy in land_back:
        copy.start()
    for copy in halo:
        copy.wait()
    trim_halo(place, values, tokens)
    save(values)
    conv_rows(values, tap_rows, conv, tokens)
    for copy in land_back:
        copy.wait()
    save(land)

    def spots(unit):
        seq, pair = lax.div(unit, pairs), lax.rem(unit, pairs)
        rows = pl.ds(pl.multiple_of(seq * tokens, tokens), tokens)
        lanes = pl.ds(pl.multiple_of(pair * PAIR, PAIR), PAIR)
        return seq, rows, lanes

    def third_scores(unit, carry):
        seq, rows, lanes = spots(unit)
        score = mm(spread_heads(land[unit, 0]), keys[rows, lanes], NT)
        valid = positions(place, tokens, 1) < length_of(bounds, seq)
        score = jnp.where(valid, score, FAR)
        top = jnp.max(score, axis=1, keepdims=True)
        weights = jnp.exp(score - top)
        expo[unit] = weights
        total = jnp.sum(weights, axis=1, keepdims=True)
        part = mm(weights.astype(jnp.bfloat16), values[seq, pl.ds(HALO, tokens), lanes])
        kv_send[unit, pl.ds(0, SEG)] = join_heads(part).astype(jnp.bfloat16)
        kv_send[unit, pl.ds(SEG, 16)] = jnp.concatenate(
            [*thirds(row_of(top)), *thirds(row_of(total)), jnp.zeros((10, PAIR), jnp.bfloat16)],
            axis=0,
        )
        return carry

    lax.fori_loop(0, units, third_scores, 0, unroll=2)
    kv_out = shared_out(place, kv_send, kv_recv, many, *kv_sem)
    for copy in kv_out:
        copy.start()
    save(expo)

    kernels = []
    same = (
        lax.broadcasted_iota(jnp.int32, (PAIR, PAIR), 0) < SEG
    ) == first_head((PAIR, PAIR))
    for own in range(many):
        both = land[first_unit + own]
        score = jnp.where(same, mm(spread_heads(both[0]), spread_heads(both[1]), NT), FAR)
        weights = jnp.exp(score - jnp.max(score, axis=1, keepdims=True))
        kernels.append(weights / jnp.sum(weights, axis=1, keepdims=True))
        kernel_two[own] = kernels[own]
    approx = newton_forward(kernels, keep)
    for own in range(many):
        approx_out[own] = approx[own]
        proxy = jnp.sqrt(
            heads_sum(jnp.sum(kernels[own] * kernels[own], axis=1, keepdims=True))
        ) * jnp.sqrt(heads_sum(jnp.sum(approx[own] * approx[own], axis=1, keepdims=True)))
        proxies[own] = jnp.broadcast_to(row_of(proxy), (8, PAIR))
    save(keep, kernel_two, approx_out, proxies)

    def first_scores(unit, carry):
        seq, rows, lanes = spots(unit)
        score = mm(spread_heads(land[unit, 1]), queries[rows, lanes], NT)
        score = score.reshape(2, SEG, tokens)
        weights = jnp.exp(score - jnp.max(score, axis=1, keepdims=True))
        weights = weights / jnp.sum(weights, axis=1, keepdims=True)
        kernel_one[unit] = weights.reshape(2 * SEG, tokens)
        return carry

    lax.fori_loop(0, units, first_scores, 0, unroll=2)
    save(kernel_one)
    for copy in kv_out:
        copy.wait()
    for own in range(many):
        parts, tops, totals = [], [], []
        for packed in [kv_send[first_unit + own]] + [
            kv_recv[step, own] for step in range(seq_size - 1)
        ]:
            packed = packed.astype(jnp.float32)
            tail = packed[SEG:]
            parts.append(packed[:SEG])
            tops.append(tail[0:1] + tail[1:2] + tail[2:3])
            totals.append(tail[3:4] + tail[4:5] + tail[5:6])
        top = tops[0]
        for other in tops[1:]:
            top = jnp.maximum(top, other)
        scales = [jnp.exp(other - top) for other in tops]
        total = sum(scale * part for scale, part in zip(scales, totals))
        kv_mean = jnp.zeros((SEG, PAIR), jnp.float32)
        for slot, (scale, part) in enumerate(zip(scales, parts)):
            share = scale / total
            shares[own, slot] = jnp.broadcast_to(share, (8, PAIR))
            kv_mean = kv_mean + join_heads(column(share)) * part
        kv_own[own] = kv_mean
        mixed[first_unit + own] = join_heads(
            mm3(split(approx[own]), split(spread_heads(kv_mean)))
        ).astype(jnp.bfloat16)
    mixed_out = passed_on(place, mixed, many, *mixed_sem)
    for copy in mixed_out:
        copy.start()
    save(kv_own, shares)
    for copy in mixed_out:
        copy.wait()
    save(mixed)

    def combine(unit, carry):
        seq, rows, lanes = spots(unit)
        attended = mm(
            kernel_one[unit].astype(jnp.bfloat16), spread_heads(mixed[unit]), TN
        )
        branch[rows, lanes] = (attended + conv[rows, lanes]).astype(jnp.bfloat16)
        return carry

    lax.fori_loop(0, units, combine, 0, unroll=2)
    save(branch)
    for copy in saves:
        copy.wait()


def attend(
    x, bounds, weight, query_bias, value_bias, taps, batch_size, seq_size, seqs
):
    rows, width = x.shape
    tokens = rows // seqs
    units = seqs * (width // PAIR)
    many = -(-units // seq_size)
    slots = seq_size * many
    f32, bf16 = jnp.float32, jnp.bfloat16
    vmem = pl.BlockSpec(memory_space=pltpu.VMEM)
    anywhere = pl.BlockSpec(memory_space=pl.ANY)
    sems = pltpu.SemaphoreType.DMA
    shapes = (
        ((rows, width), bf16),
        ((rows, width), bf16),
        ((seqs, tokens + BLOCK, width), bf16),
        ((units, 2 * SEG, tokens), f32),
        ((units, 2 * SEG, tokens), f32),
        ((slots, 2, SEG, PAIR), bf16),
        ((slots, SEG, PAIR), bf16),
        ((rows, width), bf16),
        ((many, PAIR, PAIR), f32),
        ((many, PAIR, PAIR), f32),
        ((many, 6, 4, PAIR, PAIR), f32),
        ((many, SEG, PAIR), f32),
        ((many, seq_size, 8, PAIR), f32),
        ((many, 8, PAIR), f32),
    )
    return pl.pallas_call(
        partial(attend_kernel, batch_size, seq_size, seqs, tokens, many),
        out_shape=tuple(jax.ShapeDtypeStruct(*shape) for shape in shapes),
        in_specs=[anywhere] * 2 + [vmem] * 4,
        out_specs=tuple([anywhere] * len(shapes)),
        scratch_shapes=[
            *(pltpu.VMEM(*shape) for shape in shapes),
            pltpu.VMEM(x.shape, bf16),
            pltpu.VMEM(weight.shape, bf16),
            sems((4,)),
            sems((len(shapes),)),
            pltpu.VMEM((slots, 2, SEG, PAIR), f32),
            pltpu.VMEM((seq_size - 1, many, 2, SEG, PAIR), f32),
            pltpu.VMEM((slots, SEG + 16, PAIR), bf16),
            pltpu.VMEM((seq_size - 1, many, SEG + 16, PAIR), bf16),
            pltpu.VMEM((rows, width), f32),
            pltpu.VMEM((16, 2 * BLOCK), f32),
            pltpu.VMEM((8, width), f32),
            (sems((seq_size - 1,)),) * 2,
            (sems((seq_size - 1,)),) * 2,
            (sems((seq_size - 1,)),) * 2,
            (sems((seq_size - 1,)),) * 2,
            (sems((2,)),) * 2,
        ],
        compiler_params=pltpu.CompilerParams(
            collective_id=1, has_side_effects=True, vmem_limit_bytes=58 * 2**20
        ),
        name="attend",
    )(x, weight, bounds, query_bias, value_bias, taps)


def newton_backward(kernels, approx_grads, keep, tick):
    units = range(len(kernels))
    eye = jnp.where(eye_mask(PAIR), 1.0, 0.0)
    kernel_halves = [split(kernel) for kernel in kernels]
    grads = [jnp.zeros((PAIR, PAIR), jnp.float32) for _ in units]
    after = approx_grads
    for step in reversed(range(6)):
        approx = [split(keep[u, step, 0]) for u in units]
        product = [keep[u, step, 1] for u in units]
        halves = [split(p) for p in product]
        first = [split(7.0 * eye - p) for p in product]
        second = [split(keep[u, step, 2]) for u in units]
        third = [split(keep[u, step, 3]) for u in units]
        wide = [split(0.25 * a) for a in after]
        third_grad = [split(mm3(wide[u], approx[u])) for u in units]
        second_grad = [split(-mm3(third_grad[u], halves[u])) for u in units]
        first_grad = [-mm3(second_grad[u], halves[u]) for u in units]
        product_grad = [
            split(
                -mm3(second[u], third_grad[u]) - mm3(first[u], second_grad[u]) - first_grad[u]
            )
            for u in units
        ]
        grads = [grads[u] + mm3(approx[u], product_grad[u]) for u in units]
        after = [
            mm3(third[u], wide[u]) + mm3(product_grad[u], kernel_halves[u]) for u in units
        ]
        tick(f"newton{step}")
    out = []
    for u in units:
        kernel = kernels[u]
        fro = heads_sum(jnp.sum(kernel * kernel, axis=1, keepdims=True))
        fro_grad = heads_sum(jnp.sum(after[u] * kernel, axis=1, keepdims=True)) / (fro * fro)
        out.append(grads[u].T + after[u] / fro - 2.0 * kernel * fro_grad)
    return out


def tap_grads(padded_grad, padded, vec, first_row, tokens, span):
    seqs, _, width = padded.shape
    rows = lax.broadcasted_iota(jnp.int32, (BLOCK, BLOCK), 0)
    cols = lax.broadcasted_iota(jnp.int32, (BLOCK, BLOCK), 1)
    turn = jnp.where(rows + cols == BLOCK - 1, 1.0, 0.0).astype(jnp.bfloat16)

    def step(pair, carry):
        lanes = pl.ds(pl.multiple_of(pair * PAIR, PAIR), PAIR)
        total = [jnp.zeros((BLOCK, 2 * BLOCK), jnp.float32) for _ in range(2)]
        for seq in range(seqs):
            for block in range(tokens // BLOCK):
                window = padded[seq, pl.ds(block * BLOCK, 2 * BLOCK), lanes]
                grad = padded_grad[seq, pl.ds(HALO + block * BLOCK, BLOCK), lanes]
                grad = mm(turn, grad).astype(jnp.bfloat16)
                first = first_head(grad.shape)
                zero = jnp.zeros_like(grad)
                total[0] = total[0] + mm(jnp.where(first, grad, zero), window, NT)
                total[1] = total[1] + mm(jnp.where(first, zero, grad), window, NT)
        for head in range(2):
            turned = pltpu.roll(total[head], 0, 1, stride=1, stride_axis=0)
            sums = jnp.sum(turned, axis=0, keepdims=True)
            sums = pltpu.roll(sums, BLOCK + 1, 1)
            vec[pl.ds(first_row + 2 * pair + head, 1), :] = sums[:, :PAIR]
        return carry

    lax.fori_loop(*span, step, 0)


class Ticker:
    def __init__(self, points):
        self.live = {}
        self.points = points

    def add(self, number, generator):
        next(generator)
        self.live[number] = generator

    def step(self, number):
        try:
            next(self.live[number])
        except StopIteration:
            del self.live[number]

    def tick(self, point):
        for number in self.points.get(point, ()):
            if number in self.live:
                self.step(number)

    def drain(self, order=()):
        for number in order:
            if number in self.live:
                self.step(number)
        while self.live:
            for number in list(self.live):
                self.step(number)


POINTS = {
    "back3": (0,),
    "up0": (1,),
    "out": (2, 3),
    "start": (0,),
    "wait_mixed": (1,),
    "wait_acc": (0, 1),
    "third0": (3, 2),
    "third2": (0,),
    "taps1": (1,),
    "newton5": (4, 3, 2),
    "newton3": (0,),
    "wait_back": (0, 4, 1),
    "grads": (2, 3),
}
LAST = (4, 1, 5, 0, 0, "vec", 0, 2, 3, 1, 4, 5, "vec", 1, 1, 2, 3, 4, "vec", 5, 5, 4, 2, 3, 5, "vec", 2, 3, 4, 2, 5, 3, 4, 4, 5, 5, 5)


class Sums:
    def __init__(self, ref):
        self.ref = ref

    def clear(self):
        self.ref[...] = jnp.zeros_like(self.ref)

    def add(self, row, array):
        here = pl.ds(row, 1)
        self.ref[here, :] = self.ref[here, :] + jnp.sum(array, axis=0, keepdims=True)


def normalize(hidden):
    centered = hidden - jnp.mean(hidden, axis=1, keepdims=True)
    inverse = lax.rsqrt(jnp.mean(centered * centered, axis=1, keepdims=True) + epsilon)
    return centered * inverse, inverse


def normalize_back(grad, normed, inverse):
    return inverse * (
        grad
        - jnp.mean(grad, axis=1, keepdims=True)
        - normed * jnp.mean(grad * normed, axis=1, keepdims=True)
    )


def row_vector(ref):
    return ref[...].reshape(1, ref.shape[0])


def back_kernel(
    batch_size, seq_size, seqs, tokens, many, plan,
    x_in, grad_out, branch_in, out_weight, up_weight, down_weight, qkv_weight,
    queries_in, keys_in, values_in, kernel_one_in, expo_in, keep_in, land_in, mixed_in,
    kernel_two_in, approx_in, kv_own_in, shares_in, proxies_in, bounds, taps,
    out_bias, first_gain, first_shift, up_bias, down_bias, second_gain, second_shift,
    layer_out, input_grad, gathered, vec,
    stage, whole, recv, slots, padded, grad_first, tap_rows, sums, up_sums, acc_send, acc_all,
    land_send, land_recv, land_all,
    load_sem, weight_sem, send_sem, recv_sem, free_sem, vec_sem, out_sem, halo_sem, mixed_sem,
    acc_sem, land_sem, land_back_sem,
):
    place = Place(batch_size, seq_size)
    rows, width = x_in.shape
    ff_blocks = down_weight.shape[0] // width
    pairs = width // PAIR
    units = seqs * pairs
    quarter = float(SEG) ** -0.25
    wait_greet = greet(
        [place.seq_peer(step) for step in range(1, seq_size)] + list(place.peers(("core", "z")))
    )
    ticker = Ticker(POINTS)
    tick = ticker.tick
    bf16 = jnp.bfloat16

    def piece_run(number):
        piece = plan[number]
        here = pl.ds(piece.start, piece.rows)
        yield from Reduce(
            number, lambda: Place(batch_size, seq_size), piece.orders, stage.at[:, here],
            whole.at[here], recv.at[:, piece.slots], send_sem, recv_sem, free_sem, piece.rows,
        ).run()

        def outs():
            core = Place(batch_size, seq_size).at["core"]
            return (
                pltpu.make_async_copy(
                    whole.at[here], gathered.at[core, here], out_sem.at[number, 0]
                ),
                pltpu.make_async_copy(
                    stage.at[1 - core, here], gathered.at[1 - core, here], out_sem.at[number, 1]
                ),
            )

        for out in outs():
            out.start()
        yield
        for out in outs():
            out.wait()

    done = set()

    def staged(*blocks):
        done.update(blocks)
        for number, piece in enumerate(plan):
            if done.issuperset(piece.blocks) and not set(blocks).isdisjoint(piece.blocks):
                ticker.add(number, piece_run(number))

    def store_block(block, first, grad):
        at = pl.ds(pl.multiple_of(block * width + first, 16), grad.shape[0])
        grad = grad.astype(bf16)
        stage[0, at, :] = grad[:, :HALF]
        stage[1, at, :] = grad[:, HALF:]

    def store_strip(block, part, grad):
        at = pl.ds(block * width, width)
        grad = grad.astype(bf16)
        first = part * 256
        for half in range(2):
            low, high = max(first, half * HALF), min(first + 256, (half + 1) * HALF)
            if low < high:
                lanes = pl.ds(low - half * HALF, high - low)
                stage[half, at, lanes] = grad[:, low - first : high - first]

    def loop(count, step):
        def run(index, carry):
            step(index)
            return carry

        lax.fori_loop(0, count, run, 0)

    def feed_forward(
        x, branch, grads, mid_low, turned, act_turned, low, normed_one, grad_second, inverse_one, out_w, ff_w,
        act, slope, up_bias_row,
    ):
        def load(index, source, target):
            return pltpu.make_async_copy(source, target, load_sem.at[index])

        first = [load(0, out_weight, out_w), load(1, branch_in, branch), load(2, x_in, x)]
        for copy in first:
            copy.start()
        grads_load = load(3, grad_out, grads)

        def up_load(block):
            return pltpu.make_async_copy(
                up_weight.at[:, pl.ds(block * width, width)], ff_w.at[block], weight_sem.at[block]
            )

        def down_load(block):
            return pltpu.make_async_copy(
                down_weight.at[pl.ds(block * width, width)], ff_w.at[block], weight_sem.at[block]
            )

        for block in range(ff_blocks):
            up_load(block).start()
        grads_load.start()
        total = Sums(sums)
        total.clear()
        up_bias_row[...] = row_vector(up_bias)
        for copy in first:
            copy.wait()
        tile = 128

        def strip(index):
            return pl.ds(pl.multiple_of(index * 256, 256), 256)

        def attended(index):
            normed_one[:, strip(index)] = mm(branch[...], out_w[:, strip(index)])

        def project(index):
            here = pl.ds(pl.multiple_of(index * tile, tile), tile)
            hidden = x[here, :].astype(jnp.float32) + normed_one[here, :]
            normed, inverse = normalize(hidden + row_vector(out_bias))
            normed_one[here, :] = normed
            inverse_one[here, :] = jnp.broadcast_to(inverse, (tile, PAIR))
            mid = normed * row_vector(first_gain) + row_vector(first_shift)
            mid_low[here, :] = mid.astype(bf16)

        loop(width // 256, attended)
        loop(rows // tile, project)
        for block in range(ff_blocks):
            up_load(block).wait()

            def up(index, block=block):
                part = pl.multiple_of(index * 256, 256)
                lanes = pl.ds(block * width + part, 256)
                pre = mm(mid_low[...], ff_w[block, :, pl.ds(part, 256)])
                pre = pre + up_bias_row[:, lanes]
                half = 0.5 * (1.0 + lax.erf(pre * (0.5**0.5)))
                act[:, lanes] = (pre * half).astype(bf16)
                bell = jnp.exp(-0.5 * pre * pre) * (2.0 * math.pi) ** -0.5
                slope[:, lanes] = (half + pre * bell).astype(bf16)

            loop(width // 256, up)
            down_load(block).start()
        turned[...] = mid_low[...].T
        for block in range(ff_blocks):
            down_load(block).wait()
        grads_load.wait()

        def summed(index):
            total = mm(act[:, pl.ds(0, width)], ff_w[0, :, strip(index)])
            for block in range(1, ff_blocks):
                total = total + mm(
                    act[:, pl.ds(block * width, width)], ff_w[block, :, strip(index)]
                )
            grad_second[:, strip(index)] = total

        def down(index):
            here = pl.ds(pl.multiple_of(index * tile, tile), tile)
            mid = normed_one[here, :] * row_vector(first_gain) + row_vector(first_shift)
            normed, inverse = normalize(mid + row_vector(down_bias) + grad_second[here, :])
            grad = grads[here, :].astype(jnp.float32)
            total.add(1, grad * normed)
            total.add(2, grad)
            grads[here, :] = (
                normed * row_vector(second_gain) + row_vector(second_shift)
            ).astype(bf16)
            grad = normalize_back(grad * row_vector(second_gain), normed, inverse)
            grad_second[here, :] = grad
            grad = grad.astype(bf16)
            low[here, :] = grad
            total.add(0, grad.astype(jnp.float32))

        loop(width // 256, summed)
        loop(rows // tile, down)
        out_copy = load(4, grads, layer_out)
        out_copy.start()
        for block in range(ff_blocks):

            act_turned[...] = act[:, pl.ds(block * width, width)].T
            for part in range(width // 256):
                store_strip(block, part, mm(act_turned[...], low[:, pl.ds(part * 256, 256)]))
            if block == 0:
                wait_greet()
            staged(block)
            tick(f"down{block}")
        for block in range(ff_blocks):

            def up_back(index, block=block):
                at = pl.multiple_of(index * 256, 256)
                lanes = pl.ds(block * width + at, 256)
                grad = mm(low[...], ff_w[block, pl.ds(at, 256), :], NT)
                grad = (grad * slope[:, lanes].astype(jnp.float32)).astype(bf16)
                slope[:, lanes] = grad
                up_sums[:, lanes] = jnp.sum(grad.astype(jnp.float32), axis=0, keepdims=True)

            loop(width // 256, up_back)
            up_load(block).start()
            tick(f"back{block}")
        for block in range(ff_blocks):

            for part in range(width // 256):
                lanes = pl.ds(block * width + part * 256, 256)
                store_strip(ff_blocks + block, part, mm(turned[...], slope[:, lanes]))
            staged(ff_blocks + block)
            tick(f"up{block}")
        for block in range(ff_blocks):
            up_load(block).wait()

        def mid_sum(index):
            total = grad_second[:, strip(index)]
            for block in range(ff_blocks):
                total = total + mm(
                    slope[:, pl.ds(block * width, width)], ff_w[block, strip(index), :], NT
                )
            grad_second[:, strip(index)] = total

        def mid_back(index):
            here = pl.ds(pl.multiple_of(index * tile, tile), tile)
            grad = grad_second[here, :]
            normed = normed_one[here, :]
            total.add(4, grad * normed)
            total.add(5, grad)
            grad = normalize_back(
                grad * row_vector(first_gain), normed, inverse_one[here, pl.ds(0, 1)]
            )
            grad_first[here, :] = grad
            grad = grad.astype(bf16)
            low[here, :] = grad
            total.add(3, grad.astype(jnp.float32))

        loop(width // 256, mid_sum)
        tick("mid0")
        loop(rows // tile, mid_back)
        tick("mid1")
        for seq in range(seqs):
            padded[seq, pl.ds(HALO, tokens)] = mm(
                low[pl.ds(seq * tokens, tokens), :], out_w[...], NT
            ).astype(bf16)

        def out_grad(index):
            at = pl.multiple_of(index * 256, 256)
            store_block(2 * ff_blocks, at, mm(branch[:, pl.ds(at, 256)], low[...], TN))

        loop(width // 256, out_grad)
        staged(2 * ff_blocks)
        tick("out")
        vec[...] = jnp.zeros_like(vec)
        for part in range(ff_blocks * pairs):
            vec[pl.ds(part, 1), :] = up_sums[:, pl.ds(part * PAIR, PAIR)]
        for row in range(6):
            for part in range(pairs):
                vec[pl.ds((ff_blocks + row) * pairs + part, 1), :] = sums[
                    pl.ds(row, 1), pl.ds(part * PAIR, PAIR)
                ]
        out_copy.wait()

    narrow = pltpu.VMEM((rows, width), bf16)
    wide = pltpu.VMEM((rows, width), jnp.float32)
    hidden = pltpu.VMEM((rows, ff_blocks * width), bf16)
    pl.run_scoped(
        feed_forward,
        narrow, narrow, narrow, narrow,
        pltpu.VMEM((width, rows), bf16),
        pltpu.VMEM((width, rows), bf16),
        narrow, wide, wide,
        pltpu.VMEM((rows, PAIR), jnp.float32),
        pltpu.VMEM((width, width), bf16),
        pltpu.VMEM((ff_blocks, width, width), bf16),
        hidden, hidden,
        pltpu.VMEM((1, ff_blocks * width), jnp.float32),
    )
    first_row = (ff_blocks + 6) * pairs
    tap_row = first_row + 2 * pairs
    proxy_row = tap_row + 2 * pairs

    def attention(
        x, queries, keys, values, kernel_one, expo, keep, land, mixed, kernel_two, approx, kv_own,
        shares, proxies, rest, grad_qkv, turned, rows_of_weight,
    ):
        place = Place(batch_size, seq_size)
        loads = {}
        for index, (name, source, target) in enumerate(
            (
                ("kernel_one", kernel_one_in, kernel_one),
                ("mixed", mixed_in, mixed),
                ("land", land_in, land),
                ("queries", queries_in, queries),
                ("approx", approx_in, approx),
                ("kv_own", kv_own_in, kv_own),
                ("kernel_two", kernel_two_in, kernel_two),
                ("shares", shares_in, shares),
                ("values", values_in, values),
                ("expo", expo_in, expo),
                ("keys", keys_in, keys),
                ("keep", keep_in, keep),
                ("x", x_in, x),
                ("proxies", proxies_in, proxies),
            )
        ):
            loads[name] = pltpu.make_async_copy(source, target, load_sem.at[index])
            loads[name].start()
        zero_past(padded, tokens)
        halo = halo_copies(place, padded, tokens, *halo_sem)
        for copy in halo:
            copy.start()

        def spots(unit):
            seq, pair = lax.div(unit, pairs), lax.rem(unit, pairs)
            span = pl.ds(pl.multiple_of(seq * tokens, tokens), tokens)
            lanes = pl.ds(pl.multiple_of(pair * PAIR, PAIR), PAIR)
            return seq, span, lanes

        def paced(step, name, chunks=1):
            size = -(-units // chunks)
            for chunk, first in enumerate(range(0, units, size)):
                lax.fori_loop(first, min(first + size, units), step, 0, unroll=2)
                tick(f"{name}{chunk}")

        def mixed_parts(unit, carry):
            seq, span, lanes = spots(unit)
            grad = padded[seq, pl.ds(HALO, tokens), lanes]
            land_send[unit, 0] = join_heads(mm(kernel_one[unit].astype(bf16), grad)).astype(bf16)
            return carry

        loads["kernel_one"].wait()
        lax.fori_loop(0, units, mixed_parts, 0, unroll=2)
        for unit in range(units, seq_size * many):
            land_send[unit] = jnp.ones_like(land_send[unit])
        mixed_out = shared_out(
            place, land_send.at[:, 0], land_recv.at[:, :, 0], many, *mixed_sem
        )
        for copy in mixed_out:
            copy.start()
        tick("start")

        def first_grads(unit, carry):
            seq, span, lanes = spots(unit)
            weights = kernel_one[unit]
            grad = mm(spread_heads(mixed[unit]), padded[seq, pl.ds(HALO, tokens), lanes], NT)
            both = (weights * grad).reshape(2, SEG, tokens)
            both = jnp.broadcast_to(jnp.sum(both, axis=1, keepdims=True), both.shape)
            score_grad = (weights * (grad - both.reshape(2 * SEG, tokens))).astype(bf16)
            land_send[unit, 1] = join_heads(mm(score_grad, queries[span, lanes])).astype(bf16)
            rest[0, span, lanes] = mm(score_grad, spread_heads(land[unit, 1]), TN)
            return carry

        for name in ("queries", "mixed", "land"):
            loads[name].wait()
        paced(first_grads, "first", 3)
        tick("wait_mixed")
        for copy in mixed_out:
            copy.wait()
        first_unit = place.seq * many
        for name in ("approx", "kv_own", "kernel_two", "shares"):
            loads[name].wait()
        kernels, approx_grads = [], []
        for own in range(many):
            total = land_send[first_unit + own, 0].astype(jnp.float32)
            for step in range(seq_size - 1):
                total = total + land_recv[step, own, 0].astype(jnp.float32)
            total = split(spread_heads(total))
            kv_mean = kv_own[own]
            kv_grad = join_heads(mm3(split(approx[own]), total, TN))
            approx_grads.append(mm3(split(spread_heads(kv_mean)), total, NT))
            kernels.append(kernel_two[own])
            dots = kv_grad * kv_mean
            first = first_head(dots.shape)
            dots = jnp.concatenate(
                [
                    jnp.sum(jnp.where(first, dots, 0.0), axis=1, keepdims=True),
                    jnp.sum(jnp.where(first, 0.0, dots), axis=1, keepdims=True),
                ],
                axis=0,
            )
            dots = row_of(dots)
            for slot in range(seq_size):
                share = shares[own, slot, pl.ds(0, 1), :]
                scaled = (kv_grad * join_heads(column(share))).astype(bf16)
                high, low = split(-dots * share)
                tail = jnp.concatenate([high, low, jnp.zeros((14, PAIR), bf16)], axis=0)
                acc_send[slot, own] = jnp.concatenate([scaled, tail], axis=0)
        acc_out = []
        for step in range(1, seq_size):
            acc_out.append(
                pltpu.make_async_remote_copy(
                    src_ref=acc_send.at[seq_size - step],
                    dst_ref=acc_all.at[pl.ds(first_unit, many)],
                    send_sem=acc_sem[0].at[step - 1],
                    recv_sem=acc_sem[1].at[step - 1],
                    device_id=place.seq_peer(step),
                    device_id_type=MESH_IDS,
                )
            )
        for copy in acc_out:
            copy.start()
        for own in range(many):
            acc_all[first_unit + own] = acc_send[0, own]
        tick("acc")
        for copy in halo:
            copy.wait()
        trim_halo(place, padded, tokens)
        tap_rows[...] = turned_taps(taps)
        for part in range(2):
            span = (part * pairs // 2, (part + 1) * pairs // 2)
            conv_rows(padded, tap_rows, rest.at[2], tokens, span)
            tick(f"conv{part}")
        loads["values"].wait()
        loads["expo"].wait()
        loads["keys"].wait()
        tick("wait_acc")
        for copy in acc_out:
            copy.wait()

        def third_grads(unit, carry):
            seq, span, lanes = spots(unit)
            packed = acc_all[unit]
            acc = spread_heads(packed[:SEG])
            tail = packed[SEG:].astype(jnp.float32)
            part = mm(acc, values[seq, pl.ds(HALO, tokens), lanes], NT)
            weights = expo[unit]
            score_grad = (weights * (part + column(tail[0:1] + tail[1:2]))).astype(bf16)
            land_send[unit, 0] = join_heads(mm(score_grad, keys[span, lanes])).astype(bf16)
            rest[1, span, lanes] = mm(score_grad, spread_heads(land[unit, 0]), TN)
            value_grad = mm(weights.astype(bf16), acc, TN) + rest[2, span, lanes]
            valid = positions(place, tokens, 0) < length_of(bounds, seq)
            grad_qkv[2, span, lanes] = jnp.where(valid, value_grad, 0.0).astype(bf16)
            return carry

        paced(third_grads, "third", 3)
        land_out = shared_out(place, land_send, land_recv, many, *land_sem)
        for copy in land_out:
            copy.start()
        loads["x"].wait()
        turned[...] = x[...].T

        def weight_grad(third, block):
            def step(index):
                at = pl.multiple_of(index * 256, 256)
                store_block(block, at, mm(turned[pl.ds(at, 256), :], grad_qkv[third]))

            loop(width // 256, step)

        def bias_grad(third, row):
            for pair in range(pairs):
                cols = grad_qkv[third, :, pl.ds(pair * PAIR, PAIR)].astype(jnp.float32)
                vec[pl.ds(row + pair, 1), :] = jnp.sum(cols, axis=0, keepdims=True)

        weight_grad(2, 2 * ff_blocks + 1)
        staged(2 * ff_blocks + 1)
        tick("value")
        bias_grad(2, first_row + pairs)
        for part in range(3):
            span = (part * pairs // 3, (part + 1) * pairs // 3)
            tap_grads(padded, values, vec, tap_row, tokens, span)
            tick(f"taps{part}")
        loads["keep"].wait()
        loads["proxies"].wait()
        kernel_grads = newton_backward(kernels, approx_grads, keep, tick)
        extra = []
        for own in range(many):
            kernel, grad = kernels[own], kernel_grads[own]
            score_grad = split(
                kernel * (grad - jnp.sum(kernel * grad, axis=1, keepdims=True))
            )
            both = land[first_unit + own]
            left, right = spread_heads(both[0]), spread_heads(both[1])
            extra.append(
                (
                    join_heads(mm(score_grad[0], right) + mm(score_grad[1], right)),
                    join_heads(mm(score_grad[0], left, TN) + mm(score_grad[1], left, TN)),
                )
            )
        tick("wait_land")
        for copy in land_out:
            copy.wait()
        for own in range(many):
            unit = first_unit + own
            low, high = segment_edges(bounds, jnp.minimum(lax.div(unit, pairs), seqs - 1))
            for slot in range(2):
                total = land_send[unit, slot].astype(jnp.float32) + extra[own][slot]
                for step in range(seq_size - 1):
                    total = total + land_recv[step, own, slot].astype(jnp.float32)
                land_all[unit, slot] = (total / (high - low)).astype(bf16)
            row = pl.ds(proxy_row + lax.rem(unit, pairs), 1)
            vec[row, :] = vec[row, :] + jnp.where(
                unit < units, proxies[own, pl.ds(0, 1), :], 0.0
            )
        land_back = passed_on(place, land_all, many, *land_back_sem)
        for copy in land_back:
            copy.start()
        tick("land")
        tick("wait_back")
        for copy in land_back:
            copy.wait()
        for seq in range(seqs):
            member = member_of(place, bounds, seq, tokens)
            span = pl.ds(seq * tokens, tokens)
            for pair in range(pairs):
                lanes = pl.ds(pair * PAIR, PAIR)
                both = land_all[seq * pairs + pair]
                for slot in range(2):
                    grad = (mm(member, both[slot], TN) + rest[slot, span, lanes]) * quarter
                    grad_qkv[slot, span, lanes] = grad.astype(bf16)
        tick("grads")
        weight_grad(0, 2 * ff_blocks + 2)
        weight_grad(1, 2 * ff_blocks + 3)
        staged(2 * ff_blocks + 2, 2 * ff_blocks + 3)
        bias_grad(0, first_row)
        ticker.add("vec", vec_reduce(place, vec, slots, *vec_sem))
        tick("last")

        def weight_load(tile):
            return pltpu.make_async_copy(
                qkv_weight.at[pl.ds(tile * PAIR, PAIR)],
                rows_of_weight.at[tile % 2],
                weight_sem.at[tile % 2],
            )

        weight_load(0).start()
        for tile in range(pairs):
            if tile + 1 < pairs:
                weight_load(tile + 1).start()
            weight_load(tile).wait()
            lanes = pl.ds(tile * PAIR, PAIR)
            total = grad_first[:, lanes]
            for third in range(3):
                total = total + mm(
                    grad_qkv[third], rows_of_weight[tile % 2, :, pl.ds(third * width, width)], NT
                )
            x[:, lanes] = total.astype(bf16)
            tick(f"input{tile}")
        out_copy = pltpu.make_async_copy(x, input_grad, load_sem.at[0])
        out_copy.start()
        ticker.drain(LAST)
        out_copy.wait()

    pl.run_scoped(
        attention,
        narrow, narrow, narrow,
        pltpu.VMEM(values_in.shape, bf16),
        pltpu.VMEM(kernel_one_in.shape, jnp.float32),
        pltpu.VMEM(expo_in.shape, jnp.float32),
        pltpu.VMEM(keep_in.shape, jnp.float32),
        pltpu.VMEM(land_in.shape, bf16),
        pltpu.VMEM(mixed_in.shape, bf16),
        *(
            pltpu.VMEM(ref.shape, jnp.float32)
            for ref in (kernel_two_in, approx_in, kv_own_in, shares_in, proxies_in)
        ),
        pltpu.VMEM((2 + 1, rows, width), jnp.float32),
        pltpu.VMEM((3, rows, width), bf16),
        pltpu.VMEM((width, rows), bf16),
        pltpu.VMEM((2, PAIR, 3 * width), bf16),
    )


Z_FIRST = ()


class Piece:
    def __init__(self, blocks, start, rows, orders, slots):
        self.blocks, self.start, self.rows, self.orders, self.slots = (
            blocks, start, rows, orders, slots,
        )


def make_plan(sizes, block_count, width):
    split_rows = 16 * sizes["x"] * sizes["y"] * sizes["z"]
    orders = (("x", "y", "z"), ("y", "x", "z"))
    z_first = (("z0", "z1", "x", "y"), ("z0", "z1", "y", "x"))
    if 2 * width % (2 * split_rows) == 0:
        counts = [2] * (block_count // 2)
    else:
        orders = orders[:1]
        z_first = z_first[:1]
        counts = [8, block_count - 8] if 8 * width % split_rows == 0 else [block_count]
    plan, block, slot = [], 0, 0
    for count in counts:
        rows = -(-count * width // (len(orders) * split_rows)) * len(orders) * split_rows
        own = z_first if len(plan) in Z_FIRST else orders
        need = Reduce.slots(sizes, own, rows)
        plan.append(
            Piece(list(range(block, block + count)), block * width, rows, own, pl.ds(slot, need))
        )
        block += count
        slot += need
    return plan, slot


def layer_back(
    x, grad_out, branch, out_weight, up_weight, down_weight, qkv_weight, saved, bounds, taps,
    vectors, batch_size, seq_size, seqs,
):
    (
        queries, keys, values, kernel_one, expo, land, mixed, _, kernel_two, approx, keep,
        kv_own, shares, proxies,
    ) = saved
    rows, width = x.shape
    tokens = rows // seqs
    pairs = width // PAIR
    own = -(-seqs * pairs // seq_size)
    owned = seq_size * own
    sizes = axis_sizes(batch_size, seq_size)
    ff_blocks = down_weight.shape[0] // width
    plan, slot_rows = make_plan(sizes, 2 * ff_blocks + 4, width)
    pieces, stage_rows = len(plan), plan[-1].start + plan[-1].rows
    parts = len(plan[0].orders)
    copies = max(Reduce.copies(sizes, piece.orders) for piece in plan)
    vec_axes = ("core", "x", "y", "z")
    vec_steps = sum(sizes[axis] - 1 for axis in vec_axes)
    vec_shape = (-(-((ff_blocks + 11) * pairs) // 8) * 8, PAIR)
    f32, bf16 = jnp.float32, jnp.bfloat16
    vmem = pl.BlockSpec(memory_space=pltpu.VMEM)
    anywhere = pl.BlockSpec(memory_space=pl.ANY)
    sems = pltpu.SemaphoreType.DMA
    pair_sems = (sems((seq_size - 1,)),) * 2
    return pl.pallas_call(
        partial(back_kernel, batch_size, seq_size, seqs, tokens, own, plan),
        out_shape=(
            jax.ShapeDtypeStruct((rows, width), bf16),
            jax.ShapeDtypeStruct((rows, width), bf16),
            jax.ShapeDtypeStruct((2, stage_rows, HALF), bf16),
            jax.ShapeDtypeStruct(vec_shape, f32),
        ),
        in_specs=[anywhere] * 20 + [vmem] * (2 + len(vectors)),
        out_specs=(anywhere, anywhere, anywhere, vmem),
        scratch_shapes=[
            pltpu.VMEM((2, stage_rows, HALF), bf16),
            pltpu.VMEM((stage_rows, HALF), bf16),
            pltpu.VMEM((parts, slot_rows, HALF), bf16),
            pltpu.VMEM((sum(sizes[axis] for axis in vec_axes), *vec_shape), f32),
            pltpu.VMEM(values.shape, bf16),
            pltpu.VMEM((rows, width), f32),
            pltpu.VMEM((16, 2 * BLOCK), f32),
            pltpu.VMEM((8, width), f32),
            pltpu.VMEM((1, ff_blocks * width), f32),
            pltpu.VMEM((seq_size, own, SEG + 16, PAIR), bf16),
            pltpu.VMEM((owned, SEG + 16, PAIR), bf16),
            pltpu.VMEM((owned, 2, SEG, PAIR), bf16),
            pltpu.VMEM((seq_size - 1, own, 2, SEG, PAIR), bf16),
            pltpu.VMEM((owned, 2, SEG, PAIR), bf16),
            sems((14,)),
            sems((ff_blocks,)),
            sems((pieces, copies)),
            sems((pieces, copies)),
            pltpu.SemaphoreType.REGULAR((pieces,)),
            (sems((vec_steps,)),) * 2,
            sems((pieces, 2)),
            (sems((2,)),) * 2,
            pair_sems,
            pair_sems,
            pair_sems,
            pair_sems,
        ],
        compiler_params=pltpu.CompilerParams(
            collective_id=0, has_side_effects=True, vmem_limit_bytes=63 * 2**20
        ),
        name="layer_back",
    )(
        x, grad_out, branch, out_weight, up_weight, down_weight, qkv_weight,
        queries, keys, values, kernel_one, expo, keep, land, mixed, kernel_two, approx, kv_own,
        shares, proxies, bounds, taps, *vectors,
    )


def finish_kernel(
    heads, scale, gathered, vec, layer_in, input_in,
    layer_out, input_grad, qkv_grad, query_bias_grad, value_bias_grad, tap_grad, out_grad,
    out_bias_grad, first_gain_grad, first_shift_grad, up_grad, up_bias_grad, down_grad,
    down_bias_grad, second_gain_grad, second_shift_grad, condition,
    narrow, wide, rows_through, in_sem, out_sem, pass_sem,
):
    width = down_grad.shape[1]
    pairs = width // PAIR
    blocks = down_grad.shape[0] // width
    spots = [(down_grad, block * width, 0) for block in range(blocks)]
    spots += [(up_grad, 0, block * width) for block in range(blocks)]
    spots += [(out_grad, 0, 0), (qkv_grad, 0, 2 * width), (qkv_grad, 0, 0), (qkv_grad, 0, width)]
    taken = [
        pltpu.make_async_copy(source, rows_through.at[index], pass_sem.at[index])
        for index, source in enumerate((layer_in, input_in))
    ]
    passed = [
        pltpu.make_async_copy(rows_through.at[index], target, pass_sem.at[index])
        for index, target in enumerate((layer_out, input_grad))
    ]
    slots, rows, _ = wide.shape
    tiles = [
        (target, row + part * rows, col, block * width + part * rows)
        for block, (target, row, col) in enumerate(spots)
        for part in range(width // rows)
    ]

    def fetch(index):
        return pltpu.make_async_copy(
            gathered.at[:, pl.ds(tiles[index][3], rows)],
            narrow.at[index % slots],
            in_sem.at[index % slots],
        )

    def put(index):
        target, row, col, _ = tiles[index]
        return pltpu.make_async_copy(
            wide.at[index % slots],
            target.at[pl.ds(row, rows), pl.ds(col, width)],
            out_sem.at[index % slots],
        )

    for index in range(slots):
        fetch(index).start()
    for copy in taken:
        copy.start()
    row = 0
    for target in (
        up_bias_grad, down_bias_grad, second_gain_grad, second_shift_grad, out_bias_grad,
        first_gain_grad, first_shift_grad, query_bias_grad, value_bias_grad,
    ):
        count = target.shape[0] // PAIR
        target[...] = vec[pl.ds(row, count), :].reshape(target.shape)
        row += count
    tap_grad[...] = vec[pl.ds(row, heads), pl.ds(0, tap_grad.shape[1])]
    proxy = vec[pl.ds(row + heads, pairs), :] * scale
    lanes = lax.broadcasted_iota(jnp.int32, (1, PAIR), 1)
    means = jnp.zeros((1, PAIR), jnp.float32)
    for pair in range(pairs):
        for head in range(2):
            value = proxy[pair : pair + 1, head * SEG : head * SEG + 1]
            means = means + jnp.where(lanes == 2 * pair + head, value, 0.0)
    condition[...] = means[:, :heads].reshape(heads)
    for copy in taken:
        copy.wait()
    for copy in passed:
        copy.start()
    for index in range(len(tiles)):
        slot = index % slots
        fetch(index).wait()
        if index >= slots:
            put(index - slots).wait()
        for half in range(2):
            wide[slot, :, pl.ds(half * HALF, HALF)] = narrow[slot, half].astype(jnp.float32)
        put(index).start()
        if index + slots < len(tiles):
            fetch(index + slots).start()
    for index in range(len(tiles) - slots, len(tiles)):
        put(index).wait()
    for copy in passed:
        copy.wait()


def finish(gathered, vec, layer_out, input_grad, shapes, scale):
    width = layer_out.shape[1]
    any_spec = pl.BlockSpec(memory_space=pl.ANY)
    vmem = pl.BlockSpec(memory_space=pltpu.VMEM)
    outs = [jax.ShapeDtypeStruct(shape, jnp.bfloat16) for shape in (layer_out.shape,) * 2]
    outs += [jax.ShapeDtypeStruct(shape, jnp.float32) for shape in shapes]
    return pl.pallas_call(
        partial(finish_kernel, shapes[3][0], scale),
        out_shape=tuple(outs),
        in_specs=[any_spec, vmem, any_spec, any_spec],
        out_specs=tuple(
            any_spec if out.shape[0] * math.prod(out.shape[1:]) >= width * width // 2 else vmem
            for out in outs
        ),
        scratch_shapes=[
            pltpu.VMEM((SLOTS, 2, FINISH_ROWS, HALF), jnp.bfloat16),
            pltpu.VMEM((SLOTS, FINISH_ROWS, width), jnp.float32),
            pltpu.VMEM((2, *layer_out.shape), jnp.bfloat16),
            pltpu.SemaphoreType.DMA((SLOTS,)),
            pltpu.SemaphoreType.DMA((SLOTS,)),
            pltpu.SemaphoreType.DMA((2,)),
        ],
        compiler_params=pltpu.CompilerParams(vmem_limit_bytes=62 * 2**20),
        name="finish",
    )(gathered, vec, layer_out, input_grad)


SLOTS = 4
FINISH_ROWS = 384


def body(
    hidden_in,
    seg_bounds,
    qkv_weight,
    query_bias,
    value_bias,
    conv_taps,
    out_weight,
    out_bias,
    first_gain,
    first_shift,
    up_weight,
    up_bias,
    down_weight,
    down_bias,
    second_gain,
    second_shift,
    grad_out,
):
    seq_count, tok_count, model_width = hidden_in.shape
    head_count = conv_taps.shape[0]
    row_total = seq_count * tok_count
    batch_size, seq_size = lax.axis_size("batch"), lax.axis_size("seq")
    input_rows = hidden_in.reshape(row_total, model_width)
    saved = attend(
        input_rows, seg_bounds, qkv_weight, query_bias, value_bias, conv_taps,
        batch_size, seq_size, seq_count,
    )
    layer_out, input_grad, gathered, vec = layer_back(
        input_rows,
        grad_out.reshape(row_total, model_width),
        saved[7],
        out_weight,
        up_weight,
        down_weight,
        qkv_weight,
        saved,
        seg_bounds,
        conv_taps,
        (out_bias, first_gain, first_shift, up_bias, down_bias, second_gain, second_shift),
        batch_size,
        seq_size,
        seq_count,
    )

    shapes = (
        qkv_weight.shape,
        query_bias.shape,
        value_bias.shape,
        conv_taps.shape,
        out_weight.shape,
        out_bias.shape,
        first_gain.shape,
        first_shift.shape,
        up_weight.shape,
        up_bias.shape,
        down_weight.shape,
        down_bias.shape,
        second_gain.shape,
        second_shift.shape,
        (head_count,),
    )
    layer_out, input_grad, *grads = finish(
        gathered, vec, layer_out, input_grad, shapes, 1.0 / (batch_size * seq_count)
    )
    return (
        layer_out.reshape(hidden_in.shape),
        input_grad.reshape(hidden_in.shape),
        *grads,
    )


def solution(mesh):
    placed = (
        P("batch", "seq", None),
        P("batch", None),
        P(),
        P(),
        P(),
        P(),
        P(),
        P(),
        P(),
        P(),
        P(),
        P(),
        P(),
        P(),
        P(),
        P(),
        P("batch", "seq", None),
    )
    return jax.shard_map(
        body,
        mesh=mesh,
        in_specs=placed,
        out_specs=(
            P("batch", "seq", None),
            P("batch", "seq", None),
            P(),
            P(),
            P(),
            P(),
            P(),
            P(),
            P(),
            P(),
            P(),
            P(),
            P(),
            P(),
            P(),
            P(),
            P(),
        ),
        check_vma=False,
    )
```

```python
import math
from functools import partial

import jax
import jax.numpy as jnp
from jax import lax
from jax.experimental import pallas as pl
from jax.experimental.pallas import tpu as pltpu
from jax.sharding import PartitionSpec as P

epsilon = 1e-05
MESH_IDS = pl.DeviceIdType.MESH
HALF = 384
LANES = 128


def plane_sides(count):
    wide = max(d for d in range(1, math.isqrt(count) + 1) if count % d == 0)
    return wide, count // wide


def axis_sizes(batch_size, seq_size):
    x_size, y_size = plane_sides(seq_size)
    z_size = batch_size // 2
    z_low = 2 if z_size % 2 == 0 else 1
    return {
        "core": 2, "x": x_size, "y": y_size, "z": z_size, "z0": z_low, "z1": z_size // z_low,
    }


class Place:
    def __init__(self, batch_size, seq_size):
        x_size, y_size = plane_sides(seq_size)
        self.sizes = axis_sizes(batch_size, seq_size)
        batch = lax.axis_index("batch")
        seq = lax.axis_index("seq")
        z_low = self.sizes["z0"]
        self.at = {
            "core": lax.rem(batch, 2),
            "z": lax.div(batch, 2),
            "z0": lax.rem(lax.div(batch, 2), z_low),
            "z1": lax.div(batch, 2 * z_low),
            "x": lax.rem(seq, x_size),
            "y": lax.div(seq, x_size),
        }
        self.seq_size = seq_size
        self.seq = seq
        self.batch = batch

    def peer_index(self, axis, step):
        size = self.sizes[axis]
        return lax.rem(self.at[axis] + step, size)

    def device(self, **moved):
        spot = {**self.at, **moved}
        if "z0" in moved or "z1" in moved:
            spot["z"] = spot["z1"] * self.sizes["z0"] + spot["z0"]
        return (spot["z"] * 2 + spot["core"], spot["y"] * self.sizes["x"] + spot["x"])

    def peers(self, axes):
        for axis in axes:
            for step in range(1, self.sizes[axis]):
                yield self.device(**{axis: self.peer_index(axis, step)})

    def seq_peer(self, step):
        return (self.batch, lax.rem(self.seq + step, self.seq_size))


def greet(devices):
    barrier = pltpu.get_barrier_semaphore()
    devices = list(devices)
    for device in devices:
        pl.semaphore_signal(barrier, inc=1, device_id=device, device_id_type=MESH_IDS)
    return lambda: pl.semaphore_wait(barrier, len(devices))


def tile_rows(rows):
    return max(t for t in (96, 64, 48, 32, 16) if rows % t == 0)


def add_rows(out_ref, in_ref, at, parts, rows):
    tile = tile_rows(rows)

    def step(index, carry):
        start = pl.multiple_of(at + index * tile, 16)
        total = in_ref[pl.ds(start, tile), :].astype(jnp.float32)
        for ref, first in parts:
            total = total + ref[pl.ds(pl.multiple_of(first + index * tile, 16), tile), :].astype(
                jnp.float32
            )
        out_ref[pl.ds(start, tile), :] = total.astype(out_ref.dtype)
        return carry

    lax.fori_loop(0, rows // tile, step, 0)


class Reduce:
    def __init__(
        self, number, place, orders, stage, whole, recv, send_sem, recv_sem, free_sem, rows
    ):
        self.number, self.make_place, self.orders = number, place, orders
        self.stage, self.whole, self.recv = stage, whole, recv
        self.send_sem, self.recv_sem, self.free_sem = send_sem, recv_sem, free_sem
        self.part = rows // len(orders)

    @staticmethod
    def slots(sizes, orders, rows):
        need = []
        for order in orders:
            size, slot = rows // len(orders), 0
            for axis in order:
                size //= sizes[axis]
                slot += (sizes[axis] - 1) * size
            need.append(slot)
        return max(need)

    @staticmethod
    def copies(sizes, orders):
        return 2 + 2 * sum(sizes[axis] - 1 for order in orders for axis in order)

    def level_of(self, place, half, level):
        base, size, slot = half * self.part, self.part, 0
        order = self.orders[half]
        sem = 2 + 2 * half * sum(place.sizes[axis] - 1 for axis in order)
        for axis in order[:level]:
            count = place.sizes[axis]
            size //= count
            slot += (count - 1) * size
            sem += 2 * (count - 1)
            base = base + place.at[axis] * size
        count = place.sizes[order[level]]
        return order[level], count, base, size // count, slot, sem

    def copy(self, index, src, dst, device):
        return pltpu.make_async_remote_copy(
            src_ref=src,
            dst_ref=dst,
            send_sem=self.send_sem.at[self.number, index],
            recv_sem=self.recv_sem.at[self.number, index],
            device_id=device,
            device_id_type=MESH_IDS,
        )

    @staticmethod
    def rows_of(ref, start, rows):
        return ref.at[pl.ds(pl.multiple_of(start, 16), rows)]

    def scatter(self, half, level):
        place = self.make_place()
        axis, count, base, chunk, slot, sem = self.level_of(place, half, level)
        mine = self.stage.at[place.at["core"]]
        copies = []
        for step in range(1, count):
            peer = place.peer_index(axis, step)
            copies.append(
                self.copy(
                    sem + step - 1,
                    self.rows_of(mine, base + peer * chunk, chunk),
                    self.recv.at[half, pl.ds(slot + (step - 1) * chunk, chunk)],
                    place.device(**{axis: peer}),
                )
            )
        return copies

    def spread(self, half, level):
        place = self.make_place()
        axis, count, base, chunk, slot, sem = self.level_of(place, half, level)
        here = self.rows_of(self.whole, base + place.at[axis] * chunk, chunk)
        return [
            self.copy(
                sem + count - 1 + step - 1,
                here,
                here,
                place.device(**{axis: place.peer_index(axis, step)}),
            )
            for step in range(1, count)
        ]

    def add_level(self, half, level):
        place = self.make_place()
        axis, count, base, chunk, slot, _ = self.level_of(place, half, level)
        mine = self.stage.at[place.at["core"]]
        add_rows(
            self.whole if level == len(self.orders[half]) - 1 else mine,
            mine,
            base + place.at[axis] * chunk,
            [(self.recv.at[half], slot + k * chunk) for k in range(count - 1)],
            chunk,
        )

    def core_out(self):
        place = self.make_place()
        core = place.at["core"]
        return self.copy(0, self.stage.at[1 - core], self.whole, place.device(core=1 - core))

    def core_back(self):
        place = self.make_place()
        core = place.at["core"]
        return self.copy(1, self.whole, self.stage.at[core], place.device(core=1 - core))

    def run(self):
        halves = range(len(self.orders))
        self.core_out().start()
        yield
        self.core_out().wait()
        place = self.make_place()
        other = place.device(core=1 - place.at["core"])
        pl.semaphore_signal(
            self.free_sem.at[self.number], inc=1, device_id=other, device_id_type=MESH_IDS
        )
        mine = self.stage.at[place.at["core"]]
        for half in halves:
            start = half * self.part
            add_rows(mine, mine, start, [(self.whole, start)], self.part)
            for copy in self.scatter(half, 0):
                copy.start()
        last = len(self.orders[0]) - 1
        for level in range(last + 1):
            yield
            for half in halves:
                for copy in self.scatter(half, level):
                    copy.wait()
                self.add_level(half, level)
                later = self.scatter if level < last else self.spread
                for copy in later(half, min(level + 1, last)):
                    copy.start()
        for level in reversed(range(last + 1)):
            yield
            for half in halves:
                for copy in self.spread(half, level):
                    copy.wait()
                for copy in self.spread(half, level - 1) if level else ():
                    copy.start()
        pl.semaphore_wait(self.free_sem.at[self.number], 1)
        self.core_back().start()
        yield
        self.core_back().wait()


def vec_reduce(place, acc, slots, send_sem, recv_sem):
    sem = 0
    level = 0
    for axis in ("core", "x", "y", "z"):
        count = place.sizes[axis]
        copies = []
        here = place.at[axis]
        for step in range(1, count):
            copies.append(
                pltpu.make_async_remote_copy(
                    src_ref=acc,
                    dst_ref=slots.at[level + here],
                    send_sem=send_sem.at[sem],
                    recv_sem=recv_sem.at[sem],
                    device_id=place.device(**{axis: place.peer_index(axis, step)}),
                    device_id_type=MESH_IDS,
                )
            )
            sem += 1
        for copy in copies:
            copy.start()
        slots[level + here] = acc[...]
        yield
        for copy in copies:
            copy.wait()
        total = slots[level]
        for index in range(1, count):
            total = total + slots[level + index]
        acc[...] = total
        level += count


SEG = 64
PAIR = 128
HALO = 16
BLOCK = 128
FAR = -1e30
NT = ((1,), (1,))
TN = ((0,), (0,))
NN = ((1,), (0,))


def mm(left, right, dims=NN):
    return lax.dot_general(left, right, (dims, ((), ())), preferred_element_type=jnp.float32)


def split(array):
    high = array.astype(jnp.bfloat16)
    return high, (array - high.astype(jnp.float32)).astype(jnp.bfloat16)


def thirds(array):
    high = array.astype(jnp.bfloat16)
    middle = (array - high.astype(jnp.float32)).astype(jnp.bfloat16)
    rest = array - high.astype(jnp.float32) - middle.astype(jnp.float32)
    return high, middle, rest.astype(jnp.bfloat16)


def mm3(left, right, dims=NN):
    left_high, left_low = left
    right_high, right_low = right
    (left_dim,), (right_dim,) = dims
    return mm(
        jnp.concatenate([left_high, left_high, left_low], axis=left_dim),
        jnp.concatenate([right_high, right_low, right_high], axis=right_dim),
        dims,
    )


def eye_mask(size):
    rows = lax.broadcasted_iota(jnp.int32, (size, size), 0)
    return rows == lax.broadcasted_iota(jnp.int32, (size, size), 1)


def column(row):
    return jnp.sum(jnp.where(eye_mask(row.shape[1]), row, 0.0), axis=1, keepdims=True)


def row_of(col):
    return jnp.sum(jnp.where(eye_mask(col.shape[0]), col, 0.0), axis=0, keepdims=True)


def first_head(shape):
    return lax.broadcasted_iota(jnp.int32, shape, len(shape) - 1) < SEG


def spread_heads(pair):
    first = first_head(pair.shape)
    zero = jnp.zeros_like(pair)
    return jnp.concatenate([jnp.where(first, pair, zero), jnp.where(first, zero, pair)], axis=0)


def join_heads(blocks):
    shape = (SEG, PAIR)
    return jnp.where(
        first_head(shape),
        jnp.broadcast_to(blocks[:SEG], shape),
        jnp.broadcast_to(blocks[SEG:], shape),
    )


def heads_sum(col):
    first = jnp.sum(col[:SEG], axis=0, keepdims=True)
    second = jnp.sum(col[SEG:], axis=0, keepdims=True)
    return jnp.concatenate(
        [jnp.broadcast_to(first, (SEG, 1)), jnp.broadcast_to(second, (SEG, 1))], axis=0
    )


def shared_out(place, source, target, many, send_sem, recv_sem):
    copies = []
    for step in range(1, place.seq_size):
        device = place.seq_peer(step)
        copies.append(
            pltpu.make_async_remote_copy(
                src_ref=source.at[pl.ds(device[1] * many, many)],
                dst_ref=target.at[step - 1],
                send_sem=send_sem.at[step - 1],
                recv_sem=recv_sem.at[step - 1],
                device_id=device,
                device_id_type=MESH_IDS,
            )
        )
    return copies


def passed_on(place, array, many, send_sem, recv_sem):
    copies = []
    here = array.at[pl.ds(place.seq * many, many)]
    for step in range(1, place.seq_size):
        copies.append(
            pltpu.make_async_remote_copy(
                src_ref=here,
                dst_ref=here,
                send_sem=send_sem.at[step - 1],
                recv_sem=recv_sem.at[step - 1],
                device_id=place.seq_peer(step),
                device_id_type=MESH_IDS,
            )
        )
    return copies


def halo_copies(place, padded, tokens, send_sem, recv_sem):
    copies = []
    for index, (step, first, there) in enumerate(
        ((1, tokens, 0), (place.seq_size - 1, HALO, tokens + HALO))
    ):
        copies.append(
            pltpu.make_async_remote_copy(
                src_ref=padded.at[:, pl.ds(first, HALO)],
                dst_ref=padded.at[:, pl.ds(there, HALO)],
                send_sem=send_sem.at[index],
                recv_sem=recv_sem.at[index],
                device_id=place.seq_peer(step),
                device_id_type=MESH_IDS,
            )
        )
    return copies


def trim_halo(place, padded, tokens):
    zero = jnp.zeros((padded.shape[0], HALO, padded.shape[2]), padded.dtype)
    low, high = pl.ds(0, HALO), pl.ds(tokens + HALO, HALO)
    padded[:, low] = jnp.where(place.seq > 0, padded[:, low], zero)
    padded[:, high] = jnp.where(place.seq < place.seq_size - 1, padded[:, high], zero)


def zero_past(padded, tokens):
    past = tokens + 2 * HALO
    rest = padded.shape[1] - past
    padded[:, pl.ds(past, rest)] = jnp.zeros(
        (padded.shape[0], rest, padded.shape[2]), padded.dtype
    )


def band(taps):
    wide = jnp.broadcast_to(taps, (BLOCK, 2 * BLOCK))
    return pltpu.roll(wide, 0, 1, stride=1, stride_axis=0).astype(jnp.bfloat16)


def tap_lanes(taps):
    heads, count = taps.shape
    wide = jnp.concatenate(
        [taps[...], jnp.zeros((heads, 2 * BLOCK - count), jnp.float32)], axis=1
    )
    return jnp.concatenate([wide, jnp.zeros((16 - heads, 2 * BLOCK), jnp.float32)], axis=0)


def turned_taps(taps):
    shape = (2 * BLOCK, 2 * BLOCK)
    ends = lax.broadcasted_iota(jnp.int32, shape, 0) + lax.broadcasted_iota(jnp.int32, shape, 1)
    turn = jnp.where(ends == taps.shape[1] - 1, 1.0, 0.0).astype(jnp.bfloat16)
    return mm(tap_lanes(taps).astype(jnp.bfloat16), turn)


def conv_rows(padded, taps, out, tokens, span=None):
    seqs, _, width = padded.shape

    def step(pair, carry):
        lanes = pl.ds(pl.multiple_of(pair * PAIR, PAIR), PAIR)
        first = band(taps[pl.ds(2 * pair, 1), :])
        second = band(taps[pl.ds(2 * pair + 1, 1), :])
        for seq in range(seqs):
            for block in range(tokens // BLOCK):
                window = padded[seq, pl.ds(block * BLOCK, 2 * BLOCK), lanes]
                both = jnp.where(
                    first_head((BLOCK, PAIR)), mm(first, window), mm(second, window)
                )
                out[pl.ds(seq * tokens + block * BLOCK, BLOCK), lanes] = both
        return carry

    lax.fori_loop(*(span or (0, width // PAIR)), step, 0)


def segment_edges(bounds, seq):
    low = column(bounds[pl.ds(seq, 1), pl.ds(0, SEG)].astype(jnp.float32))
    high = column(bounds[pl.ds(seq, 1), pl.ds(1, SEG)].astype(jnp.float32))
    return low, high


def positions(place, tokens, axis):
    shape = (tokens, 1) if axis == 0 else (1, tokens)
    return (place.seq * tokens + lax.broadcasted_iota(jnp.int32, shape, axis)).astype(jnp.float32)


def member_of(place, bounds, seq, tokens):
    low, high = segment_edges(bounds, seq)
    where = positions(place, tokens, 1)
    return jnp.where((where >= low) & (where < high), 1.0, 0.0).astype(jnp.bfloat16)


def length_of(bounds, seq):
    return bounds[pl.ds(seq, 1), pl.ds(SEG, 1)].astype(jnp.float32)


def newton_forward(kernels, keep):
    eye = jnp.where(eye_mask(PAIR), 1.0, 0.0)
    approx = []
    for kernel in kernels:
        fro = heads_sum(jnp.sum(kernel * kernel, axis=1, keepdims=True))
        approx.append(kernel.T / fro)
    halves = [split(kernel) for kernel in kernels]
    units = range(len(kernels))
    for step in range(6):
        wide = [split(a) for a in approx]
        product = [mm3(halves[u], wide[u]) for u in units]
        lefts = [split(p) for p in product]
        inner = [15.0 * eye - mm3(lefts[u], split(7.0 * eye - product[u])) for u in units]
        outer = [13.0 * eye - mm3(lefts[u], split(inner[u])) for u in units]
        for u in units:
            for slot, value in enumerate((approx[u], product[u], inner[u], outer[u])):
                keep[u, step, slot] = value
        approx = [0.25 * mm3(wide[u], split(outer[u])) for u in units]
    return approx


def attend_kernel(
    batch_size, seq_size, seqs, tokens, many,
    x_in, weight_in, bounds, query_bias, value_bias, taps, *refs
):
    outs, refs = refs[:14], refs[14:]
    saved, refs = refs[:14], refs[14:]
    (
        queries, keys, values, kernel_one, expo, land, mixed, branch, kernel_two, approx_out,
        keep, kv_own, shares, proxies,
    ) = saved
    (
        x, weight, load_sem, save_sem, land_send, land_recv, kv_send, kv_recv, conv, tap_rows, biases,
        land_sem, land_back_sem, kv_sem, mixed_sem, halo_sem,
    ) = refs
    place = Place(batch_size, seq_size)
    width = x.shape[1]
    loads = [pltpu.make_async_copy(x_in, x, load_sem.at[3])]
    for third in range(3):
        lanes = pl.ds(third * width, width)
        loads.append(
            pltpu.make_async_copy(
                weight_in.at[:, lanes], weight.at[:, lanes], load_sem.at[third]
            )
        )
    for copy in loads:
        copy.start()
    saves = []

    def save(*names):
        for ref in names:
            index = [ref is other for other in saved].index(True)
            copy = pltpu.make_async_copy(ref, outs[index], save_sem.at[index])
            copy.start()
            saves.append(copy)

    pairs = width // PAIR
    units = seqs * pairs
    wait_greet = greet(place.seq_peer(step) for step in range(1, seq_size))
    quarter = float(SEG) ** -0.25

    tap_rows[...] = tap_lanes(taps)
    biases[...] = jnp.zeros_like(biases)
    biases[pl.ds(0, 1), :] = query_bias[...].reshape(1, width)
    biases[pl.ds(2, 1), :] = value_bias[...].reshape(1, width)

    def project(out_ref, third):
        def step(tile, carry):
            lanes = pl.ds(pl.multiple_of(third * width + tile * 256, 256), 256)
            here = pl.ds(pl.multiple_of(tile * 256, 256), 256)
            rows = mm(x[...], weight[:, lanes]) + biases[pl.ds(third, 1), here]
            if third < 2:
                out_ref[:, here] = (rows * quarter).astype(jnp.bfloat16)
            else:
                for seq in range(seqs):
                    valid = positions(place, tokens, 0) < length_of(bounds, seq)
                    out_ref[seq, pl.ds(HALO, tokens), here] = jnp.where(
                        valid, rows[seq * tokens : (seq + 1) * tokens], 0.0
                    ).astype(jnp.bfloat16)
            return carry

        loads[1 + third].wait()
        lax.fori_loop(0, width // 256, step, 0)

    loads[0].wait()
    project(queries, 0)
    project(keys, 1)
    save(queries, keys)
    for seq in range(seqs):
        member = member_of(place, bounds, seq, tokens)
        for slot, rows in enumerate((queries, keys)):
            sums = mm(member, rows[pl.ds(seq * tokens, tokens), :])
            for pair in range(pairs):
                land_send[seq * pairs + pair, slot] = sums[:, pair * PAIR : (pair + 1) * PAIR]
    for unit in range(units, seq_size * many):
        land_send[unit] = jnp.ones_like(land_send[unit])
        kv_send[unit] = jnp.ones_like(kv_send[unit])
    wait_greet()
    land_out = shared_out(place, land_send, land_recv, many, *land_sem)
    for copy in land_out:
        copy.start()
    project(values, 2)
    halo = halo_copies(place, values, tokens, *halo_sem)
    for copy in halo:
        copy.start()
    zero_past(values, tokens)
    for copy in land_out:
        copy.wait()
    first_unit = place.seq * many
    for own in range(many):
        unit = first_unit + own
        total = land_send[unit]
        for step in range(seq_size - 1):
            total = total + land_recv[step, own]
        low, high = segment_edges(bounds, jnp.minimum(lax.div(unit, pairs), seqs - 1))
        land[unit] = (total / (high - low)).astype(jnp.bfloat16)
    land_back = passed_on(place, land, many, *land_back_sem)
    for copy in land_back:
        copy.start()
    for copy in halo:
        copy.wait()
    trim_halo(place, values, tokens)
    save(values)
    conv_rows(values, tap_rows, conv, tokens)
    for copy in land_back:
        copy.wait()
    save(land)

    def spots(unit):
        seq, pair = lax.div(unit, pairs), lax.rem(unit, pairs)
        rows = pl.ds(pl.multiple_of(seq * tokens, tokens), tokens)
        lanes = pl.ds(pl.multiple_of(pair * PAIR, PAIR), PAIR)
        return seq, rows, lanes

    def third_scores(unit, carry):
        seq, rows, lanes = spots(unit)
        score = mm(spread_heads(land[unit, 0]), keys[rows, lanes], NT)
        valid = positions(place, tokens, 1) < length_of(bounds, seq)
        score = jnp.where(valid, score, FAR)
        top = jnp.max(score, axis=1, keepdims=True)
        weights = jnp.exp(score - top)
        expo[unit] = weights
        total = jnp.sum(weights, axis=1, keepdims=True)
        part = mm(weights.astype(jnp.bfloat16), values[seq, pl.ds(HALO, tokens), lanes])
        kv_send[unit, pl.ds(0, SEG)] = join_heads(part).astype(jnp.bfloat16)
        kv_send[unit, pl.ds(SEG, 16)] = jnp.concatenate(
            [*thirds(row_of(top)), *thirds(row_of(total)), jnp.zeros((10, PAIR), jnp.bfloat16)],
            axis=0,
        )
        return carry

    lax.fori_loop(0, units, third_scores, 0, unroll=2)
    kv_out = shared_out(place, kv_send, kv_recv, many, *kv_sem)
    for copy in kv_out:
        copy.start()
    save(expo)

    kernels = []
    same = (
        lax.broadcasted_iota(jnp.int32, (PAIR, PAIR), 0) < SEG
    ) == first_head((PAIR, PAIR))
    for own in range(many):
        both = land[first_unit + own]
        score = jnp.where(same, mm(spread_heads(both[0]), spread_heads(both[1]), NT), FAR)
        weights = jnp.exp(score - jnp.max(score, axis=1, keepdims=True))
        kernels.append(weights / jnp.sum(weights, axis=1, keepdims=True))
        kernel_two[own] = kernels[own]
    approx = newton_forward(kernels, keep)
    for own in range(many):
        approx_out[own] = approx[own]
        proxy = jnp.sqrt(
            heads_sum(jnp.sum(kernels[own] * kernels[own], axis=1, keepdims=True))
        ) * jnp.sqrt(heads_sum(jnp.sum(approx[own] * approx[own], axis=1, keepdims=True)))
        proxies[own] = jnp.broadcast_to(row_of(proxy), (8, PAIR))
    save(keep, kernel_two, approx_out, proxies)

    def first_scores(unit, carry):
        seq, rows, lanes = spots(unit)
        score = mm(spread_heads(land[unit, 1]), queries[rows, lanes], NT)
        score = score.reshape(2, SEG, tokens)
        weights = jnp.exp(score - jnp.max(score, axis=1, keepdims=True))
        weights = weights / jnp.sum(weights, axis=1, keepdims=True)
        kernel_one[unit] = weights.reshape(2 * SEG, tokens)
        return carry

    lax.fori_loop(0, units, first_scores, 0, unroll=2)
    save(kernel_one)
    for copy in kv_out:
        copy.wait()
    for own in range(many):
        parts, tops, totals = [], [], []
        for packed in [kv_send[first_unit + own]] + [
            kv_recv[step, own] for step in range(seq_size - 1)
        ]:
            packed = packed.astype(jnp.float32)
            tail = packed[SEG:]
            parts.append(packed[:SEG])
            tops.append(tail[0:1] + tail[1:2] + tail[2:3])
            totals.append(tail[3:4] + tail[4:5] + tail[5:6])
        top = tops[0]
        for other in tops[1:]:
            top = jnp.maximum(top, other)
        scales = [jnp.exp(other - top) for other in tops]
        total = sum(scale * part for scale, part in zip(scales, totals))
        kv_mean = jnp.zeros((SEG, PAIR), jnp.float32)
        for slot, (scale, part) in enumerate(zip(scales, parts)):
            share = scale / total
            shares[own, slot] = jnp.broadcast_to(share, (8, PAIR))
            kv_mean = kv_mean + join_heads(column(share)) * part
        kv_own[own] = kv_mean
        mixed[first_unit + own] = join_heads(
            mm3(split(approx[own]), split(spread_heads(kv_mean)))
        ).astype(jnp.bfloat16)
    mixed_out = passed_on(place, mixed, many, *mixed_sem)
    for copy in mixed_out:
        copy.start()
    save(kv_own, shares)
    for copy in mixed_out:
        copy.wait()
    save(mixed)

    def combine(unit, carry):
        seq, rows, lanes = spots(unit)
        attended = mm(
            kernel_one[unit].astype(jnp.bfloat16), spread_heads(mixed[unit]), TN
        )
        branch[rows, lanes] = (attended + conv[rows, lanes]).astype(jnp.bfloat16)
        return carry

    lax.fori_loop(0, units, combine, 0, unroll=2)
    save(branch)
    for copy in saves:
        copy.wait()


def attend(
    x, bounds, weight, query_bias, value_bias, taps, batch_size, seq_size, seqs
):
    rows, width = x.shape
    tokens = rows // seqs
    units = seqs * (width // PAIR)
    many = -(-units // seq_size)
    slots = seq_size * many
    f32, bf16 = jnp.float32, jnp.bfloat16
    vmem = pl.BlockSpec(memory_space=pltpu.VMEM)
    anywhere = pl.BlockSpec(memory_space=pl.ANY)
    sems = pltpu.SemaphoreType.DMA
    shapes = (
        ((rows, width), bf16),
        ((rows, width), bf16),
        ((seqs, tokens + BLOCK, width), bf16),
        ((units, 2 * SEG, tokens), f32),
        ((units, 2 * SEG, tokens), f32),
        ((slots, 2, SEG, PAIR), bf16),
        ((slots, SEG, PAIR), bf16),
        ((rows, width), bf16),
        ((many, PAIR, PAIR), f32),
        ((many, PAIR, PAIR), f32),
        ((many, 6, 4, PAIR, PAIR), f32),
        ((many, SEG, PAIR), f32),
        ((many, seq_size, 8, PAIR), f32),
        ((many, 8, PAIR), f32),
    )
    return pl.pallas_call(
        partial(attend_kernel, batch_size, seq_size, seqs, tokens, many),
        out_shape=tuple(jax.ShapeDtypeStruct(*shape) for shape in shapes),
        in_specs=[anywhere] * 2 + [vmem] * 4,
        out_specs=tuple([anywhere] * len(shapes)),
        scratch_shapes=[
            *(pltpu.VMEM(*shape) for shape in shapes),
            pltpu.VMEM(x.shape, bf16),
            pltpu.VMEM(weight.shape, bf16),
            sems((4,)),
            sems((len(shapes),)),
            pltpu.VMEM((slots, 2, SEG, PAIR), f32),
            pltpu.VMEM((seq_size - 1, many, 2, SEG, PAIR), f32),
            pltpu.VMEM((slots, SEG + 16, PAIR), bf16),
            pltpu.VMEM((seq_size - 1, many, SEG + 16, PAIR), bf16),
            pltpu.VMEM((rows, width), f32),
            pltpu.VMEM((16, 2 * BLOCK), f32),
            pltpu.VMEM((8, width), f32),
            (sems((seq_size - 1,)),) * 2,
            (sems((seq_size - 1,)),) * 2,
            (sems((seq_size - 1,)),) * 2,
            (sems((seq_size - 1,)),) * 2,
            (sems((2,)),) * 2,
        ],
        compiler_params=pltpu.CompilerParams(
            collective_id=1, has_side_effects=True, vmem_limit_bytes=58 * 2**20
        ),
        name="attend",
    )(x, weight, bounds, query_bias, value_bias, taps)


def newton_backward(kernels, approx_grads, keep, tick):
    units = range(len(kernels))
    eye = jnp.where(eye_mask(PAIR), 1.0, 0.0)
    kernel_halves = [split(kernel) for kernel in kernels]
    grads = [jnp.zeros((PAIR, PAIR), jnp.float32) for _ in units]
    after = approx_grads
    for step in reversed(range(6)):
        approx = [split(keep[u, step, 0]) for u in units]
        product = [keep[u, step, 1] for u in units]
        halves = [split(p) for p in product]
        first = [split(7.0 * eye - p) for p in product]
        second = [split(keep[u, step, 2]) for u in units]
        third = [split(keep[u, step, 3]) for u in units]
        wide = [split(0.25 * a) for a in after]
        third_grad = [split(mm3(wide[u], approx[u])) for u in units]
        second_grad = [split(-mm3(third_grad[u], halves[u])) for u in units]
        first_grad = [-mm3(second_grad[u], halves[u]) for u in units]
        product_grad = [
            split(
                -mm3(second[u], third_grad[u]) - mm3(first[u], second_grad[u]) - first_grad[u]
            )
            for u in units
        ]
        grads = [grads[u] + mm3(approx[u], product_grad[u]) for u in units]
        after = [
            mm3(third[u], wide[u]) + mm3(product_grad[u], kernel_halves[u]) for u in units
        ]
        tick(f"newton{step}")
    out = []
    for u in units:
        kernel = kernels[u]
        fro = heads_sum(jnp.sum(kernel * kernel, axis=1, keepdims=True))
        fro_grad = heads_sum(jnp.sum(after[u] * kernel, axis=1, keepdims=True)) / (fro * fro)
        out.append(grads[u].T + after[u] / fro - 2.0 * kernel * fro_grad)
    return out


def tap_grads(padded_grad, padded, vec, first_row, tokens, span):
    seqs, _, width = padded.shape
    rows = lax.broadcasted_iota(jnp.int32, (BLOCK, BLOCK), 0)
    cols = lax.broadcasted_iota(jnp.int32, (BLOCK, BLOCK), 1)
    turn = jnp.where(rows + cols == BLOCK - 1, 1.0, 0.0).astype(jnp.bfloat16)

    def step(pair, carry):
        lanes = pl.ds(pl.multiple_of(pair * PAIR, PAIR), PAIR)
        total = [jnp.zeros((BLOCK, 2 * BLOCK), jnp.float32) for _ in range(2)]
        for seq in range(seqs):
            for block in range(tokens // BLOCK):
                window = padded[seq, pl.ds(block * BLOCK, 2 * BLOCK), lanes]
                grad = padded_grad[seq, pl.ds(HALO + block * BLOCK, BLOCK), lanes]
                grad = mm(turn, grad).astype(jnp.bfloat16)
                first = first_head(grad.shape)
                zero = jnp.zeros_like(grad)
                total[0] = total[0] + mm(jnp.where(first, grad, zero), window, NT)
                total[1] = total[1] + mm(jnp.where(first, zero, grad), window, NT)
        for head in range(2):
            turned = pltpu.roll(total[head], 0, 1, stride=1, stride_axis=0)
            sums = jnp.sum(turned, axis=0, keepdims=True)
            sums = pltpu.roll(sums, BLOCK + 1, 1)
            vec[pl.ds(first_row + 2 * pair + head, 1), :] = sums[:, :PAIR]
        return carry

    lax.fori_loop(*span, step, 0)


class Ticker:
    def __init__(self, points):
        self.live = {}
        self.points = points

    def add(self, number, generator):
        next(generator)
        self.live[number] = generator

    def step(self, number):
        try:
            next(self.live[number])
        except StopIteration:
            del self.live[number]

    def tick(self, point):
        for number in self.points.get(point, ()):
            if number in self.live:
                self.step(number)

    def drain(self, order=()):
        for number in order:
            if number in self.live:
                self.step(number)
        while self.live:
            for number in list(self.live):
                self.step(number)


POINTS = {
    "back1": (0, 1),
    "mid0": (1, 2, 3),
    "out": (0,),
    "first0": (1,),
    "conv0": (2, 3),
    "third0": (1,),
    "value": (2,),
    "newton5": (3, 0),
    "newton3": (4,),
    "newton1": (0,),
    "land": (0,),
    "wait_back": (1, 0, 2, 3, 4, 0, 1),
    "last": (4,),
    "taps0": (5, 1),
    "taps2": (1, 2),
    "input0": (3,),
    "input1": (1,),
}
LAST = (5, 4, 2, 3, "vec", 0, 5, 4, 5, "vec", 2, 3, 4, 0, 2, "vec", 3, 5, 0, 2, "vec", 3, 0, 4, 5, 4, 4, 5, 5, 5)


class Sums:
    def __init__(self, ref):
        self.ref = ref

    def clear(self):
        self.ref[...] = jnp.zeros_like(self.ref)

    def add(self, row, array):
        here = pl.ds(row, 1)
        self.ref[here, :] = self.ref[here, :] + jnp.sum(array, axis=0, keepdims=True)


def normalize(hidden):
    centered = hidden - jnp.mean(hidden, axis=1, keepdims=True)
    inverse = lax.rsqrt(jnp.mean(centered * centered, axis=1, keepdims=True) + epsilon)
    return centered * inverse, inverse


def normalize_back(grad, normed, inverse):
    return inverse * (
        grad
        - jnp.mean(grad, axis=1, keepdims=True)
        - normed * jnp.mean(grad * normed, axis=1, keepdims=True)
    )


def row_vector(ref):
    return ref[...].reshape(1, ref.shape[0])


def back_kernel(
    batch_size, seq_size, seqs, tokens, many, plan,
    x_in, grad_out, branch_in, out_weight, up_weight, down_weight, qkv_weight,
    queries_in, keys_in, values_in, kernel_one_in, expo_in, keep_in, land_in, mixed_in,
    kernel_two_in, approx_in, kv_own_in, shares_in, proxies_in, bounds, taps,
    out_bias, first_gain, first_shift, up_bias, down_bias, second_gain, second_shift,
    layer_out, input_grad, gathered, vec,
    stage, whole, recv, slots, padded, grad_first, tap_rows, sums, up_sums, acc_send, acc_all,
    land_send, land_recv, land_all, kernel_one, mixed, land,
    load_sem, weight_sem, send_sem, recv_sem, free_sem, vec_sem, out_sem, halo_sem, mixed_sem,
    acc_sem, land_sem, land_back_sem,
):
    place = Place(batch_size, seq_size)
    rows, width = x_in.shape
    ff_blocks = down_weight.shape[0] // width
    pairs = width // PAIR
    units = seqs * pairs
    quarter = float(SEG) ** -0.25
    wait_greet = greet(
        [place.seq_peer(step) for step in range(1, seq_size)] + list(place.peers(("core", "z")))
    )

    def early_loads():
        return [
            pltpu.make_async_copy(source, target, load_sem.at[11 + index])
            for index, (source, target) in enumerate(
                ((kernel_one_in, kernel_one), (mixed_in, mixed), (land_in, land))
            )
        ]

    ticker = Ticker(POINTS)
    tick = ticker.tick
    bf16 = jnp.bfloat16

    def piece_run(number):
        piece = plan[number]
        here = pl.ds(piece.start, piece.rows)
        yield from Reduce(
            number, lambda: Place(batch_size, seq_size), piece.orders, stage.at[:, here],
            whole.at[here], recv.at[:, piece.slots], send_sem, recv_sem, free_sem, piece.rows,
        ).run()

        def outs():
            core = Place(batch_size, seq_size).at["core"]
            return (
                pltpu.make_async_copy(
                    whole.at[here], gathered.at[core, here], out_sem.at[number, 0]
                ),
                pltpu.make_async_copy(
                    stage.at[1 - core, here], gathered.at[1 - core, here], out_sem.at[number, 1]
                ),
            )

        for out in outs():
            out.start()
        yield
        for out in outs():
            out.wait()

    done = set()

    def staged(*blocks):
        done.update(blocks)
        for number, piece in enumerate(plan):
            if done.issuperset(piece.blocks) and not set(blocks).isdisjoint(piece.blocks):
                ticker.add(number, piece_run(number))

    def store_block(block, first, grad):
        at = pl.ds(pl.multiple_of(block * width + first, 16), grad.shape[0])
        grad = grad.astype(bf16)
        stage[0, at, :] = grad[:, :HALF]
        stage[1, at, :] = grad[:, HALF:]

    def store_strip(block, part, grad):
        at = pl.ds(block * width, width)
        grad = grad.astype(bf16)
        first = part * 256
        for half in range(2):
            low, high = max(first, half * HALF), min(first + 256, (half + 1) * HALF)
            if low < high:
                lanes = pl.ds(low - half * HALF, high - low)
                stage[half, at, lanes] = grad[:, low - first : high - first]

    def loop(count, step):
        def run(index, carry):
            step(index)
            return carry

        lax.fori_loop(0, count, run, 0)

    def feed_forward(
        x, branch, grads, mid_low, turned, act_turned, low, normed_one, grad_second, inverse_one, out_w, ff_w,
        act, slope, up_bias_row,
    ):
        def load(index, source, target):
            return pltpu.make_async_copy(source, target, load_sem.at[index])

        first = [load(0, out_weight, out_w), load(1, branch_in, branch), load(2, x_in, x)]
        for copy in first:
            copy.start()
        grads_load = load(3, grad_out, grads)

        def up_load(block):
            return pltpu.make_async_copy(
                up_weight.at[:, pl.ds(block * width, width)], ff_w.at[block], weight_sem.at[block]
            )

        def down_load(block):
            return pltpu.make_async_copy(
                down_weight.at[pl.ds(block * width, width)], ff_w.at[block], weight_sem.at[block]
            )

        for block in range(ff_blocks):
            up_load(block).start()
        grads_load.start()
        for copy in early_loads():
            copy.start()
        total = Sums(sums)
        total.clear()
        up_bias_row[...] = row_vector(up_bias)
        for copy in first:
            copy.wait()
        tile = 128

        def strip(index):
            return pl.ds(pl.multiple_of(index * 256, 256), 256)

        def attended(index):
            normed_one[:, strip(index)] = mm(branch[...], out_w[:, strip(index)])

        def project(index):
            here = pl.ds(pl.multiple_of(index * tile, tile), tile)
            hidden = x[here, :].astype(jnp.float32) + normed_one[here, :]
            normed, inverse = normalize(hidden + row_vector(out_bias))
            normed_one[here, :] = normed
            inverse_one[here, :] = jnp.broadcast_to(inverse, (tile, PAIR))
            mid = normed * row_vector(first_gain) + row_vector(first_shift)
            mid_low[here, :] = mid.astype(bf16)

        loop(width // 256, attended)
        loop(rows // tile, project)
        for block in range(ff_blocks):
            up_load(block).wait()

            def up(index, block=block):
                part = pl.multiple_of(index * 256, 256)
                lanes = pl.ds(block * width + part, 256)
                pre = mm(mid_low[...], ff_w[block, :, pl.ds(part, 256)])
                pre = pre + up_bias_row[:, lanes]
                half = 0.5 * (1.0 + lax.erf(pre * (0.5**0.5)))
                act[:, lanes] = (pre * half).astype(bf16)
                bell = jnp.exp(-0.5 * pre * pre) * (2.0 * math.pi) ** -0.5
                slope[:, lanes] = (half + pre * bell).astype(bf16)

            loop(width // 256, up)
            down_load(block).start()
        turned[...] = mid_low[...].T
        for block in range(ff_blocks):
            down_load(block).wait()
        grads_load.wait()

        def summed(index):
            total = mm(act[:, pl.ds(0, width)], ff_w[0, :, strip(index)])
            for block in range(1, ff_blocks):
                total = total + mm(
                    act[:, pl.ds(block * width, width)], ff_w[block, :, strip(index)]
                )
            grad_second[:, strip(index)] = total

        def down(index):
            here = pl.ds(pl.multiple_of(index * tile, tile), tile)
            mid = normed_one[here, :] * row_vector(first_gain) + row_vector(first_shift)
            normed, inverse = normalize(mid + row_vector(down_bias) + grad_second[here, :])
            grad = grads[here, :].astype(jnp.float32)
            total.add(1, grad * normed)
            total.add(2, grad)
            grads[here, :] = (
                normed * row_vector(second_gain) + row_vector(second_shift)
            ).astype(bf16)
            grad = normalize_back(grad * row_vector(second_gain), normed, inverse)
            grad_second[here, :] = grad
            grad = grad.astype(bf16)
            low[here, :] = grad
            total.add(0, grad.astype(jnp.float32))

        loop(width // 256, summed)
        loop(rows // tile, down)
        out_copy = load(4, grads, layer_out)
        out_copy.start()
        for block in range(ff_blocks):

            act_turned[...] = act[:, pl.ds(block * width, width)].T
            for part in range(width // 256):
                store_strip(block, part, mm(act_turned[...], low[:, pl.ds(part * 256, 256)]))
            if block == 0:
                wait_greet()
            staged(block)
            tick(f"down{block}")
        for block in range(ff_blocks):

            def up_back(index, block=block):
                at = pl.multiple_of(index * 256, 256)
                lanes = pl.ds(block * width + at, 256)
                grad = mm(low[...], ff_w[block, pl.ds(at, 256), :], NT)
                grad = (grad * slope[:, lanes].astype(jnp.float32)).astype(bf16)
                slope[:, lanes] = grad
                up_sums[:, lanes] = jnp.sum(grad.astype(jnp.float32), axis=0, keepdims=True)

            loop(width // 256, up_back)
            up_load(block).start()
            tick(f"back{block}")
        for block in range(ff_blocks):

            for part in range(width // 256):
                lanes = pl.ds(block * width + part * 256, 256)
                store_strip(ff_blocks + block, part, mm(turned[...], slope[:, lanes]))
            staged(ff_blocks + block)
            tick(f"up{block}")
        for block in range(ff_blocks):
            up_load(block).wait()

        def mid_sum(index):
            total = grad_second[:, strip(index)]
            for block in range(ff_blocks):
                total = total + mm(
                    slope[:, pl.ds(block * width, width)], ff_w[block, strip(index), :], NT
                )
            grad_second[:, strip(index)] = total

        def mid_back(index):
            here = pl.ds(pl.multiple_of(index * tile, tile), tile)
            grad = grad_second[here, :]
            normed = normed_one[here, :]
            total.add(4, grad * normed)
            total.add(5, grad)
            grad = normalize_back(
                grad * row_vector(first_gain), normed, inverse_one[here, pl.ds(0, 1)]
            )
            grad_first[here, :] = grad
            grad = grad.astype(bf16)
            low[here, :] = grad
            total.add(3, grad.astype(jnp.float32))

        loop(width // 256, mid_sum)
        tick("mid0")
        loop(rows // tile, mid_back)
        tick("mid1")
        for seq in range(seqs):
            padded[seq, pl.ds(HALO, tokens)] = mm(
                low[pl.ds(seq * tokens, tokens), :], out_w[...], NT
            ).astype(bf16)

        def out_grad(index):
            at = pl.multiple_of(index * 256, 256)
            store_block(2 * ff_blocks, at, mm(branch[:, pl.ds(at, 256)], low[...], TN))

        loop(width // 256, out_grad)
        staged(2 * ff_blocks)
        tick("out")
        out_copy.wait()

    narrow = pltpu.VMEM((rows, width), bf16)
    wide = pltpu.VMEM((rows, width), jnp.float32)
    hidden = pltpu.VMEM((rows, ff_blocks * width), bf16)
    pl.run_scoped(
        feed_forward,
        narrow, narrow, narrow, narrow,
        pltpu.VMEM((width, rows), bf16),
        pltpu.VMEM((width, rows), bf16),
        narrow, wide, wide,
        pltpu.VMEM((rows, PAIR), jnp.float32),
        pltpu.VMEM((width, width), bf16),
        pltpu.VMEM((ff_blocks, width, width), bf16),
        hidden, hidden,
        pltpu.VMEM((1, ff_blocks * width), jnp.float32),
    )
    first_row = (ff_blocks + 6) * pairs
    tap_row = first_row + 2 * pairs
    proxy_row = tap_row + 2 * pairs

    def attention(
        x, queries, keys, values, expo, keep, kernel_two, approx, kv_own, shares, proxies, rest, grad_qkv, turned, rows_of_weight,
    ):
        place = Place(batch_size, seq_size)
        loads = {}
        for index, (name, source, target) in enumerate(
            (
                ("queries", queries_in, queries),
                ("approx", approx_in, approx),
                ("kv_own", kv_own_in, kv_own),
                ("kernel_two", kernel_two_in, kernel_two),
                ("shares", shares_in, shares),
                ("values", values_in, values),
                ("expo", expo_in, expo),
                ("keys", keys_in, keys),
                ("keep", keep_in, keep),
                ("x", x_in, x),
                ("proxies", proxies_in, proxies),
            )
        ):
            loads[name] = pltpu.make_async_copy(source, target, load_sem.at[index])
            loads[name].start()
        zero_past(padded, tokens)
        halo = halo_copies(place, padded, tokens, *halo_sem)
        for copy in halo:
            copy.start()

        def spots(unit):
            seq, pair = lax.div(unit, pairs), lax.rem(unit, pairs)
            span = pl.ds(pl.multiple_of(seq * tokens, tokens), tokens)
            lanes = pl.ds(pl.multiple_of(pair * PAIR, PAIR), PAIR)
            return seq, span, lanes

        def paced(step, name, chunks=1):
            size = -(-units // chunks)
            for chunk, first in enumerate(range(0, units, size)):
                lax.fori_loop(first, min(first + size, units), step, 0, unroll=2)
                tick(f"{name}{chunk}")

        def mixed_parts(unit, carry):
            seq, span, lanes = spots(unit)
            grad = padded[seq, pl.ds(HALO, tokens), lanes]
            land_send[unit, 0] = join_heads(mm(kernel_one[unit].astype(bf16), grad)).astype(bf16)
            return carry

        for copy in early_loads():
            copy.wait()
        lax.fori_loop(0, units, mixed_parts, 0, unroll=2)
        for unit in range(units, seq_size * many):
            land_send[unit] = jnp.ones_like(land_send[unit])
        mixed_out = shared_out(
            place, land_send.at[:, 0], land_recv.at[:, :, 0], many, *mixed_sem
        )
        for copy in mixed_out:
            copy.start()
        tick("start")

        def first_grads(unit, carry):
            seq, span, lanes = spots(unit)
            weights = kernel_one[unit]
            grad = mm(spread_heads(mixed[unit]), padded[seq, pl.ds(HALO, tokens), lanes], NT)
            both = (weights * grad).reshape(2, SEG, tokens)
            both = jnp.broadcast_to(jnp.sum(both, axis=1, keepdims=True), both.shape)
            score_grad = (weights * (grad - both.reshape(2 * SEG, tokens))).astype(bf16)
            land_send[unit, 1] = join_heads(mm(score_grad, queries[span, lanes])).astype(bf16)
            rest[0, span, lanes] = mm(score_grad, spread_heads(land[unit, 1]), TN)
            return carry

        loads["queries"].wait()
        paced(first_grads, "first", 3)
        tick("wait_mixed")
        for copy in mixed_out:
            copy.wait()
        first_unit = place.seq * many
        for name in ("approx", "kv_own", "kernel_two", "shares"):
            loads[name].wait()
        kernels, approx_grads = [], []
        for own in range(many):
            total = land_send[first_unit + own, 0].astype(jnp.float32)
            for step in range(seq_size - 1):
                total = total + land_recv[step, own, 0].astype(jnp.float32)
            total = split(spread_heads(total))
            kv_mean = kv_own[own]
            kv_grad = join_heads(mm3(split(approx[own]), total, TN))
            approx_grads.append(mm3(split(spread_heads(kv_mean)), total, NT))
            kernels.append(kernel_two[own])
            dots = kv_grad * kv_mean
            first = first_head(dots.shape)
            dots = jnp.concatenate(
                [
                    jnp.sum(jnp.where(first, dots, 0.0), axis=1, keepdims=True),
                    jnp.sum(jnp.where(first, 0.0, dots), axis=1, keepdims=True),
                ],
                axis=0,
            )
            dots = row_of(dots)
            for slot in range(seq_size):
                share = shares[own, slot, pl.ds(0, 1), :]
                scaled = (kv_grad * join_heads(column(share))).astype(bf16)
                high, low = split(-dots * share)
                tail = jnp.concatenate([high, low, jnp.zeros((14, PAIR), bf16)], axis=0)
                acc_send[slot, own] = jnp.concatenate([scaled, tail], axis=0)
        acc_out = []
        for step in range(1, seq_size):
            acc_out.append(
                pltpu.make_async_remote_copy(
                    src_ref=acc_send.at[seq_size - step],
                    dst_ref=acc_all.at[pl.ds(first_unit, many)],
                    send_sem=acc_sem[0].at[step - 1],
                    recv_sem=acc_sem[1].at[step - 1],
                    device_id=place.seq_peer(step),
                    device_id_type=MESH_IDS,
                )
            )
        for copy in acc_out:
            copy.start()
        for own in range(many):
            acc_all[first_unit + own] = acc_send[0, own]
        tick("acc")
        for copy in halo:
            copy.wait()
        trim_halo(place, padded, tokens)
        tap_rows[...] = turned_taps(taps)
        for part in range(2):
            span = (part * pairs // 2, (part + 1) * pairs // 2)
            conv_rows(padded, tap_rows, rest.at[2], tokens, span)
            tick(f"conv{part}")
        loads["values"].wait()
        loads["expo"].wait()
        loads["keys"].wait()
        tick("wait_acc")
        for copy in acc_out:
            copy.wait()

        def third_grads(unit, carry):
            seq, span, lanes = spots(unit)
            packed = acc_all[unit]
            acc = spread_heads(packed[:SEG])
            tail = packed[SEG:].astype(jnp.float32)
            part = mm(acc, values[seq, pl.ds(HALO, tokens), lanes], NT)
            weights = expo[unit]
            score_grad = (weights * (part + column(tail[0:1] + tail[1:2]))).astype(bf16)
            land_send[unit, 0] = join_heads(mm(score_grad, keys[span, lanes])).astype(bf16)
            rest[1, span, lanes] = mm(score_grad, spread_heads(land[unit, 0]), TN)
            value_grad = mm(weights.astype(bf16), acc, TN) + rest[2, span, lanes]
            valid = positions(place, tokens, 0) < length_of(bounds, seq)
            grad_qkv[2, span, lanes] = jnp.where(valid, value_grad, 0.0).astype(bf16)
            return carry

        paced(third_grads, "third", 3)
        land_out = shared_out(place, land_send, land_recv, many, *land_sem)
        for copy in land_out:
            copy.start()
        loads["x"].wait()
        turned[...] = x[...].T

        def weight_grad(third, block):
            def step(index):
                at = pl.multiple_of(index * 256, 256)
                store_block(block, at, mm(turned[pl.ds(at, 256), :], grad_qkv[third]))

            loop(width // 256, step)

        def bias_grad(third, row):
            for pair in range(pairs):
                cols = grad_qkv[third, :, pl.ds(pair * PAIR, PAIR)].astype(jnp.float32)
                vec[pl.ds(row + pair, 1), :] = jnp.sum(cols, axis=0, keepdims=True)

        weight_grad(2, 2 * ff_blocks + 1)
        staged(2 * ff_blocks + 1)
        tick("value")
        loads["keep"].wait()
        loads["proxies"].wait()
        kernel_grads = newton_backward(kernels, approx_grads, keep, tick)
        extra = []
        for own in range(many):
            kernel, grad = kernels[own], kernel_grads[own]
            score_grad = split(
                kernel * (grad - jnp.sum(kernel * grad, axis=1, keepdims=True))
            )
            both = land[first_unit + own]
            left, right = spread_heads(both[0]), spread_heads(both[1])
            extra.append(
                (
                    join_heads(mm(score_grad[0], right) + mm(score_grad[1], right)),
                    join_heads(mm(score_grad[0], left, TN) + mm(score_grad[1], left, TN)),
                )
            )
        tick("wait_land")
        for copy in land_out:
            copy.wait()
        for own in range(many):
            unit = first_unit + own
            low, high = segment_edges(bounds, jnp.minimum(lax.div(unit, pairs), seqs - 1))
            for slot in range(2):
                total = land_send[unit, slot].astype(jnp.float32) + extra[own][slot]
                for step in range(seq_size - 1):
                    total = total + land_recv[step, own, slot].astype(jnp.float32)
                land_all[unit, slot] = (total / (high - low)).astype(bf16)
        land_back = passed_on(place, land_all, many, *land_back_sem)
        for copy in land_back:
            copy.start()
        tick("land")
        tick("wait_back")
        for copy in land_back:
            copy.wait()
        for seq in range(seqs):
            member = member_of(place, bounds, seq, tokens)
            span = pl.ds(seq * tokens, tokens)
            for pair in range(pairs):
                lanes = pl.ds(pair * PAIR, PAIR)
                both = land_all[seq * pairs + pair]
                for slot in range(2):
                    grad = (mm(member, both[slot], TN) + rest[slot, span, lanes]) * quarter
                    grad_qkv[slot, span, lanes] = grad.astype(bf16)
        tick("grads")
        weight_grad(0, 2 * ff_blocks + 2)
        weight_grad(1, 2 * ff_blocks + 3)
        staged(2 * ff_blocks + 2, 2 * ff_blocks + 3)
        tick("last")
        vec[...] = jnp.zeros_like(vec)
        for part in range(ff_blocks * pairs):
            vec[pl.ds(part, 1), :] = up_sums[:, pl.ds(part * PAIR, PAIR)]
        for row in range(6):
            for part in range(pairs):
                vec[pl.ds((ff_blocks + row) * pairs + part, 1), :] = sums[
                    pl.ds(row, 1), pl.ds(part * PAIR, PAIR)
                ]
        for own in range(many):
            unit = first_unit + own
            row = pl.ds(proxy_row + lax.rem(unit, pairs), 1)
            vec[row, :] = vec[row, :] + jnp.where(
                unit < units, proxies[own, pl.ds(0, 1), :], 0.0
            )
        bias_grad(0, first_row)
        bias_grad(2, first_row + pairs)
        for part in range(3):
            span = (part * pairs // 3, (part + 1) * pairs // 3)
            tap_grads(padded, values, vec, tap_row, tokens, span)
            tick(f"taps{part}")
        ticker.add("vec", vec_reduce(place, vec, slots, *vec_sem))

        def weight_load(tile):
            return pltpu.make_async_copy(
                qkv_weight.at[pl.ds(tile * PAIR, PAIR)],
                rows_of_weight.at[tile % 2],
                weight_sem.at[tile % 2],
            )

        weight_load(0).start()
        for tile in range(pairs):
            if tile + 1 < pairs:
                weight_load(tile + 1).start()
            weight_load(tile).wait()
            lanes = pl.ds(tile * PAIR, PAIR)
            total = grad_first[:, lanes]
            for third in range(3):
                total = total + mm(
                    grad_qkv[third], rows_of_weight[tile % 2, :, pl.ds(third * width, width)], NT
                )
            x[:, lanes] = total.astype(bf16)
            tick(f"input{tile}")
        out_copy = pltpu.make_async_copy(x, input_grad, load_sem.at[0])
        out_copy.start()
        ticker.drain(LAST)
        out_copy.wait()

    pl.run_scoped(
        attention,
        narrow, narrow, narrow,
        pltpu.VMEM(values_in.shape, bf16),
        pltpu.VMEM(expo_in.shape, jnp.float32),
        pltpu.VMEM(keep_in.shape, jnp.float32),
        *(
            pltpu.VMEM(ref.shape, jnp.float32)
            for ref in (kernel_two_in, approx_in, kv_own_in, shares_in, proxies_in)
        ),
        pltpu.VMEM((2 + 1, rows, width), jnp.float32),
        pltpu.VMEM((3, rows, width), bf16),
        pltpu.VMEM((width, rows), bf16),
        pltpu.VMEM((2, PAIR, 3 * width), bf16),
    )


Z_FIRST = (0,)


class Piece:
    def __init__(self, blocks, start, rows, orders, slots):
        self.blocks, self.start, self.rows, self.orders, self.slots = (
            blocks, start, rows, orders, slots,
        )


def make_plan(sizes, block_count, width):
    split_rows = 16 * sizes["x"] * sizes["y"] * sizes["z"]
    orders = (("x", "y", "z"), ("y", "x", "z"))
    z_first = (("z0", "z1", "x", "y"), ("z0", "z1", "y", "x"))
    if 2 * width % (2 * split_rows) == 0:
        counts = [2] * (block_count // 2)
    else:
        orders = orders[:1]
        z_first = z_first[:1]
        counts = [8, block_count - 8] if 8 * width % split_rows == 0 else [block_count]
    plan, block, slot = [], 0, 0
    for count in counts:
        rows = -(-count * width // (len(orders) * split_rows)) * len(orders) * split_rows
        own = z_first if len(plan) in Z_FIRST else orders
        need = Reduce.slots(sizes, own, rows)
        plan.append(
            Piece(list(range(block, block + count)), block * width, rows, own, pl.ds(slot, need))
        )
        block += count
        slot += need
    return plan, slot


def layer_back(
    x, grad_out, branch, out_weight, up_weight, down_weight, qkv_weight, saved, bounds, taps,
    vectors, batch_size, seq_size, seqs,
):
    (
        queries, keys, values, kernel_one, expo, land, mixed, _, kernel_two, approx, keep,
        kv_own, shares, proxies,
    ) = saved
    rows, width = x.shape
    tokens = rows // seqs
    pairs = width // PAIR
    own = -(-seqs * pairs // seq_size)
    owned = seq_size * own
    sizes = axis_sizes(batch_size, seq_size)
    ff_blocks = down_weight.shape[0] // width
    plan, slot_rows = make_plan(sizes, 2 * ff_blocks + 4, width)
    pieces, stage_rows = len(plan), plan[-1].start + plan[-1].rows
    parts = len(plan[0].orders)
    copies = max(Reduce.copies(sizes, piece.orders) for piece in plan)
    vec_axes = ("core", "x", "y", "z")
    vec_steps = sum(sizes[axis] - 1 for axis in vec_axes)
    vec_shape = (-(-((ff_blocks + 11) * pairs) // 8) * 8, PAIR)
    f32, bf16 = jnp.float32, jnp.bfloat16
    vmem = pl.BlockSpec(memory_space=pltpu.VMEM)
    anywhere = pl.BlockSpec(memory_space=pl.ANY)
    sems = pltpu.SemaphoreType.DMA
    pair_sems = (sems((seq_size - 1,)),) * 2
    return pl.pallas_call(
        partial(back_kernel, batch_size, seq_size, seqs, tokens, own, plan),
        out_shape=(
            jax.ShapeDtypeStruct((rows, width), bf16),
            jax.ShapeDtypeStruct((rows, width), bf16),
            jax.ShapeDtypeStruct((2, stage_rows, HALF), bf16),
            jax.ShapeDtypeStruct(vec_shape, f32),
        ),
        in_specs=[anywhere] * 20 + [vmem] * (2 + len(vectors)),
        out_specs=(anywhere, anywhere, anywhere, vmem),
        scratch_shapes=[
            pltpu.VMEM((2, stage_rows, HALF), bf16),
            pltpu.VMEM((stage_rows, HALF), bf16),
            pltpu.VMEM((parts, slot_rows, HALF), bf16),
            pltpu.VMEM((sum(sizes[axis] for axis in vec_axes), *vec_shape), f32),
            pltpu.VMEM(values.shape, bf16),
            pltpu.VMEM((rows, width), f32),
            pltpu.VMEM((16, 2 * BLOCK), f32),
            pltpu.VMEM((8, width), f32),
            pltpu.VMEM((1, ff_blocks * width), f32),
            pltpu.VMEM((seq_size, own, SEG + 16, PAIR), bf16),
            pltpu.VMEM((owned, SEG + 16, PAIR), bf16),
            pltpu.VMEM((owned, 2, SEG, PAIR), bf16),
            pltpu.VMEM((seq_size - 1, own, 2, SEG, PAIR), bf16),
            pltpu.VMEM((owned, 2, SEG, PAIR), bf16),
            pltpu.VMEM(kernel_one.shape, f32),
            pltpu.VMEM(mixed.shape, bf16),
            pltpu.VMEM(land.shape, bf16),
            sems((14,)),
            sems((ff_blocks,)),
            sems((pieces, copies)),
            sems((pieces, copies)),
            pltpu.SemaphoreType.REGULAR((pieces,)),
            (sems((vec_steps,)),) * 2,
            sems((pieces, 2)),
            (sems((2,)),) * 2,
            pair_sems,
            pair_sems,
            pair_sems,
            pair_sems,
        ],
        compiler_params=pltpu.CompilerParams(
            collective_id=0, has_side_effects=True, vmem_limit_bytes=63 * 2**20
        ),
        name="layer_back",
    )(
        x, grad_out, branch, out_weight, up_weight, down_weight, qkv_weight,
        queries, keys, values, kernel_one, expo, keep, land, mixed, kernel_two, approx, kv_own,
        shares, proxies, bounds, taps, *vectors,
    )


def finish_kernel(
    heads, scale, gathered, vec, layer_in, input_in,
    layer_out, input_grad, qkv_grad, query_bias_grad, value_bias_grad, tap_grad, out_grad,
    out_bias_grad, first_gain_grad, first_shift_grad, up_grad, up_bias_grad, down_grad,
    down_bias_grad, second_gain_grad, second_shift_grad, condition,
    narrow, wide, rows_through, in_sem, out_sem, pass_sem,
):
    width = down_grad.shape[1]
    pairs = width // PAIR
    blocks = down_grad.shape[0] // width
    spots = [(down_grad, block * width, 0) for block in range(blocks)]
    spots += [(up_grad, 0, block * width) for block in range(blocks)]
    spots += [(out_grad, 0, 0), (qkv_grad, 0, 2 * width), (qkv_grad, 0, 0), (qkv_grad, 0, width)]
    taken = [
        pltpu.make_async_copy(source, rows_through.at[index], pass_sem.at[index])
        for index, source in enumerate((layer_in, input_in))
    ]
    passed = [
        pltpu.make_async_copy(rows_through.at[index], target, pass_sem.at[index])
        for index, target in enumerate((layer_out, input_grad))
    ]
    slots, rows, _ = wide.shape
    tiles = [
        (target, row + part * rows, col, block * width + part * rows)
        for block, (target, row, col) in enumerate(spots)
        for part in range(width // rows)
    ]

    def fetch(index):
        return pltpu.make_async_copy(
            gathered.at[:, pl.ds(tiles[index][3], rows)],
            narrow.at[index % slots],
            in_sem.at[index % slots],
        )

    def put(index):
        target, row, col, _ = tiles[index]
        return pltpu.make_async_copy(
            wide.at[index % slots],
            target.at[pl.ds(row, rows), pl.ds(col, width)],
            out_sem.at[index % slots],
        )

    for index in range(slots):
        fetch(index).start()
    for copy in taken:
        copy.start()
    row = 0
    for target in (
        up_bias_grad, down_bias_grad, second_gain_grad, second_shift_grad, out_bias_grad,
        first_gain_grad, first_shift_grad, query_bias_grad, value_bias_grad,
    ):
        count = target.shape[0] // PAIR
        target[...] = vec[pl.ds(row, count), :].reshape(target.shape)
        row += count
    tap_grad[...] = vec[pl.ds(row, heads), pl.ds(0, tap_grad.shape[1])]
    proxy = vec[pl.ds(row + heads, pairs), :] * scale
    lanes = lax.broadcasted_iota(jnp.int32, (1, PAIR), 1)
    means = jnp.zeros((1, PAIR), jnp.float32)
    for pair in range(pairs):
        for head in range(2):
            value = proxy[pair : pair + 1, head * SEG : head * SEG + 1]
            means = means + jnp.where(lanes == 2 * pair + head, value, 0.0)
    condition[...] = means[:, :heads].reshape(heads)
    for copy in taken:
        copy.wait()
    for copy in passed:
        copy.start()
    for index in range(len(tiles)):
        slot = index % slots
        fetch(index).wait()
        if index >= slots:
            put(index - slots).wait()
        for half in range(2):
            wide[slot, :, pl.ds(half * HALF, HALF)] = narrow[slot, half].astype(jnp.float32)
        put(index).start()
        if index + slots < len(tiles):
            fetch(index + slots).start()
    for index in range(len(tiles) - slots, len(tiles)):
        put(index).wait()
    for copy in passed:
        copy.wait()


def finish(gathered, vec, layer_out, input_grad, shapes, scale):
    width = layer_out.shape[1]
    any_spec = pl.BlockSpec(memory_space=pl.ANY)
    vmem = pl.BlockSpec(memory_space=pltpu.VMEM)
    outs = [jax.ShapeDtypeStruct(shape, jnp.bfloat16) for shape in (layer_out.shape,) * 2]
    outs += [jax.ShapeDtypeStruct(shape, jnp.float32) for shape in shapes]
    return pl.pallas_call(
        partial(finish_kernel, shapes[3][0], scale),
        out_shape=tuple(outs),
        in_specs=[any_spec, vmem, any_spec, any_spec],
        out_specs=tuple(
            any_spec if out.shape[0] * math.prod(out.shape[1:]) >= width * width // 2 else vmem
            for out in outs
        ),
        scratch_shapes=[
            pltpu.VMEM((SLOTS, 2, FINISH_ROWS, HALF), jnp.bfloat16),
            pltpu.VMEM((SLOTS, FINISH_ROWS, width), jnp.float32),
            pltpu.VMEM((2, *layer_out.shape), jnp.bfloat16),
            pltpu.SemaphoreType.DMA((SLOTS,)),
            pltpu.SemaphoreType.DMA((SLOTS,)),
            pltpu.SemaphoreType.DMA((2,)),
        ],
        compiler_params=pltpu.CompilerParams(vmem_limit_bytes=62 * 2**20),
        name="finish",
    )(gathered, vec, layer_out, input_grad)


SLOTS = 4
FINISH_ROWS = 768


def body(
    hidden_in,
    seg_bounds,
    qkv_weight,
    query_bias,
    value_bias,
    conv_taps,
    out_weight,
    out_bias,
    first_gain,
    first_shift,
    up_weight,
    up_bias,
    down_weight,
    down_bias,
    second_gain,
    second_shift,
    grad_out,
):
    seq_count, tok_count, model_width = hidden_in.shape
    head_count = conv_taps.shape[0]
    row_total = seq_count * tok_count
    batch_size, seq_size = lax.axis_size("batch"), lax.axis_size("seq")
    input_rows = hidden_in.reshape(row_total, model_width)
    saved = attend(
        input_rows, seg_bounds, qkv_weight, query_bias, value_bias, conv_taps,
        batch_size, seq_size, seq_count,
    )
    layer_out, input_grad, gathered, vec = layer_back(
        input_rows,
        grad_out.reshape(row_total, model_width),
        saved[7],
        out_weight,
        up_weight,
        down_weight,
        qkv_weight,
        saved,
        seg_bounds,
        conv_taps,
        (out_bias, first_gain, first_shift, up_bias, down_bias, second_gain, second_shift),
        batch_size,
        seq_size,
        seq_count,
    )

    shapes = (
        qkv_weight.shape,
        query_bias.shape,
        value_bias.shape,
        conv_taps.shape,
        out_weight.shape,
        out_bias.shape,
        first_gain.shape,
        first_shift.shape,
        up_weight.shape,
        up_bias.shape,
        down_weight.shape,
        down_bias.shape,
        second_gain.shape,
        second_shift.shape,
        (head_count,),
    )
    layer_out, input_grad, *grads = finish(
        gathered, vec, layer_out, input_grad, shapes, 1.0 / (batch_size * seq_count)
    )
    return (
        layer_out.reshape(hidden_in.shape),
        input_grad.reshape(hidden_in.shape),
        *grads,
    )


def solution(mesh):
    placed = (
        P("batch", "seq", None),
        P("batch", None),
        P(),
        P(),
        P(),
        P(),
        P(),
        P(),
        P(),
        P(),
        P(),
        P(),
        P(),
        P(),
        P(),
        P(),
        P("batch", "seq", None),
    )
    return jax.shard_map(
        body,
        mesh=mesh,
        in_specs=placed,
        out_specs=(
            P("batch", "seq", None),
            P("batch", "seq", None),
            P(),
            P(),
            P(),
            P(),
            P(),
            P(),
            P(),
            P(),
            P(),
            P(),
            P(),
            P(),
            P(),
            P(),
            P(),
        ),
        check_vma=False,
    )
```

```python
import math
from functools import partial

import jax
import jax.numpy as jnp
from jax import lax
from jax.experimental import pallas as pl
from jax.experimental.pallas import tpu as pltpu
from jax.sharding import PartitionSpec as P

epsilon = 1e-05
MESH_IDS = pl.DeviceIdType.MESH
HALF = 384
LANES = 128


def plane_sides(count):
    wide = max(d for d in range(1, math.isqrt(count) + 1) if count % d == 0)
    return wide, count // wide


def axis_sizes(batch_size, seq_size):
    x_size, y_size = plane_sides(seq_size)
    z_size = batch_size // 2
    z_low = 2 if z_size % 2 == 0 else 1
    return {
        "core": 2, "x": x_size, "y": y_size, "z": z_size, "z0": z_low, "z1": z_size // z_low,
    }


class Place:
    def __init__(self, batch_size, seq_size):
        x_size, y_size = plane_sides(seq_size)
        self.sizes = axis_sizes(batch_size, seq_size)
        batch = lax.axis_index("batch")
        seq = lax.axis_index("seq")
        z_low = self.sizes["z0"]
        self.at = {
            "core": lax.rem(batch, 2),
            "z": lax.div(batch, 2),
            "z0": lax.rem(lax.div(batch, 2), z_low),
            "z1": lax.div(batch, 2 * z_low),
            "x": lax.rem(seq, x_size),
            "y": lax.div(seq, x_size),
        }
        self.seq_size = seq_size
        self.seq = seq
        self.batch = batch

    def peer_index(self, axis, step):
        size = self.sizes[axis]
        return lax.rem(self.at[axis] + step, size)

    def device(self, **moved):
        spot = {**self.at, **moved}
        if "z0" in moved or "z1" in moved:
            spot["z"] = spot["z1"] * self.sizes["z0"] + spot["z0"]
        return (spot["z"] * 2 + spot["core"], spot["y"] * self.sizes["x"] + spot["x"])

    def peers(self, axes):
        for axis in axes:
            for step in range(1, self.sizes[axis]):
                yield self.device(**{axis: self.peer_index(axis, step)})

    def seq_peer(self, step):
        return (self.batch, lax.rem(self.seq + step, self.seq_size))


def greet(devices):
    barrier = pltpu.get_barrier_semaphore()
    devices = list(devices)
    for device in devices:
        pl.semaphore_signal(barrier, inc=1, device_id=device, device_id_type=MESH_IDS)
    return lambda: pl.semaphore_wait(barrier, len(devices))


def tile_rows(rows):
    return max(t for t in (96, 64, 48, 32, 16) if rows % t == 0)


def add_rows(out_ref, in_ref, at, parts, rows):
    tile = tile_rows(rows)

    def step(index, carry):
        start = pl.multiple_of(at + index * tile, 16)
        total = in_ref[pl.ds(start, tile), :].astype(jnp.float32)
        for ref, first in parts:
            total = total + ref[pl.ds(pl.multiple_of(first + index * tile, 16), tile), :].astype(
                jnp.float32
            )
        out_ref[pl.ds(start, tile), :] = total.astype(out_ref.dtype)
        return carry

    lax.fori_loop(0, rows // tile, step, 0)


class Reduce:
    def __init__(
        self, number, place, orders, stage, whole, recv, send_sem, recv_sem, free_sem, rows
    ):
        self.number, self.make_place, self.orders = number, place, orders
        self.stage, self.whole, self.recv = stage, whole, recv
        self.send_sem, self.recv_sem, self.free_sem = send_sem, recv_sem, free_sem
        self.part = rows // len(orders)

    @staticmethod
    def slots(sizes, orders, rows):
        need = []
        for order in orders:
            size, slot = rows // len(orders), 0
            for axis in order:
                size //= sizes[axis]
                slot += (sizes[axis] - 1) * size
            need.append(slot)
        return max(need)

    @staticmethod
    def copies(sizes, orders):
        return 2 + 2 * sum(sizes[axis] - 1 for order in orders for axis in order)

    def level_of(self, place, half, level):
        base, size, slot = half * self.part, self.part, 0
        order = self.orders[half]
        sem = 2 + 2 * half * sum(place.sizes[axis] - 1 for axis in order)
        for axis in order[:level]:
            count = place.sizes[axis]
            size //= count
            slot += (count - 1) * size
            sem += 2 * (count - 1)
            base = base + place.at[axis] * size
        count = place.sizes[order[level]]
        return order[level], count, base, size // count, slot, sem

    def copy(self, index, src, dst, device):
        return pltpu.make_async_remote_copy(
            src_ref=src,
            dst_ref=dst,
            send_sem=self.send_sem.at[self.number, index],
            recv_sem=self.recv_sem.at[self.number, index],
            device_id=device,
            device_id_type=MESH_IDS,
        )

    @staticmethod
    def rows_of(ref, start, rows):
        return ref.at[pl.ds(pl.multiple_of(start, 16), rows)]

    def scatter(self, half, level):
        place = self.make_place()
        axis, count, base, chunk, slot, sem = self.level_of(place, half, level)
        mine = self.stage.at[place.at["core"]]
        copies = []
        for step in range(1, count):
            peer = place.peer_index(axis, step)
            copies.append(
                self.copy(
                    sem + step - 1,
                    self.rows_of(mine, base + peer * chunk, chunk),
                    self.recv.at[half, pl.ds(slot + (step - 1) * chunk, chunk)],
                    place.device(**{axis: peer}),
                )
            )
        return copies

    def spread(self, half, level):
        place = self.make_place()
        axis, count, base, chunk, slot, sem = self.level_of(place, half, level)
        here = self.rows_of(self.whole, base + place.at[axis] * chunk, chunk)
        return [
            self.copy(
                sem + count - 1 + step - 1,
                here,
                here,
                place.device(**{axis: place.peer_index(axis, step)}),
            )
            for step in range(1, count)
        ]

    def add_level(self, half, level):
        place = self.make_place()
        axis, count, base, chunk, slot, _ = self.level_of(place, half, level)
        mine = self.stage.at[place.at["core"]]
        add_rows(
            self.whole if level == len(self.orders[half]) - 1 else mine,
            mine,
            base + place.at[axis] * chunk,
            [(self.recv.at[half], slot + k * chunk) for k in range(count - 1)],
            chunk,
        )

    def core_out(self):
        place = self.make_place()
        core = place.at["core"]
        return self.copy(0, self.stage.at[1 - core], self.whole, place.device(core=1 - core))

    def core_back(self):
        place = self.make_place()
        core = place.at["core"]
        return self.copy(1, self.whole, self.stage.at[core], place.device(core=1 - core))

    def run(self):
        halves = range(len(self.orders))
        self.core_out().start()
        yield
        self.core_out().wait()
        place = self.make_place()
        other = place.device(core=1 - place.at["core"])
        pl.semaphore_signal(
            self.free_sem.at[self.number], inc=1, device_id=other, device_id_type=MESH_IDS
        )
        mine = self.stage.at[place.at["core"]]
        for half in halves:
            start = half * self.part
            add_rows(mine, mine, start, [(self.whole, start)], self.part)
            for copy in self.scatter(half, 0):
                copy.start()
        last = len(self.orders[0]) - 1
        for level in range(last + 1):
            yield
            for half in halves:
                for copy in self.scatter(half, level):
                    copy.wait()
                self.add_level(half, level)
                later = self.scatter if level < last else self.spread
                for copy in later(half, min(level + 1, last)):
                    copy.start()
        for level in reversed(range(last + 1)):
            yield
            for half in halves:
                for copy in self.spread(half, level):
                    copy.wait()
                for copy in self.spread(half, level - 1) if level else ():
                    copy.start()
        pl.semaphore_wait(self.free_sem.at[self.number], 1)
        self.core_back().start()
        yield
        self.core_back().wait()


def vec_reduce(place, acc, slots, send_sem, recv_sem):
    sem = 0
    level = 0
    for axis in ("core", "x", "y", "z"):
        count = place.sizes[axis]
        copies = []
        here = place.at[axis]
        for step in range(1, count):
            copies.append(
                pltpu.make_async_remote_copy(
                    src_ref=acc,
                    dst_ref=slots.at[level + here],
                    send_sem=send_sem.at[sem],
                    recv_sem=recv_sem.at[sem],
                    device_id=place.device(**{axis: place.peer_index(axis, step)}),
                    device_id_type=MESH_IDS,
                )
            )
            sem += 1
        for copy in copies:
            copy.start()
        slots[level + here] = acc[...]
        yield
        for copy in copies:
            copy.wait()
        total = slots[level]
        for index in range(1, count):
            total = total + slots[level + index]
        acc[...] = total
        level += count


SEG = 64
PAIR = 128
HALO = 16
BLOCK = 128
FAR = -1e30
NT = ((1,), (1,))
TN = ((0,), (0,))
NN = ((1,), (0,))


def mm(left, right, dims=NN):
    return lax.dot_general(left, right, (dims, ((), ())), preferred_element_type=jnp.float32)


def split(array):
    high = array.astype(jnp.bfloat16)
    return high, (array - high.astype(jnp.float32)).astype(jnp.bfloat16)


def thirds(array):
    high = array.astype(jnp.bfloat16)
    middle = (array - high.astype(jnp.float32)).astype(jnp.bfloat16)
    rest = array - high.astype(jnp.float32) - middle.astype(jnp.float32)
    return high, middle, rest.astype(jnp.bfloat16)


def mm3(left, right, dims=NN):
    left_high, left_low = left
    right_high, right_low = right
    (left_dim,), (right_dim,) = dims
    return mm(
        jnp.concatenate([left_high, left_high, left_low], axis=left_dim),
        jnp.concatenate([right_high, right_low, right_high], axis=right_dim),
        dims,
    )


def eye_mask(size):
    rows = lax.broadcasted_iota(jnp.int32, (size, size), 0)
    return rows == lax.broadcasted_iota(jnp.int32, (size, size), 1)


def column(row):
    return jnp.sum(jnp.where(eye_mask(row.shape[1]), row, 0.0), axis=1, keepdims=True)


def row_of(col):
    return jnp.sum(jnp.where(eye_mask(col.shape[0]), col, 0.0), axis=0, keepdims=True)


def first_head(shape):
    return lax.broadcasted_iota(jnp.int32, shape, len(shape) - 1) < SEG


def spread_heads(pair):
    first = first_head(pair.shape)
    zero = jnp.zeros_like(pair)
    return jnp.concatenate([jnp.where(first, pair, zero), jnp.where(first, zero, pair)], axis=0)


def join_heads(blocks):
    shape = (SEG, PAIR)
    return jnp.where(
        first_head(shape),
        jnp.broadcast_to(blocks[:SEG], shape),
        jnp.broadcast_to(blocks[SEG:], shape),
    )


def heads_sum(col):
    first = jnp.sum(col[:SEG], axis=0, keepdims=True)
    second = jnp.sum(col[SEG:], axis=0, keepdims=True)
    return jnp.concatenate(
        [jnp.broadcast_to(first, (SEG, 1)), jnp.broadcast_to(second, (SEG, 1))], axis=0
    )


def shared_out(place, source, target, many, send_sem, recv_sem):
    copies = []
    for step in range(1, place.seq_size):
        device = place.seq_peer(step)
        copies.append(
            pltpu.make_async_remote_copy(
                src_ref=source.at[pl.ds(device[1] * many, many)],
                dst_ref=target.at[step - 1],
                send_sem=send_sem.at[step - 1],
                recv_sem=recv_sem.at[step - 1],
                device_id=device,
                device_id_type=MESH_IDS,
            )
        )
    return copies


def passed_on(place, array, many, send_sem, recv_sem):
    copies = []
    here = array.at[pl.ds(place.seq * many, many)]
    for step in range(1, place.seq_size):
        copies.append(
            pltpu.make_async_remote_copy(
                src_ref=here,
                dst_ref=here,
                send_sem=send_sem.at[step - 1],
                recv_sem=recv_sem.at[step - 1],
                device_id=place.seq_peer(step),
                device_id_type=MESH_IDS,
            )
        )
    return copies


def halo_copies(place, padded, tokens, send_sem, recv_sem):
    copies = []
    for index, (step, first, there) in enumerate(
        ((1, tokens, 0), (place.seq_size - 1, HALO, tokens + HALO))
    ):
        copies.append(
            pltpu.make_async_remote_copy(
                src_ref=padded.at[:, pl.ds(first, HALO)],
                dst_ref=padded.at[:, pl.ds(there, HALO)],
                send_sem=send_sem.at[index],
                recv_sem=recv_sem.at[index],
                device_id=place.seq_peer(step),
                device_id_type=MESH_IDS,
            )
        )
    return copies


def trim_halo(place, padded, tokens):
    zero = jnp.zeros((padded.shape[0], HALO, padded.shape[2]), padded.dtype)
    low, high = pl.ds(0, HALO), pl.ds(tokens + HALO, HALO)
    padded[:, low] = jnp.where(place.seq > 0, padded[:, low], zero)
    padded[:, high] = jnp.where(place.seq < place.seq_size - 1, padded[:, high], zero)


def zero_past(padded, tokens):
    past = tokens + 2 * HALO
    rest = padded.shape[1] - past
    padded[:, pl.ds(past, rest)] = jnp.zeros(
        (padded.shape[0], rest, padded.shape[2]), padded.dtype
    )


def band(taps):
    wide = jnp.broadcast_to(taps, (BLOCK, 2 * BLOCK))
    return pltpu.roll(wide, 0, 1, stride=1, stride_axis=0).astype(jnp.bfloat16)


def tap_lanes(taps):
    heads, count = taps.shape
    wide = jnp.concatenate(
        [taps[...], jnp.zeros((heads, 2 * BLOCK - count), jnp.float32)], axis=1
    )
    return jnp.concatenate([wide, jnp.zeros((16 - heads, 2 * BLOCK), jnp.float32)], axis=0)


def turned_taps(taps):
    shape = (2 * BLOCK, 2 * BLOCK)
    ends = lax.broadcasted_iota(jnp.int32, shape, 0) + lax.broadcasted_iota(jnp.int32, shape, 1)
    turn = jnp.where(ends == taps.shape[1] - 1, 1.0, 0.0).astype(jnp.bfloat16)
    return mm(tap_lanes(taps).astype(jnp.bfloat16), turn)


def conv_rows(padded, taps, out, tokens, span=None):
    seqs, _, width = padded.shape

    def step(pair, carry):
        lanes = pl.ds(pl.multiple_of(pair * PAIR, PAIR), PAIR)
        first = band(taps[pl.ds(2 * pair, 1), :])
        second = band(taps[pl.ds(2 * pair + 1, 1), :])
        for seq in range(seqs):
            for block in range(tokens // BLOCK):
                window = padded[seq, pl.ds(block * BLOCK, 2 * BLOCK), lanes]
                both = jnp.where(
                    first_head((BLOCK, PAIR)), mm(first, window), mm(second, window)
                )
                out[pl.ds(seq * tokens + block * BLOCK, BLOCK), lanes] = both
        return carry

    lax.fori_loop(*(span or (0, width // PAIR)), step, 0, unroll=3)


def segment_edges(bounds, seq):
    low = column(bounds[pl.ds(seq, 1), pl.ds(0, SEG)].astype(jnp.float32))
    high = column(bounds[pl.ds(seq, 1), pl.ds(1, SEG)].astype(jnp.float32))
    return low, high


def positions(place, tokens, axis):
    shape = (tokens, 1) if axis == 0 else (1, tokens)
    return (place.seq * tokens + lax.broadcasted_iota(jnp.int32, shape, axis)).astype(jnp.float32)


def member_of(place, bounds, seq, tokens):
    low, high = segment_edges(bounds, seq)
    where = positions(place, tokens, 1)
    return jnp.where((where >= low) & (where < high), 1.0, 0.0).astype(jnp.bfloat16)


def length_of(bounds, seq):
    return bounds[pl.ds(seq, 1), pl.ds(SEG, 1)].astype(jnp.float32)


def newton_forward(kernels, keep):
    eye = jnp.where(eye_mask(PAIR), 1.0, 0.0)
    approx = []
    for kernel in kernels:
        fro = heads_sum(jnp.sum(kernel * kernel, axis=1, keepdims=True))
        approx.append(kernel.T / fro)
    halves = [split(kernel) for kernel in kernels]
    units = range(len(kernels))
    for step in range(6):
        wide = [split(a) for a in approx]
        product = [mm3(halves[u], wide[u]) for u in units]
        lefts = [split(p) for p in product]
        inner = [15.0 * eye - mm3(lefts[u], split(7.0 * eye - product[u])) for u in units]
        outer = [13.0 * eye - mm3(lefts[u], split(inner[u])) for u in units]
        for u in units:
            for slot, value in enumerate((approx[u], product[u], inner[u], outer[u])):
                keep[u, step, slot] = value
        approx = [0.25 * mm3(wide[u], split(outer[u])) for u in units]
    return approx


def attend_kernel(
    batch_size, seq_size, seqs, tokens, many,
    x_in, weight_in, bounds, query_bias, value_bias, taps, *refs
):
    outs, refs = refs[:14], refs[14:]
    saved, refs = refs[:14], refs[14:]
    (
        queries, keys, values, kernel_one, expo, land, mixed, branch, kernel_two, approx_out,
        keep, kv_own, shares, proxies,
    ) = saved
    (
        x, weight, load_sem, save_sem, land_send, land_recv, kv_send, kv_recv, conv, tap_rows, biases,
        land_sem, land_back_sem, kv_sem, mixed_sem, halo_sem,
    ) = refs
    place = Place(batch_size, seq_size)
    width = x.shape[1]
    loads = [pltpu.make_async_copy(x_in, x, load_sem.at[3])]
    for third in range(3):
        lanes = pl.ds(third * width, width)
        loads.append(
            pltpu.make_async_copy(
                weight_in.at[:, lanes], weight.at[:, lanes], load_sem.at[third]
            )
        )
    for copy in loads:
        copy.start()
    saves = []

    def save(*names):
        for ref in names:
            index = [ref is other for other in saved].index(True)
            copy = pltpu.make_async_copy(ref, outs[index], save_sem.at[index])
            copy.start()
            saves.append(copy)

    pairs = width // PAIR
    units = seqs * pairs
    wait_greet = greet(place.seq_peer(step) for step in range(1, seq_size))
    quarter = float(SEG) ** -0.25

    tap_rows[...] = tap_lanes(taps)
    biases[...] = jnp.zeros_like(biases)
    biases[pl.ds(0, 1), :] = query_bias[...].reshape(1, width)
    biases[pl.ds(2, 1), :] = value_bias[...].reshape(1, width)

    def project(out_ref, third):
        def step(tile, carry):
            lanes = pl.ds(pl.multiple_of(third * width + tile * 256, 256), 256)
            here = pl.ds(pl.multiple_of(tile * 256, 256), 256)
            rows = mm(x[...], weight[:, lanes]) + biases[pl.ds(third, 1), here]
            if third < 2:
                out_ref[:, here] = (rows * quarter).astype(jnp.bfloat16)
            else:
                for seq in range(seqs):
                    valid = positions(place, tokens, 0) < length_of(bounds, seq)
                    out_ref[seq, pl.ds(HALO, tokens), here] = jnp.where(
                        valid, rows[seq * tokens : (seq + 1) * tokens], 0.0
                    ).astype(jnp.bfloat16)
            return carry

        loads[1 + third].wait()
        lax.fori_loop(0, width // 256, step, 0)

    loads[0].wait()
    project(queries, 0)
    project(keys, 1)
    save(queries, keys)
    for seq in range(seqs):
        member = member_of(place, bounds, seq, tokens)
        for slot, rows in enumerate((queries, keys)):
            sums = mm(member, rows[pl.ds(seq * tokens, tokens), :])
            for pair in range(pairs):
                land_send[seq * pairs + pair, slot] = sums[:, pair * PAIR : (pair + 1) * PAIR]
    for unit in range(units, seq_size * many):
        land_send[unit] = jnp.ones_like(land_send[unit])
        kv_send[unit] = jnp.ones_like(kv_send[unit])
    wait_greet()
    land_out = shared_out(place, land_send, land_recv, many, *land_sem)
    for copy in land_out:
        copy.start()
    project(values, 2)
    halo = halo_copies(place, values, tokens, *halo_sem)
    for copy in halo:
        copy.start()
    zero_past(values, tokens)
    for copy in land_out:
        copy.wait()
    first_unit = place.seq * many
    for own in range(many):
        unit = first_unit + own
        total = land_send[unit]
        for step in range(seq_size - 1):
            total = total + land_recv[step, own]
        low, high = segment_edges(bounds, jnp.minimum(lax.div(unit, pairs), seqs - 1))
        land[unit] = (total / (high - low)).astype(jnp.bfloat16)
    land_back = passed_on(place, land, many, *land_back_sem)
    for copy in land_back:
        copy.start()
    for copy in halo:
        copy.wait()
    trim_halo(place, values, tokens)
    save(values)
    conv_rows(values, tap_rows, conv, tokens)
    for copy in land_back:
        copy.wait()
    save(land)

    def spots(unit):
        seq, pair = lax.div(unit, pairs), lax.rem(unit, pairs)
        rows = pl.ds(pl.multiple_of(seq * tokens, tokens), tokens)
        lanes = pl.ds(pl.multiple_of(pair * PAIR, PAIR), PAIR)
        return seq, rows, lanes

    def third_scores(unit, carry):
        seq, rows, lanes = spots(unit)
        score = mm(spread_heads(land[unit, 0]), keys[rows, lanes], NT)
        valid = positions(place, tokens, 1) < length_of(bounds, seq)
        score = jnp.where(valid, score, FAR)
        top = jnp.max(score, axis=1, keepdims=True)
        weights = jnp.exp(score - top)
        expo[unit] = weights
        total = jnp.sum(weights, axis=1, keepdims=True)
        part = mm(weights.astype(jnp.bfloat16), values[seq, pl.ds(HALO, tokens), lanes])
        kv_send[unit, pl.ds(0, SEG)] = join_heads(part).astype(jnp.bfloat16)
        kv_send[unit, pl.ds(SEG, 16)] = jnp.concatenate(
            [*thirds(row_of(top)), *thirds(row_of(total)), jnp.zeros((10, PAIR), jnp.bfloat16)],
            axis=0,
        )
        return carry

    lax.fori_loop(0, units, third_scores, 0, unroll=6)
    kv_out = shared_out(place, kv_send, kv_recv, many, *kv_sem)
    for copy in kv_out:
        copy.start()
    save(expo)

    kernels = []
    same = (
        lax.broadcasted_iota(jnp.int32, (PAIR, PAIR), 0) < SEG
    ) == first_head((PAIR, PAIR))
    for own in range(many):
        both = land[first_unit + own]
        score = jnp.where(same, mm(spread_heads(both[0]), spread_heads(both[1]), NT), FAR)
        weights = jnp.exp(score - jnp.max(score, axis=1, keepdims=True))
        kernels.append(weights / jnp.sum(weights, axis=1, keepdims=True))
        kernel_two[own] = kernels[own]
    approx = newton_forward(kernels, keep)
    for own in range(many):
        approx_out[own] = approx[own]
        proxy = jnp.sqrt(
            heads_sum(jnp.sum(kernels[own] * kernels[own], axis=1, keepdims=True))
        ) * jnp.sqrt(heads_sum(jnp.sum(approx[own] * approx[own], axis=1, keepdims=True)))
        proxies[own] = jnp.broadcast_to(row_of(proxy), (8, PAIR))
    save(keep, kernel_two, approx_out, proxies)

    for copy in kv_out:
        copy.wait()
    for own in range(many):
        parts, tops, totals = [], [], []
        for packed in [kv_send[first_unit + own]] + [
            kv_recv[step, own] for step in range(seq_size - 1)
        ]:
            packed = packed.astype(jnp.float32)
            tail = packed[SEG:]
            parts.append(packed[:SEG])
            tops.append(tail[0:1] + tail[1:2] + tail[2:3])
            totals.append(tail[3:4] + tail[4:5] + tail[5:6])
        top = tops[0]
        for other in tops[1:]:
            top = jnp.maximum(top, other)
        scales = [jnp.exp(other - top) for other in tops]
        total = sum(scale * part for scale, part in zip(scales, totals))
        kv_mean = jnp.zeros((SEG, PAIR), jnp.float32)
        for slot, (scale, part) in enumerate(zip(scales, parts)):
            share = scale / total
            shares[own, slot] = jnp.broadcast_to(share, (8, PAIR))
            kv_mean = kv_mean + join_heads(column(share)) * part
        kv_own[own] = kv_mean
        mixed[first_unit + own] = join_heads(
            mm3(split(approx[own]), split(spread_heads(kv_mean)))
        ).astype(jnp.bfloat16)
    mixed_out = passed_on(place, mixed, many, *mixed_sem)
    for copy in mixed_out:
        copy.start()
    save(kv_own, shares)

    def first_scores(unit, carry):
        seq, rows, lanes = spots(unit)
        score = mm(spread_heads(land[unit, 1]), queries[rows, lanes], NT)
        score = score.reshape(2, SEG, tokens)
        weights = jnp.exp(score - jnp.max(score, axis=1, keepdims=True))
        weights = weights / jnp.sum(weights, axis=1, keepdims=True)
        kernel_one[unit] = weights.reshape(2 * SEG, tokens)
        return carry

    lax.fori_loop(0, units, first_scores, 0, unroll=6)
    save(kernel_one)
    for copy in mixed_out:
        copy.wait()
    save(mixed)

    def combine(unit, carry):
        seq, rows, lanes = spots(unit)
        attended = mm(
            kernel_one[unit].astype(jnp.bfloat16), spread_heads(mixed[unit]), TN
        )
        branch[rows, lanes] = (attended + conv[rows, lanes]).astype(jnp.bfloat16)
        return carry

    lax.fori_loop(0, units, combine, 0, unroll=6)
    save(branch)
    for copy in saves:
        copy.wait()


def attend(
    x, bounds, weight, query_bias, value_bias, taps, batch_size, seq_size, seqs
):
    rows, width = x.shape
    tokens = rows // seqs
    units = seqs * (width // PAIR)
    many = -(-units // seq_size)
    slots = seq_size * many
    f32, bf16 = jnp.float32, jnp.bfloat16
    vmem = pl.BlockSpec(memory_space=pltpu.VMEM)
    anywhere = pl.BlockSpec(memory_space=pl.ANY)
    sems = pltpu.SemaphoreType.DMA
    shapes = (
        ((rows, width), bf16),
        ((rows, width), bf16),
        ((seqs, tokens + BLOCK, width), bf16),
        ((units, 2 * SEG, tokens), f32),
        ((units, 2 * SEG, tokens), f32),
        ((slots, 2, SEG, PAIR), bf16),
        ((slots, SEG, PAIR), bf16),
        ((rows, width), bf16),
        ((many, PAIR, PAIR), f32),
        ((many, PAIR, PAIR), f32),
        ((many, 6, 4, PAIR, PAIR), f32),
        ((many, SEG, PAIR), f32),
        ((many, seq_size, 8, PAIR), f32),
        ((many, 8, PAIR), f32),
    )
    return pl.pallas_call(
        partial(attend_kernel, batch_size, seq_size, seqs, tokens, many),
        out_shape=tuple(jax.ShapeDtypeStruct(*shape) for shape in shapes),
        in_specs=[anywhere] * 2 + [vmem] * 4,
        out_specs=tuple([anywhere] * len(shapes)),
        scratch_shapes=[
            *(pltpu.VMEM(*shape) for shape in shapes),
            pltpu.VMEM(x.shape, bf16),
            pltpu.VMEM(weight.shape, bf16),
            sems((4,)),
            sems((len(shapes),)),
            pltpu.VMEM((slots, 2, SEG, PAIR), f32),
            pltpu.VMEM((seq_size - 1, many, 2, SEG, PAIR), f32),
            pltpu.VMEM((slots, SEG + 16, PAIR), bf16),
            pltpu.VMEM((seq_size - 1, many, SEG + 16, PAIR), bf16),
            pltpu.VMEM((rows, width), f32),
            pltpu.VMEM((16, 2 * BLOCK), f32),
            pltpu.VMEM((8, width), f32),
            (sems((seq_size - 1,)),) * 2,
            (sems((seq_size - 1,)),) * 2,
            (sems((seq_size - 1,)),) * 2,
            (sems((seq_size - 1,)),) * 2,
            (sems((2,)),) * 2,
        ],
        compiler_params=pltpu.CompilerParams(
            collective_id=1, has_side_effects=True, vmem_limit_bytes=58 * 2**20
        ),
        name="attend",
    )(x, weight, bounds, query_bias, value_bias, taps)


def newton_backward(kernels, approx_grads, keep, tick):
    units = range(len(kernels))
    eye = jnp.where(eye_mask(PAIR), 1.0, 0.0)
    kernel_halves = [split(kernel) for kernel in kernels]
    grads = [jnp.zeros((PAIR, PAIR), jnp.float32) for _ in units]
    after = approx_grads
    for step in reversed(range(6)):
        approx = [split(keep[u, step, 0]) for u in units]
        product = [keep[u, step, 1] for u in units]
        halves = [split(p) for p in product]
        first = [split(7.0 * eye - p) for p in product]
        second = [split(keep[u, step, 2]) for u in units]
        third = [split(keep[u, step, 3]) for u in units]
        wide = [split(0.25 * a) for a in after]
        third_grad = [split(mm3(wide[u], approx[u])) for u in units]
        second_grad = [split(-mm3(third_grad[u], halves[u])) for u in units]
        first_grad = [-mm3(second_grad[u], halves[u]) for u in units]
        product_grad = [
            split(
                -mm3(second[u], third_grad[u]) - mm3(first[u], second_grad[u]) - first_grad[u]
            )
            for u in units
        ]
        grads = [grads[u] + mm3(approx[u], product_grad[u]) for u in units]
        after = [
            mm3(third[u], wide[u]) + mm3(product_grad[u], kernel_halves[u]) for u in units
        ]
        tick(f"newton{step}")
    out = []
    for u in units:
        kernel = kernels[u]
        fro = heads_sum(jnp.sum(kernel * kernel, axis=1, keepdims=True))
        fro_grad = heads_sum(jnp.sum(after[u] * kernel, axis=1, keepdims=True)) / (fro * fro)
        out.append(grads[u].T + after[u] / fro - 2.0 * kernel * fro_grad)
    return out


def tap_grads(padded_grad, padded, vec, first_row, tokens, span):
    seqs, _, width = padded.shape
    rows = lax.broadcasted_iota(jnp.int32, (BLOCK, BLOCK), 0)
    cols = lax.broadcasted_iota(jnp.int32, (BLOCK, BLOCK), 1)
    turn = jnp.where(rows + cols == BLOCK - 1, 1.0, 0.0).astype(jnp.bfloat16)

    def step(pair, carry):
        lanes = pl.ds(pl.multiple_of(pair * PAIR, PAIR), PAIR)
        total = [jnp.zeros((BLOCK, 2 * BLOCK), jnp.float32) for _ in range(2)]
        for seq in range(seqs):
            for block in range(tokens // BLOCK):
                window = padded[seq, pl.ds(block * BLOCK, 2 * BLOCK), lanes]
                grad = padded_grad[seq, pl.ds(HALO + block * BLOCK, BLOCK), lanes]
                grad = mm(turn, grad).astype(jnp.bfloat16)
                first = first_head(grad.shape)
                zero = jnp.zeros_like(grad)
                total[0] = total[0] + mm(jnp.where(first, grad, zero), window, NT)
                total[1] = total[1] + mm(jnp.where(first, zero, grad), window, NT)
        for head in range(2):
            turned = pltpu.roll(total[head], 0, 1, stride=1, stride_axis=0)
            sums = jnp.sum(turned, axis=0, keepdims=True)
            sums = pltpu.roll(sums, BLOCK + 1, 1)
            vec[pl.ds(first_row + 2 * pair + head, 1), :] = sums[:, :PAIR]
        return carry

    lax.fori_loop(*span, step, 0, unroll=2)


class Ticker:
    def __init__(self, points):
        self.live = {}
        self.points = points

    def add(self, number, generator):
        next(generator)
        self.live[number] = generator

    def step(self, number):
        try:
            next(self.live[number])
        except StopIteration:
            del self.live[number]

    def tick(self, point):
        for number in self.points.get(point, ()):
            if number in self.live:
                self.step(number)

    def drain(self, order=()):
        for number in order:
            if number in self.live:
                self.step(number)
        while self.live:
            for number in list(self.live):
                self.step(number)


POINTS = {
    "back2": (0, 1),
    "mid1": (2, 3, 1),
    "first0": (0,),
    "acc": (1,),
    "conv0": (2,),
    "conv1": (3,),
    "wait_acc": (0,),
    "value": (1, 2),
    "newton5": (0,),
    "newton3": (4,),
    "newton2": (3, 0),
    "land": (0,),
    "wait_back": (0, 1, 2, 4),
    "last": (3, 1),
    "taps0": (4, 5),
    "input2": (1,),
}
LAST = (1, 2, 5, 1, 2, "vec", 5, 3, 4, 0, 3, "vec", 2, 2, 5, 2, 4, "vec", 3, 0, 3, 4, 5, "vec", 3, 0, 0, 5, 4, 4, 4, 5, 5, 5)


class Sums:
    def __init__(self, ref):
        self.ref = ref

    def clear(self):
        self.ref[...] = jnp.zeros_like(self.ref)

    def add(self, row, array):
        here = pl.ds(row, 1)
        self.ref[here, :] = self.ref[here, :] + jnp.sum(array, axis=0, keepdims=True)


def normalize(hidden):
    centered = hidden - jnp.mean(hidden, axis=1, keepdims=True)
    inverse = lax.rsqrt(jnp.mean(centered * centered, axis=1, keepdims=True) + epsilon)
    return centered * inverse, inverse


def normalize_back(grad, normed, inverse):
    return inverse * (
        grad
        - jnp.mean(grad, axis=1, keepdims=True)
        - normed * jnp.mean(grad * normed, axis=1, keepdims=True)
    )


def row_vector(ref):
    return ref[...].reshape(1, ref.shape[0])


def back_kernel(
    batch_size, seq_size, seqs, tokens, many, plan,
    x_in, grad_out, branch_in, out_weight, up_weight, down_weight, qkv_weight,
    queries_in, keys_in, values_in, kernel_one_in, expo_in, keep_in, land_in, mixed_in,
    kernel_two_in, approx_in, kv_own_in, shares_in, proxies_in, bounds, taps,
    out_bias, first_gain, first_shift, up_bias, down_bias, second_gain, second_shift,
    layer_out, input_grad, gathered, vec,
    stage, whole, recv, slots, padded, grad_first, tap_rows, sums, up_sums, acc_send, acc_all,
    land_send, land_recv, land_all, kernel_one, mixed, land,
    load_sem, weight_sem, send_sem, recv_sem, free_sem, vec_sem, out_sem, halo_sem, mixed_sem,
    acc_sem, land_sem, land_back_sem,
):
    place = Place(batch_size, seq_size)
    rows, width = x_in.shape
    ff_blocks = down_weight.shape[0] // width
    pairs = width // PAIR
    units = seqs * pairs
    quarter = float(SEG) ** -0.25
    wait_greet = greet(
        [place.seq_peer(step) for step in range(1, seq_size)] + list(place.peers(("core", "z")))
    )

    def early_loads():
        return [
            pltpu.make_async_copy(source, target, load_sem.at[11 + index])
            for index, (source, target) in enumerate(
                ((kernel_one_in, kernel_one), (mixed_in, mixed), (land_in, land))
            )
        ]

    ticker = Ticker(POINTS)
    tick = ticker.tick
    bf16 = jnp.bfloat16

    def piece_run(number):
        piece = plan[number]
        here = pl.ds(piece.start, piece.rows)
        yield from Reduce(
            number, lambda: Place(batch_size, seq_size), piece.orders, stage.at[:, here],
            whole.at[here], recv.at[:, piece.slots], send_sem, recv_sem, free_sem, piece.rows,
        ).run()

        def outs():
            core = Place(batch_size, seq_size).at["core"]
            return (
                pltpu.make_async_copy(
                    whole.at[here], gathered.at[core, here], out_sem.at[number, 0]
                ),
                pltpu.make_async_copy(
                    stage.at[1 - core, here], gathered.at[1 - core, here], out_sem.at[number, 1]
                ),
            )

        for out in outs():
            out.start()
        yield
        for out in outs():
            out.wait()

    done = set()

    def staged(*blocks):
        done.update(blocks)
        for number, piece in enumerate(plan):
            if done.issuperset(piece.blocks) and not set(blocks).isdisjoint(piece.blocks):
                ticker.add(number, piece_run(number))

    def store_block(block, first, grad):
        at = pl.ds(pl.multiple_of(block * width + first, 16), grad.shape[0])
        grad = grad.astype(bf16)
        stage[0, at, :] = grad[:, :HALF]
        stage[1, at, :] = grad[:, HALF:]

    def store_strip(block, part, grad):
        at = pl.ds(block * width, width)
        grad = grad.astype(bf16)
        first = part * 256
        for half in range(2):
            low, high = max(first, half * HALF), min(first + 256, (half + 1) * HALF)
            if low < high:
                lanes = pl.ds(low - half * HALF, high - low)
                stage[half, at, lanes] = grad[:, low - first : high - first]

    def loop(count, step):
        def run(index, carry):
            step(index)
            return carry

        lax.fori_loop(0, count, run, 0)

    def feed_forward(
        x, branch, grads, mid_low, turned, act_turned, low, normed_one, grad_second, inverse_one, out_w, ff_w,
        act, slope, up_bias_row,
    ):
        def load(index, source, target):
            return pltpu.make_async_copy(source, target, load_sem.at[index])

        first = [load(0, out_weight, out_w), load(1, branch_in, branch), load(2, x_in, x)]
        for copy in first:
            copy.start()
        grads_load = load(3, grad_out, grads)

        def up_load(block):
            return pltpu.make_async_copy(
                up_weight.at[:, pl.ds(block * width, width)], ff_w.at[block], weight_sem.at[block]
            )

        def down_load(block):
            return pltpu.make_async_copy(
                down_weight.at[pl.ds(block * width, width)], ff_w.at[block], weight_sem.at[block]
            )

        for block in range(ff_blocks):
            up_load(block).start()
        grads_load.start()
        for copy in early_loads():
            copy.start()
        total = Sums(sums)
        total.clear()
        up_bias_row[...] = row_vector(up_bias)
        for copy in first:
            copy.wait()
        tile = 128

        def strip(index):
            return pl.ds(pl.multiple_of(index * 256, 256), 256)

        def attended(index):
            normed_one[:, strip(index)] = mm(branch[...], out_w[:, strip(index)])

        def project(index):
            here = pl.ds(pl.multiple_of(index * tile, tile), tile)
            hidden = x[here, :].astype(jnp.float32) + normed_one[here, :]
            normed, inverse = normalize(hidden + row_vector(out_bias))
            normed_one[here, :] = normed
            inverse_one[here, :] = jnp.broadcast_to(inverse, (tile, PAIR))
            mid = normed * row_vector(first_gain) + row_vector(first_shift)
            mid_low[here, :] = mid.astype(bf16)

        loop(width // 256, attended)
        loop(rows // tile, project)
        for block in range(ff_blocks):
            up_load(block).wait()

            def up(index, block=block):
                part = pl.multiple_of(index * 256, 256)
                lanes = pl.ds(block * width + part, 256)
                pre = mm(mid_low[...], ff_w[block, :, pl.ds(part, 256)])
                pre = pre + up_bias_row[:, lanes]
                half = 0.5 * (1.0 + lax.erf(pre * (0.5**0.5)))
                act[:, lanes] = (pre * half).astype(bf16)
                bell = jnp.exp(-0.5 * pre * pre) * (2.0 * math.pi) ** -0.5
                slope[:, lanes] = (half + pre * bell).astype(bf16)

            loop(width // 256, up)
            down_load(block).start()
        turned[...] = mid_low[...].T
        for block in range(ff_blocks):
            down_load(block).wait()
        grads_load.wait()

        def summed(index):
            total = mm(act[:, pl.ds(0, width)], ff_w[0, :, strip(index)])
            for block in range(1, ff_blocks):
                total = total + mm(
                    act[:, pl.ds(block * width, width)], ff_w[block, :, strip(index)]
                )
            grad_second[:, strip(index)] = total

        def down(index):
            here = pl.ds(pl.multiple_of(index * tile, tile), tile)
            mid = normed_one[here, :] * row_vector(first_gain) + row_vector(first_shift)
            normed, inverse = normalize(mid + row_vector(down_bias) + grad_second[here, :])
            grad = grads[here, :].astype(jnp.float32)
            total.add(1, grad * normed)
            total.add(2, grad)
            grads[here, :] = (
                normed * row_vector(second_gain) + row_vector(second_shift)
            ).astype(bf16)
            grad = normalize_back(grad * row_vector(second_gain), normed, inverse)
            grad_second[here, :] = grad
            grad = grad.astype(bf16)
            low[here, :] = grad
            total.add(0, grad.astype(jnp.float32))

        loop(width // 256, summed)
        loop(rows // tile, down)
        out_copy = load(4, grads, layer_out)
        out_copy.start()
        for block in range(ff_blocks):

            act_turned[...] = act[:, pl.ds(block * width, width)].T
            for part in range(width // 256):
                store_strip(block, part, mm(act_turned[...], low[:, pl.ds(part * 256, 256)]))
            if block == 0:
                wait_greet()
            staged(block)
            tick(f"down{block}")
        for block in range(ff_blocks):

            def up_back(index, block=block):
                at = pl.multiple_of(index * 256, 256)
                lanes = pl.ds(block * width + at, 256)
                grad = mm(low[...], ff_w[block, pl.ds(at, 256), :], NT)
                grad = (grad * slope[:, lanes].astype(jnp.float32)).astype(bf16)
                slope[:, lanes] = grad
                up_sums[:, lanes] = jnp.sum(grad.astype(jnp.float32), axis=0, keepdims=True)

            loop(width // 256, up_back)
            up_load(block).start()
            tick(f"back{block}")
        for block in range(ff_blocks):

            for part in range(width // 256):
                lanes = pl.ds(block * width + part * 256, 256)
                store_strip(ff_blocks + block, part, mm(turned[...], slope[:, lanes]))
            staged(ff_blocks + block)
            tick(f"up{block}")
        for block in range(ff_blocks):
            up_load(block).wait()

        def mid_sum(index):
            total = grad_second[:, strip(index)]
            for block in range(ff_blocks):
                total = total + mm(
                    slope[:, pl.ds(block * width, width)], ff_w[block, strip(index), :], NT
                )
            grad_second[:, strip(index)] = total

        def mid_back(index):
            here = pl.ds(pl.multiple_of(index * tile, tile), tile)
            grad = grad_second[here, :]
            normed = normed_one[here, :]
            total.add(4, grad * normed)
            total.add(5, grad)
            grad = normalize_back(
                grad * row_vector(first_gain), normed, inverse_one[here, pl.ds(0, 1)]
            )
            grad_first[here, :] = grad
            grad = grad.astype(bf16)
            low[here, :] = grad
            total.add(3, grad.astype(jnp.float32))

        loop(width // 256, mid_sum)
        tick("mid0")
        loop(rows // tile, mid_back)
        tick("mid1")
        for seq in range(seqs):
            padded[seq, pl.ds(HALO, tokens)] = mm(
                low[pl.ds(seq * tokens, tokens), :], out_w[...], NT
            ).astype(bf16)

        def out_grad(index):
            at = pl.multiple_of(index * 256, 256)
            store_block(2 * ff_blocks, at, mm(branch[:, pl.ds(at, 256)], low[...], TN))

        loop(width // 256, out_grad)
        staged(2 * ff_blocks)
        tick("out")
        out_copy.wait()

    narrow = pltpu.VMEM((rows, width), bf16)
    wide = pltpu.VMEM((rows, width), jnp.float32)
    hidden = pltpu.VMEM((rows, ff_blocks * width), bf16)
    pl.run_scoped(
        feed_forward,
        narrow, narrow, narrow, narrow,
        pltpu.VMEM((width, rows), bf16),
        pltpu.VMEM((width, rows), bf16),
        narrow, wide, wide,
        pltpu.VMEM((rows, PAIR), jnp.float32),
        pltpu.VMEM((width, width), bf16),
        pltpu.VMEM((ff_blocks, width, width), bf16),
        hidden, hidden,
        pltpu.VMEM((1, ff_blocks * width), jnp.float32),
    )
    first_row = (ff_blocks + 6) * pairs
    tap_row = first_row + 2 * pairs
    proxy_row = tap_row + 2 * pairs

    def attention(
        x, queries, keys, values, expo, keep, kernel_two, approx, kv_own, shares, proxies, rest, grad_qkv, turned, rows_of_weight,
    ):
        place = Place(batch_size, seq_size)
        loads = {}
        for index, (name, source, target) in enumerate(
            (
                ("queries", queries_in, queries),
                ("approx", approx_in, approx),
                ("kv_own", kv_own_in, kv_own),
                ("kernel_two", kernel_two_in, kernel_two),
                ("shares", shares_in, shares),
                ("values", values_in, values),
                ("expo", expo_in, expo),
                ("keys", keys_in, keys),
                ("keep", keep_in, keep),
                ("x", x_in, x),
                ("proxies", proxies_in, proxies),
            )
        ):
            loads[name] = pltpu.make_async_copy(source, target, load_sem.at[index])
            loads[name].start()
        zero_past(padded, tokens)
        halo = halo_copies(place, padded, tokens, *halo_sem)
        for copy in halo:
            copy.start()

        def spots(unit):
            seq, pair = lax.div(unit, pairs), lax.rem(unit, pairs)
            span = pl.ds(pl.multiple_of(seq * tokens, tokens), tokens)
            lanes = pl.ds(pl.multiple_of(pair * PAIR, PAIR), PAIR)
            return seq, span, lanes

        def paced(step, name, chunks=1):
            size = -(-units // chunks)
            for chunk, first in enumerate(range(0, units, size)):
                lax.fori_loop(first, min(first + size, units), step, 0, unroll=4)
                tick(f"{name}{chunk}")

        def mixed_parts(unit, carry):
            seq, span, lanes = spots(unit)
            grad = padded[seq, pl.ds(HALO, tokens), lanes]
            land_send[unit, 0] = join_heads(mm(kernel_one[unit].astype(bf16), grad)).astype(bf16)
            return carry

        for copy in early_loads():
            copy.wait()
        lax.fori_loop(0, units, mixed_parts, 0, unroll=6)
        for unit in range(units, seq_size * many):
            land_send[unit] = jnp.ones_like(land_send[unit])
        mixed_out = shared_out(
            place, land_send.at[:, 0], land_recv.at[:, :, 0], many, *mixed_sem
        )
        for copy in mixed_out:
            copy.start()
        tick("start")

        def first_grads(unit, carry):
            seq, span, lanes = spots(unit)
            weights = kernel_one[unit]
            grad = mm(spread_heads(mixed[unit]), padded[seq, pl.ds(HALO, tokens), lanes], NT)
            both = (weights * grad).reshape(2, SEG, tokens)
            both = jnp.broadcast_to(jnp.sum(both, axis=1, keepdims=True), both.shape)
            score_grad = (weights * (grad - both.reshape(2 * SEG, tokens))).astype(bf16)
            land_send[unit, 1] = join_heads(mm(score_grad, queries[span, lanes])).astype(bf16)
            rest[0, span, lanes] = mm(score_grad, spread_heads(land[unit, 1]), TN)
            return carry

        loads["queries"].wait()
        paced(first_grads, "first", 3)
        tick("wait_mixed")
        for copy in mixed_out:
            copy.wait()
        first_unit = place.seq * many
        for name in ("approx", "kv_own", "kernel_two", "shares"):
            loads[name].wait()
        kernels, approx_grads = [], []
        for own in range(many):
            total = land_send[first_unit + own, 0].astype(jnp.float32)
            for step in range(seq_size - 1):
                total = total + land_recv[step, own, 0].astype(jnp.float32)
            total = split(spread_heads(total))
            kv_mean = kv_own[own]
            kv_grad = join_heads(mm3(split(approx[own]), total, TN))
            approx_grads.append(mm3(split(spread_heads(kv_mean)), total, NT))
            kernels.append(kernel_two[own])
            dots = kv_grad * kv_mean
            first = first_head(dots.shape)
            dots = jnp.concatenate(
                [
                    jnp.sum(jnp.where(first, dots, 0.0), axis=1, keepdims=True),
                    jnp.sum(jnp.where(first, 0.0, dots), axis=1, keepdims=True),
                ],
                axis=0,
            )
            dots = row_of(dots)
            for slot in range(seq_size):
                share = shares[own, slot, pl.ds(0, 1), :]
                scaled = (kv_grad * join_heads(column(share))).astype(bf16)
                high, low = split(-dots * share)
                tail = jnp.concatenate([high, low, jnp.zeros((14, PAIR), bf16)], axis=0)
                acc_send[slot, own] = jnp.concatenate([scaled, tail], axis=0)
        acc_out = []
        for step in range(1, seq_size):
            acc_out.append(
                pltpu.make_async_remote_copy(
                    src_ref=acc_send.at[seq_size - step],
                    dst_ref=acc_all.at[pl.ds(first_unit, many)],
                    send_sem=acc_sem[0].at[step - 1],
                    recv_sem=acc_sem[1].at[step - 1],
                    device_id=place.seq_peer(step),
                    device_id_type=MESH_IDS,
                )
            )
        for copy in acc_out:
            copy.start()
        for own in range(many):
            acc_all[first_unit + own] = acc_send[0, own]
        tick("acc")
        for copy in halo:
            copy.wait()
        trim_halo(place, padded, tokens)
        tap_rows[...] = turned_taps(taps)
        for part in range(2):
            span = (part * pairs // 2, (part + 1) * pairs // 2)
            conv_rows(padded, tap_rows, rest.at[2], tokens, span)
            tick(f"conv{part}")
        loads["values"].wait()
        loads["expo"].wait()
        loads["keys"].wait()
        tick("wait_acc")
        for copy in acc_out:
            copy.wait()

        def third_grads(unit, carry):
            seq, span, lanes = spots(unit)
            packed = acc_all[unit]
            acc = spread_heads(packed[:SEG])
            tail = packed[SEG:].astype(jnp.float32)
            part = mm(acc, values[seq, pl.ds(HALO, tokens), lanes], NT)
            weights = expo[unit]
            score_grad = (weights * (part + column(tail[0:1] + tail[1:2]))).astype(bf16)
            land_send[unit, 0] = join_heads(mm(score_grad, keys[span, lanes])).astype(bf16)
            rest[1, span, lanes] = mm(score_grad, spread_heads(land[unit, 0]), TN)
            value_grad = mm(weights.astype(bf16), acc, TN) + rest[2, span, lanes]
            valid = positions(place, tokens, 0) < length_of(bounds, seq)
            grad_qkv[2, span, lanes] = jnp.where(valid, value_grad, 0.0).astype(bf16)
            return carry

        paced(third_grads, "third", 3)
        land_out = shared_out(place, land_send, land_recv, many, *land_sem)
        for copy in land_out:
            copy.start()
        loads["x"].wait()
        turned[...] = x[...].T

        def weight_grad(third, block):
            def step(index):
                at = pl.multiple_of(index * 256, 256)
                store_block(block, at, mm(turned[pl.ds(at, 256), :], grad_qkv[third]))

            loop(width // 256, step)

        def bias_grad(third, row):
            for pair in range(pairs):
                cols = grad_qkv[third, :, pl.ds(pair * PAIR, PAIR)].astype(jnp.float32)
                vec[pl.ds(row + pair, 1), :] = jnp.sum(cols, axis=0, keepdims=True)

        weight_grad(2, 2 * ff_blocks + 1)
        staged(2 * ff_blocks + 1)
        tick("value")
        loads["keep"].wait()
        loads["proxies"].wait()
        kernel_grads = newton_backward(kernels, approx_grads, keep, tick)
        extra = []
        for own in range(many):
            kernel, grad = kernels[own], kernel_grads[own]
            score_grad = split(
                kernel * (grad - jnp.sum(kernel * grad, axis=1, keepdims=True))
            )
            both = land[first_unit + own]
            left, right = spread_heads(both[0]), spread_heads(both[1])
            extra.append(
                (
                    join_heads(mm(score_grad[0], right) + mm(score_grad[1], right)),
                    join_heads(mm(score_grad[0], left, TN) + mm(score_grad[1], left, TN)),
                )
            )
        tick("wait_land")
        for copy in land_out:
            copy.wait()
        for own in range(many):
            unit = first_unit + own
            low, high = segment_edges(bounds, jnp.minimum(lax.div(unit, pairs), seqs - 1))
            for slot in range(2):
                total = land_send[unit, slot].astype(jnp.float32) + extra[own][slot]
                for step in range(seq_size - 1):
                    total = total + land_recv[step, own, slot].astype(jnp.float32)
                land_all[unit, slot] = (total / (high - low)).astype(bf16)
        land_back = passed_on(place, land_all, many, *land_back_sem)
        for copy in land_back:
            copy.start()
        tick("land")
        tick("wait_back")
        for copy in land_back:
            copy.wait()
        for seq in range(seqs):
            member = member_of(place, bounds, seq, tokens)
            span = pl.ds(seq * tokens, tokens)
            for pair in range(pairs):
                lanes = pl.ds(pair * PAIR, PAIR)
                both = land_all[seq * pairs + pair]
                for slot in range(2):
                    grad = (mm(member, both[slot], TN) + rest[slot, span, lanes]) * quarter
                    grad_qkv[slot, span, lanes] = grad.astype(bf16)
        tick("grads")
        weight_grad(0, 2 * ff_blocks + 2)
        weight_grad(1, 2 * ff_blocks + 3)
        staged(2 * ff_blocks + 2, 2 * ff_blocks + 3)
        tick("last")
        vec[...] = jnp.zeros_like(vec)
        for part in range(ff_blocks * pairs):
            vec[pl.ds(part, 1), :] = up_sums[:, pl.ds(part * PAIR, PAIR)]
        for row in range(6):
            for part in range(pairs):
                vec[pl.ds((ff_blocks + row) * pairs + part, 1), :] = sums[
                    pl.ds(row, 1), pl.ds(part * PAIR, PAIR)
                ]
        for own in range(many):
            unit = first_unit + own
            row = pl.ds(proxy_row + lax.rem(unit, pairs), 1)
            vec[row, :] = vec[row, :] + jnp.where(
                unit < units, proxies[own, pl.ds(0, 1), :], 0.0
            )
        bias_grad(0, first_row)
        bias_grad(2, first_row + pairs)
        for part in range(3):
            span = (part * pairs // 3, (part + 1) * pairs // 3)
            tap_grads(padded, values, vec, tap_row, tokens, span)
            tick(f"taps{part}")
        ticker.add("vec", vec_reduce(place, vec, slots, *vec_sem))

        def weight_load(tile):
            return pltpu.make_async_copy(
                qkv_weight.at[pl.ds(tile * PAIR, PAIR)],
                rows_of_weight.at[tile % 2],
                weight_sem.at[tile % 2],
            )

        weight_load(0).start()
        for tile in range(pairs):
            if tile + 1 < pairs:
                weight_load(tile + 1).start()
            weight_load(tile).wait()
            lanes = pl.ds(tile * PAIR, PAIR)
            total = grad_first[:, lanes]
            for third in range(3):
                total = total + mm(
                    grad_qkv[third], rows_of_weight[tile % 2, :, pl.ds(third * width, width)], NT
                )
            x[:, lanes] = total.astype(bf16)
            tick(f"input{tile}")
        out_copy = pltpu.make_async_copy(x, input_grad, load_sem.at[0])
        out_copy.start()
        ticker.drain(LAST)
        out_copy.wait()

    pl.run_scoped(
        attention,
        narrow, narrow, narrow,
        pltpu.VMEM(values_in.shape, bf16),
        pltpu.VMEM(expo_in.shape, jnp.float32),
        pltpu.VMEM(keep_in.shape, jnp.float32),
        *(
            pltpu.VMEM(ref.shape, jnp.float32)
            for ref in (kernel_two_in, approx_in, kv_own_in, shares_in, proxies_in)
        ),
        pltpu.VMEM((2 + 1, rows, width), jnp.float32),
        pltpu.VMEM((3, rows, width), bf16),
        pltpu.VMEM((width, rows), bf16),
        pltpu.VMEM((2, PAIR, 3 * width), bf16),
    )


Z_FIRST = (0,)


class Piece:
    def __init__(self, blocks, start, rows, orders, slots):
        self.blocks, self.start, self.rows, self.orders, self.slots = (
            blocks, start, rows, orders, slots,
        )


def make_plan(sizes, block_count, width):
    split_rows = 16 * sizes["x"] * sizes["y"] * sizes["z"]
    orders = (("x", "y", "z"), ("y", "x", "z"))
    z_first = (("z0", "z1", "x", "y"), ("z0", "z1", "y", "x"))
    if 2 * width % (2 * split_rows) == 0:
        counts = [2] * (block_count // 2)
    else:
        orders = orders[:1]
        z_first = z_first[:1]
        counts = [8, block_count - 8] if 8 * width % split_rows == 0 else [block_count]
    plan, block, slot = [], 0, 0
    for count in counts:
        rows = -(-count * width // (len(orders) * split_rows)) * len(orders) * split_rows
        own = z_first if len(plan) in Z_FIRST else orders
        need = Reduce.slots(sizes, own, rows)
        plan.append(
            Piece(list(range(block, block + count)), block * width, rows, own, pl.ds(slot, need))
        )
        block += count
        slot += need
    return plan, slot


def layer_back(
    x, grad_out, branch, out_weight, up_weight, down_weight, qkv_weight, saved, bounds, taps,
    vectors, batch_size, seq_size, seqs,
):
    (
        queries, keys, values, kernel_one, expo, land, mixed, _, kernel_two, approx, keep,
        kv_own, shares, proxies,
    ) = saved
    rows, width = x.shape
    tokens = rows // seqs
    pairs = width // PAIR
    own = -(-seqs * pairs // seq_size)
    owned = seq_size * own
    sizes = axis_sizes(batch_size, seq_size)
    ff_blocks = down_weight.shape[0] // width
    plan, slot_rows = make_plan(sizes, 2 * ff_blocks + 4, width)
    pieces, stage_rows = len(plan), plan[-1].start + plan[-1].rows
    parts = len(plan[0].orders)
    copies = max(Reduce.copies(sizes, piece.orders) for piece in plan)
    vec_axes = ("core", "x", "y", "z")
    vec_steps = sum(sizes[axis] - 1 for axis in vec_axes)
    vec_shape = (-(-((ff_blocks + 11) * pairs) // 8) * 8, PAIR)
    f32, bf16 = jnp.float32, jnp.bfloat16
    vmem = pl.BlockSpec(memory_space=pltpu.VMEM)
    anywhere = pl.BlockSpec(memory_space=pl.ANY)
    sems = pltpu.SemaphoreType.DMA
    pair_sems = (sems((seq_size - 1,)),) * 2
    return pl.pallas_call(
        partial(back_kernel, batch_size, seq_size, seqs, tokens, own, plan),
        out_shape=(
            jax.ShapeDtypeStruct((rows, width), bf16),
            jax.ShapeDtypeStruct((rows, width), bf16),
            jax.ShapeDtypeStruct((2, stage_rows, HALF), bf16),
            jax.ShapeDtypeStruct(vec_shape, f32),
        ),
        in_specs=[anywhere] * 20 + [vmem] * (2 + len(vectors)),
        out_specs=(anywhere, anywhere, anywhere, vmem),
        scratch_shapes=[
            pltpu.VMEM((2, stage_rows, HALF), bf16),
            pltpu.VMEM((stage_rows, HALF), bf16),
            pltpu.VMEM((parts, slot_rows, HALF), bf16),
            pltpu.VMEM((sum(sizes[axis] for axis in vec_axes), *vec_shape), f32),
            pltpu.VMEM(values.shape, bf16),
            pltpu.VMEM((rows, width), f32),
            pltpu.VMEM((16, 2 * BLOCK), f32),
            pltpu.VMEM((8, width), f32),
            pltpu.VMEM((1, ff_blocks * width), f32),
            pltpu.VMEM((seq_size, own, SEG + 16, PAIR), bf16),
            pltpu.VMEM((owned, SEG + 16, PAIR), bf16),
            pltpu.VMEM((owned, 2, SEG, PAIR), bf16),
            pltpu.VMEM((seq_size - 1, own, 2, SEG, PAIR), bf16),
            pltpu.VMEM((owned, 2, SEG, PAIR), bf16),
            pltpu.VMEM(kernel_one.shape, f32),
            pltpu.VMEM(mixed.shape, bf16),
            pltpu.VMEM(land.shape, bf16),
            sems((14,)),
            sems((ff_blocks,)),
            sems((pieces, copies)),
            sems((pieces, copies)),
            pltpu.SemaphoreType.REGULAR((pieces,)),
            (sems((vec_steps,)),) * 2,
            sems((pieces, 2)),
            (sems((2,)),) * 2,
            pair_sems,
            pair_sems,
            pair_sems,
            pair_sems,
        ],
        compiler_params=pltpu.CompilerParams(
            collective_id=0, has_side_effects=True, vmem_limit_bytes=63 * 2**20
        ),
        name="layer_back",
    )(
        x, grad_out, branch, out_weight, up_weight, down_weight, qkv_weight,
        queries, keys, values, kernel_one, expo, keep, land, mixed, kernel_two, approx, kv_own,
        shares, proxies, bounds, taps, *vectors,
    )


def finish_kernel(
    heads, scale, gathered, vec, layer_in, input_in,
    layer_out, input_grad, qkv_grad, query_bias_grad, value_bias_grad, tap_grad, out_grad,
    out_bias_grad, first_gain_grad, first_shift_grad, up_grad, up_bias_grad, down_grad,
    down_bias_grad, second_gain_grad, second_shift_grad, condition,
    narrow, wide, rows_through, in_sem, out_sem, pass_sem,
):
    width = down_grad.shape[1]
    pairs = width // PAIR
    blocks = down_grad.shape[0] // width
    spots = [(down_grad, block * width, 0) for block in range(blocks)]
    spots += [(up_grad, 0, block * width) for block in range(blocks)]
    spots += [(out_grad, 0, 0), (qkv_grad, 0, 2 * width), (qkv_grad, 0, 0), (qkv_grad, 0, width)]
    taken = [
        pltpu.make_async_copy(source, rows_through.at[index], pass_sem.at[index])
        for index, source in enumerate((layer_in, input_in))
    ]
    passed = [
        pltpu.make_async_copy(rows_through.at[index], target, pass_sem.at[index])
        for index, target in enumerate((layer_out, input_grad))
    ]
    slots, rows, _ = wide.shape
    tiles = [
        (target, row + part * rows, col, block * width + part * rows)
        for block, (target, row, col) in enumerate(spots)
        for part in range(width // rows)
    ]

    def fetch(index):
        return pltpu.make_async_copy(
            gathered.at[:, pl.ds(tiles[index][3], rows)],
            narrow.at[index % slots],
            in_sem.at[index % slots],
        )

    def put(index):
        target, row, col, _ = tiles[index]
        return pltpu.make_async_copy(
            wide.at[index % slots],
            target.at[pl.ds(row, rows), pl.ds(col, width)],
            out_sem.at[index % slots],
        )

    for index in range(slots):
        fetch(index).start()
    for copy in taken:
        copy.start()
    row = 0
    for target in (
        up_bias_grad, down_bias_grad, second_gain_grad, second_shift_grad, out_bias_grad,
        first_gain_grad, first_shift_grad, query_bias_grad, value_bias_grad,
    ):
        count = target.shape[0] // PAIR
        target[...] = vec[pl.ds(row, count), :].reshape(target.shape)
        row += count
    tap_grad[...] = vec[pl.ds(row, heads), pl.ds(0, tap_grad.shape[1])]
    proxy = vec[pl.ds(row + heads, pairs), :] * scale
    lanes = lax.broadcasted_iota(jnp.int32, (1, PAIR), 1)
    means = jnp.zeros((1, PAIR), jnp.float32)
    for pair in range(pairs):
        for head in range(2):
            value = proxy[pair : pair + 1, head * SEG : head * SEG + 1]
            means = means + jnp.where(lanes == 2 * pair + head, value, 0.0)
    condition[...] = means[:, :heads].reshape(heads)
    for copy in taken:
        copy.wait()
    for copy in passed:
        copy.start()
    for index in range(len(tiles)):
        slot = index % slots
        fetch(index).wait()
        if index >= slots:
            put(index - slots).wait()
        for half in range(2):
            wide[slot, :, pl.ds(half * HALF, HALF)] = narrow[slot, half].astype(jnp.float32)
        put(index).start()
        if index + slots < len(tiles):
            fetch(index + slots).start()
    for index in range(len(tiles) - slots, len(tiles)):
        put(index).wait()
    for copy in passed:
        copy.wait()


def finish(gathered, vec, layer_out, input_grad, shapes, scale):
    width = layer_out.shape[1]
    any_spec = pl.BlockSpec(memory_space=pl.ANY)
    vmem = pl.BlockSpec(memory_space=pltpu.VMEM)
    outs = [jax.ShapeDtypeStruct(shape, jnp.bfloat16) for shape in (layer_out.shape,) * 2]
    outs += [jax.ShapeDtypeStruct(shape, jnp.float32) for shape in shapes]
    return pl.pallas_call(
        partial(finish_kernel, shapes[3][0], scale),
        out_shape=tuple(outs),
        in_specs=[any_spec, vmem, any_spec, any_spec],
        out_specs=tuple(
            any_spec if out.shape[0] * math.prod(out.shape[1:]) >= width * width // 2 else vmem
            for out in outs
        ),
        scratch_shapes=[
            pltpu.VMEM((SLOTS, 2, FINISH_ROWS, HALF), jnp.bfloat16),
            pltpu.VMEM((SLOTS, FINISH_ROWS, width), jnp.float32),
            pltpu.VMEM((2, *layer_out.shape), jnp.bfloat16),
            pltpu.SemaphoreType.DMA((SLOTS,)),
            pltpu.SemaphoreType.DMA((SLOTS,)),
            pltpu.SemaphoreType.DMA((2,)),
        ],
        compiler_params=pltpu.CompilerParams(vmem_limit_bytes=62 * 2**20),
        name="finish",
    )(gathered, vec, layer_out, input_grad)


SLOTS = 4
FINISH_ROWS = 768


def body(
    hidden_in,
    seg_bounds,
    qkv_weight,
    query_bias,
    value_bias,
    conv_taps,
    out_weight,
    out_bias,
    first_gain,
    first_shift,
    up_weight,
    up_bias,
    down_weight,
    down_bias,
    second_gain,
    second_shift,
    grad_out,
):
    seq_count, tok_count, model_width = hidden_in.shape
    head_count = conv_taps.shape[0]
    row_total = seq_count * tok_count
    batch_size, seq_size = lax.axis_size("batch"), lax.axis_size("seq")
    input_rows = hidden_in.reshape(row_total, model_width)
    saved = attend(
        input_rows, seg_bounds, qkv_weight, query_bias, value_bias, conv_taps,
        batch_size, seq_size, seq_count,
    )
    layer_out, input_grad, gathered, vec = layer_back(
        input_rows,
        grad_out.reshape(row_total, model_width),
        saved[7],
        out_weight,
        up_weight,
        down_weight,
        qkv_weight,
        saved,
        seg_bounds,
        conv_taps,
        (out_bias, first_gain, first_shift, up_bias, down_bias, second_gain, second_shift),
        batch_size,
        seq_size,
        seq_count,
    )

    shapes = (
        qkv_weight.shape,
        query_bias.shape,
        value_bias.shape,
        conv_taps.shape,
        out_weight.shape,
        out_bias.shape,
        first_gain.shape,
        first_shift.shape,
        up_weight.shape,
        up_bias.shape,
        down_weight.shape,
        down_bias.shape,
        second_gain.shape,
        second_shift.shape,
        (head_count,),
    )
    layer_out, input_grad, *grads = finish(
        gathered, vec, layer_out, input_grad, shapes, 1.0 / (batch_size * seq_count)
    )
    return (
        layer_out.reshape(hidden_in.shape),
        input_grad.reshape(hidden_in.shape),
        *grads,
    )


def solution(mesh):
    placed = (
        P("batch", "seq", None),
        P("batch", None),
        P(),
        P(),
        P(),
        P(),
        P(),
        P(),
        P(),
        P(),
        P(),
        P(),
        P(),
        P(),
        P(),
        P(),
        P("batch", "seq", None),
    )
    return jax.shard_map(
        body,
        mesh=mesh,
        in_specs=placed,
        out_specs=(
            P("batch", "seq", None),
            P("batch", "seq", None),
            P(),
            P(),
            P(),
            P(),
            P(),
            P(),
            P(),
            P(),
            P(),
            P(),
            P(),
            P(),
            P(),
            P(),
            P(),
        ),
        check_vma=False,
    )
```

```python
import math
from functools import partial

import jax
import jax.numpy as jnp
from jax import lax
from jax.experimental import pallas as pl
from jax.experimental.pallas import tpu as pltpu
from jax.sharding import PartitionSpec as P

epsilon = 1e-05
MESH_IDS = pl.DeviceIdType.MESH
HALF = 384
LANES = 128


def plane_sides(count):
    wide = max(d for d in range(1, math.isqrt(count) + 1) if count % d == 0)
    return wide, count // wide


def axis_sizes(batch_size, seq_size):
    x_size, y_size = plane_sides(seq_size)
    z_size = batch_size // 2
    z_low = 2 if z_size % 2 == 0 else 1
    return {
        "core": 2, "x": x_size, "y": y_size, "z": z_size, "z0": z_low, "z1": z_size // z_low,
    }


class Place:
    def __init__(self, batch_size, seq_size):
        x_size, y_size = plane_sides(seq_size)
        self.sizes = axis_sizes(batch_size, seq_size)
        batch = lax.axis_index("batch")
        seq = lax.axis_index("seq")
        z_low = self.sizes["z0"]
        self.at = {
            "core": lax.rem(batch, 2),
            "z": lax.div(batch, 2),
            "z0": lax.rem(lax.div(batch, 2), z_low),
            "z1": lax.div(batch, 2 * z_low),
            "x": lax.rem(seq, x_size),
            "y": lax.div(seq, x_size),
        }
        self.seq_size = seq_size
        self.seq = seq
        self.batch = batch

    def peer_index(self, axis, step):
        size = self.sizes[axis]
        return lax.rem(self.at[axis] + step, size)

    def device(self, **moved):
        spot = {**self.at, **moved}
        if "z0" in moved or "z1" in moved:
            spot["z"] = spot["z1"] * self.sizes["z0"] + spot["z0"]
        return (spot["z"] * 2 + spot["core"], spot["y"] * self.sizes["x"] + spot["x"])

    def peers(self, axes):
        for axis in axes:
            for step in range(1, self.sizes[axis]):
                yield self.device(**{axis: self.peer_index(axis, step)})

    def seq_peer(self, step):
        return (self.batch, lax.rem(self.seq + step, self.seq_size))


def greet(devices):
    barrier = pltpu.get_barrier_semaphore()
    devices = list(devices)
    for device in devices:
        pl.semaphore_signal(barrier, inc=1, device_id=device, device_id_type=MESH_IDS)
    return lambda: pl.semaphore_wait(barrier, len(devices))


def tile_rows(rows):
    return max(t for t in (96, 64, 48, 32, 16) if rows % t == 0)


def add_rows(out_ref, in_ref, at, parts, rows):
    tile = tile_rows(rows)

    def step(index, carry):
        start = pl.multiple_of(at + index * tile, 16)
        total = in_ref[pl.ds(start, tile), :].astype(jnp.float32)
        for ref, first in parts:
            total = total + ref[pl.ds(pl.multiple_of(first + index * tile, 16), tile), :].astype(
                jnp.float32
            )
        out_ref[pl.ds(start, tile), :] = total.astype(out_ref.dtype)
        return carry

    lax.fori_loop(0, rows // tile, step, 0)


class Reduce:
    def __init__(
        self, number, place, orders, stage, whole, recv, send_sem, recv_sem, free_sem, rows
    ):
        self.number, self.make_place, self.orders = number, place, orders
        self.stage, self.whole, self.recv = stage, whole, recv
        self.send_sem, self.recv_sem, self.free_sem = send_sem, recv_sem, free_sem
        self.part = rows // len(orders)

    @staticmethod
    def slots(sizes, orders, rows):
        need = []
        for order in orders:
            size, slot = rows // len(orders), 0
            for axis in order:
                size //= sizes[axis]
                slot += (sizes[axis] - 1) * size
            need.append(slot)
        return max(need)

    @staticmethod
    def copies(sizes, orders):
        return 2 + 2 * sum(sizes[axis] - 1 for order in orders for axis in order)

    def level_of(self, place, half, level):
        base, size, slot = half * self.part, self.part, 0
        order = self.orders[half]
        sem = 2 + 2 * half * sum(place.sizes[axis] - 1 for axis in order)
        for axis in order[:level]:
            count = place.sizes[axis]
            size //= count
            slot += (count - 1) * size
            sem += 2 * (count - 1)
            base = base + place.at[axis] * size
        count = place.sizes[order[level]]
        return order[level], count, base, size // count, slot, sem

    def copy(self, index, src, dst, device):
        return pltpu.make_async_remote_copy(
            src_ref=src,
            dst_ref=dst,
            send_sem=self.send_sem.at[self.number, index],
            recv_sem=self.recv_sem.at[self.number, index],
            device_id=device,
            device_id_type=MESH_IDS,
        )

    @staticmethod
    def rows_of(ref, start, rows):
        return ref.at[pl.ds(pl.multiple_of(start, 16), rows)]

    def scatter(self, half, level):
        place = self.make_place()
        axis, count, base, chunk, slot, sem = self.level_of(place, half, level)
        mine = self.stage.at[place.at["core"]]
        copies = []
        for step in range(1, count):
            peer = place.peer_index(axis, step)
            copies.append(
                self.copy(
                    sem + step - 1,
                    self.rows_of(mine, base + peer * chunk, chunk),
                    self.recv.at[half, pl.ds(slot + (step - 1) * chunk, chunk)],
                    place.device(**{axis: peer}),
                )
            )
        return copies

    def spread(self, half, level):
        place = self.make_place()
        axis, count, base, chunk, slot, sem = self.level_of(place, half, level)
        here = self.rows_of(self.whole, base + place.at[axis] * chunk, chunk)
        return [
            self.copy(
                sem + count - 1 + step - 1,
                here,
                here,
                place.device(**{axis: place.peer_index(axis, step)}),
            )
            for step in range(1, count)
        ]

    def add_level(self, half, level):
        place = self.make_place()
        axis, count, base, chunk, slot, _ = self.level_of(place, half, level)
        mine = self.stage.at[place.at["core"]]
        add_rows(
            self.whole if level == len(self.orders[half]) - 1 else mine,
            mine,
            base + place.at[axis] * chunk,
            [(self.recv.at[half], slot + k * chunk) for k in range(count - 1)],
            chunk,
        )

    def core_out(self):
        place = self.make_place()
        core = place.at["core"]
        return self.copy(0, self.stage.at[1 - core], self.whole, place.device(core=1 - core))

    def core_back(self):
        place = self.make_place()
        core = place.at["core"]
        return self.copy(1, self.whole, self.stage.at[core], place.device(core=1 - core))

    def run(self):
        halves = range(len(self.orders))
        self.core_out().start()
        yield
        self.core_out().wait()
        place = self.make_place()
        other = place.device(core=1 - place.at["core"])
        pl.semaphore_signal(
            self.free_sem.at[self.number], inc=1, device_id=other, device_id_type=MESH_IDS
        )
        mine = self.stage.at[place.at["core"]]
        for half in halves:
            start = half * self.part
            add_rows(mine, mine, start, [(self.whole, start)], self.part)
            for copy in self.scatter(half, 0):
                copy.start()
        last = len(self.orders[0]) - 1
        for level in range(last + 1):
            yield
            for half in halves:
                for copy in self.scatter(half, level):
                    copy.wait()
                self.add_level(half, level)
                later = self.scatter if level < last else self.spread
                for copy in later(half, min(level + 1, last)):
                    copy.start()
        for level in reversed(range(last + 1)):
            yield
            for half in halves:
                for copy in self.spread(half, level):
                    copy.wait()
                for copy in self.spread(half, level - 1) if level else ():
                    copy.start()
        pl.semaphore_wait(self.free_sem.at[self.number], 1)
        self.core_back().start()
        yield
        self.core_back().wait()


def vec_reduce(place, acc, slots, send_sem, recv_sem):
    sem = 0
    level = 0
    for axis in ("core", "x", "y", "z"):
        count = place.sizes[axis]
        copies = []
        here = place.at[axis]
        for step in range(1, count):
            copies.append(
                pltpu.make_async_remote_copy(
                    src_ref=acc,
                    dst_ref=slots.at[level + here],
                    send_sem=send_sem.at[sem],
                    recv_sem=recv_sem.at[sem],
                    device_id=place.device(**{axis: place.peer_index(axis, step)}),
                    device_id_type=MESH_IDS,
                )
            )
            sem += 1
        for copy in copies:
            copy.start()
        slots[level + here] = acc[...]
        yield
        for copy in copies:
            copy.wait()
        total = slots[level]
        for index in range(1, count):
            total = total + slots[level + index]
        acc[...] = total
        level += count


SEG = 64
PAIR = 128
HALO = 16
BLOCK = 128
FAR = -1e30
NT = ((1,), (1,))
TN = ((0,), (0,))
NN = ((1,), (0,))


def mm(left, right, dims=NN):
    return lax.dot_general(left, right, (dims, ((), ())), preferred_element_type=jnp.float32)


def split(array):
    high = array.astype(jnp.bfloat16)
    return high, (array - high.astype(jnp.float32)).astype(jnp.bfloat16)


def thirds(array):
    high = array.astype(jnp.bfloat16)
    middle = (array - high.astype(jnp.float32)).astype(jnp.bfloat16)
    rest = array - high.astype(jnp.float32) - middle.astype(jnp.float32)
    return high, middle, rest.astype(jnp.bfloat16)


def mm3(left, right, dims=NN):
    left_high, left_low = left
    right_high, right_low = right
    (left_dim,), (right_dim,) = dims
    return mm(
        jnp.concatenate([left_high, left_high, left_low], axis=left_dim),
        jnp.concatenate([right_high, right_low, right_high], axis=right_dim),
        dims,
    )


def eye_mask(size):
    rows = lax.broadcasted_iota(jnp.int32, (size, size), 0)
    return rows == lax.broadcasted_iota(jnp.int32, (size, size), 1)


def column(row):
    return jnp.sum(jnp.where(eye_mask(row.shape[1]), row, 0.0), axis=1, keepdims=True)


def row_of(col):
    return jnp.sum(jnp.where(eye_mask(col.shape[0]), col, 0.0), axis=0, keepdims=True)


def first_head(shape):
    return lax.broadcasted_iota(jnp.int32, shape, len(shape) - 1) < SEG


def spread_heads(pair):
    first = first_head(pair.shape)
    zero = jnp.zeros_like(pair)
    return jnp.concatenate([jnp.where(first, pair, zero), jnp.where(first, zero, pair)], axis=0)


def join_heads(blocks):
    shape = (SEG, PAIR)
    return jnp.where(
        first_head(shape),
        jnp.broadcast_to(blocks[:SEG], shape),
        jnp.broadcast_to(blocks[SEG:], shape),
    )


def heads_sum(col):
    first = jnp.sum(col[:SEG], axis=0, keepdims=True)
    second = jnp.sum(col[SEG:], axis=0, keepdims=True)
    return jnp.concatenate(
        [jnp.broadcast_to(first, (SEG, 1)), jnp.broadcast_to(second, (SEG, 1))], axis=0
    )


def shared_out(place, source, target, many, send_sem, recv_sem):
    copies = []
    for step in range(1, place.seq_size):
        device = place.seq_peer(step)
        copies.append(
            pltpu.make_async_remote_copy(
                src_ref=source.at[pl.ds(device[1] * many, many)],
                dst_ref=target.at[step - 1],
                send_sem=send_sem.at[step - 1],
                recv_sem=recv_sem.at[step - 1],
                device_id=device,
                device_id_type=MESH_IDS,
            )
        )
    return copies


def passed_on(place, array, many, send_sem, recv_sem):
    copies = []
    here = array.at[pl.ds(place.seq * many, many)]
    for step in range(1, place.seq_size):
        copies.append(
            pltpu.make_async_remote_copy(
                src_ref=here,
                dst_ref=here,
                send_sem=send_sem.at[step - 1],
                recv_sem=recv_sem.at[step - 1],
                device_id=place.seq_peer(step),
                device_id_type=MESH_IDS,
            )
        )
    return copies


def halo_copies(place, padded, tokens, send_sem, recv_sem):
    copies = []
    for index, (step, first, there) in enumerate(
        ((1, tokens, 0), (place.seq_size - 1, HALO, tokens + HALO))
    ):
        copies.append(
            pltpu.make_async_remote_copy(
                src_ref=padded.at[:, pl.ds(first, HALO)],
                dst_ref=padded.at[:, pl.ds(there, HALO)],
                send_sem=send_sem.at[index],
                recv_sem=recv_sem.at[index],
                device_id=place.seq_peer(step),
                device_id_type=MESH_IDS,
            )
        )
    return copies


def trim_halo(place, padded, tokens):
    zero = jnp.zeros((padded.shape[0], HALO, padded.shape[2]), padded.dtype)
    low, high = pl.ds(0, HALO), pl.ds(tokens + HALO, HALO)
    padded[:, low] = jnp.where(place.seq > 0, padded[:, low], zero)
    padded[:, high] = jnp.where(place.seq < place.seq_size - 1, padded[:, high], zero)


def zero_past(padded, tokens):
    past = tokens + 2 * HALO
    rest = padded.shape[1] - past
    padded[:, pl.ds(past, rest)] = jnp.zeros(
        (padded.shape[0], rest, padded.shape[2]), padded.dtype
    )


def band(taps):
    wide = jnp.broadcast_to(taps, (BLOCK, 2 * BLOCK))
    return pltpu.roll(wide, 0, 1, stride=1, stride_axis=0).astype(jnp.bfloat16)


def tap_lanes(taps):
    heads, count = taps.shape
    wide = jnp.concatenate(
        [taps[...], jnp.zeros((heads, 2 * BLOCK - count), jnp.float32)], axis=1
    )
    return jnp.concatenate([wide, jnp.zeros((16 - heads, 2 * BLOCK), jnp.float32)], axis=0)


def turned_taps(taps):
    shape = (2 * BLOCK, 2 * BLOCK)
    ends = lax.broadcasted_iota(jnp.int32, shape, 0) + lax.broadcasted_iota(jnp.int32, shape, 1)
    turn = jnp.where(ends == taps.shape[1] - 1, 1.0, 0.0).astype(jnp.bfloat16)
    return mm(tap_lanes(taps).astype(jnp.bfloat16), turn)


def conv_rows(padded, taps, out, tokens, span=None):
    seqs, _, width = padded.shape

    def step(pair, carry):
        lanes = pl.ds(pl.multiple_of(pair * PAIR, PAIR), PAIR)
        first = band(taps[pl.ds(2 * pair, 1), :])
        second = band(taps[pl.ds(2 * pair + 1, 1), :])
        for seq in range(seqs):
            for block in range(tokens // BLOCK):
                window = padded[seq, pl.ds(block * BLOCK, 2 * BLOCK), lanes]
                both = jnp.where(
                    first_head((BLOCK, PAIR)), mm(first, window), mm(second, window)
                )
                out[pl.ds(seq * tokens + block * BLOCK, BLOCK), lanes] = both
        return carry

    lax.fori_loop(*(span or (0, width // PAIR)), step, 0, unroll=3)


def segment_edges(bounds, seq):
    low = column(bounds[pl.ds(seq, 1), pl.ds(0, SEG)].astype(jnp.float32))
    high = column(bounds[pl.ds(seq, 1), pl.ds(1, SEG)].astype(jnp.float32))
    return low, high


def positions(place, tokens, axis):
    shape = (tokens, 1) if axis == 0 else (1, tokens)
    return (place.seq * tokens + lax.broadcasted_iota(jnp.int32, shape, axis)).astype(jnp.float32)


def member_of(place, bounds, seq, tokens):
    low, high = segment_edges(bounds, seq)
    where = positions(place, tokens, 1)
    return jnp.where((where >= low) & (where < high), 1.0, 0.0).astype(jnp.bfloat16)


def length_of(bounds, seq):
    return bounds[pl.ds(seq, 1), pl.ds(SEG, 1)].astype(jnp.float32)


def newton_forward(kernels, keep):
    eye = jnp.where(eye_mask(PAIR), 1.0, 0.0)
    approx = []
    for kernel in kernels:
        fro = heads_sum(jnp.sum(kernel * kernel, axis=1, keepdims=True))
        approx.append(kernel.T / fro)
    halves = [split(kernel) for kernel in kernels]
    units = range(len(kernels))
    for step in range(6):
        wide = [split(a) for a in approx]
        product = [mm3(halves[u], wide[u]) for u in units]
        lefts = [split(p) for p in product]
        inner = [15.0 * eye - mm3(lefts[u], split(7.0 * eye - product[u])) for u in units]
        outer = [13.0 * eye - mm3(lefts[u], split(inner[u])) for u in units]
        for u in units:
            for slot, value in enumerate((approx[u], product[u], inner[u], outer[u])):
                keep[u, step, slot] = value
        approx = [0.25 * mm3(wide[u], split(outer[u])) for u in units]
    return approx


def attend_kernel(
    batch_size, seq_size, seqs, tokens, many,
    x_in, weight_in, bounds, query_bias, value_bias, taps, *refs
):
    outs, refs = refs[:14], refs[14:]
    saved, refs = refs[:14], refs[14:]
    (
        queries, keys, values, kernel_one, expo, land, mixed, branch, kernel_two, approx_out,
        keep, kv_own, shares, proxies,
    ) = saved
    (
        x, weight, load_sem, save_sem, land_send, land_recv, kv_send, kv_recv, conv, tap_rows, biases,
        land_sem, land_back_sem, kv_sem, mixed_sem, halo_sem,
    ) = refs
    place = Place(batch_size, seq_size)
    width = x.shape[1]
    loads = [pltpu.make_async_copy(x_in, x, load_sem.at[3])]
    for third in range(3):
        lanes = pl.ds(third * width, width)
        loads.append(
            pltpu.make_async_copy(
                weight_in.at[:, lanes], weight.at[:, lanes], load_sem.at[third]
            )
        )
    for copy in loads:
        copy.start()
    saves = []

    def save(*names):
        for ref in names:
            index = [ref is other for other in saved].index(True)
            copy = pltpu.make_async_copy(ref, outs[index], save_sem.at[index])
            copy.start()
            saves.append(copy)

    pairs = width // PAIR
    units = seqs * pairs
    wait_greet = greet(place.seq_peer(step) for step in range(1, seq_size))
    quarter = float(SEG) ** -0.25

    tap_rows[...] = tap_lanes(taps)
    biases[...] = jnp.zeros_like(biases)
    biases[pl.ds(0, 1), :] = query_bias[...].reshape(1, width)
    biases[pl.ds(2, 1), :] = value_bias[...].reshape(1, width)

    def project(out_ref, third):
        def step(tile, carry):
            lanes = pl.ds(pl.multiple_of(third * width + tile * 256, 256), 256)
            here = pl.ds(pl.multiple_of(tile * 256, 256), 256)
            rows = mm(x[...], weight[:, lanes]) + biases[pl.ds(third, 1), here]
            if third < 2:
                out_ref[:, here] = (rows * quarter).astype(jnp.bfloat16)
            else:
                for seq in range(seqs):
                    valid = positions(place, tokens, 0) < length_of(bounds, seq)
                    out_ref[seq, pl.ds(HALO, tokens), here] = jnp.where(
                        valid, rows[seq * tokens : (seq + 1) * tokens], 0.0
                    ).astype(jnp.bfloat16)
            return carry

        loads[1 + third].wait()
        lax.fori_loop(0, width // 256, step, 0)

    def send_sums(slot, rows):
        for seq in range(seqs):
            member = member_of(place, bounds, seq, tokens)
            sums = mm(member, rows[pl.ds(seq * tokens, tokens), :])
            for pair in range(pairs):
                land_send[seq * pairs + pair, slot] = sums[:, pair * PAIR : (pair + 1) * PAIR]
        if slot == 0:
            wait_greet()
        copies = shared_out(
            place, land_send.at[:, slot], land_recv.at[:, :, slot], many, *land_sem[slot]
        )
        for copy in copies:
            copy.start()
        return copies

    for unit in range(units, seq_size * many):
        land_send[unit] = jnp.ones_like(land_send[unit])
        kv_send[unit] = jnp.ones_like(kv_send[unit])
    loads[0].wait()
    project(queries, 0)
    land_out = send_sums(0, queries)
    project(keys, 1)
    land_out += send_sums(1, keys)
    save(queries, keys)
    project(values, 2)
    halo = halo_copies(place, values, tokens, *halo_sem)
    for copy in halo:
        copy.start()
    zero_past(values, tokens)
    for copy in land_out:
        copy.wait()
    first_unit = place.seq * many
    for own in range(many):
        unit = first_unit + own
        total = land_send[unit]
        for step in range(seq_size - 1):
            total = total + land_recv[step, own]
        low, high = segment_edges(bounds, jnp.minimum(lax.div(unit, pairs), seqs - 1))
        land[unit] = (total / (high - low)).astype(jnp.bfloat16)
    land_back = passed_on(place, land, many, *land_back_sem)
    for copy in land_back:
        copy.start()
    for copy in halo:
        copy.wait()
    trim_halo(place, values, tokens)
    save(values)
    conv_rows(values, tap_rows, conv, tokens)
    for copy in land_back:
        copy.wait()
    save(land)

    def spots(unit):
        seq, pair = lax.div(unit, pairs), lax.rem(unit, pairs)
        rows = pl.ds(pl.multiple_of(seq * tokens, tokens), tokens)
        lanes = pl.ds(pl.multiple_of(pair * PAIR, PAIR), PAIR)
        return seq, rows, lanes

    def third_scores(unit, carry):
        seq, rows, lanes = spots(unit)
        score = mm(spread_heads(land[unit, 0]), keys[rows, lanes], NT)
        valid = positions(place, tokens, 1) < length_of(bounds, seq)
        score = jnp.where(valid, score, FAR)
        top = jnp.max(score, axis=1, keepdims=True)
        weights = jnp.exp(score - top)
        expo[unit] = weights
        total = jnp.sum(weights, axis=1, keepdims=True)
        part = mm(weights.astype(jnp.bfloat16), values[seq, pl.ds(HALO, tokens), lanes])
        kv_send[unit, pl.ds(0, SEG)] = join_heads(part).astype(jnp.bfloat16)
        kv_send[unit, pl.ds(SEG, 16)] = jnp.concatenate(
            [*thirds(row_of(top)), *thirds(row_of(total)), jnp.zeros((10, PAIR), jnp.bfloat16)],
            axis=0,
        )
        return carry

    lax.fori_loop(0, units, third_scores, 0, unroll=6)
    kv_out = shared_out(place, kv_send, kv_recv, many, *kv_sem)
    for copy in kv_out:
        copy.start()
    save(expo)

    kernels = []
    same = (
        lax.broadcasted_iota(jnp.int32, (PAIR, PAIR), 0) < SEG
    ) == first_head((PAIR, PAIR))
    for own in range(many):
        both = land[first_unit + own]
        score = jnp.where(same, mm(spread_heads(both[0]), spread_heads(both[1]), NT), FAR)
        weights = jnp.exp(score - jnp.max(score, axis=1, keepdims=True))
        kernels.append(weights / jnp.sum(weights, axis=1, keepdims=True))
        kernel_two[own] = kernels[own]
    approx = newton_forward(kernels, keep)
    for own in range(many):
        approx_out[own] = approx[own]
        proxy = jnp.sqrt(
            heads_sum(jnp.sum(kernels[own] * kernels[own], axis=1, keepdims=True))
        ) * jnp.sqrt(heads_sum(jnp.sum(approx[own] * approx[own], axis=1, keepdims=True)))
        proxies[own] = jnp.broadcast_to(row_of(proxy), (8, PAIR))
    save(keep, kernel_two, approx_out, proxies)

    for copy in kv_out:
        copy.wait()
    for own in range(many):
        parts, tops, totals = [], [], []
        for packed in [kv_send[first_unit + own]] + [
            kv_recv[step, own] for step in range(seq_size - 1)
        ]:
            packed = packed.astype(jnp.float32)
            tail = packed[SEG:]
            parts.append(packed[:SEG])
            tops.append(tail[0:1] + tail[1:2] + tail[2:3])
            totals.append(tail[3:4] + tail[4:5] + tail[5:6])
        top = tops[0]
        for other in tops[1:]:
            top = jnp.maximum(top, other)
        scales = [jnp.exp(other - top) for other in tops]
        total = sum(scale * part for scale, part in zip(scales, totals))
        kv_mean = jnp.zeros((SEG, PAIR), jnp.float32)
        for slot, (scale, part) in enumerate(zip(scales, parts)):
            share = scale / total
            shares[own, slot] = jnp.broadcast_to(share, (8, PAIR))
            kv_mean = kv_mean + join_heads(column(share)) * part
        kv_own[own] = kv_mean
        mixed[first_unit + own] = join_heads(
            mm3(split(approx[own]), split(spread_heads(kv_mean)))
        ).astype(jnp.bfloat16)
    mixed_out = passed_on(place, mixed, many, *mixed_sem)
    for copy in mixed_out:
        copy.start()
    save(kv_own, shares)

    def first_scores(unit, carry):
        seq, rows, lanes = spots(unit)
        score = mm(spread_heads(land[unit, 1]), queries[rows, lanes], NT)
        score = score.reshape(2, SEG, tokens)
        weights = jnp.exp(score - jnp.max(score, axis=1, keepdims=True))
        weights = weights / jnp.sum(weights, axis=1, keepdims=True)
        kernel_one[unit] = weights.reshape(2 * SEG, tokens)
        return carry

    lax.fori_loop(0, units, first_scores, 0, unroll=6)
    save(kernel_one)
    for copy in mixed_out:
        copy.wait()
    save(mixed)

    def combine(unit, carry):
        seq, rows, lanes = spots(unit)
        attended = mm(
            kernel_one[unit].astype(jnp.bfloat16), spread_heads(mixed[unit]), TN
        )
        branch[rows, lanes] = (attended + conv[rows, lanes]).astype(jnp.bfloat16)
        return carry

    lax.fori_loop(0, units, combine, 0, unroll=6)
    save(branch)
    for copy in saves:
        copy.wait()


def attend(
    x, bounds, weight, query_bias, value_bias, taps, batch_size, seq_size, seqs
):
    rows, width = x.shape
    tokens = rows // seqs
    units = seqs * (width // PAIR)
    many = -(-units // seq_size)
    slots = seq_size * many
    f32, bf16 = jnp.float32, jnp.bfloat16
    vmem = pl.BlockSpec(memory_space=pltpu.VMEM)
    anywhere = pl.BlockSpec(memory_space=pl.ANY)
    sems = pltpu.SemaphoreType.DMA
    shapes = (
        ((rows, width), bf16),
        ((rows, width), bf16),
        ((seqs, tokens + BLOCK, width), bf16),
        ((units, 2 * SEG, tokens), f32),
        ((units, 2 * SEG, tokens), f32),
        ((slots, 2, SEG, PAIR), bf16),
        ((slots, SEG, PAIR), bf16),
        ((rows, width), bf16),
        ((many, PAIR, PAIR), f32),
        ((many, PAIR, PAIR), f32),
        ((many, 6, 4, PAIR, PAIR), f32),
        ((many, SEG, PAIR), f32),
        ((many, seq_size, 8, PAIR), f32),
        ((many, 8, PAIR), f32),
    )
    return pl.pallas_call(
        partial(attend_kernel, batch_size, seq_size, seqs, tokens, many),
        out_shape=tuple(jax.ShapeDtypeStruct(*shape) for shape in shapes),
        in_specs=[anywhere] * 2 + [vmem] * 4,
        out_specs=tuple([anywhere] * len(shapes)),
        scratch_shapes=[
            *(pltpu.VMEM(*shape) for shape in shapes),
            pltpu.VMEM(x.shape, bf16),
            pltpu.VMEM(weight.shape, bf16),
            sems((4,)),
            sems((len(shapes),)),
            pltpu.VMEM((slots, 2, SEG, PAIR), f32),
            pltpu.VMEM((seq_size - 1, many, 2, SEG, PAIR), f32),
            pltpu.VMEM((slots, SEG + 16, PAIR), bf16),
            pltpu.VMEM((seq_size - 1, many, SEG + 16, PAIR), bf16),
            pltpu.VMEM((rows, width), f32),
            pltpu.VMEM((16, 2 * BLOCK), f32),
            pltpu.VMEM((8, width), f32),
            ((sems((seq_size - 1,)),) * 2,) * 2,
            (sems((seq_size - 1,)),) * 2,
            (sems((seq_size - 1,)),) * 2,
            (sems((seq_size - 1,)),) * 2,
            (sems((2,)),) * 2,
        ],
        compiler_params=pltpu.CompilerParams(
            collective_id=1, has_side_effects=True, vmem_limit_bytes=58 * 2**20
        ),
        name="attend",
    )(x, weight, bounds, query_bias, value_bias, taps)


def newton_backward(kernels, approx_grads, keep, tick):
    units = range(len(kernels))
    eye = jnp.where(eye_mask(PAIR), 1.0, 0.0)
    kernel_halves = [split(kernel) for kernel in kernels]
    grads = [jnp.zeros((PAIR, PAIR), jnp.float32) for _ in units]
    after = approx_grads
    for step in reversed(range(6)):
        approx = [split(keep[u, step, 0]) for u in units]
        product = [keep[u, step, 1] for u in units]
        halves = [split(p) for p in product]
        first = [split(7.0 * eye - p) for p in product]
        second = [split(keep[u, step, 2]) for u in units]
        third = [split(keep[u, step, 3]) for u in units]
        wide = [split(0.25 * a) for a in after]
        third_grad = [split(mm3(wide[u], approx[u])) for u in units]
        second_grad = [split(-mm3(third_grad[u], halves[u])) for u in units]
        first_grad = [-mm3(second_grad[u], halves[u]) for u in units]
        product_grad = [
            split(
                -mm3(second[u], third_grad[u]) - mm3(first[u], second_grad[u]) - first_grad[u]
            )
            for u in units
        ]
        grads = [grads[u] + mm3(approx[u], product_grad[u]) for u in units]
        after = [
            mm3(third[u], wide[u]) + mm3(product_grad[u], kernel_halves[u]) for u in units
        ]
        tick(f"newton{step}")
    out = []
    for u in units:
        kernel = kernels[u]
        fro = heads_sum(jnp.sum(kernel * kernel, axis=1, keepdims=True))
        fro_grad = heads_sum(jnp.sum(after[u] * kernel, axis=1, keepdims=True)) / (fro * fro)
        out.append(grads[u].T + after[u] / fro - 2.0 * kernel * fro_grad)
    return out


def tap_grads(padded_grad, padded, vec, first_row, tokens, span):
    seqs, _, width = padded.shape
    rows = lax.broadcasted_iota(jnp.int32, (BLOCK, BLOCK), 0)
    cols = lax.broadcasted_iota(jnp.int32, (BLOCK, BLOCK), 1)
    turn = jnp.where(rows + cols == BLOCK - 1, 1.0, 0.0).astype(jnp.bfloat16)

    def step(pair, carry):
        lanes = pl.ds(pl.multiple_of(pair * PAIR, PAIR), PAIR)
        total = [jnp.zeros((BLOCK, 2 * BLOCK), jnp.float32) for _ in range(2)]
        for seq in range(seqs):
            for block in range(tokens // BLOCK):
                window = padded[seq, pl.ds(block * BLOCK, 2 * BLOCK), lanes]
                grad = padded_grad[seq, pl.ds(HALO + block * BLOCK, BLOCK), lanes]
                grad = mm(turn, grad).astype(jnp.bfloat16)
                first = first_head(grad.shape)
                zero = jnp.zeros_like(grad)
                total[0] = total[0] + mm(jnp.where(first, grad, zero), window, NT)
                total[1] = total[1] + mm(jnp.where(first, zero, grad), window, NT)
        for head in range(2):
            turned = pltpu.roll(total[head], 0, 1, stride=1, stride_axis=0)
            sums = jnp.sum(turned, axis=0, keepdims=True)
            sums = pltpu.roll(sums, BLOCK + 1, 1)
            vec[pl.ds(first_row + 2 * pair + head, 1), :] = sums[:, :PAIR]
        return carry

    lax.fori_loop(*span, step, 0, unroll=2)


class Ticker:
    def __init__(self, points):
        self.live = {}
        self.points = points

    def add(self, number, generator):
        next(generator)
        self.live[number] = generator

    def step(self, number):
        try:
            next(self.live[number])
        except StopIteration:
            del self.live[number]

    def tick(self, point):
        for number in self.points.get(point, ()):
            if number in self.live:
                self.step(number)

    def drain(self, order=()):
        for number in order:
            if number in self.live:
                self.step(number)
        while self.live:
            for number in list(self.live):
                self.step(number)


POINTS = {
    "back2": (0, 1),
    "mid1": (2, 3, 1),
    "first0": (0,),
    "acc": (1,),
    "conv0": (2,),
    "conv1": (3,),
    "wait_acc": (0,),
    "value": (1, 2),
    "newton5": (0,),
    "newton3": (4,),
    "newton2": (3, 0),
    "land": (0,),
    "wait_back": (0, 1, 2, 4),
    "last": (3, 1),
    "taps0": (4, 5),
    "input2": (1,),
}
LAST = (1, 2, 5, 1, 2, "vec", 5, 3, 4, 0, 3, "vec", 2, 2, 5, 2, 4, "vec", 3, 0, 3, 4, 5, "vec", 3, 0, 0, 5, 4, 4, 4, 5, 5, 5)


class Sums:
    def __init__(self, ref):
        self.ref = ref

    def clear(self):
        self.ref[...] = jnp.zeros_like(self.ref)

    def add(self, row, array):
        here = pl.ds(row, 1)
        self.ref[here, :] = self.ref[here, :] + jnp.sum(array, axis=0, keepdims=True)


def normalize(hidden):
    centered = hidden - jnp.mean(hidden, axis=1, keepdims=True)
    inverse = lax.rsqrt(jnp.mean(centered * centered, axis=1, keepdims=True) + epsilon)
    return centered * inverse, inverse


def normalize_back(grad, normed, inverse):
    return inverse * (
        grad
        - jnp.mean(grad, axis=1, keepdims=True)
        - normed * jnp.mean(grad * normed, axis=1, keepdims=True)
    )


def row_vector(ref):
    return ref[...].reshape(1, ref.shape[0])


def back_kernel(
    batch_size, seq_size, seqs, tokens, many, plan,
    x_in, grad_out, branch_in, out_weight, up_weight, down_weight, qkv_weight,
    queries_in, keys_in, values_in, kernel_one_in, expo_in, keep_in, land_in, mixed_in,
    kernel_two_in, approx_in, kv_own_in, shares_in, proxies_in, bounds, taps,
    out_bias, first_gain, first_shift, up_bias, down_bias, second_gain, second_shift,
    layer_out, input_grad, gathered, vec,
    stage, whole, recv, slots, padded, grad_first, tap_rows, sums, up_sums, acc_send, acc_all,
    land_send, land_recv, land_all, kernel_one, mixed, land,
    load_sem, weight_sem, send_sem, recv_sem, free_sem, vec_sem, out_sem, halo_sem, mixed_sem,
    acc_sem, land_sem, land_back_sem,
):
    place = Place(batch_size, seq_size)
    rows, width = x_in.shape
    ff_blocks = down_weight.shape[0] // width
    pairs = width // PAIR
    units = seqs * pairs
    quarter = float(SEG) ** -0.25
    wait_greet = greet(
        [place.seq_peer(step) for step in range(1, seq_size)] + list(place.peers(("core", "z")))
    )

    def early_loads():
        return [
            pltpu.make_async_copy(source, target, load_sem.at[11 + index])
            for index, (source, target) in enumerate(
                ((kernel_one_in, kernel_one), (mixed_in, mixed), (land_in, land))
            )
        ]

    ticker = Ticker(POINTS)
    tick = ticker.tick
    bf16 = jnp.bfloat16

    def piece_run(number):
        piece = plan[number]
        here = pl.ds(piece.start, piece.rows)
        yield from Reduce(
            number, lambda: Place(batch_size, seq_size), piece.orders, stage.at[:, here],
            whole.at[here], recv.at[:, piece.slots], send_sem, recv_sem, free_sem, piece.rows,
        ).run()

        def outs():
            core = Place(batch_size, seq_size).at["core"]
            return (
                pltpu.make_async_copy(
                    whole.at[here], gathered.at[core, here], out_sem.at[number, 0]
                ),
                pltpu.make_async_copy(
                    stage.at[1 - core, here], gathered.at[1 - core, here], out_sem.at[number, 1]
                ),
            )

        for out in outs():
            out.start()
        yield
        for out in outs():
            out.wait()

    done = set()

    def staged(*blocks):
        done.update(blocks)
        for number, piece in enumerate(plan):
            if done.issuperset(piece.blocks) and not set(blocks).isdisjoint(piece.blocks):
                ticker.add(number, piece_run(number))

    def store_block(block, first, grad):
        at = pl.ds(pl.multiple_of(block * width + first, 16), grad.shape[0])
        grad = grad.astype(bf16)
        stage[0, at, :] = grad[:, :HALF]
        stage[1, at, :] = grad[:, HALF:]

    def store_strip(block, part, grad):
        at = pl.ds(block * width, width)
        grad = grad.astype(bf16)
        first = part * 256
        for half in range(2):
            low, high = max(first, half * HALF), min(first + 256, (half + 1) * HALF)
            if low < high:
                lanes = pl.ds(low - half * HALF, high - low)
                stage[half, at, lanes] = grad[:, low - first : high - first]

    def loop(count, step):
        def run(index, carry):
            step(index)
            return carry

        lax.fori_loop(0, count, run, 0)

    def feed_forward(
        x, branch, grads, mid_low, turned, act_turned, low, normed_one, grad_second, inverse_one, out_w, ff_w,
        act, slope, up_bias_row,
    ):
        def load(index, source, target):
            return pltpu.make_async_copy(source, target, load_sem.at[index])

        first = [load(0, out_weight, out_w), load(1, branch_in, branch), load(2, x_in, x)]
        for copy in first:
            copy.start()
        grads_load = load(3, grad_out, grads)

        def up_load(block):
            return pltpu.make_async_copy(
                up_weight.at[:, pl.ds(block * width, width)], ff_w.at[block], weight_sem.at[block]
            )

        def down_load(block):
            return pltpu.make_async_copy(
                down_weight.at[pl.ds(block * width, width)], ff_w.at[block], weight_sem.at[block]
            )

        for block in range(ff_blocks):
            up_load(block).start()
        grads_load.start()
        for copy in early_loads():
            copy.start()
        total = Sums(sums)
        total.clear()
        up_bias_row[...] = row_vector(up_bias)
        for copy in first:
            copy.wait()
        tile = 128

        def strip(index):
            return pl.ds(pl.multiple_of(index * 256, 256), 256)

        def attended(index):
            normed_one[:, strip(index)] = mm(branch[...], out_w[:, strip(index)])

        def project(index):
            here = pl.ds(pl.multiple_of(index * tile, tile), tile)
            hidden = x[here, :].astype(jnp.float32) + normed_one[here, :]
            normed, inverse = normalize(hidden + row_vector(out_bias))
            normed_one[here, :] = normed
            inverse_one[here, :] = jnp.broadcast_to(inverse, (tile, PAIR))
            mid = normed * row_vector(first_gain) + row_vector(first_shift)
            mid_low[here, :] = mid.astype(bf16)

        loop(width // 256, attended)
        loop(rows // tile, project)
        for block in range(ff_blocks):
            up_load(block).wait()

            def up(index, block=block):
                part = pl.multiple_of(index * 256, 256)
                lanes = pl.ds(block * width + part, 256)
                pre = mm(mid_low[...], ff_w[block, :, pl.ds(part, 256)])
                pre = pre + up_bias_row[:, lanes]
                half = 0.5 * (1.0 + lax.erf(pre * (0.5**0.5)))
                act[:, lanes] = (pre * half).astype(bf16)
                bell = jnp.exp(-0.5 * pre * pre) * (2.0 * math.pi) ** -0.5
                slope[:, lanes] = (half + pre * bell).astype(bf16)

            loop(width // 256, up)
            down_load(block).start()
        turned[...] = mid_low[...].T
        for block in range(ff_blocks):
            down_load(block).wait()
        grads_load.wait()

        def summed(index):
            total = mm(act[:, pl.ds(0, width)], ff_w[0, :, strip(index)])
            for block in range(1, ff_blocks):
                total = total + mm(
                    act[:, pl.ds(block * width, width)], ff_w[block, :, strip(index)]
                )
            grad_second[:, strip(index)] = total

        def down(index):
            here = pl.ds(pl.multiple_of(index * tile, tile), tile)
            mid = normed_one[here, :] * row_vector(first_gain) + row_vector(first_shift)
            normed, inverse = normalize(mid + row_vector(down_bias) + grad_second[here, :])
            grad = grads[here, :].astype(jnp.float32)
            total.add(1, grad * normed)
            total.add(2, grad)
            grads[here, :] = (
                normed * row_vector(second_gain) + row_vector(second_shift)
            ).astype(bf16)
            grad = normalize_back(grad * row_vector(second_gain), normed, inverse)
            grad_second[here, :] = grad
            grad = grad.astype(bf16)
            low[here, :] = grad
            total.add(0, grad.astype(jnp.float32))

        loop(width // 256, summed)
        loop(rows // tile, down)
        out_copy = load(4, grads, layer_out)
        out_copy.start()
        for block in range(ff_blocks):

            act_turned[...] = act[:, pl.ds(block * width, width)].T
            for part in range(width // 256):
                store_strip(block, part, mm(act_turned[...], low[:, pl.ds(part * 256, 256)]))
            if block == 0:
                wait_greet()
            staged(block)
            tick(f"down{block}")
        for block in range(ff_blocks):

            def up_back(index, block=block):
                at = pl.multiple_of(index * 256, 256)
                lanes = pl.ds(block * width + at, 256)
                grad = mm(low[...], ff_w[block, pl.ds(at, 256), :], NT)
                grad = (grad * slope[:, lanes].astype(jnp.float32)).astype(bf16)
                slope[:, lanes] = grad
                up_sums[:, lanes] = jnp.sum(grad.astype(jnp.float32), axis=0, keepdims=True)

            loop(width // 256, up_back)
            up_load(block).start()
            tick(f"back{block}")
        for block in range(ff_blocks):

            for part in range(width // 256):
                lanes = pl.ds(block * width + part * 256, 256)
                store_strip(ff_blocks + block, part, mm(turned[...], slope[:, lanes]))
            staged(ff_blocks + block)
            tick(f"up{block}")
        for block in range(ff_blocks):
            up_load(block).wait()

        def mid_sum(index):
            total = grad_second[:, strip(index)]
            for block in range(ff_blocks):
                total = total + mm(
                    slope[:, pl.ds(block * width, width)], ff_w[block, strip(index), :], NT
                )
            grad_second[:, strip(index)] = total

        def mid_back(index):
            here = pl.ds(pl.multiple_of(index * tile, tile), tile)
            grad = grad_second[here, :]
            normed = normed_one[here, :]
            total.add(4, grad * normed)
            total.add(5, grad)
            grad = normalize_back(
                grad * row_vector(first_gain), normed, inverse_one[here, pl.ds(0, 1)]
            )
            grad_first[here, :] = grad
            grad = grad.astype(bf16)
            low[here, :] = grad
            total.add(3, grad.astype(jnp.float32))

        loop(width // 256, mid_sum)
        tick("mid0")
        loop(rows // tile, mid_back)
        tick("mid1")
        for seq in range(seqs):
            padded[seq, pl.ds(HALO, tokens)] = mm(
                low[pl.ds(seq * tokens, tokens), :], out_w[...], NT
            ).astype(bf16)

        def out_grad(index):
            at = pl.multiple_of(index * 256, 256)
            store_block(2 * ff_blocks, at, mm(branch[:, pl.ds(at, 256)], low[...], TN))

        loop(width // 256, out_grad)
        staged(2 * ff_blocks)
        tick("out")
        out_copy.wait()

    narrow = pltpu.VMEM((rows, width), bf16)
    wide = pltpu.VMEM((rows, width), jnp.float32)
    hidden = pltpu.VMEM((rows, ff_blocks * width), bf16)
    pl.run_scoped(
        feed_forward,
        narrow, narrow, narrow, narrow,
        pltpu.VMEM((width, rows), bf16),
        pltpu.VMEM((width, rows), bf16),
        narrow, wide, wide,
        pltpu.VMEM((rows, PAIR), jnp.float32),
        pltpu.VMEM((width, width), bf16),
        pltpu.VMEM((ff_blocks, width, width), bf16),
        hidden, hidden,
        pltpu.VMEM((1, ff_blocks * width), jnp.float32),
    )
    first_row = (ff_blocks + 6) * pairs
    tap_row = first_row + 2 * pairs
    proxy_row = tap_row + 2 * pairs

    def attention(
        x, queries, keys, values, expo, keep, kernel_two, approx, kv_own, shares, proxies, rest, grad_qkv, turned, rows_of_weight,
    ):
        place = Place(batch_size, seq_size)
        loads = {}
        for index, (name, source, target) in enumerate(
            (
                ("queries", queries_in, queries),
                ("approx", approx_in, approx),
                ("kv_own", kv_own_in, kv_own),
                ("kernel_two", kernel_two_in, kernel_two),
                ("shares", shares_in, shares),
                ("values", values_in, values),
                ("expo", expo_in, expo),
                ("keys", keys_in, keys),
                ("keep", keep_in, keep),
                ("x", x_in, x),
                ("proxies", proxies_in, proxies),
            )
        ):
            loads[name] = pltpu.make_async_copy(source, target, load_sem.at[index])
            loads[name].start()
        zero_past(padded, tokens)
        halo = halo_copies(place, padded, tokens, *halo_sem)
        for copy in halo:
            copy.start()

        def spots(unit):
            seq, pair = lax.div(unit, pairs), lax.rem(unit, pairs)
            span = pl.ds(pl.multiple_of(seq * tokens, tokens), tokens)
            lanes = pl.ds(pl.multiple_of(pair * PAIR, PAIR), PAIR)
            return seq, span, lanes

        def paced(step, name, chunks=1):
            size = -(-units // chunks)
            for chunk, first in enumerate(range(0, units, size)):
                lax.fori_loop(first, min(first + size, units), step, 0, unroll=4)
                tick(f"{name}{chunk}")

        def mixed_parts(unit, carry):
            seq, span, lanes = spots(unit)
            grad = padded[seq, pl.ds(HALO, tokens), lanes]
            land_send[unit, 0] = join_heads(mm(kernel_one[unit].astype(bf16), grad)).astype(bf16)
            return carry

        for copy in early_loads():
            copy.wait()
        lax.fori_loop(0, units, mixed_parts, 0, unroll=6)
        for unit in range(units, seq_size * many):
            land_send[unit] = jnp.ones_like(land_send[unit])
        mixed_out = shared_out(
            place, land_send.at[:, 0], land_recv.at[:, :, 0], many, *mixed_sem
        )
        for copy in mixed_out:
            copy.start()
        tick("start")

        def first_grads(unit, carry):
            seq, span, lanes = spots(unit)
            weights = kernel_one[unit]
            grad = mm(spread_heads(mixed[unit]), padded[seq, pl.ds(HALO, tokens), lanes], NT)
            both = (weights * grad).reshape(2, SEG, tokens)
            both = jnp.broadcast_to(jnp.sum(both, axis=1, keepdims=True), both.shape)
            score_grad = (weights * (grad - both.reshape(2 * SEG, tokens))).astype(bf16)
            land_send[unit, 1] = join_heads(mm(score_grad, queries[span, lanes])).astype(bf16)
            rest[0, span, lanes] = mm(score_grad, spread_heads(land[unit, 1]), TN)
            return carry

        loads["queries"].wait()
        paced(first_grads, "first", 3)
        tick("wait_mixed")
        for copy in mixed_out:
            copy.wait()
        first_unit = place.seq * many
        for name in ("approx", "kv_own", "kernel_two", "shares"):
            loads[name].wait()
        kernels, approx_grads = [], []
        for own in range(many):
            total = land_send[first_unit + own, 0].astype(jnp.float32)
            for step in range(seq_size - 1):
                total = total + land_recv[step, own, 0].astype(jnp.float32)
            total = split(spread_heads(total))
            kv_mean = kv_own[own]
            kv_grad = join_heads(mm3(split(approx[own]), total, TN))
            approx_grads.append(mm3(split(spread_heads(kv_mean)), total, NT))
            kernels.append(kernel_two[own])
            dots = kv_grad * kv_mean
            first = first_head(dots.shape)
            dots = jnp.concatenate(
                [
                    jnp.sum(jnp.where(first, dots, 0.0), axis=1, keepdims=True),
                    jnp.sum(jnp.where(first, 0.0, dots), axis=1, keepdims=True),
                ],
                axis=0,
            )
            dots = row_of(dots)
            for slot in range(seq_size):
                share = shares[own, slot, pl.ds(0, 1), :]
                scaled = (kv_grad * join_heads(column(share))).astype(bf16)
                high, low = split(-dots * share)
                tail = jnp.concatenate([high, low, jnp.zeros((14, PAIR), bf16)], axis=0)
                acc_send[slot, own] = jnp.concatenate([scaled, tail], axis=0)
        acc_out = []
        for step in range(1, seq_size):
            acc_out.append(
                pltpu.make_async_remote_copy(
                    src_ref=acc_send.at[seq_size - step],
                    dst_ref=acc_all.at[pl.ds(first_unit, many)],
                    send_sem=acc_sem[0].at[step - 1],
                    recv_sem=acc_sem[1].at[step - 1],
                    device_id=place.seq_peer(step),
                    device_id_type=MESH_IDS,
                )
            )
        for copy in acc_out:
            copy.start()
        for own in range(many):
            acc_all[first_unit + own] = acc_send[0, own]
        tick("acc")
        for copy in halo:
            copy.wait()
        trim_halo(place, padded, tokens)
        tap_rows[...] = turned_taps(taps)
        for part in range(2):
            span = (part * pairs // 2, (part + 1) * pairs // 2)
            conv_rows(padded, tap_rows, rest.at[2], tokens, span)
            tick(f"conv{part}")
        loads["values"].wait()
        loads["expo"].wait()
        loads["keys"].wait()
        tick("wait_acc")
        for copy in acc_out:
            copy.wait()

        def third_grads(unit, carry):
            seq, span, lanes = spots(unit)
            packed = acc_all[unit]
            acc = spread_heads(packed[:SEG])
            tail = packed[SEG:].astype(jnp.float32)
            part = mm(acc, values[seq, pl.ds(HALO, tokens), lanes], NT)
            weights = expo[unit]
            score_grad = (weights * (part + column(tail[0:1] + tail[1:2]))).astype(bf16)
            land_send[unit, 0] = join_heads(mm(score_grad, keys[span, lanes])).astype(bf16)
            rest[1, span, lanes] = mm(score_grad, spread_heads(land[unit, 0]), TN)
            value_grad = mm(weights.astype(bf16), acc, TN) + rest[2, span, lanes]
            valid = positions(place, tokens, 0) < length_of(bounds, seq)
            grad_qkv[2, span, lanes] = jnp.where(valid, value_grad, 0.0).astype(bf16)
            return carry

        paced(third_grads, "third", 3)
        land_out = shared_out(place, land_send, land_recv, many, *land_sem)
        for copy in land_out:
            copy.start()
        loads["x"].wait()
        turned[...] = x[...].T

        def weight_grad(third, block):
            def step(index):
                at = pl.multiple_of(index * 256, 256)
                store_block(block, at, mm(turned[pl.ds(at, 256), :], grad_qkv[third]))

            loop(width // 256, step)

        def bias_grad(third, row):
            for pair in range(pairs):
                cols = grad_qkv[third, :, pl.ds(pair * PAIR, PAIR)].astype(jnp.float32)
                vec[pl.ds(row + pair, 1), :] = jnp.sum(cols, axis=0, keepdims=True)

        weight_grad(2, 2 * ff_blocks + 1)
        staged(2 * ff_blocks + 1)
        tick("value")
        loads["keep"].wait()
        loads["proxies"].wait()
        kernel_grads = newton_backward(kernels, approx_grads, keep, tick)
        extra = []
        for own in range(many):
            kernel, grad = kernels[own], kernel_grads[own]
            score_grad = split(
                kernel * (grad - jnp.sum(kernel * grad, axis=1, keepdims=True))
            )
            both = land[first_unit + own]
            left, right = spread_heads(both[0]), spread_heads(both[1])
            extra.append(
                (
                    join_heads(mm(score_grad[0], right) + mm(score_grad[1], right)),
                    join_heads(mm(score_grad[0], left, TN) + mm(score_grad[1], left, TN)),
                )
            )
        tick("wait_land")
        for copy in land_out:
            copy.wait()
        for own in range(many):
            unit = first_unit + own
            low, high = segment_edges(bounds, jnp.minimum(lax.div(unit, pairs), seqs - 1))
            for slot in range(2):
                total = land_send[unit, slot].astype(jnp.float32) + extra[own][slot]
                for step in range(seq_size - 1):
                    total = total + land_recv[step, own, slot].astype(jnp.float32)
                land_all[unit, slot] = (total / (high - low)).astype(bf16)
        land_back = passed_on(place, land_all, many, *land_back_sem)
        for copy in land_back:
            copy.start()
        tick("land")
        tick("wait_back")
        for copy in land_back:
            copy.wait()
        for seq in range(seqs):
            member = member_of(place, bounds, seq, tokens)
            span = pl.ds(seq * tokens, tokens)
            for pair in range(pairs):
                lanes = pl.ds(pair * PAIR, PAIR)
                both = land_all[seq * pairs + pair]
                for slot in range(2):
                    grad = (mm(member, both[slot], TN) + rest[slot, span, lanes]) * quarter
                    grad_qkv[slot, span, lanes] = grad.astype(bf16)
        tick("grads")
        weight_grad(0, 2 * ff_blocks + 2)
        weight_grad(1, 2 * ff_blocks + 3)
        staged(2 * ff_blocks + 2, 2 * ff_blocks + 3)
        tick("last")
        vec[...] = jnp.zeros_like(vec)
        for part in range(ff_blocks * pairs):
            vec[pl.ds(part, 1), :] = up_sums[:, pl.ds(part * PAIR, PAIR)]
        for row in range(6):
            for part in range(pairs):
                vec[pl.ds((ff_blocks + row) * pairs + part, 1), :] = sums[
                    pl.ds(row, 1), pl.ds(part * PAIR, PAIR)
                ]
        for own in range(many):
            unit = first_unit + own
            row = pl.ds(proxy_row + lax.rem(unit, pairs), 1)
            vec[row, :] = vec[row, :] + jnp.where(
                unit < units, proxies[own, pl.ds(0, 1), :], 0.0
            )
        bias_grad(0, first_row)
        bias_grad(2, first_row + pairs)
        for part in range(3):
            span = (part * pairs // 3, (part + 1) * pairs // 3)
            tap_grads(padded, values, vec, tap_row, tokens, span)
            tick(f"taps{part}")
        ticker.add("vec", vec_reduce(place, vec, slots, *vec_sem))

        def weight_load(tile):
            return pltpu.make_async_copy(
                qkv_weight.at[pl.ds(tile * PAIR, PAIR)],
                rows_of_weight.at[tile % 2],
                weight_sem.at[tile % 2],
            )

        weight_load(0).start()
        for tile in range(pairs):
            if tile + 1 < pairs:
                weight_load(tile + 1).start()
            weight_load(tile).wait()
            lanes = pl.ds(tile * PAIR, PAIR)
            total = grad_first[:, lanes]
            for third in range(3):
                total = total + mm(
                    grad_qkv[third], rows_of_weight[tile % 2, :, pl.ds(third * width, width)], NT
                )
            x[:, lanes] = total.astype(bf16)
            tick(f"input{tile}")
        out_copy = pltpu.make_async_copy(x, input_grad, load_sem.at[0])
        out_copy.start()
        ticker.drain(LAST)
        out_copy.wait()

    pl.run_scoped(
        attention,
        narrow, narrow, narrow,
        pltpu.VMEM(values_in.shape, bf16),
        pltpu.VMEM(expo_in.shape, jnp.float32),
        pltpu.VMEM(keep_in.shape, jnp.float32),
        *(
            pltpu.VMEM(ref.shape, jnp.float32)
            for ref in (kernel_two_in, approx_in, kv_own_in, shares_in, proxies_in)
        ),
        pltpu.VMEM((2 + 1, rows, width), jnp.float32),
        pltpu.VMEM((3, rows, width), bf16),
        pltpu.VMEM((width, rows), bf16),
        pltpu.VMEM((2, PAIR, 3 * width), bf16),
    )


Z_FIRST = (0,)


class Piece:
    def __init__(self, blocks, start, rows, orders, slots):
        self.blocks, self.start, self.rows, self.orders, self.slots = (
            blocks, start, rows, orders, slots,
        )


def make_plan(sizes, block_count, width):
    split_rows = 16 * sizes["x"] * sizes["y"] * sizes["z"]
    orders = (("x", "y", "z"), ("y", "x", "z"))
    z_first = (("z0", "z1", "x", "y"), ("z0", "z1", "y", "x"))
    if 2 * width % (2 * split_rows) == 0:
        counts = [2] * (block_count // 2)
    else:
        orders = orders[:1]
        z_first = z_first[:1]
        counts = [8, block_count - 8] if 8 * width % split_rows == 0 else [block_count]
    plan, block, slot = [], 0, 0
    for count in counts:
        rows = -(-count * width // (len(orders) * split_rows)) * len(orders) * split_rows
        own = z_first if len(plan) in Z_FIRST else orders
        need = Reduce.slots(sizes, own, rows)
        plan.append(
            Piece(list(range(block, block + count)), block * width, rows, own, pl.ds(slot, need))
        )
        block += count
        slot += need
    return plan, slot


def layer_back(
    x, grad_out, branch, out_weight, up_weight, down_weight, qkv_weight, saved, bounds, taps,
    vectors, batch_size, seq_size, seqs,
):
    (
        queries, keys, values, kernel_one, expo, land, mixed, _, kernel_two, approx, keep,
        kv_own, shares, proxies,
    ) = saved
    rows, width = x.shape
    tokens = rows // seqs
    pairs = width // PAIR
    own = -(-seqs * pairs // seq_size)
    owned = seq_size * own
    sizes = axis_sizes(batch_size, seq_size)
    ff_blocks = down_weight.shape[0] // width
    plan, slot_rows = make_plan(sizes, 2 * ff_blocks + 4, width)
    pieces, stage_rows = len(plan), plan[-1].start + plan[-1].rows
    parts = len(plan[0].orders)
    copies = max(Reduce.copies(sizes, piece.orders) for piece in plan)
    vec_axes = ("core", "x", "y", "z")
    vec_steps = sum(sizes[axis] - 1 for axis in vec_axes)
    vec_shape = (-(-((ff_blocks + 11) * pairs) // 8) * 8, PAIR)
    f32, bf16 = jnp.float32, jnp.bfloat16
    vmem = pl.BlockSpec(memory_space=pltpu.VMEM)
    anywhere = pl.BlockSpec(memory_space=pl.ANY)
    sems = pltpu.SemaphoreType.DMA
    pair_sems = (sems((seq_size - 1,)),) * 2
    return pl.pallas_call(
        partial(back_kernel, batch_size, seq_size, seqs, tokens, own, plan),
        out_shape=(
            jax.ShapeDtypeStruct((rows, width), bf16),
            jax.ShapeDtypeStruct((rows, width), bf16),
            jax.ShapeDtypeStruct((2, stage_rows, HALF), bf16),
            jax.ShapeDtypeStruct(vec_shape, f32),
        ),
        in_specs=[anywhere] * 20 + [vmem] * (2 + len(vectors)),
        out_specs=(anywhere, anywhere, anywhere, vmem),
        scratch_shapes=[
            pltpu.VMEM((2, stage_rows, HALF), bf16),
            pltpu.VMEM((stage_rows, HALF), bf16),
            pltpu.VMEM((parts, slot_rows, HALF), bf16),
            pltpu.VMEM((sum(sizes[axis] for axis in vec_axes), *vec_shape), f32),
            pltpu.VMEM(values.shape, bf16),
            pltpu.VMEM((rows, width), f32),
            pltpu.VMEM((16, 2 * BLOCK), f32),
            pltpu.VMEM((8, width), f32),
            pltpu.VMEM((1, ff_blocks * width), f32),
            pltpu.VMEM((seq_size, own, SEG + 16, PAIR), bf16),
            pltpu.VMEM((owned, SEG + 16, PAIR), bf16),
            pltpu.VMEM((owned, 2, SEG, PAIR), bf16),
            pltpu.VMEM((seq_size - 1, own, 2, SEG, PAIR), bf16),
            pltpu.VMEM((owned, 2, SEG, PAIR), bf16),
            pltpu.VMEM(kernel_one.shape, f32),
            pltpu.VMEM(mixed.shape, bf16),
            pltpu.VMEM(land.shape, bf16),
            sems((14,)),
            sems((ff_blocks,)),
            sems((pieces, copies)),
            sems((pieces, copies)),
            pltpu.SemaphoreType.REGULAR((pieces,)),
            (sems((vec_steps,)),) * 2,
            sems((pieces, 2)),
            (sems((2,)),) * 2,
            pair_sems,
            pair_sems,
            pair_sems,
            pair_sems,
        ],
        compiler_params=pltpu.CompilerParams(
            collective_id=0, has_side_effects=True, vmem_limit_bytes=63 * 2**20
        ),
        name="layer_back",
    )(
        x, grad_out, branch, out_weight, up_weight, down_weight, qkv_weight,
        queries, keys, values, kernel_one, expo, keep, land, mixed, kernel_two, approx, kv_own,
        shares, proxies, bounds, taps, *vectors,
    )


def finish_kernel(
    heads, scale, gathered, vec, layer_in, input_in,
    layer_out, input_grad, qkv_grad, query_bias_grad, value_bias_grad, tap_grad, out_grad,
    out_bias_grad, first_gain_grad, first_shift_grad, up_grad, up_bias_grad, down_grad,
    down_bias_grad, second_gain_grad, second_shift_grad, condition,
    narrow, wide, rows_through, in_sem, out_sem, pass_sem,
):
    width = down_grad.shape[1]
    pairs = width // PAIR
    blocks = down_grad.shape[0] // width
    spots = [(down_grad, block * width, 0) for block in range(blocks)]
    spots += [(up_grad, 0, block * width) for block in range(blocks)]
    spots += [(out_grad, 0, 0), (qkv_grad, 0, 2 * width), (qkv_grad, 0, 0), (qkv_grad, 0, width)]
    taken = [
        pltpu.make_async_copy(source, rows_through.at[index], pass_sem.at[index])
        for index, source in enumerate((layer_in, input_in))
    ]
    passed = [
        pltpu.make_async_copy(rows_through.at[index], target, pass_sem.at[index])
        for index, target in enumerate((layer_out, input_grad))
    ]
    slots, rows, _ = wide.shape
    tiles = [
        (target, row + part * rows, col, block * width + part * rows)
        for block, (target, row, col) in enumerate(spots)
        for part in range(width // rows)
    ]

    def fetch(index):
        return pltpu.make_async_copy(
            gathered.at[:, pl.ds(tiles[index][3], rows)],
            narrow.at[index % slots],
            in_sem.at[index % slots],
        )

    def put(index):
        target, row, col, _ = tiles[index]
        return pltpu.make_async_copy(
            wide.at[index % slots],
            target.at[pl.ds(row, rows), pl.ds(col, width)],
            out_sem.at[index % slots],
        )

    for index in range(slots):
        fetch(index).start()
    for copy in taken:
        copy.start()
    row = 0
    for target in (
        up_bias_grad, down_bias_grad, second_gain_grad, second_shift_grad, out_bias_grad,
        first_gain_grad, first_shift_grad, query_bias_grad, value_bias_grad,
    ):
        count = target.shape[0] // PAIR
        target[...] = vec[pl.ds(row, count), :].reshape(target.shape)
        row += count
    tap_grad[...] = vec[pl.ds(row, heads), pl.ds(0, tap_grad.shape[1])]
    proxy = vec[pl.ds(row + heads, pairs), :] * scale
    lanes = lax.broadcasted_iota(jnp.int32, (1, PAIR), 1)
    means = jnp.zeros((1, PAIR), jnp.float32)
    for pair in range(pairs):
        for head in range(2):
            value = proxy[pair : pair + 1, head * SEG : head * SEG + 1]
            means = means + jnp.where(lanes == 2 * pair + head, value, 0.0)
    condition[...] = means[:, :heads].reshape(heads)
    for copy in taken:
        copy.wait()
    for copy in passed:
        copy.start()
    for index in range(len(tiles)):
        slot = index % slots
        fetch(index).wait()
        if index >= slots:
            put(index - slots).wait()
        for half in range(2):
            wide[slot, :, pl.ds(half * HALF, HALF)] = narrow[slot, half].astype(jnp.float32)
        put(index).start()
        if index + slots < len(tiles):
            fetch(index + slots).start()
    for index in range(len(tiles) - slots, len(tiles)):
        put(index).wait()
    for copy in passed:
        copy.wait()


def finish(gathered, vec, layer_out, input_grad, shapes, scale):
    width = layer_out.shape[1]
    any_spec = pl.BlockSpec(memory_space=pl.ANY)
    vmem = pl.BlockSpec(memory_space=pltpu.VMEM)
    outs = [jax.ShapeDtypeStruct(shape, jnp.bfloat16) for shape in (layer_out.shape,) * 2]
    outs += [jax.ShapeDtypeStruct(shape, jnp.float32) for shape in shapes]
    return pl.pallas_call(
        partial(finish_kernel, shapes[3][0], scale),
        out_shape=tuple(outs),
        in_specs=[any_spec, vmem, any_spec, any_spec],
        out_specs=tuple(
            any_spec if out.shape[0] * math.prod(out.shape[1:]) >= width * width // 2 else vmem
            for out in outs
        ),
        scratch_shapes=[
            pltpu.VMEM((SLOTS, 2, FINISH_ROWS, HALF), jnp.bfloat16),
            pltpu.VMEM((SLOTS, FINISH_ROWS, width), jnp.float32),
            pltpu.VMEM((2, *layer_out.shape), jnp.bfloat16),
            pltpu.SemaphoreType.DMA((SLOTS,)),
            pltpu.SemaphoreType.DMA((SLOTS,)),
            pltpu.SemaphoreType.DMA((2,)),
        ],
        compiler_params=pltpu.CompilerParams(vmem_limit_bytes=62 * 2**20),
        name="finish",
    )(gathered, vec, layer_out, input_grad)


SLOTS = 4
FINISH_ROWS = 768


def body(
    hidden_in,
    seg_bounds,
    qkv_weight,
    query_bias,
    value_bias,
    conv_taps,
    out_weight,
    out_bias,
    first_gain,
    first_shift,
    up_weight,
    up_bias,
    down_weight,
    down_bias,
    second_gain,
    second_shift,
    grad_out,
):
    seq_count, tok_count, model_width = hidden_in.shape
    head_count = conv_taps.shape[0]
    row_total = seq_count * tok_count
    batch_size, seq_size = lax.axis_size("batch"), lax.axis_size("seq")
    input_rows = hidden_in.reshape(row_total, model_width)
    saved = attend(
        input_rows, seg_bounds, qkv_weight, query_bias, value_bias, conv_taps,
        batch_size, seq_size, seq_count,
    )
    layer_out, input_grad, gathered, vec = layer_back(
        input_rows,
        grad_out.reshape(row_total, model_width),
        saved[7],
        out_weight,
        up_weight,
        down_weight,
        qkv_weight,
        saved,
        seg_bounds,
        conv_taps,
        (out_bias, first_gain, first_shift, up_bias, down_bias, second_gain, second_shift),
        batch_size,
        seq_size,
        seq_count,
    )

    shapes = (
        qkv_weight.shape,
        query_bias.shape,
        value_bias.shape,
        conv_taps.shape,
        out_weight.shape,
        out_bias.shape,
        first_gain.shape,
        first_shift.shape,
        up_weight.shape,
        up_bias.shape,
        down_weight.shape,
        down_bias.shape,
        second_gain.shape,
        second_shift.shape,
        (head_count,),
    )
    layer_out, input_grad, *grads = finish(
        gathered, vec, layer_out, input_grad, shapes, 1.0 / (batch_size * seq_count)
    )
    return (
        layer_out.reshape(hidden_in.shape),
        input_grad.reshape(hidden_in.shape),
        *grads,
    )


def solution(mesh):
    placed = (
        P("batch", "seq", None),
        P("batch", None),
        P(),
        P(),
        P(),
        P(),
        P(),
        P(),
        P(),
        P(),
        P(),
        P(),
        P(),
        P(),
        P(),
        P(),
        P("batch", "seq", None),
    )
    return jax.shard_map(
        body,
        mesh=mesh,
        in_specs=placed,
        out_specs=(
            P("batch", "seq", None),
            P("batch", "seq", None),
            P(),
            P(),
            P(),
            P(),
            P(),
            P(),
            P(),
            P(),
            P(),
            P(),
            P(),
            P(),
            P(),
            P(),
            P(),
        ),
        check_vma=False,
    )
```
